128 devices in a mesh: expert: 16 (over z, x), shard: 8 (over y, core).
Axes of the slice: x: 4, y: 4, z: 4, core: 2. Of those that a mesh axis runs over, the one named last changes fastest.
Arguments:
- block_input: bfloat16 [16384, 2048], P(('expert', 'shard')), may hold values from -6 to 6
- out_grad: bfloat16 [16384, 2048], P(('expert', 'shard')), may hold values from -6 to 6
- norm1_gain: bfloat16 [2048], replicated, may hold values from 0.5 to 1.5
- w_query: bfloat16 [2048, 4096], P(None, 'shard'), may hold values from -0.125 to 0.125
- w_key: bfloat16 [2048, 512], P(None, 'shard'), may hold values from -0.125 to 0.125
- w_value: bfloat16 [2048, 512], P(None, 'shard'), may hold values from -0.125 to 0.125
- query_gain: bfloat16 [128], replicated, may hold values from 0.25 to 1.75
- key_gain: bfloat16 [128], replicated, may hold values from 0.25 to 1.75
- w_out: bfloat16 [4096, 2048], P('shard'), may hold values from -0.375 to 0.375
- norm2_gain: bfloat16 [2048], replicated, may hold values from 0.5 to 1.5
- w_router: bfloat16 [2048, 128], replicated, may hold values from -0.0625 to 0.0625
- w_gate: bfloat16 [128, 2048, 768], P(('expert', 'shard')), may hold values from -0.125 to 0.125
- w_up: bfloat16 [128, 2048, 768], P(('expert', 'shard')), may hold values from -0.125 to 0.125
- w_down: bfloat16 [128, 768, 2048], P(('expert', 'shard')), may hold values from -0.4375 to 0.4375
- seq_lengths: int32 [16, 4], P('expert'), may hold values from 1 to 768, 1024 in all within a row
- token_places: int32 [16, 1024], P('expert'), may hold values from 0 to 1023, each once within a row
- expert_routes: int32 [16384, 4], P(('expert', 'shard')), may hold values from 0 to 127, all different within a row; in each aligned block of 128 rows (0 to 127, 128 to 255, ...) at most 5 rows name the same one
Outputs:
- result: bfloat16 [16384, 2048], P(('expert', 'shard'))
- grad_input: float32 [16384, 2048], P(('expert', 'shard'))
- grad_norm1_gain: float32 [2048], replicated
- grad_w_query: float32 [2048, 4096], P(None, 'shard')
- grad_w_key: float32 [2048, 512], P(None, 'shard')
- grad_w_value: float32 [2048, 512], P(None, 'shard')
- grad_query_gain: float32 [128], replicated
- grad_key_gain: float32 [128], replicated
- grad_w_out: float32 [4096, 2048], P('shard')
- grad_norm2_gain: float32 [2048], replicated
- grad_w_router: float32 [2048, 128], replicated
- grad_w_gate: float32 [128, 2048, 768], P(('expert', 'shard'))
- grad_w_up: float32 [128, 2048, 768], P(('expert', 'shard'))
- grad_w_down: float32 [128, 768, 2048], P(('expert', 'shard'))
The draws below stay inside these ranges and needn't reach their ends.
Inputs may be any that keep to these rules, and one draw needn't show every extreme that they name: `seq_lengths`: each group's 4 lengths sum to 1024, and the longest is exactly 768. `token_places`: each row is a permutation of the 1024 places of its group. `expert_routes`: each token names 4 different experts; among the rows of one device no expert is named more than 5 times, a bound that some block reaches.
All inputs are finite; a program needn't handle non-finite values.
Results may differ from the reference program's by a relative error of at most 0.025.
Values may be sent and summed in bfloat16 or wider, within the bound.
No kernel may reach another device: no remote copies, remote signals or barrier semaphores. Data moves between devices by JAX's collectives and lax.ppermute only.
A program may use at most 192 MiB of HBM per device.

```python
import math
import jax
import jax.numpy as jnp
import numpy as np
from jax import lax

D = 2048
HEADS = 32
KV_HEADS = 4
HEAD = 128
F = 768
TOK_DEV = 128
TOP = 4
SEQS = 4
EXPERTS = 128
GROUPS = 16
GROUP_TOK = 1024
TOKENS = 16384
MAXLEN = 768
CAP = 5
QW = 4096
KVW = 512
N_EXPERT = 16
N_SHARD = 8


def block_levels(rng, dims, split, least, top_value):
    loudness = 1.0
    for position, shards_of in split:
        steps = jax.random.uniform(jax.random.fold_in(jax.random.fold_in(rng, 6), position), (shards_of,), jnp.float32, least / len(split), top_value / len(split))
        loudness = loudness * jnp.repeat(jnp.exp(steps), dims[position] // shards_of).reshape((-1,) + (1,) * (len(dims) - 1 - position))
    return loudness


def split_up(count, total, bound, lean):
    portions = [(1 << 20) // math.isqrt(standing ** lean) + 1 for standing in range(2, count + 1)]
    spare, holding = total - bound - (count - 1), [1] * (count - 1)
    while spare > 0:
        candidates = [i for i in range(count - 1) if holding[i] < bound]
        mass, budget = sum([portions[i] for i in candidates]), spare
        for i in candidates:
            more = min(bound - holding[i], max(1, budget * portions[i] // mass), spare)
            holding[i] = holding[i] + more
            spare = spare - more
    return np.array([bound] + holding)


def ragged_sizes(stream_key, count, total, limit, skew):
    if count == 2:
        one = jax.random.randint(stream_key, (), max(1, total - limit), min(limit, total - 1) + 1)
        return jnp.stack([one, total - one])
    tallies = jnp.asarray(split_up(count, total, limit, skew), jnp.int32)
    couples = (count - 1) // 2
    donor, sink = tallies[1:1 + 2 * couples:2], tallies[2:2 + 2 * couples:2]
    room = jnp.minimum(donor - 1, limit - sink)
    moved = jax.random.randint(jax.random.fold_in(stream_key, 1), (couples,), 0, 1 << 20) % (room + 1)
    tallies = tallies.at[1:1 + 2 * couples:2].set(donor - moved).at[2:2 + 2 * couples:2].set(sink + moved)
    return tallies[jax.random.permutation(jax.random.fold_in(stream_key, 2), count)]


def shared_out(stream_key, own, number, rows, amount, top, reach, lean):
    ranking = jax.random.permutation(stream_key, amount)
    heavy_load, ordinary = shares(amount, rows * top, reach, lean, True), shares(amount, rows * top, reach, lean, False)
    places = jnp.arange(amount)

    def named(lengths, rotation):
        used = int((lengths > 0).sum())
        fixed = max(1, used // 4)
        shifted = fixed + (places - fixed + rotation * (used - fixed)) % max(1, amount - fixed)
        return jnp.zeros((amount,), jnp.int32).at[ranking[jnp.where(places < fixed, places, shifted)]].set(jnp.asarray(lengths, jnp.int32))

    lengths = jnp.where(number % 4 == 0, named(heavy_load, number // 4), named(ordinary, number - number // 4 - 1))
    mixed = jax.random.permutation(jax.random.fold_in(own, 3), amount)
    source_of, sink = mixed[0:amount // 2 * 2:2], mixed[1:amount // 2 * 2:2]
    room = jnp.minimum(lengths[source_of] - 1, reach - lengths[sink]) // 2
    room = jnp.where((source_of == ranking[0]) | (sink == ranking[0]) | (lengths[sink] == 0), 0, jnp.maximum(room, 0))
    shifted = jax.random.randint(jax.random.fold_in(own, 4), (amount // 2,), 0, 1 << 20) % (room + 1)
    lengths = lengths.at[source_of].add(-shifted).at[sink].add(shifted)
    labels = jnp.searchsorted(jnp.cumsum(lengths), jnp.arange(rows * top), side="right").astype(jnp.int32)
    grid = labels.reshape(top, rows).T
    grid = grid[jax.random.permutation(jax.random.fold_in(own, 1), rows)]
    rotation = jax.random.randint(jax.random.fold_in(own, 2), (rows, 1), 0, top)
    return jnp.take_along_axis(grid, (jnp.arange(top)[None, :] + rotation) % top, axis=1)


def shares(number_of, total, limit, lean, full):
    weights = [(1 << 20) // math.isqrt(grade ** lean) + 1 for grade in range(1, number_of + 1)]
    largest = limit if full else min(limit, max(-(-total // number_of), total * weights[0] // sum(weights)))
    least = 1 if total - largest >= number_of - 1 else 0
    holding, surplus = [largest] + [least] * (number_of - 1), total - largest - least * (number_of - 1)
    while surplus > 0:
        movable = [i for i in range(1, number_of) if holding[i] < largest] or [i for i in range(1, number_of) if holding[i] < limit]
        whole, budget = sum([weights[i] for i in movable]), surplus
        for i in movable:
            extra = min(limit - holding[i], max(1, budget * weights[i] // whole), surplus)
            holding[i] = holding[i] + extra
            surplus = surplus - extra
    return np.array(holding)


def centred(stream_key, dims, spread, bound, cuts=(), kind=jnp.bfloat16):
    loudness = block_levels(stream_key, dims, cuts, -0.22, 0.18) if cuts else 1.0
    values = jax.random.normal(stream_key, dims, jnp.float32) * spread * loudness
    return jnp.minimum(jnp.maximum(values, -bound), bound).astype(kind)


def setup_inputs(seed: int = 0) -> dict:
    splits = jax.random.split(jax.random.key(seed), 18)
    block_input = centred(splits[0], (TOKENS, D), 1.0, 6.0, ((0, 128),))
    out_grad = centred(splits[1], (TOKENS, D), 1.0, 6.0, ((0, 128),))
    norm1_gain = jnp.clip(1.0 + 0.1 * jax.random.normal(splits[2], (D,), jnp.float32), 0.5, 1.5).astype(jnp.bfloat16)
    w_query = centred(splits[3], (D, QW), D ** -0.5, 0.125, ((1, 8),))
    w_key = centred(splits[4], (D, KVW), D ** -0.5, 0.125, ((1, 8),))
    w_value = centred(splits[5], (D, KVW), D ** -0.5, 0.125, ((1, 8),))
    query_gain = jnp.clip(1.0 + 0.15 * jax.random.normal(splits[6], (HEAD,), jnp.float32), 0.25, 1.75).astype(jnp.bfloat16)
    key_gain = jnp.clip(1.0 + 0.15 * jax.random.normal(splits[7], (HEAD,), jnp.float32), 0.25, 1.75).astype(jnp.bfloat16)
    w_out = centred(splits[8], (QW, D), (QW // 16) ** -0.5, 0.375, ((0, 8),))
    norm2_gain = jnp.clip(1.0 + 0.1 * jax.random.normal(splits[9], (D,), jnp.float32), 0.5, 1.5).astype(jnp.bfloat16)
    w_router = centred(splits[10], (D, EXPERTS), (4 * D) ** -0.5, 0.0625)
    w_gate = centred(splits[11], (EXPERTS, D, F), D ** -0.5, 0.125, ((0, 128),))
    w_up = centred(splits[12], (EXPERTS, D, F), D ** -0.5, 0.125, ((0, 128),))
    w_down = centred(splits[13], (EXPERTS, F, D), (F // 4) ** -0.5, 0.4375, ((0, 128),))
    seq_lengths = jax.vmap(lambda own: ragged_sizes(own, SEQS, GROUP_TOK, MAXLEN, 2))(jax.random.split(splits[14], GROUPS)).reshape((GROUPS, SEQS)).astype(jnp.int32)
    token_places = jax.vmap(lambda own: jax.random.permutation(own, GROUP_TOK))(jax.random.split(splits[15], GROUPS)).reshape((GROUPS, GROUP_TOK)).astype(jnp.int32)
    expert_routes_keys = jax.random.split(jax.random.fold_in(splits[16], 1), TOKENS // TOK_DEV)
    expert_routes_turns = jax.random.permutation(jax.random.fold_in(splits[16], 3), TOKENS // TOK_DEV)
    expert_routes = jax.vmap(lambda own, number: shared_out(jax.random.fold_in(splits[16], 2), own, number, TOK_DEV, EXPERTS, TOP, CAP, 2))(expert_routes_keys, expert_routes_turns).reshape((TOKENS, TOP))
    return {"block_input": block_input, "out_grad": out_grad, "norm1_gain": norm1_gain, "w_query": w_query, "w_key": w_key, "w_value": w_value, "query_gain": query_gain, "key_gain": key_gain, "w_out": w_out, "norm2_gain": norm2_gain, "w_router": w_router, "w_gate": w_gate, "w_up": w_up, "w_down": w_down, "seq_lengths": seq_lengths, "token_places": token_places, "expert_routes": expert_routes}


norm_eps = 1e-06
rope_base = 1000000.0
masked_score = -1e+30
highest = lax.Precision.HIGHEST

@jax.custom_vjp
def low(v):
    return lax.optimization_barrier(v.astype(jnp.bfloat16)).astype(jnp.float32)

@jax.custom_vjp
def low_back(v):
    return v

def low_keep(v):
    return (low(v), None)

def low_pass(kept, grad):
    return (grad,)

def back_keep(v):
    return (v, None)

def back_low(kept, grad):
    return (low(grad),)
low.defvjp(low_keep, low_pass)
low_back.defvjp(back_keep, back_low)

def rms_gain(values, gain):
    return values * lax.rsqrt(lax.optimization_barrier(jnp.mean(values * values, axis=-1, keepdims=True)) + norm_eps) * gain

def rotate(values, cosine, sine):
    half_size = values.shape[-1] // 2
    turned = jnp.concatenate([-values[..., half_size:], values[..., :half_size]], axis=-1)
    return values * cosine + turned * sine

def rope_tables(positions, head_size):
    inverse_freq = rope_base ** (-jnp.arange(0, head_size, 2).astype(jnp.float32) / head_size)
    angles = positions.astype(jnp.float32)[:, None] * inverse_freq[None, :]
    angles = jnp.concatenate([angles, angles], axis=-1)
    return (jnp.cos(angles), jnp.sin(angles))

def place_info(lengths_row, group_tokens):
    position_ids = jnp.arange(group_tokens, dtype=jnp.int32)
    seq_ends = jnp.cumsum(lengths_row).astype(jnp.int32)
    passed = position_ids[:, None] >= seq_ends[None, :]
    starts = lax.optimization_barrier(jnp.sum(jnp.where(passed, lengths_row[None, :], 0), axis=1)).astype(jnp.int32)
    documents = lax.optimization_barrier(jnp.sum(passed.astype(jnp.int32), axis=1)).astype(jnp.int32)
    return (documents, position_ids - starts)

def slot_table(route_block, experts, capacity):
    flattened = route_block.reshape(-1).astype(jnp.int32)
    assignments = flattened.shape[0]
    one_hot = (flattened[:, None] == jnp.arange(experts, dtype=jnp.int32)[None, :]).astype(jnp.int32)
    before = (jnp.cumsum(one_hot, axis=0) - one_hot).astype(jnp.int32)
    slot_ids = lax.optimization_barrier(jnp.sum(before * one_hot, axis=1)).astype(jnp.int32)
    targets = flattened * capacity + slot_ids
    owner_table = jnp.full((experts * capacity,), assignments, jnp.int32).at[targets].set(jnp.arange(assignments, dtype=jnp.int32))
    return (slot_ids, owner_table)

def head_path(raw, gain, cosine, sine, factor):
    return rotate(rms_gain(raw, gain), cosine[:, None, :], sine[:, None, :]) * factor

def attend_group(pieces, weights):
    normed_rows, places, lengths_row = pieces
    w_query, w_key, w_value, query_gain, key_gain, w_out = weights
    position_ids = jnp.arange(GROUP_TOK, dtype=jnp.int32)
    inverse = jnp.zeros((GROUP_TOK,), jnp.int32).at[places].set(position_ids)
    stream = normed_rows[inverse]
    documents, positions = place_info(lengths_row, GROUP_TOK)
    cosine, sine = rope_tables(positions, HEAD)
    query_raw = low_back(jnp.dot(stream, w_query, precision=highest)).reshape(GROUP_TOK, HEADS, HEAD)
    key_raw = low(low_back(jnp.dot(stream, w_key, precision=highest))).reshape(GROUP_TOK, KV_HEADS, HEAD)
    value_raw = low(low_back(jnp.dot(stream, w_value, precision=highest))).reshape(GROUP_TOK, KV_HEADS, HEAD)
    queries = low(head_path(query_raw, query_gain, cosine, sine, HEAD ** (-0.5)))
    keys = low(head_path(key_raw, key_gain, cosine, sine, 1.0))
    grouped = queries.reshape(GROUP_TOK, KV_HEADS, HEADS // KV_HEADS, HEAD)
    scores = low_back(jnp.einsum('qkgd,pkd->kgqp', grouped, keys, precision=highest))
    allowed = (documents[:, None] == documents[None, :]) & (position_ids[None, :] <= position_ids[:, None])
    scores = jnp.where(allowed, scores, masked_score)
    soft_weights = jax.nn.softmax(scores, axis=-1)
    mixed = jnp.einsum('kgqp,pkd->qkgd', low(soft_weights), value_raw, precision=highest).reshape(GROUP_TOK, HEADS * HEAD)
    mixed = low(low_back(mixed))
    return jnp.dot(mixed, w_out, precision=highest)[places]

def forward(block_input, norm1_gain, w_query, w_key, w_value, query_gain, key_gain, w_out, norm2_gain, w_router, w_gate, w_up, w_down, seq_lengths, token_places, expert_routes):
    normed1 = low(rms_gain(block_input, norm1_gain))
    weights = (w_query, w_key, w_value, query_gain, key_gain, w_out)

    def group_step(pieces):
        return attend_group(pieces, weights)
    attention = lax.map(jax.checkpoint(group_step), (normed1.reshape(GROUPS, GROUP_TOK, D), token_places, seq_lengths))
    attention = low_back(attention.reshape(TOKENS, D))
    hidden = block_input + attention
    normed2 = low(rms_gain(hidden, norm2_gain))
    logits = low_back(jnp.dot(normed2, w_router, precision=highest))
    router_probs = jax.nn.softmax(logits, axis=-1)
    chosen = jnp.take_along_axis(router_probs, expert_routes, axis=1)
    gates = chosen / lax.optimization_barrier(jnp.sum(chosen, axis=1, keepdims=True))
    device_count = N_EXPERT * N_SHARD

    def block_table(block_routes):
        return slot_table(block_routes, EXPERTS, CAP)
    slot_ids, tables = jax.vmap(block_table)(expert_routes.reshape(device_count, TOK_DEV, TOP))
    sentinel = TOK_DEV * TOP
    device_ids = jnp.arange(device_count, dtype=jnp.int32)
    global_ids = jnp.where(tables == sentinel, TOKENS * TOP, device_ids[:, None] * sentinel + tables).astype(jnp.int32)
    per_expert = global_ids.reshape(device_count, EXPERTS, CAP).transpose(1, 0, 2).reshape(EXPERTS, device_count * CAP)
    padded_rows = jnp.concatenate([normed2, jnp.zeros((1, D), jnp.float32)], axis=0)
    padded_gates = jnp.concatenate([gates.reshape(-1), jnp.zeros((1,), jnp.float32)], axis=0)

    def expert_step(mixture, item):
        assigned, gate_weight, up_weight, down_weight = item
        token_ids = (assigned // TOP).astype(jnp.int32)
        rows_in = low_back(padded_rows[token_ids])
        gate_pre = low_back(jnp.dot(rows_in, gate_weight, precision=highest))
        up_pre = low_back(jnp.dot(rows_in, up_weight, precision=highest))
        activated = low(jax.nn.silu(gate_pre) * up_pre)
        returned = low(low_back(jnp.dot(activated, down_weight, precision=highest)))
        mixture = mixture.at[token_ids].add(padded_gates[assigned][:, None] * returned)
        return (mixture, None)
    mixture, unused = lax.scan(jax.checkpoint(expert_step), jnp.zeros((TOKENS + 1, D), jnp.float32), (per_expert, w_gate, w_up, w_down))
    return hidden + mixture[:TOKENS]

def reference(block_input, out_grad, norm1_gain, w_query, w_key, w_value, query_gain, key_gain, w_out, norm2_gain, w_router, w_gate, w_up, w_down, seq_lengths, token_places, expert_routes):
    floats = tuple((array_in.astype(jnp.float32) for array_in in (block_input, norm1_gain, w_query, w_key, w_value, query_gain, key_gain, w_out, norm2_gain, w_router, w_gate, w_up, w_down)))

    def layer(*arrays):
        return forward(*arrays, seq_lengths, token_places, expert_routes)
    output, pullback = jax.vjp(layer, *floats)
    grads = pullback(out_grad.astype(jnp.float32))
    return (output.astype(jnp.bfloat16), grads[0], grads[1], grads[2], grads[3], grads[4], grads[5], grads[6], grads[7], grads[8], grads[9], grads[10], grads[11], grads[12])
```

```python
import functools

import jax
import jax.numpy as jnp
from jax import lax
from jax.experimental import pallas as pl
from jax.experimental.pallas import tpu as pltpu
from jax.sharding import PartitionSpec as P

EPS = 1e-06
ROPE_BASE = 1000000.0
LOG2E = 1.4426950408889634
T = 128
D = 2048
HEAD = 128
LH = 4
E = 128
CAP = 5
SLOTS = E * CAP
SEG = D // 128
ROWS = 1024
HALF = 512
F = 768
bf16 = jnp.bfloat16
f32 = jnp.float32
ALL = ("expert", "shard")


def dot(a, b):
    return jnp.dot(a, b, preferred_element_type=f32)


def dot_t(a, b):
    return lax.dot_general(a, b, (((1,), (1,)), ((), ())), preferred_element_type=f32)


def call(kernel, name, outs, scratch, args, flops=0, smem=()):
    in_specs = [
        pl.BlockSpec(memory_space=pltpu.SMEM if i in smem else pltpu.VMEM)
        for i in range(len(args))
    ]
    bytes_accessed = sum(a.size * a.dtype.itemsize for a in args) + sum(
        s.size * s.dtype.itemsize for s in outs
    )
    return pl.pallas_call(
        kernel,
        out_shape=outs,
        in_specs=in_specs,
        out_specs=[pl.BlockSpec(memory_space=pltpu.VMEM) for _ in outs],
        scratch_shapes=scratch,
        compiler_params=pltpu.CompilerParams(vmem_limit_bytes=56 * 1024 * 1024),
        cost_estimate=pl.CostEstimate(
            flops=flops, bytes_accessed=bytes_accessed, transcendentals=0
        ),
        name=name,
    )(*args)


def sds(shape, dtype):
    return jax.ShapeDtypeStruct(shape, dtype)


def load_rows(payload_ref, buf):
    def body(i, carry):
        rows = pl.ds(pl.multiple_of(i * SLOTS, SLOTS), SLOTS)
        buf[rows, :] = payload_ref[rows, :].astype(f32)
        return carry

    lax.fori_loop(0, SEG, body, 0)


def rows_chunk(buf, j):
    low = buf[pl.ds(2 * j, SLOTS, stride=SEG), :]
    high = buf[pl.ds(2 * j + 1, SLOTS, stride=SEG), :]
    return jnp.concatenate([low, high], axis=1).astype(bf16)


def put_chunk(buf, j, values):
    buf[pl.ds(2 * j, SLOTS, stride=SEG), :] = values[:, :128]
    buf[pl.ds(2 * j + 1, SLOTS, stride=SEG), :] = values[:, 128:]


def store_rows(payload_ref, buf):
    def body(i, carry):
        rows = pl.ds(pl.multiple_of(i * SLOTS, SLOTS), SLOTS)
        payload_ref[rows, :] = buf[rows, :].astype(bf16)
        return carry

    lax.fori_loop(0, SEG, body, 0)


def pack_body(x_ref, at_ref, out_ref, buf):
    slot = lax.broadcasted_iota(jnp.int32, (SLOTS, T), 0)
    hit = slot == at_ref[0:1, :]
    for k in range(1, 4):
        hit = hit | (slot == at_ref[k : k + 1, :])
    pick = jnp.where(hit, 1.0, 0.0).astype(bf16)
    for j in range(SEG // 2):
        put_chunk(buf, j, dot(pick, x_ref[:, j * 256 : (j + 1) * 256]))
    store_rows(out_ref, buf)


def pack(x, assign_t):
    return call(
        pack_body,
        "pack_rows",
        [sds((SLOTS * SEG, 128), bf16)],
        [pltpu.VMEM((SLOTS * SEG, 128), f32)],
        (x, assign_t),
        flops=2 * SLOTS * T * D,
    )[0]


def gate_matrix(assign_ref, gates_ref):
    lane = lax.broadcasted_iota(jnp.int32, (T, SLOTS), 1)
    total = jnp.where(lane == assign_ref[:, 0:1], gates_ref[:, 0:1], 0.0)
    for k in range(1, 4):
        total = total + jnp.where(lane == assign_ref[:, k : k + 1], gates_ref[:, k : k + 1], 0.0)
    high = total.astype(bf16)
    return high, (total - high.astype(f32)).astype(bf16)


def qkv_body(piece, xa, xb, g1, wt, gq, gk, cos, sin, qraw, qt, kraw, kt, vt, n1):
    for half, ref in ((0, xa), (1, xb)):
        x = ref[...].astype(f32)
        r = lax.rsqrt(jnp.mean(x * x, axis=-1, keepdims=True) + EPS)
        n1[half * T : (half + 1) * T, :] = (x * r * g1[...]).astype(bf16)
    raw = dot_t(wt[...], n1[...])
    first, second = piece * T, HALF + piece * T
    c = jnp.concatenate([cos[:, first : first + T], cos[:, second : second + T]], axis=1)
    s = jnp.concatenate([sin[:, first : first + T], sin[:, second : second + T]], axis=1)

    def path(v, gain, factor):
        v = v * lax.rsqrt(jnp.mean(v * v, axis=0, keepdims=True) + EPS) * gain
        low, high = v[:64], v[64:]
        return (
            ((low * c - high * s) * factor).astype(bf16),
            ((high * c + low * s) * factor).astype(bf16),
        )

    qraw[...] = raw[: LH * HEAD]
    for h in range(LH):
        low, high = path(raw[h * HEAD : (h + 1) * HEAD], gq[...], HEAD ** (-0.5))
        qt[h * HEAD : h * HEAD + 64, :] = low
        qt[h * HEAD + 64 : (h + 1) * HEAD, :] = high
    key = raw[LH * HEAD : (LH + 1) * HEAD].astype(bf16)
    kraw[...] = key
    low, high = path(key.astype(f32), gk[...], 1.0)
    kt[:64, :] = low
    kt[64:, :] = high
    vt[...] = raw[(LH + 1) * HEAD :].astype(bf16)


def qkv(piece, xa, xb, g1, wt, gq, gk, cos, sin):
    return call(
        functools.partial(qkv_body, piece),
        f"qkv{piece}",
        [
            sds((LH * HEAD, 2 * T), f32),
            sds((LH * HEAD, 2 * T), bf16),
            sds((HEAD, 2 * T), bf16),
            sds((HEAD, 2 * T), bf16),
            sds((HEAD, 2 * T), bf16),
            sds((2 * T, D), bf16),
        ],
        [],
        (xa, xb, g1, wt, gq, gk, cos, sin),
        flops=2 * 2 * T * D * 768,
    )


def build_mask(info, mask):
    for b in range(8):
        keys = jnp.broadcast_to(info[0:1, b * T : (b + 1) * T], (T, T)).T
        for j in range(8):
            cols = slice(j * T, (j + 1) * T)
            inside = (keys >= info[1:2, cols]) & (keys <= info[0:1, cols])
            mask[b * T : (b + 1) * T, cols] = jnp.where(inside, 1.0, 0.0)


def attend_body(*refs):
    q, k, v = refs[0:4], refs[4:8], refs[8:12]
    info, ot0, ot1, linv, qt, kt, kn, vn, mask, vt = refs[12:]
    for dy in range(4):
        for dc in range(2):
            to = slice(dc * HALF + dy * T, dc * HALF + (dy + 1) * T)
            src = slice(dc * T, (dc + 1) * T)
            qt[:, to] = q[dy][:, src]
            kt[:, to] = k[dy][:, src]
            vt[:, to] = v[dy][:, src]
    for b in range(8):
        rows = slice(b * T, (b + 1) * T)
        kn[rows, :] = kt[:, rows].astype(f32).T.astype(bf16)
        vn[rows, :] = vt[:, rows].astype(f32).T.astype(bf16)
    build_mask(info, mask)
    for half, out in ((1, ot1), (0, ot0)):

        def body(i, carry):
            local = pl.ds(pl.multiple_of(i * 256, 256), 256)
            cols = pl.ds(pl.multiple_of(half * HALF + i * 256, 256), 256)
            for h in range(LH):
                heads = slice(h * HEAD, (h + 1) * HEAD)
                scores = dot(kn[...], qt[heads, cols])
                weights = jnp.exp2(scores * LOG2E) * mask[:, cols]
                inverse = 1.0 / jnp.sum(weights, axis=0, keepdims=True)
                out[heads, local] = (dot(vt[...], weights.astype(bf16)) * inverse).astype(bf16)
                linv[h : h + 1, cols] = inverse
            return carry

        lax.fori_loop(0, 2, body, 0)


def attend(q, k, v, info):
    return call(
        attend_body,
        "attend",
        [
            sds((LH * HEAD, HALF), bf16),
            sds((LH * HEAD, HALF), bf16),
            sds((8, ROWS), f32),
            sds((LH * HEAD, ROWS), bf16),
            sds((HEAD, ROWS), bf16),
            sds((ROWS, HEAD), bf16),
            sds((ROWS, HEAD), bf16),
        ],
        [pltpu.VMEM((ROWS, ROWS), f32), pltpu.VMEM((HEAD, ROWS), bf16)],
        (*q, *k, *v, info),
        flops=4 * LH * ROWS * ROWS * HEAD,
    )


def outproj_body(ot0, otr, wa, wb, b0, b1, b2, b3):
    def body(i, carry):
        rows = pl.ds(pl.multiple_of(i * 512, 512), 512)
        total = dot(wa[rows, :], ot0[...]) + dot(wb[rows, :], otr[...])
        for dy, out in enumerate((b0, b1, b2, b3)):
            out[rows, :] = total[:, dy * T : (dy + 1) * T].astype(bf16)
        return carry

    lax.fori_loop(0, 4, body, 0)


def outproj(ot0, otr, wa, wb):
    return call(
        outproj_body,
        "out_projection",
        [sds((D, T), bf16)] * 4,
        [],
        (ot0, otr, wa, wb),
        flops=2 * D * 1024 * HALF,
    )


def router_body(
    b0, b1, b2, b3, x0, g2, wr, routes, at, hidden, n2, probs, gates, payload, buf
):
    for j in range(SEG):
        rows = slice(j * 128, (j + 1) * 128)
        total = (
            b0[rows, :].astype(f32)
            + b1[rows, :].astype(f32)
            + b2[rows, :].astype(f32)
            + b3[rows, :].astype(f32)
        )
        hidden[:, rows] = x0[:, rows].astype(f32) + total.T
    v = hidden[...]
    r = lax.rsqrt(jnp.mean(v * v, axis=-1, keepdims=True) + EPS)
    n2[...] = (v * r * g2[...]).astype(bf16)
    pack_body(n2, at, payload, buf)
    logits = dot(n2[...], wr[...])
    expo = jnp.exp(logits - jnp.max(logits, axis=-1, keepdims=True))
    p = expo / jnp.sum(expo, axis=-1, keepdims=True)
    probs[...] = p
    lane = lax.broadcasted_iota(jnp.int32, (T, E), 1)
    chosen = [
        jnp.sum(jnp.where(lane == routes[:, k : k + 1], p, 0.0), axis=-1, keepdims=True)
        for k in range(4)
    ]
    total = chosen[0] + chosen[1] + chosen[2] + chosen[3]
    packed = jnp.where(lane == 4, total, 0.0)
    for k in range(4):
        packed = jnp.where(lane == k, chosen[k] / total, packed)
    gates[...] = packed


def router(b, x0, g2, wr, routes, assign_t):
    return call(
        router_body,
        "router",
        [
            sds((T, D), f32),
            sds((T, D), bf16),
            sds((T, E), f32),
            sds((T, E), f32),
            sds((SLOTS * SEG, 128), bf16),
        ],
        [pltpu.VMEM((SLOTS * SEG, 128), f32)],
        (*b, x0, g2, wr, routes, assign_t),
        flops=2 * SLOTS * T * D,
    )


def expert_grad_body(payload, wd, gr, ga, buf):
    load_rows(payload, buf)
    for j in range(SEG // 2):
        gr[:, j * 256 : (j + 1) * 256] = rows_chunk(buf, j)

    def body(i, carry):
        cols = pl.ds(pl.multiple_of(i * 256, 256), 256)
        ga[:, cols] = dot_t(gr[...], wd[cols, :])
        return carry

    lax.fori_loop(0, F // 256, body, 0)


def expert_grad(payload, wd):
    return call(
        expert_grad_body,
        "expert_grad_rows",
        [sds((SLOTS, D), bf16), sds((SLOTS, F), f32)],
        [pltpu.VMEM((SLOTS * SEG, 128), f32)],
        (payload, wd),
        flops=2 * SLOTS * D * F,
    )


def expert_main_body(payload, wg, wu, ga, back, xr, act, dg, du, sc, buf):
    load_rows(payload, buf)
    for j in range(SEG // 2):
        xr[:, j * 256 : (j + 1) * 256] = rows_chunk(buf, j)
    sc[...] = jnp.zeros_like(sc)

    def forward(i, carry):
        cols = pl.ds(pl.multiple_of(i * 256, 256), 256)
        gate = dot(xr[...], wg[:, cols])
        up = dot(xr[...], wu[:, cols])
        grad = ga[:, cols]
        s = 1.0 / (1.0 + jnp.exp(-gate))
        silu = gate * s
        a = (silu * up).astype(bf16)
        act[:, cols] = a
        dg[:, cols] = (grad * up * s * (1.0 + gate * (1.0 - s))).astype(bf16)
        du[:, cols] = (grad * silu).astype(bf16)
        sc[...] += jnp.sum(a.astype(f32) * grad, axis=1, keepdims=True)
        return carry

    lax.fori_loop(0, F // 256, forward, 0)
    for j in range(SEG // 2):
        rows = slice(j * 256, (j + 1) * 256)
        put_chunk(buf, j, dot_t(dg[...], wg[rows, :]) + dot_t(du[...], wu[rows, :]))
    store_rows(back, buf)


def expert_main(payload, wg, wu, ga):
    return call(
        expert_main_body,
        "expert_main",
        [
            sds((SLOTS * SEG, 128), bf16),
            sds((SLOTS, D), bf16),
            sds((SLOTS, F), bf16),
            sds((SLOTS, F), bf16),
            sds((SLOTS, F), bf16),
            sds((SLOTS, 1), f32),
        ],
        [pltpu.VMEM((SLOTS * SEG, 128), f32)],
        (payload, wg, wu, ga),
        flops=8 * SLOTS * D * F,
    )


def expert_out_body(act, wd, payload, buf):
    for j in range(SEG // 2):
        put_chunk(buf, j, dot(act[...], wd[:, j * 256 : (j + 1) * 256]))
    store_rows(payload, buf)


def expert_out(act, wd):
    return call(
        expert_out_body,
        "expert_out",
        [sds((SLOTS * SEG, 128), bf16)],
        [pltpu.VMEM((SLOTS * SEG, 128), f32)],
        (act, wd),
        flops=2 * SLOTS * D * F,
    )[0]


def combine_body(
    payload, scin, hidden, n2, probs, gates, routes, slots, assign, og, g2, wr,
    ghid, gatt, grouter, gg2, buf, gn2,
):
    load_rows(payload, buf)
    high, low = gate_matrix(assign, gates)
    lane = lax.broadcasted_iota(jnp.int32, (T, E), 1)
    grads = []
    for k in range(4):
        hot = jnp.where(lane == routes[:, k : k + 1], 1.0, 0.0)
        rows = lax.dot_general(
            hot, scin[...], (((1,), (0,)), ((), ())),
            precision=lax.Precision.HIGHEST, preferred_element_type=f32,
        )
        picked = jnp.where(lane == slots[:, k : k + 1], rows, 0.0)
        grads.append(jnp.sum(picked, axis=-1, keepdims=True))
    inner = sum(grads[k] * gates[:, k : k + 1] for k in range(4))
    inverse = 1.0 / gates[:, 4:5]
    grad_probs = jnp.zeros((T, E), f32)
    for k in range(4):
        grad_probs = jnp.where(
            lane == routes[:, k : k + 1], (grads[k] - inner) * inverse, grad_probs
        )
    p = probs[...]
    gl = (p * (grad_probs - jnp.sum(p * grad_probs, axis=-1, keepdims=True))).astype(bf16)
    for j in range(SEG // 2):
        cols = slice(j * 256, (j + 1) * 256)
        rows = rows_chunk(buf, j)
        gn2[:, cols] = dot(high, rows) + dot(low, rows) + dot_t(gl, wr[cols, :])
    c = gn2[...]
    v = hidden[...]
    r = lax.rsqrt(jnp.mean(v * v, axis=-1, keepdims=True) + EPS)
    u = c * g2[...]
    m = jnp.mean(u * v, axis=-1, keepdims=True)
    total = og[...].astype(f32) + r * u - v * (r * r * r * m)
    ghid[...] = total
    gatt[...] = total.astype(bf16)
    gg2[...] = jnp.sum(c * (v * r), axis=0, keepdims=True)
    for j in range(SEG):
        cols = slice(j * 128, (j + 1) * 128)
        grouter[cols, :] = dot(n2[:, cols].astype(f32).T.astype(bf16), gl).astype(bf16)


def combine(payload, scin, hidden, n2, probs, gates, routes, slots, assign, og, g2, wr):
    return call(
        combine_body,
        "combine_grads",
        [sds((T, D), f32), sds((T, D), bf16), sds((D, E), bf16), sds((1, D), f32)],
        [pltpu.VMEM((SLOTS * SEG, 128), f32), pltpu.VMEM((T, D), f32)],
        (payload, scin, hidden, n2, probs, gates, routes, slots, assign, og, g2, wr),
        flops=4 * SLOTS * T * D,
    )


def result_body(payload, hidden, gates, assign, out, buf):
    load_rows(payload, buf)
    high, low = gate_matrix(assign, gates)
    for j in range(SEG // 2):
        cols = slice(j * 256, (j + 1) * 256)
        rows = rows_chunk(buf, j)
        out[:, cols] = (hidden[:, cols] + dot(high, rows) + dot(low, rows)).astype(bf16)


def result_rows(payload, hidden, gates, assign):
    return call(
        result_body,
        "result",
        [sds((T, D), bf16)],
        [pltpu.VMEM((SLOTS * SEG, 128), f32)],
        (payload, hidden, gates, assign),
        flops=4 * SLOTS * T * D,
    )[0]


def pre_body(*refs):
    blocks, (ot0, ot1, wo, gw, dt, rows_all) = refs[:8], refs[8:]
    for b in range(8):
        rows_all[b * T : (b + 1) * T, :] = blocks[b][...]

    def weight(i, carry):
        cols = pl.ds(pl.multiple_of(i * 256, 256), 256)
        gw[:, cols] = (
            dot(ot0[...], rows_all[:HALF, cols]) + dot(ot1[...], rows_all[HALF:, cols])
        ).astype(bf16)
        return carry

    lax.fori_loop(0, 8, weight, 0)

    def heads(i, carry):
        tokens = pl.ds(pl.multiple_of(i * 256, 256), 256)
        dt[:, tokens] = dot_t(wo[...], rows_all[tokens, :]).astype(bf16)
        return carry

    lax.fori_loop(0, 4, heads, 0)


def pre(blocks, ot0, ot1, wo):
    return call(
        pre_body,
        "out_projection_grad",
        [sds((LH * HEAD, D), bf16), sds((LH * HEAD, ROWS), bf16)],
        [pltpu.VMEM((ROWS, D), bf16)],
        (*blocks, ot0, ot1, wo),
        flops=4 * 512 * ROWS * D,
    )


def bwd_body(*refs):
    qr, kr = refs[0:4], refs[4:8]
    (qt, kt, kn, vn, dt, ot0, ot1, linv, info, cos, sin, gq, gk) = refs[8:21]
    dq0, dq1, dkv, ggq, ggk, mask, wb, sb, dqt, dk, dv, raw = refs[21:]
    build_mask(info, mask)
    dk[...] = jnp.zeros_like(dk)
    dv[...] = jnp.zeros_like(dv)
    for half, out in ((0, ot0), (1, ot1)):

        def body(i, carry):
            local = pl.ds(pl.multiple_of(i * 256, 256), 256)
            cols = pl.ds(pl.multiple_of(half * HALF + i * 256, 256), 256)
            for h in range(LH):
                heads = slice(h * HEAD, (h + 1) * HEAD)
                part = slice(h * 256, (h + 1) * 256)
                scores = dot(kn[...], qt[heads, cols])
                weights = jnp.exp2(scores * LOG2E) * (mask[:, cols] * linv[h : h + 1, cols])
                grad = dt[heads, cols]
                delta = jnp.sum(
                    grad.astype(f32) * out[heads, local].astype(f32), axis=0, keepdims=True
                )
                wb[:, part] = weights.astype(bf16)
                sb[:, part] = (weights * (dot(vn[...], grad) - delta)).astype(bf16)
                dqt[heads, cols] = dot(kt[...], sb[:, part])
            grads = jnp.concatenate(
                [dt[h * HEAD : (h + 1) * HEAD, cols] for h in range(LH)], axis=1
            )
            queries = jnp.concatenate(
                [qt[h * HEAD : (h + 1) * HEAD, cols] for h in range(LH)], axis=1
            )
            dv[...] += dot_t(wb[...], grads)
            dk[...] += dot_t(sb[...], queries)
            return carry

        lax.fori_loop(0, 2, body, 0)

    def unrope(v):
        low, high = v[:64], v[64:]
        c, s = cos[...], sin[...]
        return jnp.concatenate([low * c + high * s, high * c - low * s], axis=0)

    def norm_back(v, grad, gain):
        r = lax.rsqrt(jnp.mean(v * v, axis=0, keepdims=True) + EPS)
        n = v * r
        gain_grad = jnp.sum(grad * n, axis=1, keepdims=True)
        u = grad * gain
        return r * (u - n * jnp.mean(u * n, axis=0, keepdims=True)), gain_grad

    total = jnp.zeros((HEAD, 1), f32)
    for h in range(LH):
        heads = slice(h * HEAD, (h + 1) * HEAD)
        for dy in range(4):
            for dc in range(2):
                to = slice(dc * HALF + dy * T, dc * HALF + (dy + 1) * T)
                raw[:, to] = qr[dy][heads, dc * T : (dc + 1) * T]
        grad, part = norm_back(raw[...], unrope(dqt[heads, :] * (HEAD ** (-0.5))), gq[...])
        total = total + part
        dq0[heads, :] = grad[:, :HALF].astype(bf16)
        dq1[heads, :] = grad[:, HALF:].astype(bf16)
    ggq[...] = total
    for dy in range(4):
        for dc in range(2):
            to = slice(dc * HALF + dy * T, dc * HALF + (dy + 1) * T)
            raw[:, to] = kr[dy][:, dc * T : (dc + 1) * T].astype(f32)
    grad, part = norm_back(raw[...], unrope(dk[...].T), gk[...])
    ggk[...] = part
    dkv[:HEAD, :] = grad.astype(bf16)
    dkv[HEAD:, :] = dv[...].T.astype(bf16)


def bwd(qr, kr, *rest):
    return call(
        bwd_body,
        "attend_grad",
        [
            sds((LH * HEAD, HALF), bf16),
            sds((LH * HEAD, HALF), bf16),
            sds((2 * HEAD, ROWS), bf16),
            sds((HEAD, 1), f32),
            sds((HEAD, 1), f32),
        ],
        [
            pltpu.VMEM((ROWS, ROWS), f32),
            pltpu.VMEM((ROWS, LH * 256), bf16),
            pltpu.VMEM((ROWS, LH * 256), bf16),
            pltpu.VMEM((LH * HEAD, ROWS), f32),
            pltpu.VMEM((ROWS, HEAD), f32),
            pltpu.VMEM((ROWS, HEAD), f32),
            pltpu.VMEM((HEAD, ROWS), f32),
        ],
        (*qr, *kr, *rest),
        flops=10 * LH * ROWS * ROWS * HEAD,
    )


def qkv_grad_body(core, n1t, dq0, dq1, own, sib, out, tot, dt):
    tot[:, :HALF] = (own[:, :HALF].astype(f32) + sib[:, HALF:].astype(f32)).astype(bf16)
    tot[:, HALF:] = (own[:, HALF:].astype(f32) + sib[:, :HALF].astype(f32)).astype(bf16)
    dt[:512, :HALF] = dq0[...]
    dt[:512, HALF:] = dq1[...]
    upper = core[0] == 1
    dt[512:576, :] = jnp.where(upper, tot[64:128, :], tot[:64, :])
    dt[576:, :] = jnp.where(upper, tot[192:, :], tot[128:192, :])

    def body(i, carry):
        rows = pl.ds(pl.multiple_of(i * 512, 512), 512)
        out[rows, :] = dot_t(n1t[rows, :], dt[...]).astype(bf16)
        return carry

    lax.fori_loop(0, 4, body, 0)


def qkv_grad(core, n1t, dq0, dq1, own, sib):
    return call(
        qkv_grad_body,
        "qkv_weight_grad",
        [sds((D, 640), bf16), sds((2 * HEAD, ROWS), bf16)],
        [pltpu.VMEM((640, ROWS), bf16)],
        (core, n1t, dq0, dq1, own, sib),
        flops=2 * D * 640 * ROWS,
        smem=(0,),
    )


def normed_grad_body(wa, wb, wkv, dq0, dqr, tot, n1t, g1, b0, b1, b2, b3, gg1):
    def body(i, carry):
        rows = pl.ds(pl.multiple_of(i * 512, 512), 512)
        total = (
            dot(wa[rows, :], dq0[...])
            + dot(wb[rows, :], dqr[...])
            + dot(wkv[rows, :], tot[:, :HALF])
        )
        for dy, out in enumerate((b0, b1, b2, b3)):
            out[rows, :] = total[:, dy * T : (dy + 1) * T].astype(bf16)
        gain = jnp.sum(total * n1t[rows, :HALF].astype(f32), axis=1, keepdims=True)
        gg1[rows, :] = gain / g1[rows, :]
        return carry

    lax.fori_loop(0, 4, body, 0)


def normed_grad(wa, wb, wkv, dq0, dqr, tot, n1t, g1):
    return call(
        normed_grad_body,
        "normed_grad",
        [sds((D, T), bf16)] * 4 + [sds((D, 1), f32)],
        [],
        (wa, wb, wkv, dq0, dqr, tot, n1t, g1),
        flops=2 * D * 1280 * HALF,
    )


def final_body(b0, b1, b2, b3, x0, ghid, g1, out, c):
    for j in range(SEG):
        rows = slice(j * 128, (j + 1) * 128)
        total = (
            b0[rows, :].astype(f32)
            + b1[rows, :].astype(f32)
            + b2[rows, :].astype(f32)
            + b3[rows, :].astype(f32)
        )
        c[:, rows] = total.T
    v = x0[...].astype(f32)
    r = lax.rsqrt(jnp.mean(v * v, axis=-1, keepdims=True) + EPS)
    u = c[...] * g1[...]
    m = jnp.mean(u * v, axis=-1, keepdims=True)
    out[...] = ghid[...] + r * u - v * (r * r * r * m)


def final(b, x0, ghid, g1):
    return call(
        final_body,
        "input_grad",
        [sds((T, D), f32)],
        [pltpu.VMEM((T, D), f32)],
        (*b, x0, ghid, g1),
        flops=T * D * 10,
    )[0]


def sibling(x):
    return lax.ppermute(x, "shard", [(i, i ^ 1) for i in range(8)])


def from_chip(x, dy):
    return lax.ppermute(x, "shard", [(i, (i - 2 * dy) % 8) for i in range(8)])


def to_chip(x, dy):
    return lax.ppermute(x, "shard", [(i, (i + 2 * dy) % 8) for i in range(8)])


def gather_blocks(x):
    first = [x] + [from_chip(x, dy) for dy in (1, 2, 3)]
    return first, [sibling(b) for b in first]


def exchange(x):
    return lax.all_to_all(x, ALL, split_axis=0, concat_axis=0, tiled=True)


def exchange_rows(payload):
    return exchange(payload.reshape(E, CAP * SEG, 128)).reshape(SLOTS * SEG, 128)


def exchange_slots(values):
    wide = jnp.pad(values.reshape(E, CAP), ((0, 0), (0, 128 - CAP)))
    return exchange(wide.reshape(E, 1, 128)).reshape(E, 128)


def on_device(
    block_input, out_grad, norm1_gain, w_query, w_key, w_value, query_gain, key_gain, w_out,
    norm2_gain, w_router, w_gate, w_up, w_down, seq_lengths, token_places, expert_routes,
):
    shard = lax.axis_index("shard")
    chip, core = shard // 2, shard % 2
    g1 = norm1_gain.astype(f32).reshape(1, D)
    g2 = norm2_gain.astype(f32).reshape(1, D)
    g1_col = norm1_gain.astype(f32).reshape(D, 1)
    gq = query_gain.astype(f32).reshape(HEAD, 1)
    gk = key_gain.astype(f32).reshape(HEAD, 1)

    x_own, x_sib = gather_blocks(block_input)

    chips = (chip + jnp.arange(4)) % 4
    order = jnp.concatenate([chips * 2 + core, chips * 2 + 1 - core])
    places = token_places[0].reshape(8, T)[order].reshape(ROWS)
    lengths = seq_lengths[0]
    ends = jnp.cumsum(lengths)
    starts = jnp.sum(
        jnp.where(places[:, None] >= ends[None, :], lengths[None, :], 0), axis=1
    )
    positions = (places - starts).astype(f32)
    info = jnp.concatenate(
        [places[None].astype(f32), starts[None].astype(f32), jnp.zeros((6, ROWS), f32)], axis=0
    )
    inverse_freq = ROPE_BASE ** (-jnp.arange(0, HEAD, 2).astype(f32) / HEAD)
    angles = inverse_freq[:, None] * positions[None, :]
    cos, sin = jnp.cos(angles), jnp.sin(angles)

    routes = expert_routes
    hot = (routes[:, :, None] == jnp.arange(E, dtype=jnp.int32)).astype(f32)
    earlier = jnp.tril(jnp.ones((T, T), bf16), -1)
    before = dot(earlier, jnp.sum(hot, axis=1).astype(bf16))
    slots = jnp.sum(before[:, None, :] * hot, axis=2).astype(jnp.int32)
    assign = routes * CAP + slots
    assign_t = assign.T

    wkv_t = jnp.concatenate([w_key.T, w_value.T], axis=0)
    wkv_ts = sibling(wkv_t)
    lower = core == 0
    wkv_low = jnp.where(lower, wkv_t, wkv_ts)
    wkv_high = jnp.where(lower, wkv_ts, wkv_t)
    wkv_ft = jnp.concatenate([wkv_low[:64], wkv_high[:64], wkv_low[64:], wkv_high[64:]], axis=0)
    w_t = jnp.concatenate([w_query.T, wkv_ft], axis=0)
    wo_t = w_out.T
    wo_ts = sibling(wo_t)
    wq_s = sibling(w_query)

    pieces = [qkv(dy, x_own[dy], x_sib[dy], g1, w_t, gq, gk, cos, sin) for dy in range(4)]
    q_raw, q, k_raw, k, v, n1 = zip(*pieces)
    og_payload = pack(out_grad, assign_t)
    og_payload, _ = lax.optimization_barrier((og_payload, x_own[2]))
    got_grads = exchange_rows(og_payload)
    ot0, ot1, linv, qt, kt, kn, vn = attend(q, k, v, info)
    blocks = outproj(ot0, sibling(ot1), wo_t, wo_ts)
    blocks = [blocks[0]] + [to_chip(blocks[dy], dy) for dy in (1, 2, 3)]
    hidden, n2, probs, gates, payload = router(blocks, block_input, g2, w_router, routes, assign_t)
    got_rows = exchange_rows(payload)

    n1, wkv_ft, gates_late, _ = lax.optimization_barrier((n1, wkv_ft, gates, payload))
    slot_ids = jnp.arange(SLOTS, dtype=jnp.int32)
    slot_gates = jnp.sum(
        jnp.where(
            assign.reshape(-1)[:, None] == slot_ids[None, :],
            gates_late[:, :4].reshape(-1)[:, None],
            0.0,
        ),
        axis=0,
    )
    got_gates = exchange_slots(slot_gates)
    n1_t = jnp.concatenate([p[:T] for p in n1] + [p[T:] for p in n1], axis=0).T
    wkv_full = wkv_ft.T
    grad_rows, grad_act = expert_grad(got_grads, w_down[0])

    back, rows, act, dg, du, sc = expert_main(got_rows, w_gate[0], w_up[0], grad_act)
    back_sc = exchange_slots(sc)
    back_grads = exchange_rows(back)

    out_payload = expert_out(act, w_down[0])
    gate_col = got_gates[:, :CAP].reshape(SLOTS, 1)
    scaled_rows = (rows.astype(f32) * gate_col).astype(bf16)
    scaled_act = (act.astype(f32) * gate_col).astype(bf16)

    def weight_grad(a, b):
        return lax.dot_general(a, b, (((0,), (0,)), ((), ())), preferred_element_type=f32)

    grad_wgate = weight_grad(scaled_rows, dg)
    grad_wup = weight_grad(scaled_rows, du)
    grad_wdown = weight_grad(scaled_act, grad_rows)

    ghid, gatt, grouter, gg2 = combine(
        back_grads, back_sc, hidden, n2, probs, gates, routes, slots, assign, out_grad, g2, w_router
    )
    g_own, g_sib = gather_blocks(gatt)
    out_payload, grouter, _ = lax.optimization_barrier((out_payload, grouter, g_own[2]))
    returned = exchange_rows(out_payload)
    result = result_rows(returned, hidden, gates, assign)

    gwout, dt = pre(g_own + g_sib, ot0, ot1, w_out)
    grad_wout = lax.psum(gwout, "expert").astype(f32)
    router_parts = exchange(grouter.reshape(E, SEG, 128))
    router_sum = jnp.sum(router_parts.astype(f32), axis=0).astype(bf16)
    grad_router = exchange(jnp.broadcast_to(router_sum[None], (E, SEG, 128)))
    grad_router = grad_router.reshape(D, E).astype(f32)

    dq0, dq1, dkv, ggq, ggk = bwd(
        q_raw, k_raw, qt, kt, kn, vn, dt, ot0, ot1, linv, info, cos, sin, gq, gk
    )
    dq_sib, dkv_sib = sibling(dq1), sibling(dkv)
    gw, dkv_total = qkv_grad(core.reshape(1), n1_t, dq0, dq1, dkv, dkv_sib)
    gw = lax.psum(gw, "expert").astype(f32)
    blocks = normed_grad(w_query, wq_s, wkv_full, dq0, dq_sib, dkv_total, n1_t, g1_col)
    gg1 = blocks[4]
    blocks = [blocks[0]] + [to_chip(blocks[dy], dy) for dy in (1, 2, 3)]
    grad_input = final(blocks, block_input, ghid, g1)

    vector = jnp.concatenate([gg1.reshape(-1), gg2.reshape(-1), ggq.reshape(-1), ggk.reshape(-1)])
    per = vector.shape[0] // E
    wide = jnp.pad(vector.reshape(E, per), ((0, 0), (0, 128 - per))).reshape(E, 1, 128)
    mine = jnp.sum(exchange(wide), axis=0, keepdims=True)
    vector = exchange(jnp.broadcast_to(mine, (E, 1, 128)))[:, 0, :per].reshape(-1)
    return (
        result,
        grad_input,
        vector[:D],
        gw[:, :512],
        gw[:, 512:576],
        gw[:, 576:],
        vector[2 * D : 2 * D + HEAD],
        vector[2 * D + HEAD :],
        grad_wout,
        vector[D : 2 * D],
        grad_router,
        grad_wgate[None],
        grad_wup[None],
        grad_wdown[None],
    )


def solution(mesh):
    rows = P(("expert", "shard"), None)
    experts = P(("expert", "shard"), None, None)
    columns = P(None, "shard")
    return jax.shard_map(
        on_device,
        mesh=mesh,
        in_specs=(
            rows, rows, P(), columns, columns, columns, P(), P(), P("shard", None), P(), P(),
            experts, experts, experts, P("expert", None), P("expert", None), rows,
        ),
        out_specs=(
            rows, rows, P(), columns, columns, columns, P(), P(), P("shard", None), P(), P(),
            experts, experts, experts,
        ),
        check_vma=False,
    )
```

```python
import functools

import jax
import jax.numpy as jnp
from jax import lax
from jax.experimental import pallas as pl
from jax.experimental.pallas import tpu as pltpu
from jax.sharding import PartitionSpec as P

EPS = 1e-06
ROPE_BASE = 1000000.0
LOG2E = 1.4426950408889634
T = 128
D = 2048
HEAD = 128
LH = 4
E = 128
CAP = 5
SLOTS = E * CAP
SEG = D // 128
WIRE = CAP * SEG + 8
ROWS = 1024
HALF = 512
F = 768
bf16 = jnp.bfloat16
f32 = jnp.float32
ALL = ("expert", "shard")


def dot(a, b):
    return jnp.dot(a, b, preferred_element_type=f32)


def dot_t(a, b):
    return lax.dot_general(a, b, (((1,), (1,)), ((), ())), preferred_element_type=f32)


def call(kernel, name, outs, scratch, args, flops=0, smem=()):
    in_specs = [
        pl.BlockSpec(memory_space=pltpu.SMEM if i in smem else pltpu.VMEM)
        for i in range(len(args))
    ]
    bytes_accessed = sum(a.size * a.dtype.itemsize for a in args) + sum(
        s.size * s.dtype.itemsize for s in outs
    )
    return pl.pallas_call(
        kernel,
        out_shape=outs,
        in_specs=in_specs,
        out_specs=[pl.BlockSpec(memory_space=pltpu.VMEM) for _ in outs],
        scratch_shapes=scratch,
        compiler_params=pltpu.CompilerParams(vmem_limit_bytes=56 * 1024 * 1024),
        cost_estimate=pl.CostEstimate(
            flops=flops, bytes_accessed=bytes_accessed, transcendentals=0
        ),
        name=name,
    )(*args)


def grid_call(kernel, name, grid, in_specs, out_specs, outs, scratch, args, flops=0, scalars=0):
    bytes_accessed = sum(a.size * a.dtype.itemsize for a in args) + sum(
        s.size * s.dtype.itemsize for s in outs
    )
    return pl.pallas_call(
        kernel,
        out_shape=outs,
        grid_spec=pltpu.PrefetchScalarGridSpec(
            num_scalar_prefetch=scalars,
            grid=grid,
            in_specs=in_specs,
            out_specs=out_specs,
            scratch_shapes=scratch,
        ),
        compiler_params=pltpu.CompilerParams(
            vmem_limit_bytes=56 * 1024 * 1024, dimension_semantics=("arbitrary",)
        ),
        cost_estimate=pl.CostEstimate(
            flops=flops, bytes_accessed=bytes_accessed, transcendentals=0
        ),
        name=name,
    )(*args)


def whole(shape):
    return pl.BlockSpec(shape, lambda i, *_: (0,) * len(shape))


def rows_of(shape):
    return pl.BlockSpec(shape, lambda i, *_: (i, 0))


def cols_of(shape):
    return pl.BlockSpec(shape, lambda i, *_: (0, i))


def sds(shape, dtype):
    return jax.ShapeDtypeStruct(shape, dtype)


def split_rows(wire, dest):
    for s in range(CAP):
        for h in range(2):
            rows = slice(s * E + h * 64, s * E + (h + 1) * 64)
            block = wire[h * 64 : (h + 1) * 64, s * SEG : (s + 1) * SEG, :]
            dest[rows, :] = block.reshape(64, D)


def join_rows(source, wire):
    for s in range(CAP):
        for h in range(2):
            rows = slice(s * E + h * 64, s * E + (h + 1) * 64)
            wire[h * 64 : (h + 1) * 64, s * SEG : (s + 1) * SEG, :] = source[rows, :].reshape(
                64, SEG, 128
            )


def put_numbers(columns, wire):
    lane = lax.broadcasted_iota(jnp.int32, (E, 128), 1)
    plane = jnp.zeros((E, 128), f32)
    for s in range(CAP):
        plane = jnp.where(lane == s, columns[s], plane)
    first = plane.astype(bf16)
    rest = plane - first.astype(f32)
    second = rest.astype(bf16)
    third = (rest - second.astype(f32)).astype(bf16)
    none = jnp.zeros((E, 5 * 128), bf16)
    wide = jnp.concatenate([first, second, third, none], axis=1)
    wire[:, CAP * SEG :, :] = wide.reshape(E, 8, 128)


def get_numbers(wire):
    wide = wire[:, CAP * SEG :, :].reshape(E, 8 * 128)
    return (
        wide[:, :128].astype(f32) + wide[:, 128:256].astype(f32) + wide[:, 256:384].astype(f32)
    )


def pack_rows(x_ref, at_ref, wire, rows):
    slot = lax.broadcasted_iota(jnp.int32, (SLOTS, T), 0)
    hit = slot == at_ref[0:1, :]
    for k in range(1, 4):
        hit = hit | (slot == at_ref[k : k + 1, :])
    pick = jnp.where(hit, 1.0, 0.0).astype(bf16)
    for j in range(8):
        cols = slice(j * 256, (j + 1) * 256)
        rows[:, cols] = dot(pick, x_ref[:, cols]).astype(bf16)
    join_rows(rows, wire)


def pack_body(x_ref, at_ref, wire, rows):
    pack_rows(x_ref, at_ref, wire, rows)
    wire[:, CAP * SEG :, :] = jnp.zeros((E, 8, 128), bf16)


def pack(x, assign_t):
    return call(
        pack_body,
        "pack_rows",
        [sds((E, WIRE, 128), bf16)],
        [pltpu.VMEM((SLOTS, D), bf16)],
        (x, assign_t),
        flops=2 * SLOTS * T * D,
    )[0]


def sum_rows(wire, experts, slots, gates, out):
    def body(i, carry):
        for u in range(8):
            t = i * 8 + u
            total = None
            for k in range(4):
                p = t * 4 + k
                rows = pl.ds(pl.multiple_of(slots[p] * SEG, SEG), SEG)
                part = wire[experts[p], rows, :].astype(f32) * gates[p]
                total = part if total is None else total + part
            out[pl.ds(pl.multiple_of(t * SEG, SEG), SEG), :] = total
        return carry

    lax.fori_loop(0, T // 8, body, 0)


def column(row):
    return jnp.broadcast_to(row, (128, 128)).T[:, 0:1]


def qkv_body(
    piece, core, xa, xb, g1, wqt, wk, wks, wv, wvs, gq, gk, cos, sin,
    qraw, qt, kraw, kt, vt, n1, wkv,
):
    lower = core[0] == 0
    wkv[0:64, :] = jnp.where(lower, wk[...], wks[...])
    wkv[64:128, :] = jnp.where(lower, wks[...], wk[...])
    wkv[128:192, :] = jnp.where(lower, wv[...], wvs[...])
    wkv[192:256, :] = jnp.where(lower, wvs[...], wv[...])
    for half, ref in ((0, xa), (1, xb)):
        x = ref[...].astype(f32)
        r = lax.rsqrt(jnp.mean(x * x, axis=-1, keepdims=True) + EPS)
        n1[half * T : (half + 1) * T, :] = (x * r * g1[...]).astype(bf16)
    raw = dot_t(wqt[...], n1[...])
    raw_kv = dot_t(wkv[...], n1[...])
    gain_q, gain_k = column(gq[...]), column(gk[...])
    first, second = piece * T, HALF + piece * T
    c = jnp.concatenate([cos[:, first : first + T], cos[:, second : second + T]], axis=1)
    s = jnp.concatenate([sin[:, first : first + T], sin[:, second : second + T]], axis=1)

    def path(v, gain, factor):
        v = v * lax.rsqrt(jnp.mean(v * v, axis=0, keepdims=True) + EPS) * gain
        low, high = v[:64], v[64:]
        return (
            ((low * c - high * s) * factor).astype(bf16),
            ((high * c + low * s) * factor).astype(bf16),
        )

    qraw[...] = raw
    for h in range(LH):
        low, high = path(raw[h * HEAD : (h + 1) * HEAD], gain_q, HEAD ** (-0.5))
        qt[h * HEAD : h * HEAD + 64, :] = low
        qt[h * HEAD + 64 : (h + 1) * HEAD, :] = high
    key = raw_kv[:HEAD].astype(bf16)
    kraw[...] = key
    low, high = path(key.astype(f32), gain_k, 1.0)
    kt[:64, :] = low
    kt[64:, :] = high
    vt[...] = raw_kv[HEAD:].astype(bf16)


def qkv(piece, *args):
    return call(
        functools.partial(qkv_body, piece),
        f"qkv{piece}",
        [
            sds((LH * HEAD, 2 * T), f32),
            sds((LH * HEAD, 2 * T), bf16),
            sds((HEAD, 2 * T), bf16),
            sds((HEAD, 2 * T), bf16),
            sds((HEAD, 2 * T), bf16),
            sds((2 * T, D), bf16),
            sds((2 * HEAD, D), bf16),
        ],
        [],
        args,
        flops=2 * 2 * T * D * 768,
        smem=(0,),
    )


def build_mask(info, mask):
    for b in range(8):
        keys = jnp.broadcast_to(info[0:1, b * T : (b + 1) * T], (T, T)).T
        for j in range(8):
            cols = slice(j * T, (j + 1) * T)
            inside = (keys >= info[1:2, cols]) & (keys <= info[0:1, cols])
            mask[b * T : (b + 1) * T, cols] = jnp.where(inside, 1.0, 0.0)


def attend_body(*refs):
    q, k, v = refs[0:4], refs[4:8], refs[8:12]
    info, ot0, ot1, linv, qt, kt, kn, vn, mask, vt = refs[12:]
    for dy in range(4):
        for dc in range(2):
            to = slice(dc * HALF + dy * T, dc * HALF + (dy + 1) * T)
            src = slice(dc * T, (dc + 1) * T)
            qt[:, to] = q[dy][:, src]
            kt[:, to] = k[dy][:, src]
            vt[:, to] = v[dy][:, src]
    for b in range(8):
        rows = slice(b * T, (b + 1) * T)
        kn[rows, :] = kt[:, rows].astype(f32).T.astype(bf16)
        vn[rows, :] = vt[:, rows].astype(f32).T.astype(bf16)
    build_mask(info, mask)
    for half, out in ((1, ot1), (0, ot0)):

        def body(i, carry):
            local = pl.ds(pl.multiple_of(i * 256, 256), 256)
            cols = pl.ds(pl.multiple_of(half * HALF + i * 256, 256), 256)
            for h in range(LH):
                heads = slice(h * HEAD, (h + 1) * HEAD)
                scores = dot(kn[...], qt[heads, cols])
                weights = jnp.exp2(scores * LOG2E) * mask[:, cols]
                inverse = 1.0 / jnp.sum(weights, axis=0, keepdims=True)
                out[heads, local] = (dot(vt[...], weights.astype(bf16)) * inverse).astype(bf16)
                linv[h : h + 1, cols] = inverse
            return carry

        lax.fori_loop(0, 2, body, 0)


def attend(q, k, v, info):
    return call(
        attend_body,
        "attend",
        [
            sds((LH * HEAD, HALF), bf16),
            sds((LH * HEAD, HALF), bf16),
            sds((8, ROWS), f32),
            sds((LH * HEAD, ROWS), bf16),
            sds((HEAD, ROWS), bf16),
            sds((ROWS, HEAD), bf16),
            sds((ROWS, HEAD), bf16),
        ],
        [pltpu.VMEM((ROWS, ROWS), f32), pltpu.VMEM((HEAD, ROWS), bf16)],
        (*q, *k, *v, info),
        flops=4 * LH * ROWS * ROWS * HEAD,
    )


def outproj_body(ot0, otr, wa, wb, b0, b1, b2, b3):
    total = dot(wa[...], ot0[...]) + dot(wb[...], otr[...])
    for dy, out in enumerate((b0, b1, b2, b3)):
        out[...] = total[:, dy * T : (dy + 1) * T].astype(bf16)


def outproj(ot0, otr, wa, wb):
    return grid_call(
        outproj_body,
        "out_projection",
        (4,),
        [whole((512, HALF)), whole((512, HALF)), rows_of((512, 512)), rows_of((512, 512))],
        [rows_of((512, T))] * 4,
        [sds((D, T), bf16)] * 4,
        [],
        (ot0, otr, wa, wb),
        flops=2 * D * 1024 * HALF,
    )


def route_body(rt, ids, ids_t):
    lane = lax.broadcasted_iota(jnp.int32, (T, E), 1)
    row = lax.broadcasted_iota(jnp.int32, (T, E), 0)
    wide = jnp.concatenate([rt[...].astype(f32), jnp.zeros((124, T), f32)], axis=0).T
    hot = [jnp.where(lane.astype(f32) == wide[:, k : k + 1], 1.0, 0.0) for k in range(4)]
    earlier = jnp.where(lane < row, 1.0, 0.0).astype(bf16)
    before = dot(earlier, (hot[0] + hot[1] + hot[2] + hot[3]).astype(bf16))
    table = wide
    for k in range(4):
        slot = jnp.sum(before * hot[k], axis=1, keepdims=True)
        table = jnp.where(lane == 4 + k, slot, table)
        table = jnp.where(lane == 8 + k, slot * E + wide[:, k : k + 1], table)
    ids[...] = table.astype(jnp.int32)
    ids_t[...] = table.T[0:16, :].astype(jnp.int32)


def route_tables(routes_t):
    return call(
        route_body,
        "route_tables",
        [sds((T, 128), jnp.int32), sds((16, T), jnp.int32)],
        [],
        (routes_t,),
        flops=2 * T * T * E,
    )


def router_body(b0, b1, b2, b3, x0, g2, wr, ids, at, hidden, n2, probs, gates, wire, rows):
    for j in range(SEG):
        part = slice(j * 128, (j + 1) * 128)
        total = (
            b0[part, :].astype(f32)
            + b1[part, :].astype(f32)
            + b2[part, :].astype(f32)
            + b3[part, :].astype(f32)
        )
        hidden[:, part] = x0[:, part].astype(f32) + total.T
    v = hidden[...]
    r = lax.rsqrt(jnp.mean(v * v, axis=-1, keepdims=True) + EPS)
    n2[...] = (v * r * g2[...]).astype(bf16)
    logits = dot(n2[...], wr[...])
    pack_rows(n2, at, wire, rows)
    expo = jnp.exp(logits - jnp.max(logits, axis=-1, keepdims=True))
    p = expo / jnp.sum(expo, axis=-1, keepdims=True)
    probs[...] = p
    lane = lax.broadcasted_iota(jnp.int32, (T, E), 1)
    chosen = [
        jnp.sum(jnp.where(lane == ids[:, k : k + 1], p, 0.0), axis=-1, keepdims=True)
        for k in range(4)
    ]
    total = chosen[0] + chosen[1] + chosen[2] + chosen[3]
    packed = jnp.where(lane == 4, total, 0.0)
    for k in range(4):
        packed = jnp.where(lane == k, chosen[k] / total, packed)
    gates[...] = packed
    across = packed.T
    expert = lax.broadcasted_iota(jnp.int32, (E, T), 0)
    columns = []
    for s in range(CAP):
        mine = jnp.zeros((E, T), f32)
        for k in range(4):
            mine = jnp.where(expert + s * E == at[k : k + 1, :], across[k : k + 1, :], mine)
        columns.append(jnp.sum(mine, axis=1, keepdims=True))
    put_numbers(columns, wire)


def router(b, x0, g2, wr, ids, assign_t):
    return call(
        router_body,
        "router",
        [
            sds((T, D), f32),
            sds((T, D), bf16),
            sds((T, E), f32),
            sds((T, E), f32),
            sds((E, WIRE, 128), bf16),
        ],
        [pltpu.VMEM((SLOTS, D), bf16)],
        (*b, x0, g2, wr, ids, assign_t),
        flops=2 * SLOTS * T * D,
    )


def expert_grad_body(wire, wd, gr, ga):
    split_rows(wire, gr)

    def body(i, carry):
        cols = pl.ds(pl.multiple_of(i * 256, 256), 256)
        ga[:, cols] = dot_t(gr[...], wd[cols, :])
        return carry

    lax.fori_loop(0, F // 256, body, 0)


def expert_grad(wire, wd):
    return call(
        expert_grad_body,
        "expert_grad_rows",
        [sds((SLOTS, D), bf16), sds((SLOTS, F), f32)],
        [],
        (wire, wd),
        flops=2 * SLOTS * D * F,
    )


def expert_main_body(wire, wg, wu, ga, back, xs, act, acts, dg, du, xr, sc):
    split_rows(wire, xr)
    gates = get_numbers(wire)
    sc[...] = jnp.zeros_like(sc)

    def forward(i, carry):
        cols = pl.ds(pl.multiple_of(i * 256, 256), 256)
        gate = dot(xr[...], wg[:, cols])
        up = dot(xr[...], wu[:, cols])
        grad = ga[:, cols]
        s = 1.0 / (1.0 + jnp.exp(-gate))
        silu = gate * s
        a = silu * up
        act[:, cols] = a.astype(bf16)
        dg[:, cols] = (grad * up * s * (1.0 + gate * (1.0 - s))).astype(bf16)
        du[:, cols] = (grad * silu).astype(bf16)
        sc[...] += jnp.sum(a * grad, axis=1, keepdims=True)
        return carry

    lax.fori_loop(0, F // 256, forward, 0)
    for s in range(CAP):
        part = slice(s * E, (s + 1) * E)
        gate = gates[:, s : s + 1]
        xs[part, :] = (xr[part, :].astype(f32) * gate).astype(bf16)
        acts[part, :] = (act[part, :].astype(f32) * gate).astype(bf16)
    for j in range(8):
        part = slice(j * 256, (j + 1) * 256)
        xr[:, part] = (dot_t(dg[...], wg[part, :]) + dot_t(du[...], wu[part, :])).astype(bf16)
    join_rows(xr, back)
    put_numbers([sc[s * E : (s + 1) * E, :] for s in range(CAP)], back)


def expert_main(wire, wg, wu, ga):
    return call(
        expert_main_body,
        "expert_main",
        [
            sds((E, WIRE, 128), bf16),
            sds((SLOTS, D), bf16),
            sds((SLOTS, F), bf16),
            sds((SLOTS, F), bf16),
            sds((SLOTS, F), bf16),
            sds((SLOTS, F), bf16),
        ],
        [pltpu.VMEM((SLOTS, D), bf16), pltpu.VMEM((SLOTS, 1), f32)],
        (wire, wg, wu, ga),
        flops=8 * SLOTS * D * F,
    )


def expert_out_body(act, wd, wire, rows):
    for j in range(8):
        cols = slice(j * 256, (j + 1) * 256)
        rows[:, cols] = dot(act[...], wd[:, cols]).astype(bf16)
    join_rows(rows, wire)


def expert_out(act, wd):
    return call(
        expert_out_body,
        "expert_out",
        [sds((E, CAP * SEG, 128), bf16)],
        [pltpu.VMEM((SLOTS, D), bf16)],
        (act, wd),
        flops=2 * SLOTS * D * F,
    )[0]


def combine_body(
    where, experts, slots, gate_list, wire, hidden, n2, probs, gates, ids, og, g2, wr,
    ghid, gatt, grouter, gg2, sums, gn2,
):
    sum_rows(wire, experts, slots, gate_list, sums)
    scores = get_numbers(wire)
    lane = lax.broadcasted_iota(jnp.int32, (T, E), 1)
    grads = []
    for k in range(4):
        hot = jnp.where(lane == ids[:, k : k + 1], 1.0, 0.0)
        rows = lax.dot_general(
            hot, scores, (((1,), (0,)), ((), ())),
            precision=lax.Precision.HIGHEST, preferred_element_type=f32,
        )
        picked = jnp.where(lane == ids[:, 4 + k : 5 + k], rows, 0.0)
        grads.append(jnp.sum(picked, axis=-1, keepdims=True))
    inner = sum(grads[k] * gates[:, k : k + 1] for k in range(4))
    inverse = 1.0 / gates[:, 4:5]
    grad_probs = jnp.zeros((T, E), f32)
    for k in range(4):
        grad_probs = jnp.where(
            lane == ids[:, k : k + 1], (grads[k] - inner) * inverse, grad_probs
        )
    p = probs[...]
    gl = (p * (grad_probs - jnp.sum(p * grad_probs, axis=-1, keepdims=True))).astype(bf16)
    for h in range(2):
        tokens = slice(h * 64, (h + 1) * 64)
        gn2[tokens, :] = sums[h * 1024 : (h + 1) * 1024, :].reshape(64, D)
    gn2[...] += dot_t(gl, wr[...])
    c = gn2[...]
    v = hidden[...]
    r = lax.rsqrt(jnp.mean(v * v, axis=-1, keepdims=True) + EPS)
    u = c * g2[...]
    m = jnp.mean(u * v, axis=-1, keepdims=True)
    total = og[...].astype(f32) + r * u - v * (r * r * r * m)
    ghid[...] = total
    gatt[...] = total.astype(bf16)
    gg2[...] = jnp.sum(c * (v * r), axis=0, keepdims=True)
    for j in range(SEG):
        cols = slice(j * 128, (j + 1) * 128)
        grouter[cols, :] = dot(n2[:, cols].astype(f32).T.astype(bf16), gl).astype(bf16)


def combine(*args):
    return call(
        combine_body,
        "combine_grads",
        [sds((T, D), f32), sds((T, D), bf16), sds((D, E), bf16), sds((1, D), f32)],
        [pltpu.VMEM((T * SEG, 128), f32), pltpu.VMEM((T, D), f32)],
        args,
        flops=4 * SLOTS * T * D,
        smem=(0, 1, 2, 3),
    )


def result_body(experts, slots, gate_list, wire, hidden, out, sums):
    sum_rows(wire, experts, slots, gate_list, sums)
    for h in range(2):
        tokens = slice(h * 64, (h + 1) * 64)
        mixture = sums[h * 1024 : (h + 1) * 1024, :].reshape(64, D)
        out[tokens, :] = (hidden[tokens, :] + mixture).astype(bf16)


def result_rows(*args):
    return call(
        result_body,
        "result",
        [sds((T, D), bf16)],
        [pltpu.VMEM((T * SEG, 128), f32)],
        args,
        flops=4 * SLOTS * T * D,
        smem=(0, 1, 2),
    )[0]


def pre_body(*refs):
    blocks, (ot0, ot1, wo, gw, dt, rows_all, total) = refs[:8], refs[8:]
    step = pl.program_id(0)
    for b in range(8):
        rows_all[b * T : (b + 1) * T, :] = blocks[b][...]
    gw[...] = (dot(ot0[...], rows_all[:HALF, :]) + dot(ot1[...], rows_all[HALF:, :])).astype(bf16)
    part = dot_t(wo[...], rows_all[...])

    @pl.when(step == 0)
    def _():
        total[...] = part

    @pl.when(step > 0)
    def _():
        total[...] += part

    @pl.when(step == 3)
    def _():
        dt[...] = total[...].astype(bf16)


def pre(blocks, ot0, ot1, wo):
    return grid_call(
        pre_body,
        "out_projection_grad",
        (4,),
        [cols_of((T, 512))] * 8 + [whole((512, HALF))] * 2 + [cols_of((512, 512))],
        [cols_of((512, 512)), whole((512, ROWS))],
        [sds((LH * HEAD, D), bf16), sds((LH * HEAD, ROWS), bf16)],
        [pltpu.VMEM((ROWS, 512), bf16), pltpu.VMEM((512, ROWS), f32)],
        (*blocks, ot0, ot1, wo),
        flops=4 * 512 * ROWS * D,
    )


def bwd_body(*refs):
    qr, kr = refs[0:4], refs[4:8]
    (qt, kt, kn, vn, dt, ot0, ot1, linv, info, cos, sin, gq, gk) = refs[8:21]
    dq0, dq1, dkv, ggq, ggk, mask, wb, sb, dqt, dk, dv, raw = refs[21:]
    build_mask(info, mask)
    dk[...] = jnp.zeros_like(dk)
    dv[...] = jnp.zeros_like(dv)
    for half, out in ((0, ot0), (1, ot1)):

        def body(i, carry):
            local = pl.ds(pl.multiple_of(i * 256, 256), 256)
            cols = pl.ds(pl.multiple_of(half * HALF + i * 256, 256), 256)
            for h in range(LH):
                heads = slice(h * HEAD, (h + 1) * HEAD)
                part = slice(h * 256, (h + 1) * 256)
                scores = dot(kn[...], qt[heads, cols])
                weights = jnp.exp2(scores * LOG2E) * (mask[:, cols] * linv[h : h + 1, cols])
                grad = dt[heads, cols]
                delta = jnp.sum(
                    grad.astype(f32) * out[heads, local].astype(f32), axis=0, keepdims=True
                )
                wb[:, part] = weights.astype(bf16)
                sb[:, part] = (weights * (dot(vn[...], grad) - delta)).astype(bf16)
                dqt[heads, cols] = dot(kt[...], sb[:, part])
            grads = jnp.concatenate(
                [dt[h * HEAD : (h + 1) * HEAD, cols] for h in range(LH)], axis=1
            )
            queries = jnp.concatenate(
                [qt[h * HEAD : (h + 1) * HEAD, cols] for h in range(LH)], axis=1
            )
            dv[...] += dot_t(wb[...], grads)
            dk[...] += dot_t(sb[...], queries)
            return carry

        lax.fori_loop(0, 2, body, 0)

    def unrope(v):
        low, high = v[:64], v[64:]
        c, s = cos[...], sin[...]
        return jnp.concatenate([low * c + high * s, high * c - low * s], axis=0)

    def norm_back(v, grad, gain):
        r = lax.rsqrt(jnp.mean(v * v, axis=0, keepdims=True) + EPS)
        n = v * r
        gain_grad = jnp.sum(grad * n, axis=1, keepdims=True)
        u = grad * gain
        return r * (u - n * jnp.mean(u * n, axis=0, keepdims=True)), gain_grad

    gain_q, gain_k = column(gq[...]), column(gk[...])
    total = jnp.zeros((HEAD, 1), f32)
    for h in range(LH):
        heads = slice(h * HEAD, (h + 1) * HEAD)
        for dy in range(4):
            for dc in range(2):
                to = slice(dc * HALF + dy * T, dc * HALF + (dy + 1) * T)
                raw[:, to] = qr[dy][heads, dc * T : (dc + 1) * T]
        grad, part = norm_back(raw[...], unrope(dqt[heads, :] * (HEAD ** (-0.5))), gain_q)
        total = total + part
        dq0[heads, :] = grad[:, :HALF].astype(bf16)
        dq1[heads, :] = grad[:, HALF:].astype(bf16)
    ggq[...] = jnp.broadcast_to(total, (HEAD, 128)).T[0:8, :]
    for dy in range(4):
        for dc in range(2):
            to = slice(dc * HALF + dy * T, dc * HALF + (dy + 1) * T)
            raw[:, to] = kr[dy][:, dc * T : (dc + 1) * T].astype(f32)
    grad, part = norm_back(raw[...], unrope(dk[...].T), gain_k)
    ggk[...] = jnp.broadcast_to(part, (HEAD, 128)).T[0:8, :]
    dkv[:HEAD, :] = grad.astype(bf16)
    dkv[HEAD:, :] = dv[...].T.astype(bf16)


def bwd(qr, kr, *rest):
    return call(
        bwd_body,
        "attend_grad",
        [
            sds((LH * HEAD, HALF), bf16),
            sds((LH * HEAD, HALF), bf16),
            sds((2 * HEAD, ROWS), bf16),
            sds((8, HEAD), f32),
            sds((8, HEAD), f32),
        ],
        [
            pltpu.VMEM((ROWS, ROWS), f32),
            pltpu.VMEM((ROWS, LH * 256), bf16),
            pltpu.VMEM((ROWS, LH * 256), bf16),
            pltpu.VMEM((LH * HEAD, ROWS), f32),
            pltpu.VMEM((ROWS, HEAD), f32),
            pltpu.VMEM((ROWS, HEAD), f32),
            pltpu.VMEM((HEAD, ROWS), f32),
        ],
        (*qr, *kr, *rest),
        flops=10 * LH * ROWS * ROWS * HEAD,
    )


def qkv_grad_body(where, n1t, dq0, dq1, own, sib, wa, wb, tot, dt):
    @pl.when(pl.program_id(0) == 0)
    def _():
        tot[:, :HALF] = (own[:, :HALF].astype(f32) + sib[:, HALF:].astype(f32)).astype(bf16)
        tot[:, HALF:] = (own[:, HALF:].astype(f32) + sib[:, :HALF].astype(f32)).astype(bf16)
        dt[:512, :HALF] = dq0[...]
        dt[:512, HALF:] = dq1[...]
        upper = where[2] == 1
        dt[512:576, :] = jnp.where(upper, tot[64:128, :], tot[:64, :])
        dt[576:, :] = jnp.where(upper, tot[192:, :], tot[128:192, :])

    grad = dot_t(n1t[...], dt[...]).astype(bf16)
    for col in range(4):
        dx = lax.rem(col + 4 - where[1], 4)
        wa[0, dx] = grad[col * 128 : col * 128 + 64, :]
        wb[dx, 0] = grad[col * 128 + 64 : (col + 1) * 128, :]


def qkv_grad(where, n1t, dq0, dq1, own, sib):
    return grid_call(
        qkv_grad_body,
        "qkv_weight_grad",
        (4,),
        [
            rows_of((512, ROWS)),
            whole((512, HALF)),
            whole((512, HALF)),
            whole((2 * HEAD, ROWS)),
            whole((2 * HEAD, ROWS)),
        ],
        [
            pl.BlockSpec((1, 4, 64, 640), lambda i, w: (lax.rem(i + 4 - w[0], 4), 0, 0, 0)),
            pl.BlockSpec((4, 1, 64, 640), lambda i, w: (0, lax.rem(i + 4 - w[0], 4), 0, 0)),
            whole((2 * HEAD, ROWS)),
        ],
        [
            sds((4, 4, 64, 640), bf16),
            sds((4, 4, 64, 640), bf16),
            sds((2 * HEAD, ROWS), bf16),
        ],
        [pltpu.VMEM((640, ROWS), bf16)],
        (where, n1t, dq0, dq1, own, sib),
        flops=2 * D * 640 * ROWS,
        scalars=1,
    )


def normed_grad_body(wa, wb, wkv, dq0, dqr, tot, n1t, b0, b1, b2, b3, gg1):
    total = dot(wa[...], dq0[...]) + dot(wb[...], dqr[...]) + dot(wkv[...], tot[...])
    for dy, out in enumerate((b0, b1, b2, b3)):
        out[...] = total[:, dy * T : (dy + 1) * T].astype(bf16)
    gain = jnp.sum(total * n1t[...].astype(f32), axis=1, keepdims=True)
    for b in range(4):
        rows = slice(b * 128, (b + 1) * 128)
        gg1[:, rows] = jnp.broadcast_to(gain[rows, :], (128, 128)).T[0:8, :]


def normed_grad(wa, wb, wkv, dq0, dqr, tot, n1t):
    return grid_call(
        normed_grad_body,
        "normed_grad",
        (4,),
        [
            rows_of((512, 512)),
            rows_of((512, 512)),
            rows_of((512, 256)),
            whole((512, HALF)),
            whole((512, HALF)),
            whole((2 * HEAD, HALF)),
            rows_of((512, HALF)),
        ],
        [rows_of((512, T))] * 4 + [cols_of((8, 512))],
        [sds((D, T), bf16)] * 4 + [sds((8, D), f32)],
        [],
        (wa, wb, wkv, dq0, dqr, tot, n1t),
        flops=2 * D * 1280 * HALF,
    )


def place_body(where, *refs):
    first, second, (gq, gkt, gvt) = refs[:4], refs[4:8], refs[8:]
    for dz in range(4):
        for dx in range(4):
            chunk = lax.rem(where[0] + dz, 4) * 4 + lax.rem(where[1] + dx, 4)
            start = pl.multiple_of(chunk * 128, 128)
            a = first[dz][dx].astype(f32)
            b = second[dx][dz].astype(f32)
            gq[pl.ds(start, 64), :] = a[:, :512]
            gq[pl.ds(start + 64, 64), :] = b[:, :512]
            both = jnp.concatenate([a[:, 512:], b[:, 512:]], axis=0).T
            gkt[:, pl.ds(start, 128)] = both[:64]
            gvt[:, pl.ds(start, 128)] = both[64:]


def place(where, first, second):
    return call(
        place_body,
        "place_weight_grads",
        [sds((D, 512), f32), sds((64, D), f32), sds((64, D), f32)],
        [],
        (where, *first, *second),
        smem=(0,),
    )


def final_body(b0, b1, b2, b3, x0, ghid, g1, out, c):
    for j in range(SEG):
        rows = slice(j * 128, (j + 1) * 128)
        total = (
            b0[rows, :].astype(f32)
            + b1[rows, :].astype(f32)
            + b2[rows, :].astype(f32)
            + b3[rows, :].astype(f32)
        )
        c[:, rows] = total.T
    v = x0[...].astype(f32)
    r = lax.rsqrt(jnp.mean(v * v, axis=-1, keepdims=True) + EPS)
    u = c[...] * g1[...]
    m = jnp.mean(u * v, axis=-1, keepdims=True)
    out[...] = ghid[...] + r * u - v * (r * r * r * m)


def final(b, x0, ghid, g1):
    return call(
        final_body,
        "input_grad",
        [sds((T, D), f32)],
        [pltpu.VMEM((T, D), f32)],
        (*b, x0, ghid, g1),
        flops=T * D * 10,
    )[0]


def sibling(x):
    return lax.ppermute(x, "shard", [(i, i ^ 1) for i in range(8)])


def from_chip(x, dy):
    return lax.ppermute(x, "shard", [(i, (i - 2 * dy) % 8) for i in range(8)])


def to_chip(x, dy):
    return lax.ppermute(x, "shard", [(i, (i + 2 * dy) % 8) for i in range(8)])


def gather_blocks(x):
    first = [x] + [from_chip(x, dy) for dy in (1, 2, 3)]
    return first, [sibling(b) for b in first]


def exchange(x):
    return lax.all_to_all(x, ALL, split_axis=0, concat_axis=0, tiled=True)


def spread(x):
    return [to_chip(x[d], d) for d in (1, 3, 2)]


def on_expert(x, dz, dx):
    pairs = [
        (z * 4 + c, ((z + dz) % 4) * 4 + (c + dx) % 4) for z in range(4) for c in range(4)
    ]
    return lax.ppermute(x, "expert", pairs)


def move(x, axis, distance):
    return on_expert(x, distance, 0) if axis == 0 else on_expert(x, 0, distance)


def reduce_step(x, axis):
    got = [move(x[d], axis, d) for d in (1, 3, 2)]
    return (
        x[0].astype(f32) + got[0].astype(f32) + got[1].astype(f32) + got[2].astype(f32)
    ).astype(bf16)


def gather_step(x, axis):
    return [x] + [move(x, axis, (4 - d) % 4) for d in (1, 2, 3)]


def sum_over_experts(a, b):
    a1, b1 = reduce_step(a, 0), reduce_step(b, 1)
    a2, b2 = reduce_step(a1, 1), reduce_step(b1, 0)
    a3, b3 = jnp.stack(gather_step(a2, 1)), jnp.stack(gather_step(b2, 0))
    return gather_step(a3, 0), gather_step(b3, 1)


def after(value, *others):
    return lax.optimization_barrier((value, *others))[0]


def on_device(
    block_input, out_grad, norm1_gain, w_query, w_key, w_value, query_gain, key_gain, w_out,
    norm2_gain, w_router, w_gate, w_up, w_down, seq_lengths, token_places, expert_routes,
):
    shard, owner = lax.axis_index("shard"), lax.axis_index("expert")
    chip, core = shard // 2, shard % 2
    where = jnp.stack([owner // 4, owner % 4, core]).astype(jnp.int32)
    core_id = core.reshape(1)
    g1 = norm1_gain.astype(f32).reshape(1, D)
    g2 = norm2_gain.astype(f32).reshape(1, D)
    gq = query_gain.astype(f32).reshape(1, HEAD)
    gk = key_gain.astype(f32).reshape(1, HEAD)

    x_own, x_sib = gather_blocks(block_input)

    chips = (chip + jnp.arange(4)) % 4
    order = jnp.concatenate([chips * 2 + core, chips * 2 + 1 - core])
    places = token_places[0].reshape(8, T)[order].reshape(ROWS)
    lengths = seq_lengths[0]
    ends = jnp.cumsum(lengths)
    starts = jnp.sum(
        jnp.where(places[:, None] >= ends[None, :], lengths[None, :], 0), axis=1
    )
    positions = (places - starts).astype(f32)
    info = jnp.concatenate(
        [places[None].astype(f32), starts[None].astype(f32), jnp.zeros((6, ROWS), f32)], axis=0
    )
    inverse_freq = ROPE_BASE ** (-jnp.arange(0, HEAD, 2).astype(f32) / HEAD)
    angles = inverse_freq[:, None] * positions[None, :]
    cos, sin = jnp.cos(angles), jnp.sin(angles)

    ids, ids_t = route_tables(expert_routes.T)
    assign_t = ids_t[8:12]
    expert_list = ids[:, 0:4].reshape(-1)
    slot_list = ids[:, 4:8].reshape(-1)

    wk_t, wv_t = w_key.T, w_value.T
    wk_s, wv_s = sibling(wk_t), sibling(wv_t)
    wq_t = w_query.T
    wo_t = w_out.T
    wo_ts = sibling(wo_t)
    wq_s = sibling(w_query)

    def piece(dy):
        return qkv(
            dy, core_id, x_own[dy], x_sib[dy], g1, wq_t, wk_t, wk_s, wv_t, wv_s, gq, gk, cos, sin
        )

    pieces = [piece(dy) for dy in range(4)]
    q_raw, q, k_raw, k, v, n1, wkv = zip(*pieces)
    got_grads = exchange(pack(out_grad, assign_t))
    ot0, ot1, linv, qt, kt, kn, vn = attend(q, k, v, info)
    blocks = outproj(ot0, sibling(ot1), wo_t, wo_ts)
    blocks = [blocks[0]] + spread(blocks)
    hidden, n2, probs, gates, wire = router(blocks, block_input, g2, w_router, ids, assign_t)
    got_rows = exchange(wire)

    n1 = after(n1, wire)
    n1_t = jnp.concatenate([p[:T] for p in n1] + [p[T:] for p in n1], axis=0).T
    wkv_full = after(wkv[0], wire).T
    gate_list = gates[:, :4].reshape(-1)
    grad_rows, grad_act = expert_grad(after(got_grads, wire), w_down[0])
    got_rows, n1_t, wkv_full, grad_act, gate_list = lax.optimization_barrier(
        (got_rows, n1_t, wkv_full, grad_act, gate_list)
    )

    back, rows, act, scaled_act, dg, du = expert_main(got_rows, w_gate[0], w_up[0], grad_act)
    back_wire = exchange(back)

    rows, act, scaled_act, dg, du = after((rows, act, scaled_act, dg, du), back)
    out_wire = expert_out(act, w_down[0])

    def weight_grad(a, b):
        return lax.dot_general(a, b, (((0,), (0,)), ((), ())), preferred_element_type=f32)

    grad_wgate = weight_grad(rows, dg)
    grad_wup = weight_grad(rows, du)
    grad_wdown = weight_grad(scaled_act, grad_rows)
    back_wire, out_wire, grad_wgate, grad_wup, grad_wdown = lax.optimization_barrier(
        (back_wire, out_wire, grad_wgate, grad_wup, grad_wdown)
    )

    ghid, gatt, grouter, gg2 = combine(
        where, expert_list, slot_list, gate_list, back_wire, hidden, n2, probs, gates, ids,
        out_grad, g2, w_router,
    )
    g_own, g_sib = gather_blocks(gatt)
    router_parts = exchange(grouter.reshape(E, SEG, 128))
    router_sum = jnp.sum(router_parts.astype(f32), axis=0).astype(bf16)
    returned = exchange(after(out_wire, g_own[2]))

    gwout, dt = pre(g_own + g_sib, ot0, ot1, w_out)
    grad_wout = lax.psum(gwout, "expert").astype(f32)
    dq0, dq1, dkv, ggq, ggk = bwd(
        q_raw, k_raw, qt, kt, kn, vn, dt, ot0, ot1, linv, info, cos, sin, gq, gk
    )
    dq_sib, dkv_sib = sibling(dq1), sibling(dkv)
    gw_a, gw_b, dkv_total = qkv_grad(where, n1_t, dq0, dq1, dkv, dkv_sib)
    gw_a, gw_b = sum_over_experts(gw_a, gw_b)
    blocks = normed_grad(w_query, wq_s, wkv_full, dq0, dq_sib, dkv_total, n1_t)
    gg1 = blocks[4][0]
    blocks, returned, router_sum = lax.optimization_barrier((blocks[:4], returned, router_sum))
    blocks = [blocks[0]] + spread(blocks)
    result = result_rows(expert_list, slot_list, gate_list, returned, hidden)

    vector = jnp.concatenate([gg1 / g1[0], gg2[0], ggq[0], ggk[0]])
    per = vector.shape[0] // E
    wide = jnp.pad(vector.reshape(E, per), ((0, 0), (0, 128 - per))).reshape(E, 1, 128)
    mine = jnp.sum(exchange(wide), axis=0)
    first = mine.astype(bf16)
    second = (mine - first.astype(f32)).astype(bf16)
    shared = jnp.concatenate([router_sum, first, second, jnp.zeros((6, 128), bf16)], axis=0)
    shared = exchange(jnp.broadcast_to(shared[None], (E, 24, 128)))
    grad_router = shared[:, :SEG].reshape(D, E).astype(f32)
    vector = (
        (shared[:, SEG].astype(f32) + shared[:, SEG + 1].astype(f32))[:, :per].reshape(-1)
    )
    grad_input = final(blocks, block_input, ghid, g1)
    grad_wq, grad_wk, grad_wv = place(where, gw_a, gw_b)
    return (
        result,
        grad_input,
        vector[:D],
        grad_wq,
        grad_wk.T,
        grad_wv.T,
        vector[2 * D : 2 * D + HEAD],
        vector[2 * D + HEAD :],
        grad_wout,
        vector[D : 2 * D],
        grad_router,
        grad_wgate[None],
        grad_wup[None],
        grad_wdown[None],
    )


def solution(mesh):
    rows = P(("expert", "shard"), None)
    experts = P(("expert", "shard"), None, None)
    columns = P(None, "shard")
    return jax.shard_map(
        on_device,
        mesh=mesh,
        in_specs=(
            rows, rows, P(), columns, columns, columns, P(), P(), P("shard", None), P(), P(),
            experts, experts, experts, P("expert", None), P("expert", None), rows,
        ),
        out_specs=(
            rows, rows, P(), columns, columns, columns, P(), P(), P("shard", None), P(), P(),
            experts, experts, experts,
        ),
        check_vma=False,
    )
```

```python
import functools

import jax
import jax.numpy as jnp
from jax import lax
from jax.experimental import pallas as pl
from jax.experimental.pallas import tpu as pltpu
from jax.sharding import PartitionSpec as P

EPS = 1e-06
ROPE_BASE = 1000000.0
LOG2E = 1.4426950408889634
T = 128
D = 2048
HEAD = 128
LH = 4
E = 128
CAP = 5
SLOTS = E * CAP
SEG = D // 128
WIRE = CAP * SEG + 8
ROWS = 1024
HALF = 512
F = 768
bf16 = jnp.bfloat16
f32 = jnp.float32
ALL = ("expert", "shard")
COSTS = {
    "qkv0": 4,
    "qkv1": 4,
    "qkv2": 4,
    "qkv3": 4,
    "pack_rows": 4,
    "route_tables": 2,
    "attend": 11,
    "out_projection": 5,
    "router": 6,
    "transpose_rows": 6,
    "expert_grad_rows": 8,
    "expert_main": 18,
    "expert_out": 7,
    "combine_grads": 7,
    "head_grad": 4,
    "out_projection_grad": 7,
    "attend_grad": 19,
    "qkv_weight_grad": 8,
    "normed_grad": 7,
    "result": 4,
    "input_grad": 3,
    "place_weight_grads": 4,
}


def cost(micros):
    return pl.CostEstimate(
        flops=1, bytes_accessed=int(micros * 0.6e6) + 1, transcendentals=0
    )


def dot(a, b):
    return jnp.dot(a, b, preferred_element_type=f32)


def dot_t(a, b):
    return lax.dot_general(a, b, (((1,), (1,)), ((), ())), preferred_element_type=f32)


def call(kernel, name, outs, scratch, args, smem=()):
    in_specs = [
        pl.BlockSpec(memory_space=pltpu.SMEM if i in smem else pltpu.VMEM)
        for i in range(len(args))
    ]
    return pl.pallas_call(
        kernel,
        out_shape=outs,
        in_specs=in_specs,
        out_specs=[pl.BlockSpec(memory_space=pltpu.VMEM) for _ in outs],
        scratch_shapes=scratch,
        compiler_params=pltpu.CompilerParams(vmem_limit_bytes=56 * 1024 * 1024),
        cost_estimate=cost(COSTS.get(name, 0)),
        name=name,
    )(*args)


def grid_call(kernel, name, grid, in_specs, out_specs, outs, scratch, args, scalars=0):
    return pl.pallas_call(
        kernel,
        out_shape=outs,
        grid_spec=pltpu.PrefetchScalarGridSpec(
            num_scalar_prefetch=scalars,
            grid=grid,
            in_specs=in_specs,
            out_specs=out_specs,
            scratch_shapes=scratch,
        ),
        compiler_params=pltpu.CompilerParams(
            vmem_limit_bytes=56 * 1024 * 1024, dimension_semantics=("arbitrary",)
        ),
        cost_estimate=cost(COSTS.get(name, 0)),
        name=name,
    )(*args)


def whole(shape):
    return pl.BlockSpec(shape, lambda i, *_: (0,) * len(shape))


def rows_of(shape):
    return pl.BlockSpec(shape, lambda i, *_: (i, 0))


def cols_of(shape):
    return pl.BlockSpec(shape, lambda i, *_: (0, i))


def sds(shape, dtype):
    return jax.ShapeDtypeStruct(shape, dtype)


def split_rows(wire, dest):
    for s in range(CAP):
        for h in range(2):
            rows = slice(s * E + h * 64, s * E + (h + 1) * 64)
            block = wire[h * 64 : (h + 1) * 64, s * SEG : (s + 1) * SEG, :]
            dest[rows, :] = block.reshape(64, D)


def join_rows(source, wire):
    for s in range(CAP):
        for h in range(2):
            rows = slice(s * E + h * 64, s * E + (h + 1) * 64)
            wire[h * 64 : (h + 1) * 64, s * SEG : (s + 1) * SEG, :] = source[rows, :].reshape(
                64, SEG, 128
            )


def put_numbers(columns, wire):
    lane = lax.broadcasted_iota(jnp.int32, (E, 128), 1)
    plane = jnp.zeros((E, 128), f32)
    for s in range(CAP):
        plane = jnp.where(lane == s, columns[s], plane)
    first = plane.astype(bf16)
    rest = plane - first.astype(f32)
    second = rest.astype(bf16)
    third = (rest - second.astype(f32)).astype(bf16)
    none = jnp.zeros((E, 5 * 128), bf16)
    wide = jnp.concatenate([first, second, third, none], axis=1)
    wire[:, CAP * SEG :, :] = wide.reshape(E, 8, 128)


def get_numbers(wire):
    wide = wire[:, CAP * SEG :, :].reshape(E, 8 * 128)
    return (
        wide[:, :128].astype(f32) + wide[:, 128:256].astype(f32) + wide[:, 256:384].astype(f32)
    )


def pack_rows(x_ref, at_ref, wire, rows):
    slot = lax.broadcasted_iota(jnp.int32, (SLOTS, T), 0)
    hit = slot == at_ref[0:1, :]
    for k in range(1, 4):
        hit = hit | (slot == at_ref[k : k + 1, :])
    pick = jnp.where(hit, 1.0, 0.0).astype(bf16)
    for j in range(8):
        cols = slice(j * 256, (j + 1) * 256)
        rows[:, cols] = dot(pick, x_ref[:, cols]).astype(bf16)
    join_rows(rows, wire)


def pack_body(x_ref, at_ref, wire, rows):
    pack_rows(x_ref, at_ref, wire, rows)
    wire[:, CAP * SEG :, :] = jnp.zeros((E, 8, 128), bf16)


def pack(x, assign_t):
    return call(
        pack_body,
        "pack_rows",
        [sds((E, WIRE, 128), bf16)],
        [pltpu.VMEM((SLOTS, D), bf16)],
        (x, assign_t),
    )[0]


def sum_rows(wire, experts, slots, gates, out):
    def body(i, carry):
        for u in range(8):
            t = i * 8 + u
            total = None
            for k in range(4):
                p = t * 4 + k
                rows = pl.ds(pl.multiple_of(slots[p] * SEG, SEG), SEG)
                part = wire[experts[p], rows, :].astype(f32) * gates[p]
                total = part if total is None else total + part
            out[pl.ds(pl.multiple_of(t * SEG, SEG), SEG), :] = total
        return carry

    lax.fori_loop(0, T // 8, body, 0)


def column(row):
    return jnp.broadcast_to(row, (128, 128)).T[:, 0:1]


def qkv_body(
    piece, core, xa, xb, g1, wqt, wk, wks, wv, wvs, gq, gk, cos, sin,
    qn, qt, kn, kt, vt, scale, n1, wkv,
):
    lower = core[0] == 0
    wkv[0:64, :] = jnp.where(lower, wk[...], wks[...])
    wkv[64:128, :] = jnp.where(lower, wks[...], wk[...])
    wkv[128:192, :] = jnp.where(lower, wv[...], wvs[...])
    wkv[192:256, :] = jnp.where(lower, wvs[...], wv[...])
    for half, ref in ((0, xa), (1, xb)):
        x = ref[...].astype(f32)
        r = lax.rsqrt(jnp.mean(x * x, axis=-1, keepdims=True) + EPS)
        n1[half * T : (half + 1) * T, :] = (x * r * g1[...]).astype(bf16)
    raw = dot_t(wqt[...], n1[...])
    raw_kv = dot_t(wkv[...], n1[...])
    gain_q, gain_k = column(gq[...]), column(gk[...])
    first, second = piece * T, HALF + piece * T
    c = jnp.concatenate([cos[:, first : first + T], cos[:, second : second + T]], axis=1)
    s = jnp.concatenate([sin[:, first : first + T], sin[:, second : second + T]], axis=1)

    def path(v, gain, factor, keep, index):
        r = lax.rsqrt(jnp.mean(v * v, axis=0, keepdims=True) + EPS)
        scale[index : index + 1, :] = r
        v = v * r
        keep[...] = v.astype(bf16)
        v = v * gain
        low, high = v[:64], v[64:]
        return (
            ((low * c - high * s) * factor).astype(bf16),
            ((high * c + low * s) * factor).astype(bf16),
        )

    scale[...] = jnp.zeros_like(scale)
    for h in range(LH):
        heads = slice(h * HEAD, (h + 1) * HEAD)
        low, high = path(raw[heads], gain_q, HEAD ** (-0.5), qn.at[heads, :], h)
        qt[h * HEAD : h * HEAD + 64, :] = low
        qt[h * HEAD + 64 : (h + 1) * HEAD, :] = high
    key = raw_kv[:HEAD].astype(bf16)
    low, high = path(key.astype(f32), gain_k, 1.0, kn, LH)
    kt[:64, :] = low
    kt[64:, :] = high
    vt[...] = raw_kv[HEAD:].astype(bf16)


def qkv(piece, *args):
    return call(
        functools.partial(qkv_body, piece),
        f"qkv{piece}",
        [
            sds((LH * HEAD, 2 * T), bf16),
            sds((LH * HEAD, 2 * T), bf16),
            sds((HEAD, 2 * T), bf16),
            sds((HEAD, 2 * T), bf16),
            sds((HEAD, 2 * T), bf16),
            sds((8, 2 * T), f32),
            sds((2 * T, D), bf16),
        ]
        + ([sds((2 * HEAD, D), bf16)] if piece == 0 else []),
        [] if piece == 0 else [pltpu.VMEM((2 * HEAD, D), bf16)],
        args,
        smem=(0,),
    )


def build_mask(info, mask):
    for b in range(8):
        keys = jnp.broadcast_to(info[0:1, b * T : (b + 1) * T], (T, T)).T
        for j in range(8):
            cols = slice(j * T, (j + 1) * T)
            inside = (keys >= info[1:2, cols]) & (keys <= info[0:1, cols])
            mask[b * T : (b + 1) * T, cols] = jnp.where(inside, 1.0, 0.0)


def attend_body(*refs):
    q, k, v = refs[0:4], refs[4:8], refs[8:12]
    info, ot0, ot1, linv, qt, kt, kn, vn, mask, vt = refs[12:]
    for dy in range(4):
        for dc in range(2):
            to = slice(dc * HALF + dy * T, dc * HALF + (dy + 1) * T)
            src = slice(dc * T, (dc + 1) * T)
            qt[:, to] = q[dy][:, src]
            kt[:, to] = k[dy][:, src]
            vt[:, to] = v[dy][:, src]
    for b in range(8):
        rows = slice(b * T, (b + 1) * T)
        kn[rows, :] = kt[:, rows].astype(f32).T.astype(bf16)
        vn[rows, :] = vt[:, rows].astype(f32).T.astype(bf16)
    build_mask(info, mask)
    for half, out in ((1, ot1), (0, ot0)):

        def body(i, carry):
            local = pl.ds(pl.multiple_of(i * 256, 256), 256)
            cols = pl.ds(pl.multiple_of(half * HALF + i * 256, 256), 256)
            for h in range(LH):
                heads = slice(h * HEAD, (h + 1) * HEAD)
                scores = dot(kn[...], qt[heads, cols])
                weights = jnp.exp2(scores * LOG2E) * mask[:, cols]
                inverse = 1.0 / jnp.sum(weights, axis=0, keepdims=True)
                out[heads, local] = (dot(vt[...], weights.astype(bf16)) * inverse).astype(bf16)
                linv[h : h + 1, cols] = inverse
            return carry

        lax.fori_loop(0, 2, body, 0)


def attend(q, k, v, info):
    return call(
        attend_body,
        "attend",
        [
            sds((LH * HEAD, HALF), bf16),
            sds((LH * HEAD, HALF), bf16),
            sds((8, ROWS), f32),
            sds((LH * HEAD, ROWS), bf16),
            sds((HEAD, ROWS), bf16),
            sds((ROWS, HEAD), bf16),
            sds((ROWS, HEAD), bf16),
        ],
        [pltpu.VMEM((ROWS, ROWS), f32), pltpu.VMEM((HEAD, ROWS), bf16)],
        (*q, *k, *v, info),
    )


def flip(source, dest, row, col):
    height, width = source.shape
    for a in range(height // 128):
        for b in range(width // 128):
            block = source[a * 128 : (a + 1) * 128, b * 128 : (b + 1) * 128]
            rows = slice(row + b * 128, row + (b + 1) * 128)
            dest[rows, col + a * 128 : col + (a + 1) * 128] = block.astype(f32).T.astype(bf16)


def outproj_body(ot0, otr, wa, wb, b0, b1, b2, b3, heads):
    @pl.when(pl.program_id(0) == 0)
    def _():
        flip(ot0, heads, 0, 0)
        flip(otr, heads, 0, 512)

    total = dot(heads[:, :512], wa[...]) + dot(heads[:, 512:], wb[...])
    for dy, out in enumerate((b0, b1, b2, b3)):
        out[...] = total[dy * T : (dy + 1) * T, :].astype(bf16)


def outproj(ot0, otr, wa, wb):
    return grid_call(
        outproj_body,
        "out_projection",
        (4,),
        [whole((512, HALF)), whole((512, HALF)), cols_of((512, 512)), cols_of((512, 512))],
        [cols_of((T, 512))] * 4,
        [sds((T, D), bf16)] * 4,
        [pltpu.VMEM((HALF, 1024), bf16)],
        (ot0, otr, wa, wb),
    )


def transpose_body(n0, n1, n2, n3, out):
    for dy, piece in enumerate((n0, n1, n2, n3)):
        for dc in range(2):
            flip(piece.at[dc * T : (dc + 1) * T, :], out, 0, dc * HALF + dy * T)


def transpose_rows(pieces):
    return call(transpose_body, "transpose_rows", [sds((D, ROWS), bf16)], [], tuple(pieces))[0]


def route_body(rt, ids, ids_t):
    lane = lax.broadcasted_iota(jnp.int32, (T, E), 1)
    row = lax.broadcasted_iota(jnp.int32, (T, E), 0)
    wide = jnp.concatenate([rt[...].astype(f32), jnp.zeros((124, T), f32)], axis=0).T
    hot = [jnp.where(lane.astype(f32) == wide[:, k : k + 1], 1.0, 0.0) for k in range(4)]
    earlier = jnp.where(lane < row, 1.0, 0.0).astype(bf16)
    before = dot(earlier, (hot[0] + hot[1] + hot[2] + hot[3]).astype(bf16))
    table = wide
    for k in range(4):
        slot = jnp.sum(before * hot[k], axis=1, keepdims=True)
        table = jnp.where(lane == 4 + k, slot, table)
        table = jnp.where(lane == 8 + k, slot * E + wide[:, k : k + 1], table)
    ids[...] = table.astype(jnp.int32)
    ids_t[...] = table.T[0:16, :].astype(jnp.int32)


def route_tables(routes_t):
    return call(
        route_body,
        "route_tables",
        [sds((T, 128), jnp.int32), sds((16, T), jnp.int32)],
        [],
        (routes_t,),
    )


def router_body(b0, b1, b2, b3, x0, g2, wr, ids, at, hidden, n2, probs, gates, wire, rows):
    v = x0[...].astype(f32) + (
        (b0[...].astype(f32) + b1[...].astype(f32))
        + (b2[...].astype(f32) + b3[...].astype(f32))
    )
    hidden[...] = v
    r = lax.rsqrt(jnp.mean(v * v, axis=-1, keepdims=True) + EPS)
    n2[...] = (v * r * g2[...]).astype(bf16)
    logits = dot(n2[...], wr[...])
    pack_rows(n2, at, wire, rows)
    expo = jnp.exp(logits - jnp.max(logits, axis=-1, keepdims=True))
    p = expo / jnp.sum(expo, axis=-1, keepdims=True)
    probs[...] = p
    lane = lax.broadcasted_iota(jnp.int32, (T, E), 1)
    chosen = [
        jnp.sum(jnp.where(lane == ids[:, k : k + 1], p, 0.0), axis=-1, keepdims=True)
        for k in range(4)
    ]
    total = chosen[0] + chosen[1] + chosen[2] + chosen[3]
    packed = jnp.where(lane == 4, total, 0.0)
    for k in range(4):
        packed = jnp.where(lane == k, chosen[k] / total, packed)
    gates[...] = packed
    across = packed.T
    expert = lax.broadcasted_iota(jnp.int32, (E, T), 0)
    columns = []
    for s in range(CAP):
        mine = jnp.zeros((E, T), f32)
        for k in range(4):
            mine = jnp.where(expert + s * E == at[k : k + 1, :], across[k : k + 1, :], mine)
        columns.append(jnp.sum(mine, axis=1, keepdims=True))
    put_numbers(columns, wire)


def router(b, x0, g2, wr, ids, assign_t):
    return call(
        router_body,
        "router",
        [
            sds((T, D), f32),
            sds((T, D), bf16),
            sds((T, E), f32),
            sds((T, E), f32),
            sds((E, WIRE, 128), bf16),
        ],
        [pltpu.VMEM((SLOTS, D), bf16)],
        (*b, x0, g2, wr, ids, assign_t),
    )


def expert_grad_body(wire, wd, gr, ga):
    split_rows(wire, gr)

    def body(i, carry):
        cols = pl.ds(pl.multiple_of(i * 256, 256), 256)
        ga[:, cols] = dot_t(gr[...], wd[cols, :])
        return carry

    lax.fori_loop(0, F // 256, body, 0)


def expert_grad(wire, wd):
    return call(
        expert_grad_body,
        "expert_grad_rows",
        [sds((SLOTS, D), bf16), sds((SLOTS, F), f32)],
        [],
        (wire, wd),
    )


def expert_main_body(wire, wg, wu, ga, back, xs, act, acts, dg, du, xr, sc):
    split_rows(wire, xr)
    gates = get_numbers(wire)
    sc[...] = jnp.zeros_like(sc)

    def forward(i, carry):
        cols = pl.ds(pl.multiple_of(i * 256, 256), 256)
        gate = dot(xr[...], wg[:, cols])
        up = dot(xr[...], wu[:, cols])
        grad = ga[:, cols]
        s = 1.0 / (1.0 + jnp.exp(-gate))
        silu = gate * s
        a = silu * up
        act[:, cols] = a.astype(bf16)
        dg[:, cols] = (grad * up * s * (1.0 + gate * (1.0 - s))).astype(bf16)
        du[:, cols] = (grad * silu).astype(bf16)
        sc[...] += jnp.sum(a * grad, axis=1, keepdims=True)
        return carry

    lax.fori_loop(0, F // 256, forward, 0)
    for s in range(CAP):
        part = slice(s * E, (s + 1) * E)
        gate = gates[:, s : s + 1]
        xs[part, :] = (xr[part, :].astype(f32) * gate).astype(bf16)
        acts[part, :] = (act[part, :].astype(f32) * gate).astype(bf16)
    for j in range(8):
        part = slice(j * 256, (j + 1) * 256)
        xr[:, part] = (dot_t(dg[...], wg[part, :]) + dot_t(du[...], wu[part, :])).astype(bf16)
    join_rows(xr, back)
    put_numbers([sc[s * E : (s + 1) * E, :] for s in range(CAP)], back)


def expert_main(wire, wg, wu, ga):
    return call(
        expert_main_body,
        "expert_main",
        [
            sds((E, WIRE, 128), bf16),
            sds((SLOTS, D), bf16),
            sds((SLOTS, F), bf16),
            sds((SLOTS, F), bf16),
            sds((SLOTS, F), bf16),
            sds((SLOTS, F), bf16),
        ],
        [pltpu.VMEM((SLOTS, D), bf16), pltpu.VMEM((SLOTS, 1), f32)],
        (wire, wg, wu, ga),
    )


def expert_out_body(act, wd, wire, rows):
    for j in range(8):
        cols = slice(j * 256, (j + 1) * 256)
        rows[:, cols] = dot(act[...], wd[:, cols]).astype(bf16)
    join_rows(rows, wire)


def expert_out(act, wd):
    return call(
        expert_out_body,
        "expert_out",
        [sds((E, CAP * SEG, 128), bf16)],
        [pltpu.VMEM((SLOTS, D), bf16)],
        (act, wd),
    )[0]


def combine_body(
    where, experts, slots, gate_list, wire, hidden, n2, probs, gates, ids, og, g2, wr,
    ghid, gatt, grouter, gg2, sums, gn2,
):
    sum_rows(wire, experts, slots, gate_list, sums)
    scores = get_numbers(wire)
    lane = lax.broadcasted_iota(jnp.int32, (T, E), 1)
    grads = []
    for k in range(4):
        hot = jnp.where(lane == ids[:, k : k + 1], 1.0, 0.0)
        rows = lax.dot_general(
            hot, scores, (((1,), (0,)), ((), ())),
            precision=lax.Precision.HIGHEST, preferred_element_type=f32,
        )
        picked = jnp.where(lane == ids[:, 4 + k : 5 + k], rows, 0.0)
        grads.append(jnp.sum(picked, axis=-1, keepdims=True))
    inner = sum(grads[k] * gates[:, k : k + 1] for k in range(4))
    inverse = 1.0 / gates[:, 4:5]
    grad_probs = jnp.zeros((T, E), f32)
    for k in range(4):
        grad_probs = jnp.where(
            lane == ids[:, k : k + 1], (grads[k] - inner) * inverse, grad_probs
        )
    p = probs[...]
    gl = (p * (grad_probs - jnp.sum(p * grad_probs, axis=-1, keepdims=True))).astype(bf16)
    for h in range(2):
        tokens = slice(h * 64, (h + 1) * 64)
        gn2[tokens, :] = sums[h * 1024 : (h + 1) * 1024, :].reshape(64, D)
    gn2[...] += dot_t(gl, wr[...])
    c = gn2[...]
    v = hidden[...]
    r = lax.rsqrt(jnp.mean(v * v, axis=-1, keepdims=True) + EPS)
    u = c * g2[...]
    m = jnp.mean(u * v, axis=-1, keepdims=True)
    total = og[...].astype(f32) + r * u - v * (r * r * r * m)
    ghid[...] = total
    gatt[...] = total.astype(bf16)
    gg2[...] = jnp.sum(c * (v * r), axis=0, keepdims=True)
    for j in range(SEG):
        cols = slice(j * 128, (j + 1) * 128)
        grouter[cols, :] = dot(n2[:, cols].astype(f32).T.astype(bf16), gl).astype(bf16)


def combine(*args):
    return call(
        combine_body,
        "combine_grads",
        [sds((T, D), f32), sds((T, D), bf16), sds((D, E), bf16), sds((1, D), f32)],
        [pltpu.VMEM((T * SEG, 128), f32), pltpu.VMEM((T, D), f32)],
        args,
        smem=(0, 1, 2, 3),
    )


def result_body(experts, slots, gate_list, wire, hidden, out, sums):
    sum_rows(wire, experts, slots, gate_list, sums)
    for h in range(2):
        tokens = slice(h * 64, (h + 1) * 64)
        mixture = sums[h * 1024 : (h + 1) * 1024, :].reshape(64, D)
        out[tokens, :] = (hidden[tokens, :] + mixture).astype(bf16)


def result_rows(*args):
    return call(
        result_body,
        "result",
        [sds((T, D), bf16)],
        [pltpu.VMEM((T * SEG, 128), f32)],
        args,
        smem=(0, 1, 2),
    )[0]


def head_grad_body(*refs):
    blocks, (wo, dt, rows_all) = refs[:6], refs[6:]
    for b in range(6):
        rows_all[b * T : (b + 1) * T, :] = blocks[b][...]
    for b in range(3):
        rows = slice(b * 256, (b + 1) * 256)
        dt[:, rows] = dot_t(wo[...], rows_all[rows, :]).astype(bf16)


def head_grad(blocks, wo):
    return call(
        head_grad_body,
        "head_grad",
        [sds((LH * HEAD, 6 * T), bf16)],
        [pltpu.VMEM((6 * T, D), bf16)],
        (*blocks, wo),
    )[0]


def pre_body(*refs):
    blocks, (ot0, ot1, wo, gw, dt, rows_all, total) = refs[:8], refs[8:]
    step = pl.program_id(0)
    for b in range(8):
        rows_all[b * T : (b + 1) * T, :] = blocks[b][...]
    gw[...] = (dot(ot0[...], rows_all[:HALF, :]) + dot(ot1[...], rows_all[HALF:, :])).astype(bf16)
    last = jnp.concatenate([blocks[2][...], blocks[6][...]], axis=0)
    part = dot_t(wo[...], last)

    @pl.when(step == 0)
    def _():
        total[...] = part

    @pl.when(step > 0)
    def _():
        total[...] += part

    @pl.when(step == 3)
    def _():
        dt[...] = total[...].astype(bf16)


def pre(blocks, ot0, ot1, wo):
    return grid_call(
        pre_body,
        "out_projection_grad",
        (4,),
        [cols_of((T, 512))] * 8 + [whole((512, HALF))] * 2 + [cols_of((512, 512))],
        [cols_of((512, 512)), whole((512, 2 * T))],
        [sds((LH * HEAD, D), bf16), sds((LH * HEAD, 2 * T), bf16)],
        [pltpu.VMEM((ROWS, 512), bf16), pltpu.VMEM((512, 2 * T), f32)],
        (*blocks, ot0, ot1, wo),
    )


def bwd_body(*refs):
    qh, kh, scales = refs[0:4], refs[4:8], refs[8:12]
    (qt, kt, kn, vn, dta, dtb, ot0, ot1, linv, info, cos, sin, gq, gk) = refs[12:26]
    dq0, dq1, dkv, ggq, ggk, mask, wb, sb, dqt, dk, dv, raw, dt, scale = refs[26:]
    for dc in range(2):
        for place, dy in enumerate((0, 1, 3)):
            to = slice(dc * HALF + dy * T, dc * HALF + (dy + 1) * T)
            dt[:, to] = dta[:, (place * 2 + dc) * T : (place * 2 + dc + 1) * T]
        dt[:, dc * HALF + 2 * T : dc * HALF + 3 * T] = dtb[:, dc * T : (dc + 1) * T]
        for dy in range(4):
            to = slice(dc * HALF + dy * T, dc * HALF + (dy + 1) * T)
            scale[:, to] = scales[dy][:, dc * T : (dc + 1) * T]
    build_mask(info, mask)
    dk[...] = jnp.zeros_like(dk)
    dv[...] = jnp.zeros_like(dv)
    for half, out in ((0, ot0), (1, ot1)):

        def body(i, carry):
            local = pl.ds(pl.multiple_of(i * 256, 256), 256)
            cols = pl.ds(pl.multiple_of(half * HALF + i * 256, 256), 256)
            for h in range(LH):
                heads = slice(h * HEAD, (h + 1) * HEAD)
                part = slice(h * 256, (h + 1) * 256)
                scores = dot(kn[...], qt[heads, cols])
                weights = jnp.exp2(scores * LOG2E) * (mask[:, cols] * linv[h : h + 1, cols])
                grad = dt[heads, cols]
                delta = jnp.sum(
                    grad.astype(f32) * out[heads, local].astype(f32), axis=0, keepdims=True
                )
                wb[:, part] = weights.astype(bf16)
                sb[:, part] = (weights * (dot(vn[...], grad) - delta)).astype(bf16)
                dqt[heads, cols] = dot(kt[...], sb[:, part])
            grads = jnp.concatenate(
                [dt[h * HEAD : (h + 1) * HEAD, cols] for h in range(LH)], axis=1
            )
            queries = jnp.concatenate(
                [qt[h * HEAD : (h + 1) * HEAD, cols] for h in range(LH)], axis=1
            )
            dv[...] += dot_t(wb[...], grads)
            dk[...] += dot_t(sb[...], queries)
            return carry

        lax.fori_loop(0, 2, body, 0)

    def unrope(v):
        low, high = v[:64], v[64:]
        c, s = cos[...], sin[...]
        return jnp.concatenate([low * c + high * s, high * c - low * s], axis=0)

    def norm_back(n, r, grad, gain):
        gain_grad = jnp.sum(grad * n, axis=1, keepdims=True)
        u = grad * gain
        return r * (u - n * jnp.mean(u * n, axis=0, keepdims=True)), gain_grad

    gain_q, gain_k = column(gq[...]), column(gk[...])
    total = jnp.zeros((HEAD, 1), f32)
    for h in range(LH):
        heads = slice(h * HEAD, (h + 1) * HEAD)
        for dy in range(4):
            for dc in range(2):
                to = slice(dc * HALF + dy * T, dc * HALF + (dy + 1) * T)
                raw[:, to] = qh[dy][heads, dc * T : (dc + 1) * T].astype(f32)
        grad, part = norm_back(raw[...], scale[h : h + 1, :], unrope(dqt[heads, :] * (HEAD ** (-0.5))), gain_q)
        total = total + part
        dq0[heads, :] = grad[:, :HALF].astype(bf16)
        dq1[heads, :] = grad[:, HALF:].astype(bf16)
    ggq[...] = jnp.broadcast_to(total, (HEAD, 128)).T[0:8, :]
    for dy in range(4):
        for dc in range(2):
            to = slice(dc * HALF + dy * T, dc * HALF + (dy + 1) * T)
            raw[:, to] = kh[dy][:, dc * T : (dc + 1) * T].astype(f32)
    grad, part = norm_back(raw[...], scale[LH : LH + 1, :], unrope(dk[...].T), gain_k)
    ggk[...] = jnp.broadcast_to(part, (HEAD, 128)).T[0:8, :]
    dkv[:HEAD, :] = grad.astype(bf16)
    dkv[HEAD:, :] = dv[...].T.astype(bf16)


def bwd(qh, kh, scales, *rest):
    return call(
        bwd_body,
        "attend_grad",
        [
            sds((LH * HEAD, HALF), bf16),
            sds((LH * HEAD, HALF), bf16),
            sds((2 * HEAD, ROWS), bf16),
            sds((8, HEAD), f32),
            sds((8, HEAD), f32),
        ],
        [
            pltpu.VMEM((ROWS, ROWS), f32),
            pltpu.VMEM((ROWS, LH * 256), bf16),
            pltpu.VMEM((ROWS, LH * 256), bf16),
            pltpu.VMEM((LH * HEAD, ROWS), f32),
            pltpu.VMEM((ROWS, HEAD), f32),
            pltpu.VMEM((ROWS, HEAD), f32),
            pltpu.VMEM((HEAD, ROWS), f32),
            pltpu.VMEM((LH * HEAD, ROWS), bf16),
            pltpu.VMEM((8, ROWS), f32),
        ],
        (*qh, *kh, *scales, *rest),
    )


def qkv_grad_body(where, n1t, dq0, dq1, own, sib, wa, wb, tot, dt):
    @pl.when(pl.program_id(0) == 0)
    def _():
        tot[:, :HALF] = (own[:, :HALF].astype(f32) + sib[:, HALF:].astype(f32)).astype(bf16)
        tot[:, HALF:] = (own[:, HALF:].astype(f32) + sib[:, :HALF].astype(f32)).astype(bf16)
        dt[:512, :HALF] = dq0[...]
        dt[:512, HALF:] = dq1[...]
        upper = where[2] == 1
        dt[512:576, :] = jnp.where(upper, tot[64:128, :], tot[:64, :])
        dt[576:, :] = jnp.where(upper, tot[192:, :], tot[128:192, :])

    grad = dot_t(n1t[...], dt[...]).astype(bf16)
    for col in range(4):
        dx = lax.rem(col + 4 - where[1], 4)
        wa[0, dx] = grad[col * 128 : col * 128 + 64, :]
        wb[dx, 0] = grad[col * 128 + 64 : (col + 1) * 128, :]


def qkv_grad(where, n1t, dq0, dq1, own, sib):
    return grid_call(
        qkv_grad_body,
        "qkv_weight_grad",
        (4,),
        [
            rows_of((512, ROWS)),
            whole((512, HALF)),
            whole((512, HALF)),
            whole((2 * HEAD, ROWS)),
            whole((2 * HEAD, ROWS)),
        ],
        [
            pl.BlockSpec((1, 4, 64, 640), lambda i, w: (lax.rem(i + 4 - w[0], 4), 0, 0, 0)),
            pl.BlockSpec((4, 1, 64, 640), lambda i, w: (0, lax.rem(i + 4 - w[0], 4), 0, 0)),
            whole((2 * HEAD, ROWS)),
        ],
        [
            sds((4, 4, 64, 640), bf16),
            sds((4, 4, 64, 640), bf16),
            sds((2 * HEAD, ROWS), bf16),
        ],
        [pltpu.VMEM((640, ROWS), bf16)],
        (where, n1t, dq0, dq1, own, sib),
        scalars=1,
    )


def normed_grad_body(wa, wb, wkv, dq0, dqr, tot, n0, n1, n2, n3, b0, b1, b2, b3, gg1, grads):
    @pl.when(pl.program_id(0) == 0)
    def _():
        flip(dq0, grads, 0, 0)
        flip(dqr, grads, 0, 512)
        flip(tot, grads, 0, 1024)

    total = (
        dot(grads[:, :512], wa[...])
        + dot(grads[:, 512:1024], wb[...])
        + dot(grads[:, 1024:], wkv[...])
    )
    gain = jnp.zeros((1, 512), f32)
    for dy, (out, rows) in enumerate(((b0, n0), (b1, n1), (b2, n2), (b3, n3))):
        part = total[dy * T : (dy + 1) * T, :]
        out[...] = part.astype(bf16)
        gain = gain + jnp.sum(part * rows[...].astype(f32), axis=0, keepdims=True)
    gg1[...] = jnp.broadcast_to(gain, (8, 512))


def normed_grad(wa, wb, wkv, dq0, dqr, tot, n1):
    return grid_call(
        normed_grad_body,
        "normed_grad",
        (4,),
        [
            cols_of((512, 512)),
            cols_of((512, 512)),
            cols_of((256, 512)),
            whole((512, HALF)),
            whole((512, HALF)),
            whole((2 * HEAD, HALF)),
        ]
        + [cols_of((T, 512))] * 4,
        [cols_of((T, 512))] * 4 + [cols_of((8, 512))],
        [sds((T, D), bf16)] * 4 + [sds((8, D), f32)],
        [pltpu.VMEM((HALF, 1280), bf16)],
        (wa, wb, wkv, dq0, dqr, tot, *n1),
    )


def place_body(where, *refs):
    first, second, (gq, gkt, gvt) = refs[:4], refs[4:8], refs[8:]
    for dz in range(4):
        for dx in range(4):
            chunk = lax.rem(where[0] + dz, 4) * 4 + lax.rem(where[1] + dx, 4)
            start = pl.multiple_of(chunk * 128, 128)
            a = first[dz][dx].astype(f32)
            b = second[dx][dz].astype(f32)
            gq[pl.ds(start, 64), :] = a[:, :512]
            gq[pl.ds(start + 64, 64), :] = b[:, :512]
            both = jnp.concatenate([a[:, 512:], b[:, 512:]], axis=0).T
            gkt[:, pl.ds(start, 128)] = both[:64]
            gvt[:, pl.ds(start, 128)] = both[64:]


def place(where, first, second):
    return call(
        place_body,
        "place_weight_grads",
        [sds((D, 512), f32), sds((64, D), f32), sds((64, D), f32)],
        [],
        (where, *first, *second),
        smem=(0,),
    )


def final_body(b0, b1, b2, b3, x0, ghid, g1, out):
    c = (b0[...].astype(f32) + b1[...].astype(f32)) + (b2[...].astype(f32) + b3[...].astype(f32))
    v = x0[...].astype(f32)
    r = lax.rsqrt(jnp.mean(v * v, axis=-1, keepdims=True) + EPS)
    u = c * g1[...]
    m = jnp.mean(u * v, axis=-1, keepdims=True)
    out[...] = ghid[...] + r * u - v * (r * r * r * m)


def final(b, x0, ghid, g1):
    return call(final_body, "input_grad", [sds((T, D), f32)], [], (*b, x0, ghid, g1))[0]


def sibling(x):
    return lax.ppermute(x, "shard", [(i, i ^ 1) for i in range(8)])


def from_chip(x, dy):
    return lax.ppermute(x, "shard", [(i, (i - 2 * dy) % 8) for i in range(8)])


def to_chip(x, dy):
    return lax.ppermute(x, "shard", [(i, (i + 2 * dy) % 8) for i in range(8)])


def gather_blocks(x):
    first = [x] + [from_chip(x, dy) for dy in (1, 2, 3)]
    return first, [sibling(b) for b in first]


def exchange(x):
    return lax.all_to_all(x, ALL, split_axis=0, concat_axis=0, tiled=True)


def spread(x):
    return [to_chip(x[d], d) for d in (1, 3, 2)]


def on_expert(x, dz, dx):
    pairs = [
        (z * 4 + c, ((z + dz) % 4) * 4 + (c + dx) % 4) for z in range(4) for c in range(4)
    ]
    return lax.ppermute(x, "expert", pairs)


def move(x, axis, distance):
    return on_expert(x, distance, 0) if axis == 0 else on_expert(x, 0, distance)


def reduce_step(x, axis):
    got = [move(x[d], axis, d) for d in (1, 3, 2)]
    return (
        x[0].astype(f32) + got[0].astype(f32) + got[1].astype(f32) + got[2].astype(f32)
    ).astype(bf16)


def gather_step(x, axis):
    return [x] + [move(x, axis, (4 - d) % 4) for d in (1, 2, 3)]


def sum_over_experts(a, b, other):
    a1, b1 = reduce_step(a, 0), reduce_step(b, 1)
    a2, b2 = reduce_step(a1, 1), reduce_step(b1, 0)
    a3, b3 = jnp.stack(gather_step(a2, 1)), jnp.stack(gather_step(b2, 0))
    a3, b3, other = lax.optimization_barrier((a3, b3, other))
    return gather_step(a3, 0), gather_step(b3, 1), other, (a1, b1)


def sum_everywhere(x):
    x = x + sibling(x)
    moved = [to_chip(x, d) for d in (1, 3, 2)]
    x = x + moved[0] + moved[1] + moved[2]
    for axis in (0, 1):
        moved = [move(x, axis, d) for d in (1, 3, 2)]
        x = x + moved[0] + moved[1] + moved[2]
    return x


def after(value, *others):
    return lax.optimization_barrier((value, *others))[0]


def on_device(
    block_input, out_grad, norm1_gain, w_query, w_key, w_value, query_gain, key_gain, w_out,
    norm2_gain, w_router, w_gate, w_up, w_down, seq_lengths, token_places, expert_routes,
):
    shard, owner = lax.axis_index("shard"), lax.axis_index("expert")
    chip, core = shard // 2, shard % 2
    where = jnp.stack([owner // 4, owner % 4, core]).astype(jnp.int32)
    core_id = core.reshape(1)
    g1 = norm1_gain.astype(f32).reshape(1, D)
    g2 = norm2_gain.astype(f32).reshape(1, D)
    gq = query_gain.astype(f32).reshape(1, HEAD)
    gk = key_gain.astype(f32).reshape(1, HEAD)

    x_own, x_sib = gather_blocks(block_input)

    chips = (chip + jnp.arange(4)) % 4
    order = jnp.concatenate([chips * 2 + core, chips * 2 + 1 - core])
    places = token_places[0].reshape(8, T)[order].reshape(ROWS)
    lengths = seq_lengths[0]
    ends = jnp.cumsum(lengths)
    starts = jnp.sum(
        jnp.where(places[:, None] >= ends[None, :], lengths[None, :], 0), axis=1
    )
    positions = (places - starts).astype(f32)
    info = jnp.concatenate(
        [places[None].astype(f32), starts[None].astype(f32), jnp.zeros((6, ROWS), f32)], axis=0
    )
    inverse_freq = ROPE_BASE ** (-jnp.arange(0, HEAD, 2).astype(f32) / HEAD)
    angles = inverse_freq[:, None] * positions[None, :]
    cos, sin = jnp.cos(angles), jnp.sin(angles)

    ids, ids_t = route_tables(expert_routes.T)
    assign_t = ids_t[8:12]
    expert_list = ids[:, 0:4].reshape(-1)
    slot_list = ids[:, 4:8].reshape(-1)

    wk_t, wv_t = w_key.T, w_value.T
    wk_s, wv_s = sibling(wk_t), sibling(wv_t)
    wq_t = w_query.T
    wo_s = sibling(w_out)
    wq_ts = sibling(wq_t)

    def piece(dy):
        return qkv(
            dy, core_id, x_own[dy], x_sib[dy], g1, wq_t, wk_t, wk_s, wv_t, wv_s, gq, gk, cos, sin
        )

    pieces = {dy: piece(dy) for dy in (0, 1, 3, 2)}
    wkv = pieces[0][7]
    qh, q, kh, k, v, scales, n1 = zip(*(pieces[dy][:7] for dy in range(4)))
    og_wire = after(pack(out_grad, assign_t), x_own[2], q[0], q[1], q[3])
    got_grads = exchange(og_wire)
    ot0, ot1, linv, qt, kt, kn, vn = attend(q, k, v, info)
    blocks = outproj(ot0, sibling(ot1), w_out, wo_s)
    blocks = [blocks[0]] + spread(blocks)
    hidden, n2, probs, gates, wire = router(blocks, block_input, g2, w_router, ids, assign_t)
    got_rows = exchange(wire)

    n1_t = transpose_rows(after(n1, wire))
    gate_list = gates[:, :4].reshape(-1)
    grad_rows, grad_act = expert_grad(after(got_grads, wire), w_down[0])
    got_rows, n1_t, grad_act, gate_list, wq_ts = lax.optimization_barrier(
        (got_rows, n1_t, grad_act, gate_list, wq_ts)
    )

    back, rows, act, scaled_act, dg, du = expert_main(got_rows, w_gate[0], w_up[0], grad_act)
    back_wire = exchange(back)

    rows, act, scaled_act, dg, du = after((rows, act, scaled_act, dg, du), back)
    out_wire = expert_out(act, w_down[0])

    def weight_grad(a, b):
        return lax.dot_general(a, b, (((0,), (0,)), ((), ())), preferred_element_type=f32)

    grad_wgate = weight_grad(rows, dg)
    grad_wup = weight_grad(rows, du)
    grad_wdown = weight_grad(scaled_act, grad_rows)
    back_wire, out_wire, grad_wgate, grad_wup, grad_wdown = lax.optimization_barrier(
        (back_wire, out_wire, grad_wgate, grad_wup, grad_wdown)
    )

    ghid, gatt, grouter, gg2 = combine(
        where, expert_list, slot_list, gate_list, back_wire, hidden, n2, probs, gates, ids,
        out_grad, g2, w_router,
    )
    g_own, g_sib = gather_blocks(gatt)
    router_parts = lax.all_to_all(
        grouter.reshape(8, 2 * T, E), "shard", split_axis=0, concat_axis=0, tiled=True
    )
    router_sum = jnp.sum(router_parts.astype(f32), axis=0).astype(bf16)
    dt_near = head_grad(
        [g_own[0], g_sib[0], g_own[1], g_sib[1], g_own[3], g_sib[3]], w_out
    )
    g_far, dt_near, router_sum = lax.optimization_barrier(
        ((g_own[2], g_sib[2]), dt_near, router_sum)
    )
    g_own[2], g_sib[2] = g_far

    gwout, dt_far = pre(g_own + g_sib, ot0, ot1, w_out)
    early_sums = lax.psum((gwout, router_sum), "expert")
    returned = exchange(after(out_wire, dt_far))

    dq0, dq1, dkv, ggq, ggk = bwd(
        qh, kh, scales, qt, kt, kn, vn, dt_near, dt_far, ot0, ot1, linv, info, cos, sin, gq, gk
    )
    dq_sib, dkv_sib = sibling(dq1), sibling(dkv)
    gw_a, gw_b, dkv_total = qkv_grad(where, n1_t, dq0, dq1, dkv, dkv_sib)
    returned, dq0 = lax.optimization_barrier((returned, dq0))
    result = result_rows(expert_list, slot_list, gate_list, returned, hidden)
    blocks = normed_grad(wq_t, wq_ts, wkv, dq0, dq_sib, dkv_total, n1)
    gg1 = blocks[4][0:1] / g1
    blocks = [blocks[0]] + spread(blocks)
    gw_a, gw_b, (blocks, early_sums), begun = sum_over_experts(gw_a, gw_b, (blocks, early_sums))
    grad_wout = early_sums[0].astype(f32)
    grad_router = lax.all_gather(early_sums[1], "shard", axis=0, tiled=True).astype(f32)
    grad_input = final(blocks, block_input, ghid, g1)

    vector = sum_everywhere(
        after(jnp.concatenate(
            [
                gg1.reshape(SEG, 128),
                gg2.reshape(SEG, 128),
                ggq[0:1],
                ggk[0:1],
                jnp.zeros((6, 128), f32),
            ],
            axis=0,
        ), *begun)
    )
    grad_wq, grad_wk, grad_wv = place(where, gw_a, gw_b)
    return (
        result,
        grad_input,
        vector[:SEG].reshape(D),
        grad_wq,
        grad_wk.T,
        grad_wv.T,
        vector[2 * SEG],
        vector[2 * SEG + 1],
        grad_wout,
        vector[SEG : 2 * SEG].reshape(D),
        grad_router,
        grad_wgate[None],
        grad_wup[None],
        grad_wdown[None],
    )


def solution(mesh):
    rows = P(("expert", "shard"), None)
    experts = P(("expert", "shard"), None, None)
    columns = P(None, "shard")
    return jax.shard_map(
        on_device,
        mesh=mesh,
        in_specs=(
            rows, rows, P(), columns, columns, columns, P(), P(), P("shard", None), P(), P(),
            experts, experts, experts, P("expert", None), P("expert", None), rows,
        ),
        out_specs=(
            rows, rows, P(), columns, columns, columns, P(), P(), P("shard", None), P(), P(),
            experts, experts, experts,
        ),
        check_vma=False,
    )
```

```python
import functools

import jax
import jax.numpy as jnp
from jax import lax
from jax.experimental import pallas as pl
from jax.experimental.pallas import tpu as pltpu
from jax.sharding import PartitionSpec as P

EPS = 1e-06
ROPE_BASE = 1000000.0
LOG2E = 1.4426950408889634
T = 128
D = 2048
HEAD = 128
LH = 4
E = 128
CAP = 5
SLOTS = E * CAP
SEG = D // 128
WIRE = CAP * SEG + 8
ROWS = 1024
HALF = 512
F = 768
bf16 = jnp.bfloat16
f32 = jnp.float32
ALL = ("expert", "shard")
COSTS = {
    "attend": 11,
    "out_projection": 5,
    "router": 6,
    "transpose_rows": 6,
    "expert_grad_rows": 8,
    "expert_main": 18,
    "expert_out": 7,
    "combine_grads": 7,
    "head_grad": 4,
    "out_projection_grad": 7,
}


def cost(micros):
    return pl.CostEstimate(
        flops=1, bytes_accessed=int(micros * 0.6e6) + 1, transcendentals=0
    )


def dot(a, b):
    return jnp.dot(a, b, preferred_element_type=f32)


def dot_t(a, b):
    return lax.dot_general(a, b, (((1,), (1,)), ((), ())), preferred_element_type=f32)


def call(kernel, name, outs, scratch, args, smem=()):
    in_specs = [
        pl.BlockSpec(memory_space=pltpu.SMEM if i in smem else pltpu.VMEM)
        for i in range(len(args))
    ]
    return pl.pallas_call(
        kernel,
        out_shape=outs,
        in_specs=in_specs,
        out_specs=[pl.BlockSpec(memory_space=pltpu.VMEM) for _ in outs],
        scratch_shapes=scratch,
        compiler_params=pltpu.CompilerParams(vmem_limit_bytes=63 * 1024 * 1024),
        cost_estimate=cost(COSTS.get(name, 0)),
        name=name,
    )(*args)


def grid_call(kernel, name, grid, in_specs, out_specs, outs, scratch, args, scalars=0):
    return pl.pallas_call(
        kernel,
        out_shape=outs,
        grid_spec=pltpu.PrefetchScalarGridSpec(
            num_scalar_prefetch=scalars,
            grid=grid,
            in_specs=in_specs,
            out_specs=out_specs,
            scratch_shapes=scratch,
        ),
        compiler_params=pltpu.CompilerParams(
            vmem_limit_bytes=63 * 1024 * 1024, dimension_semantics=("arbitrary",)
        ),
        cost_estimate=cost(COSTS.get(name, 0)),
        name=name,
    )(*args)


def whole(shape):
    return pl.BlockSpec(shape, lambda i, *_: (0,) * len(shape))


def rows_of(shape):
    return pl.BlockSpec(shape, lambda i, *_: (i, 0))


def cols_of(shape):
    return pl.BlockSpec(shape, lambda i, *_: (0, i))


def sds(shape, dtype):
    return jax.ShapeDtypeStruct(shape, dtype)


def split_rows(wire, dest):
    for s in range(CAP):
        for h in range(2):
            rows = slice(s * E + h * 64, s * E + (h + 1) * 64)
            block = wire[h * 64 : (h + 1) * 64, s * SEG : (s + 1) * SEG, :]
            dest[rows, :] = block.reshape(64, D)


def join_rows(source, wire):
    for s in range(CAP):
        for h in range(2):
            rows = slice(s * E + h * 64, s * E + (h + 1) * 64)
            wire[h * 64 : (h + 1) * 64, s * SEG : (s + 1) * SEG, :] = source[rows, :].reshape(
                64, SEG, 128
            )


def put_numbers(columns, wire):
    lane = lax.broadcasted_iota(jnp.int32, (E, 128), 1)
    plane = jnp.zeros((E, 128), f32)
    for s in range(CAP):
        plane = jnp.where(lane == s, columns[s], plane)
    first = plane.astype(bf16)
    rest = plane - first.astype(f32)
    second = rest.astype(bf16)
    third = (rest - second.astype(f32)).astype(bf16)
    none = jnp.zeros((E, 5 * 128), bf16)
    wide = jnp.concatenate([first, second, third, none], axis=1)
    wire[:, CAP * SEG :, :] = wide.reshape(E, 8, 128)


def get_numbers(wire):
    wide = wire[:, CAP * SEG :, :].reshape(E, 8 * 128)
    return (
        wide[:, :128].astype(f32) + wide[:, 128:256].astype(f32) + wide[:, 256:384].astype(f32)
    )


def pack_rows(x_ref, at_ref, wire, rows):
    slot = lax.broadcasted_iota(jnp.int32, (SLOTS, T), 0)
    hit = slot == at_ref[0:1, :]
    for k in range(1, 4):
        hit = hit | (slot == at_ref[k : k + 1, :])
    pick = jnp.where(hit, 1.0, 0.0).astype(bf16)
    for j in range(8):
        cols = slice(j * 256, (j + 1) * 256)
        rows[:, cols] = dot(pick, x_ref[:, cols]).astype(bf16)
    join_rows(rows, wire)


def pack_body(x_ref, at_ref, wire, rows):
    pack_rows(x_ref, at_ref, wire, rows)
    wire[:, CAP * SEG :, :] = jnp.zeros((E, 8, 128), bf16)


def pack(x, assign_t):
    return call(
        pack_body,
        "pack_rows",
        [sds((E, WIRE, 128), bf16)],
        [pltpu.VMEM((SLOTS, D), bf16)],
        (x, assign_t),
    )[0]


def sum_rows(wire, experts, slots, gates, out):
    def body(i, carry):
        for u in range(8):
            t = i * 8 + u
            total = None
            for k in range(4):
                p = t * 4 + k
                rows = pl.ds(pl.multiple_of(slots[p] * SEG, SEG), SEG)
                part = wire[experts[p], rows, :].astype(f32) * gates[p]
                total = part if total is None else total + part
            out[pl.ds(pl.multiple_of(t * SEG, SEG), SEG), :] = total
        return carry

    lax.fori_loop(0, T // 8, body, 0)


def column(row):
    return jnp.broadcast_to(row, (128, 128)).T[:, 0:1]


def qkv_body(pieces, *refs):
    count = len(pieces)
    core, blocks = refs[0], refs[1 : 1 + 2 * count]
    g1, wqt, wk, wks, wv, wvs, gq, gk, cos, sin = refs[1 + 2 * count : 11 + 2 * count]
    outs = refs[11 + 2 * count :]
    wkv = outs[-1]
    lower = core[0] == 0
    wkv[0:64, :] = jnp.where(lower, wk[...], wks[...])
    wkv[64:128, :] = jnp.where(lower, wks[...], wk[...])
    wkv[128:192, :] = jnp.where(lower, wv[...], wvs[...])
    wkv[192:256, :] = jnp.where(lower, wvs[...], wv[...])
    gain_q, gain_k = column(gq[...]), column(gk[...])
    for number, piece in enumerate(pieces):
        qn, qt, kn, kt, vt, scale, n1 = outs[7 * number : 7 * number + 7]
        for half in range(2):
            x = blocks[2 * number + half][...].astype(f32)
            r = lax.rsqrt(jnp.mean(x * x, axis=-1, keepdims=True) + EPS)
            n1[half * T : (half + 1) * T, :] = (x * r * g1[...]).astype(bf16)
        raw = dot_t(wqt[...], n1[...])
        raw_kv = dot_t(wkv[...], n1[...])
        first, second = piece * T, HALF + piece * T
        c = jnp.concatenate([cos[:, first : first + T], cos[:, second : second + T]], axis=1)
        s = jnp.concatenate([sin[:, first : first + T], sin[:, second : second + T]], axis=1)

        def path(v, gain, factor, keep, index):
            r = lax.rsqrt(jnp.mean(v * v, axis=0, keepdims=True) + EPS)
            scale[index : index + 1, :] = r
            v = v * r
            keep[...] = v.astype(bf16)
            v = v * gain
            low, high = v[:64], v[64:]
            return (
                ((low * c - high * s) * factor).astype(bf16),
                ((high * c + low * s) * factor).astype(bf16),
            )

        scale[...] = jnp.zeros_like(scale)
        for h in range(LH):
            heads = slice(h * HEAD, (h + 1) * HEAD)
            low, high = path(raw[heads], gain_q, HEAD ** (-0.5), qn.at[heads, :], h)
            qt[h * HEAD : h * HEAD + 64, :] = low
            qt[h * HEAD + 64 : (h + 1) * HEAD, :] = high
        key = raw_kv[:HEAD].astype(bf16)
        low, high = path(key.astype(f32), gain_k, 1.0, kn, LH)
        kt[:64, :] = low
        kt[64:, :] = high
        vt[...] = raw_kv[HEAD:].astype(bf16)


def qkv(pieces, core, blocks, *args):
    outs = [
        sds((LH * HEAD, 2 * T), bf16),
        sds((LH * HEAD, 2 * T), bf16),
        sds((HEAD, 2 * T), bf16),
        sds((HEAD, 2 * T), bf16),
        sds((HEAD, 2 * T), bf16),
        sds((8, 2 * T), f32),
        sds((2 * T, D), bf16),
    ] * len(pieces)
    keep = 0 in pieces
    return call(
        functools.partial(qkv_body, pieces),
        "qkv" + "".join(str(p) for p in pieces),
        outs + ([sds((2 * HEAD, D), bf16)] if keep else []),
        [] if keep else [pltpu.VMEM((2 * HEAD, D), bf16)],
        (core, *blocks, *args),
        smem=(0,),
    )


def build_mask(info, mask):
    for b in range(8):
        keys = jnp.broadcast_to(info[0:1, b * T : (b + 1) * T], (T, T)).T
        for j in range(8):
            cols = slice(j * T, (j + 1) * T)
            inside = (keys >= info[1:2, cols]) & (keys <= info[0:1, cols])
            mask[b * T : (b + 1) * T, cols] = jnp.where(inside, 1.0, 0.0)


def attend_body(*refs):
    q, k, v = refs[0:4], refs[4:8], refs[8:12]
    info, ot0, ot1, linv, qt, kt, kn, vn, mask, vt = refs[12:]
    for dy in range(4):
        for dc in range(2):
            to = slice(dc * HALF + dy * T, dc * HALF + (dy + 1) * T)
            src = slice(dc * T, (dc + 1) * T)
            qt[:, to] = q[dy][:, src]
            kt[:, to] = k[dy][:, src]
            vt[:, to] = v[dy][:, src]
    for b in range(8):
        rows = slice(b * T, (b + 1) * T)
        kn[rows, :] = kt[:, rows].astype(f32).T.astype(bf16)
        vn[rows, :] = vt[:, rows].astype(f32).T.astype(bf16)
    build_mask(info, mask)
    for half, out in ((1, ot1), (0, ot0)):

        def body(i, carry):
            local = pl.ds(pl.multiple_of(i * 256, 256), 256)
            cols = pl.ds(pl.multiple_of(half * HALF + i * 256, 256), 256)
            for h in range(LH):
                heads = slice(h * HEAD, (h + 1) * HEAD)
                scores = dot(kn[...], qt[heads, cols])
                weights = jnp.exp2(scores * LOG2E) * mask[:, cols]
                inverse = 1.0 / jnp.sum(weights, axis=0, keepdims=True)
                out[heads, local] = (dot(vt[...], weights.astype(bf16)) * inverse).astype(bf16)
                linv[h : h + 1, cols] = inverse
            return carry

        lax.fori_loop(0, 2, body, 0)


def attend(q, k, v, info):
    return call(
        attend_body,
        "attend",
        [
            sds((LH * HEAD, HALF), bf16),
            sds((LH * HEAD, HALF), bf16),
            sds((8, ROWS), f32),
            sds((LH * HEAD, ROWS), bf16),
            sds((HEAD, ROWS), bf16),
            sds((ROWS, HEAD), bf16),
            sds((ROWS, HEAD), bf16),
        ],
        [pltpu.VMEM((ROWS, ROWS), f32), pltpu.VMEM((HEAD, ROWS), bf16)],
        (*q, *k, *v, info),
    )


def flip(source, dest, row, col):
    height, width = source.shape
    for a in range(height // 128):
        for b in range(width // 128):
            block = source[a * 128 : (a + 1) * 128, b * 128 : (b + 1) * 128]
            rows = slice(row + b * 128, row + (b + 1) * 128)
            dest[rows, col + a * 128 : col + (a + 1) * 128] = block.astype(f32).T.astype(bf16)


def outproj_body(ot0, otr, wa, wb, b0, b1, b2, b3, heads):
    @pl.when(pl.program_id(0) == 0)
    def _():
        flip(ot0, heads, 0, 0)
        flip(otr, heads, 0, 512)

    total = dot(heads[:, :512], wa[...]) + dot(heads[:, 512:], wb[...])
    for dy, out in enumerate((b0, b1, b2, b3)):
        out[...] = total[dy * T : (dy + 1) * T, :].astype(bf16)


def outproj(ot0, otr, wa, wb):
    return grid_call(
        outproj_body,
        "out_projection",
        (4,),
        [whole((512, HALF)), whole((512, HALF)), cols_of((512, 512)), cols_of((512, 512))],
        [cols_of((T, 512))] * 4,
        [sds((T, D), bf16)] * 4,
        [pltpu.VMEM((HALF, 1024), bf16)],
        (ot0, otr, wa, wb),
    )


def transpose_body(n0, n1, n2, n3, out):
    for dy, piece in enumerate((n0, n1, n2, n3)):
        for dc in range(2):
            flip(piece.at[dc * T : (dc + 1) * T, :], out, 0, dc * HALF + dy * T)


def transpose_rows(pieces):
    return call(transpose_body, "transpose_rows", [sds((D, ROWS), bf16)], [], tuple(pieces))[0]


def route_body(rt, ids, ids_t):
    lane = lax.broadcasted_iota(jnp.int32, (T, E), 1)
    row = lax.broadcasted_iota(jnp.int32, (T, E), 0)
    wide = jnp.concatenate([rt[...].astype(f32), jnp.zeros((124, T), f32)], axis=0).T
    hot = [jnp.where(lane.astype(f32) == wide[:, k : k + 1], 1.0, 0.0) for k in range(4)]
    earlier = jnp.where(lane < row, 1.0, 0.0).astype(bf16)
    before = dot(earlier, (hot[0] + hot[1] + hot[2] + hot[3]).astype(bf16))
    table = wide
    for k in range(4):
        slot = jnp.sum(before * hot[k], axis=1, keepdims=True)
        table = jnp.where(lane == 4 + k, slot, table)
        table = jnp.where(lane == 8 + k, slot * E + wide[:, k : k + 1], table)
    ids[...] = table.astype(jnp.int32)
    ids_t[...] = table.T[0:16, :].astype(jnp.int32)


def route_tables(routes_t):
    return call(
        route_body,
        "route_tables",
        [sds((T, 128), jnp.int32), sds((16, T), jnp.int32)],
        [],
        (routes_t,),
    )


def router_body(b0, b1, b2, b3, x0, g2, wr, ids, at, hidden, n2, probs, gates, wire, rows):
    v = x0[...].astype(f32) + (
        (b0[...].astype(f32) + b1[...].astype(f32))
        + (b2[...].astype(f32) + b3[...].astype(f32))
    )
    hidden[...] = v
    r = lax.rsqrt(jnp.mean(v * v, axis=-1, keepdims=True) + EPS)
    n2[...] = (v * r * g2[...]).astype(bf16)
    logits = dot(n2[...], wr[...])
    pack_rows(n2, at, wire, rows)
    expo = jnp.exp(logits - jnp.max(logits, axis=-1, keepdims=True))
    p = expo / jnp.sum(expo, axis=-1, keepdims=True)
    probs[...] = p
    lane = lax.broadcasted_iota(jnp.int32, (T, E), 1)
    chosen = [
        jnp.sum(jnp.where(lane == ids[:, k : k + 1], p, 0.0), axis=-1, keepdims=True)
        for k in range(4)
    ]
    total = chosen[0] + chosen[1] + chosen[2] + chosen[3]
    packed = jnp.where(lane == 4, total, 0.0)
    for k in range(4):
        packed = jnp.where(lane == k, chosen[k] / total, packed)
    gates[...] = packed
    across = packed.T
    expert = lax.broadcasted_iota(jnp.int32, (E, T), 0)
    columns = []
    for s in range(CAP):
        mine = jnp.zeros((E, T), f32)
        for k in range(4):
            mine = jnp.where(expert + s * E == at[k : k + 1, :], across[k : k + 1, :], mine)
        columns.append(jnp.sum(mine, axis=1, keepdims=True))
    put_numbers(columns, wire)


def router(b, x0, g2, wr, ids, assign_t):
    return call(
        router_body,
        "router",
        [
            sds((T, D), f32),
            sds((T, D), bf16),
            sds((T, E), f32),
            sds((T, E), f32),
            sds((E, WIRE, 128), bf16),
        ],
        [pltpu.VMEM((SLOTS, D), bf16)],
        (*b, x0, g2, wr, ids, assign_t),
    )


def expert_grad_body(wire, wd, gr, ga):
    split_rows(wire, gr)

    def body(i, carry):
        cols = pl.ds(pl.multiple_of(i * 256, 256), 256)
        ga[:, cols] = dot_t(gr[...], wd[cols, :])
        return carry

    lax.fori_loop(0, F // 256, body, 0)


def expert_grad(wire, wd):
    return call(
        expert_grad_body,
        "expert_grad_rows",
        [sds((SLOTS, D), bf16), sds((SLOTS, F), f32)],
        [],
        (wire, wd),
    )


def expert_main_body(wire, wg, wu, ga, back, xs, act, acts, dg, du, xr, sc):
    split_rows(wire, xr)
    gates = get_numbers(wire)
    sc[...] = jnp.zeros_like(sc)

    def forward(i, carry):
        cols = pl.ds(pl.multiple_of(i * 256, 256), 256)
        gate = dot(xr[...], wg[:, cols])
        up = dot(xr[...], wu[:, cols])
        grad = ga[:, cols]
        s = 1.0 / (1.0 + jnp.exp(-gate))
        silu = gate * s
        a = silu * up
        act[:, cols] = a.astype(bf16)
        dg[:, cols] = (grad * up * s * (1.0 + gate * (1.0 - s))).astype(bf16)
        du[:, cols] = (grad * silu).astype(bf16)
        sc[...] += jnp.sum(a * grad, axis=1, keepdims=True)
        return carry

    lax.fori_loop(0, F // 256, forward, 0)
    for s in range(CAP):
        part = slice(s * E, (s + 1) * E)
        gate = gates[:, s : s + 1]
        xs[part, :] = (xr[part, :].astype(f32) * gate).astype(bf16)
        acts[part, :] = (act[part, :].astype(f32) * gate).astype(bf16)
    for j in range(8):
        part = slice(j * 256, (j + 1) * 256)
        xr[:, part] = (dot_t(dg[...], wg[part, :]) + dot_t(du[...], wu[part, :])).astype(bf16)
    join_rows(xr, back)
    put_numbers([sc[s * E : (s + 1) * E, :] for s in range(CAP)], back)


def expert_main(wire, wg, wu, ga):
    return call(
        expert_main_body,
        "expert_main",
        [
            sds((E, WIRE, 128), bf16),
            sds((SLOTS, D), bf16),
            sds((SLOTS, F), bf16),
            sds((SLOTS, F), bf16),
            sds((SLOTS, F), bf16),
            sds((SLOTS, F), bf16),
        ],
        [pltpu.VMEM((SLOTS, D), bf16), pltpu.VMEM((SLOTS, 1), f32)],
        (wire, wg, wu, ga),
    )


def expert_out_body(act, wd, wire, rows):
    for j in range(8):
        cols = slice(j * 256, (j + 1) * 256)
        rows[:, cols] = dot(act[...], wd[:, cols]).astype(bf16)
    join_rows(rows, wire)


def expert_out(act, wd):
    return call(
        expert_out_body,
        "expert_out",
        [sds((E, CAP * SEG, 128), bf16)],
        [pltpu.VMEM((SLOTS, D), bf16)],
        (act, wd),
    )[0]


def combine_body(
    where, experts, slots, gate_list, wire, hidden, n2, probs, gates, ids, og, g2, wr,
    ghid, gatt, grouter, gg2, sums, gn2,
):
    sum_rows(wire, experts, slots, gate_list, sums)
    scores = get_numbers(wire)
    lane = lax.broadcasted_iota(jnp.int32, (T, E), 1)
    grads = []
    for k in range(4):
        hot = jnp.where(lane == ids[:, k : k + 1], 1.0, 0.0)
        rows = lax.dot_general(
            hot, scores, (((1,), (0,)), ((), ())),
            precision=lax.Precision.HIGHEST, preferred_element_type=f32,
        )
        picked = jnp.where(lane == ids[:, 4 + k : 5 + k], rows, 0.0)
        grads.append(jnp.sum(picked, axis=-1, keepdims=True))
    inner = sum(grads[k] * gates[:, k : k + 1] for k in range(4))
    inverse = 1.0 / gates[:, 4:5]
    grad_probs = jnp.zeros((T, E), f32)
    for k in range(4):
        grad_probs = jnp.where(
            lane == ids[:, k : k + 1], (grads[k] - inner) * inverse, grad_probs
        )
    p = probs[...]
    gl = (p * (grad_probs - jnp.sum(p * grad_probs, axis=-1, keepdims=True))).astype(bf16)
    for h in range(2):
        tokens = slice(h * 64, (h + 1) * 64)
        gn2[tokens, :] = sums[h * 1024 : (h + 1) * 1024, :].reshape(64, D)
    gn2[...] += dot_t(gl, wr[...])
    c = gn2[...]
    v = hidden[...]
    r = lax.rsqrt(jnp.mean(v * v, axis=-1, keepdims=True) + EPS)
    u = c * g2[...]
    m = jnp.mean(u * v, axis=-1, keepdims=True)
    total = og[...].astype(f32) + r * u - v * (r * r * r * m)
    ghid[...] = total
    gatt[...] = total.astype(bf16)
    gg2[...] = jnp.sum(c * (v * r), axis=0, keepdims=True)
    for j in range(SEG):
        cols = slice(j * 128, (j + 1) * 128)
        grouter[cols, :] = dot(n2[:, cols].astype(f32).T.astype(bf16), gl).astype(bf16)


def combine(*args):
    return call(
        combine_body,
        "combine_grads",
        [sds((T, D), f32), sds((T, D), bf16), sds((D, E), bf16), sds((1, D), f32)],
        [pltpu.VMEM((T * SEG, 128), f32), pltpu.VMEM((T, D), f32)],
        args,
        smem=(0, 1, 2, 3),
    )


def result_body(experts, slots, gate_list, wire, hidden, out, sums):
    sum_rows(wire, experts, slots, gate_list, sums)
    for h in range(2):
        tokens = slice(h * 64, (h + 1) * 64)
        mixture = sums[h * 1024 : (h + 1) * 1024, :].reshape(64, D)
        out[tokens, :] = (hidden[tokens, :] + mixture).astype(bf16)


def result_rows(*args):
    return call(
        result_body,
        "result",
        [sds((T, D), bf16)],
        [pltpu.VMEM((T * SEG, 128), f32)],
        args,
        smem=(0, 1, 2),
    )[0]


def head_grad_body(*refs):
    blocks, (wo, dt, rows_all) = refs[:6], refs[6:]
    for b in range(6):
        rows_all[b * T : (b + 1) * T, :] = blocks[b][...]
    for b in range(3):
        rows = slice(b * 256, (b + 1) * 256)
        dt[:, rows] = dot_t(wo[...], rows_all[rows, :]).astype(bf16)


def head_grad(blocks, wo):
    return call(
        head_grad_body,
        "head_grad",
        [sds((LH * HEAD, 6 * T), bf16)],
        [pltpu.VMEM((6 * T, D), bf16)],
        (*blocks, wo),
    )[0]


def pre_body(*refs):
    blocks, (ot0, ot1, wo, gw, dt, rows_all, total) = refs[:8], refs[8:]
    step = pl.program_id(0)
    for b in range(8):
        rows_all[b * T : (b + 1) * T, :] = blocks[b][...]
    gw[...] = (dot(ot0[...], rows_all[:HALF, :]) + dot(ot1[...], rows_all[HALF:, :])).astype(bf16)
    last = jnp.concatenate([blocks[2][...], blocks[6][...]], axis=0)
    part = dot_t(wo[...], last)

    @pl.when(step == 0)
    def _():
        total[...] = part

    @pl.when(step > 0)
    def _():
        total[...] += part

    @pl.when(step == 3)
    def _():
        dt[...] = total[...].astype(bf16)


def pre(blocks, ot0, ot1, wo):
    return grid_call(
        pre_body,
        "out_projection_grad",
        (4,),
        [cols_of((T, 512))] * 8 + [whole((512, HALF))] * 2 + [cols_of((512, 512))],
        [cols_of((512, 512)), whole((512, 2 * T))],
        [sds((LH * HEAD, D), bf16), sds((LH * HEAD, 2 * T), bf16)],
        [pltpu.VMEM((ROWS, 512), bf16), pltpu.VMEM((512, 2 * T), f32)],
        (*blocks, ot0, ot1, wo),
    )


def bwd_body(*refs):
    qh, kh, scales = refs[0:4], refs[4:8], refs[8:12]
    (qt, kt, kn, vn, dta, dtb, ot0, ot1, linv, info, cos, sin, gq, gk) = refs[12:26]
    dq0, dq1, dkv, ggq, ggk, mask, wb, sb, dqt, dk, dv, raw, dt, scale = refs[26:]
    for dc in range(2):
        for place, dy in enumerate((0, 1, 3)):
            to = slice(dc * HALF + dy * T, dc * HALF + (dy + 1) * T)
            dt[:, to] = dta[:, (place * 2 + dc) * T : (place * 2 + dc + 1) * T]
        dt[:, dc * HALF + 2 * T : dc * HALF + 3 * T] = dtb[:, dc * T : (dc + 1) * T]
        for dy in range(4):
            to = slice(dc * HALF + dy * T, dc * HALF + (dy + 1) * T)
            scale[:, to] = scales[dy][:, dc * T : (dc + 1) * T]
    build_mask(info, mask)
    dk[...] = jnp.zeros_like(dk)
    dv[...] = jnp.zeros_like(dv)
    for half, out in ((0, ot0), (1, ot1)):

        def body(i, carry):
            local = pl.ds(pl.multiple_of(i * 256, 256), 256)
            cols = pl.ds(pl.multiple_of(half * HALF + i * 256, 256), 256)
            for h in range(LH):
                heads = slice(h * HEAD, (h + 1) * HEAD)
                part = slice(h * 256, (h + 1) * 256)
                scores = dot(kn[...], qt[heads, cols])
                weights = jnp.exp2(scores * LOG2E) * (mask[:, cols] * linv[h : h + 1, cols])
                grad = dt[heads, cols]
                delta = jnp.sum(
                    grad.astype(f32) * out[heads, local].astype(f32), axis=0, keepdims=True
                )
                wb[:, part] = weights.astype(bf16)
                sb[:, part] = (weights * (dot(vn[...], grad) - delta)).astype(bf16)
                dqt[heads, cols] = dot(kt[...], sb[:, part])
            grads = jnp.concatenate(
                [dt[h * HEAD : (h + 1) * HEAD, cols] for h in range(LH)], axis=1
            )
            queries = jnp.concatenate(
                [qt[h * HEAD : (h + 1) * HEAD, cols] for h in range(LH)], axis=1
            )
            dv[...] += dot_t(wb[...], grads)
            dk[...] += dot_t(sb[...], queries)
            return carry

        lax.fori_loop(0, 2, body, 0)

    def unrope(v):
        low, high = v[:64], v[64:]
        c, s = cos[...], sin[...]
        return jnp.concatenate([low * c + high * s, high * c - low * s], axis=0)

    def norm_back(n, r, grad, gain):
        gain_grad = jnp.sum(grad * n, axis=1, keepdims=True)
        u = grad * gain
        return r * (u - n * jnp.mean(u * n, axis=0, keepdims=True)), gain_grad

    gain_q, gain_k = column(gq[...]), column(gk[...])
    total = jnp.zeros((HEAD, 1), f32)
    for h in range(LH):
        heads = slice(h * HEAD, (h + 1) * HEAD)
        for dy in range(4):
            for dc in range(2):
                to = slice(dc * HALF + dy * T, dc * HALF + (dy + 1) * T)
                raw[:, to] = qh[dy][heads, dc * T : (dc + 1) * T].astype(f32)
        grad, part = norm_back(raw[...], scale[h : h + 1, :], unrope(dqt[heads, :] * (HEAD ** (-0.5))), gain_q)
        total = total + part
        dq0[heads, :] = grad[:, :HALF].astype(bf16)
        dq1[heads, :] = grad[:, HALF:].astype(bf16)
    ggq[...] = jnp.broadcast_to(total, (HEAD, 128)).T[0:8, :]
    for dy in range(4):
        for dc in range(2):
            to = slice(dc * HALF + dy * T, dc * HALF + (dy + 1) * T)
            raw[:, to] = kh[dy][:, dc * T : (dc + 1) * T].astype(f32)
    grad, part = norm_back(raw[...], scale[LH : LH + 1, :], unrope(dk[...].T), gain_k)
    ggk[...] = jnp.broadcast_to(part, (HEAD, 128)).T[0:8, :]
    dkv[:HEAD, :] = grad.astype(bf16)
    dkv[HEAD:, :] = dv[...].T.astype(bf16)


def bwd(qh, kh, scales, *rest):
    return call(
        bwd_body,
        "attend_grad",
        [
            sds((LH * HEAD, HALF), bf16),
            sds((LH * HEAD, HALF), bf16),
            sds((2 * HEAD, ROWS), bf16),
            sds((8, HEAD), f32),
            sds((8, HEAD), f32),
        ],
        [
            pltpu.VMEM((ROWS, ROWS), f32),
            pltpu.VMEM((ROWS, LH * 256), bf16),
            pltpu.VMEM((ROWS, LH * 256), bf16),
            pltpu.VMEM((LH * HEAD, ROWS), f32),
            pltpu.VMEM((ROWS, HEAD), f32),
            pltpu.VMEM((ROWS, HEAD), f32),
            pltpu.VMEM((HEAD, ROWS), f32),
            pltpu.VMEM((LH * HEAD, ROWS), bf16),
            pltpu.VMEM((8, ROWS), f32),
        ],
        (*qh, *kh, *scales, *rest),
    )


def qkv_grad_body(where, n1t, dq0, dq1, own, sib, w0, w1, w2, w3, tot, dt):
    step = pl.program_id(0)

    @pl.when(step == 0)
    def _():
        tot[:, :HALF] = (own[:, :HALF].astype(f32) + sib[:, HALF:].astype(f32)).astype(bf16)
        tot[:, HALF:] = (own[:, HALF:].astype(f32) + sib[:, :HALF].astype(f32)).astype(bf16)
        dt[:512, :HALF] = dq0[...]
        dt[:512, HALF:] = dq1[...]
        upper = where[2] == 1
        dt[512:576, :] = jnp.where(upper, tot[64:128, :], tot[:64, :])
        dt[576:, :] = jnp.where(upper, tot[192:, :], tot[128:192, :])

    grad = dot_t(n1t[...], dt[...]).astype(bf16)
    for dz, out in enumerate((w0, w1, w2, w3)):

        @pl.when(step == dz)
        def _():
            for col in range(4):
                dx = lax.rem(col + 4 - where[1], 4)
                out[dx] = grad[col * 128 : (col + 1) * 128, :]


def qkv_grad(where, n1t, dq0, dq1, own, sib):
    return grid_call(
        qkv_grad_body,
        "qkv_weight_grad",
        (4,),
        [
            pl.BlockSpec((512, ROWS), lambda i, w: (lax.rem(i + w[0], 4), 0)),
            whole((512, HALF)),
            whole((512, HALF)),
            whole((2 * HEAD, ROWS)),
            whole((2 * HEAD, ROWS)),
        ],
        [whole((4, 128, 640))] * 4 + [whole((2 * HEAD, ROWS))],
        [sds((4, 128, 640), bf16)] * 4 + [sds((2 * HEAD, ROWS), bf16)],
        [pltpu.VMEM((640, ROWS), bf16)],
        (where, n1t, dq0, dq1, own, sib),
        scalars=1,
    )


def add_body(a, b, c, d, *outs):
    for i, out in enumerate(outs):
        out[...] = (
            (a[i].astype(f32) + b[i].astype(f32)) + (c[i].astype(f32) + d[i].astype(f32))
        ).astype(bf16)


def add_parts(parts):
    return call(add_body, "add_parts", [sds((128, 640), bf16)] * 4, [], tuple(parts))


def normed_grad_body(wa, wb, wkv, dq0, dqr, tot, n0, n1, n2, n3, b0, b1, b2, b3, gg1, grads):
    @pl.when(pl.program_id(0) == 0)
    def _():
        flip(dq0, grads, 0, 0)
        flip(dqr, grads, 0, 512)
        flip(tot, grads, 0, 1024)

    total = (
        dot(grads[:, :512], wa[...])
        + dot(grads[:, 512:1024], wb[...])
        + dot(grads[:, 1024:], wkv[...])
    )
    gain = jnp.zeros((1, 512), f32)
    for dy, (out, rows) in enumerate(((b0, n0), (b1, n1), (b2, n2), (b3, n3))):
        part = total[dy * T : (dy + 1) * T, :]
        out[...] = part.astype(bf16)
        gain = gain + jnp.sum(part * rows[...].astype(f32), axis=0, keepdims=True)
    gg1[...] = jnp.broadcast_to(gain, (8, 512))


def normed_grad(wa, wb, wkv, dq0, dqr, tot, n1):
    return grid_call(
        normed_grad_body,
        "normed_grad",
        (4,),
        [
            cols_of((512, 512)),
            cols_of((512, 512)),
            cols_of((256, 512)),
            whole((512, HALF)),
            whole((512, HALF)),
            whole((2 * HEAD, HALF)),
        ]
        + [cols_of((T, 512))] * 4,
        [cols_of((T, 512))] * 4 + [cols_of((8, 512))],
        [sds((T, D), bf16)] * 4 + [sds((8, D), f32)],
        [pltpu.VMEM((HALF, 1280), bf16)],
        (wa, wb, wkv, dq0, dqr, tot, *n1),
    )


def add_last_body(a, b, c, d, out):
    out[...] = (
        (a[...].astype(f32) + b[...].astype(f32)) + (c[...].astype(f32) + d[...].astype(f32))
    ).astype(bf16)


def add_last(parts):
    return call(add_last_body, "add_last", [sds((128, 640), bf16)], [], tuple(parts))[0]


def stack_body(a, b, c, d, out):
    for i, part in enumerate((a, b, c, d)):
        out[i] = part[...]


def stack(parts):
    return call(stack_body, "stack_parts", [sds((4, 128, 640), bf16)], [], tuple(parts))[0]


def place_body(where, c0, c1, c2, c3, gq, gkt, gvt):
    for dz, chunks in enumerate((c0, c1, c2, c3)):
        for dx in range(4):
            chunk = lax.rem(where[0] + dz, 4) * 4 + lax.rem(where[1] + dx, 4)
            rows = pl.ds(pl.multiple_of(chunk * 128, 128), 128)
            gq[rows, :] = chunks[dx, :, :512].astype(f32)
            both = chunks[dx, :, 512:].astype(f32).T
            gkt[:, rows] = both[:64]
            gvt[:, rows] = both[64:]


def place(where, chunks):
    return call(
        place_body,
        "place_weight_grads",
        [sds((D, 512), f32), sds((64, D), f32), sds((64, D), f32)],
        [],
        (where, *chunks),
        smem=(0,),
    )


def final_body(b0, b1, b2, b3, x0, ghid, g1, out):
    c = (b0[...].astype(f32) + b1[...].astype(f32)) + (b2[...].astype(f32) + b3[...].astype(f32))
    v = x0[...].astype(f32)
    r = lax.rsqrt(jnp.mean(v * v, axis=-1, keepdims=True) + EPS)
    u = c * g1[...]
    m = jnp.mean(u * v, axis=-1, keepdims=True)
    out[...] = ghid[...] + r * u - v * (r * r * r * m)


def final(b, x0, ghid, g1):
    return call(final_body, "input_grad", [sds((T, D), f32)], [], (*b, x0, ghid, g1))[0]


def sibling(x):
    return lax.ppermute(x, "shard", [(i, i ^ 1) for i in range(8)])


def from_chip(x, dy):
    return lax.ppermute(x, "shard", [(i, (i - 2 * dy) % 8) for i in range(8)])


def to_chip(x, dy):
    return lax.ppermute(x, "shard", [(i, (i + 2 * dy) % 8) for i in range(8)])


def exchange(x):
    return lax.all_to_all(x, ALL, split_axis=0, concat_axis=0, tiled=True)


def spread(x):
    return [to_chip(x[d], d) for d in (1, 3, 2)]


def on_expert(x, dz, dx):
    pairs = [
        (z * 4 + c, ((z + dz) % 4) * 4 + (c + dx) % 4) for z in range(4) for c in range(4)
    ]
    return lax.ppermute(x, "expert", pairs)


def move(x, axis, distance):
    return on_expert(x, distance, 0) if axis == 0 else on_expert(x, 0, distance)


def collect(parts, axis):
    return [parts[0]] + [move(parts[d], axis, d) for d in (1, 3, 2)]


def share(x, axis):
    return [x] + [move(x, axis, (4 - d) % 4) for d in (1, 2, 3)]


def after(value, *others):
    return lax.optimization_barrier((value, *others))[0]


def on_device(
    block_input, out_grad, norm1_gain, w_query, w_key, w_value, query_gain, key_gain, w_out,
    norm2_gain, w_router, w_gate, w_up, w_down, seq_lengths, token_places, expert_routes,
):
    shard, owner = lax.axis_index("shard"), lax.axis_index("expert")
    chip, core = shard // 2, shard % 2
    where = jnp.stack([owner // 4, owner % 4, core]).astype(jnp.int32)
    core_id = core.reshape(1)
    g1 = norm1_gain.astype(f32).reshape(1, D)
    g2 = norm2_gain.astype(f32).reshape(1, D)
    gq = query_gain.astype(f32).reshape(1, HEAD)
    gk = key_gain.astype(f32).reshape(1, HEAD)

    x_own = [block_input] + [from_chip(block_input, dy) for dy in (1, 2, 3)]
    x_sib = [sibling(block_input)]

    chips = (chip + jnp.arange(4)) % 4
    order = jnp.concatenate([chips * 2 + core, chips * 2 + 1 - core])
    places = token_places[0].reshape(8, T)[order].reshape(ROWS)
    lengths = seq_lengths[0]
    ends = jnp.cumsum(lengths)
    starts = jnp.sum(
        jnp.where(places[:, None] >= ends[None, :], lengths[None, :], 0), axis=1
    )
    positions = (places - starts).astype(f32)
    info = jnp.concatenate(
        [places[None].astype(f32), starts[None].astype(f32), jnp.zeros((6, ROWS), f32)], axis=0
    )
    inverse_freq = ROPE_BASE ** (-jnp.arange(0, HEAD, 2).astype(f32) / HEAD)
    angles = inverse_freq[:, None] * positions[None, :]
    cos, sin = jnp.cos(angles), jnp.sin(angles)

    ids, ids_t = route_tables(expert_routes.T)
    assign_t = ids_t[8:12]
    expert_list = ids[:, 0:4].reshape(-1)
    slot_list = ids[:, 4:8].reshape(-1)

    wk_t, wv_t = w_key.T, w_value.T
    wk_s, wv_s = sibling(wk_t), sibling(wv_t)
    wq_t = w_query.T
    wo_s = sibling(w_out)
    wq_ts = sibling(wq_t)

    weights = (g1, wq_t, wk_t, wk_s, wv_t, wv_s, gq, gk, cos, sin)
    zero = qkv((0,), core_id, (x_own[0], x_sib[0]), *weights)
    og_wire = pack(out_grad, assign_t)
    x_own[1], x_own[3], q_first, og_wire = lax.optimization_barrier(
        (x_own[1], x_own[3], zero[1], og_wire)
    )
    x_sib = [x_sib[0], sibling(x_own[1]), None, sibling(x_own[3])]
    x_sib[1], x_sib[3], x_own[2], og_wire = lax.optimization_barrier(
        (x_sib[1], x_sib[3], x_own[2], og_wire)
    )
    x_sib[2] = sibling(x_own[2])
    near = qkv((1, 3), core_id, (x_own[1], x_sib[1], x_own[3], x_sib[3]), *weights)
    far = qkv((2,), core_id, (x_own[2], x_sib[2]), *weights)
    wkv = zero[7]
    pieces = [zero[:7], near[:7], far[:7], near[7:14]]
    qh, q, kh, k, v, scales, n1 = zip(*pieces)
    q = (q_first,) + q[1:]
    got_grads = exchange(og_wire)
    ot0, ot1, linv, qt, kt, kn, vn = attend(q, k, v, info)
    blocks = outproj(ot0, sibling(ot1), w_out, wo_s)
    blocks = [blocks[0]] + spread(blocks)
    hidden, n2, probs, gates, wire = router(blocks, block_input, g2, w_router, ids, assign_t)
    got_rows = exchange(wire)

    n1_t = transpose_rows(after(n1, wire))
    gate_list = gates[:, :4].reshape(-1)
    grad_rows, grad_act = expert_grad(after(got_grads, wire), w_down[0])
    got_rows, n1_t, grad_act, gate_list, wq_ts = lax.optimization_barrier(
        (got_rows, n1_t, grad_act, gate_list, wq_ts)
    )

    back, rows, act, scaled_act, dg, du = expert_main(got_rows, w_gate[0], w_up[0], grad_act)
    back_wire = exchange(back)

    rows, act, scaled_act, dg, du = after((rows, act, scaled_act, dg, du), back)
    out_wire = expert_out(act, w_down[0])

    def weight_grad(a, b):
        return lax.dot_general(a, b, (((0,), (0,)), ((), ())), preferred_element_type=f32)

    grad_wgate = weight_grad(rows, dg)
    grad_wup = weight_grad(rows, du)
    grad_wdown = weight_grad(scaled_act, grad_rows)
    back_wire, out_wire, grad_wgate, grad_wup, grad_wdown = lax.optimization_barrier(
        (back_wire, out_wire, grad_wgate, grad_wup, grad_wdown)
    )

    ghid, gatt, grouter, gg2 = combine(
        where, expert_list, slot_list, gate_list, back_wire, hidden, n2, probs, gates, ids,
        out_grad, g2, w_router,
    )
    g_own = [gatt] + [from_chip(gatt, dy) for dy in (1, 2, 3)]
    router_parts = lax.all_to_all(
        grouter.reshape(8, 2 * T, E), "shard", split_axis=0, concat_axis=0, tiled=True
    )
    router_sum = jnp.sum(router_parts.astype(f32), axis=0).astype(bf16)
    g_own[1], g_own[2], g_own[3], router_sum = lax.optimization_barrier(
        (g_own[1], g_own[2], g_own[3], router_sum)
    )
    g_sib = [sibling(block) for block in g_own]
    dt_near = head_grad(
        [g_own[0], g_sib[0], g_own[1], g_sib[1], g_own[3], g_sib[3]], w_out
    )
    g_far, dt_near = lax.optimization_barrier(((g_own[2], g_sib[2]), dt_near))
    g_own[2], g_sib[2] = g_far

    gwout, dt_far = pre(g_own + g_sib, ot0, ot1, w_out)
    early_sums = lax.psum((gwout, router_sum), "expert")
    returned = exchange(after(out_wire, dt_far))

    dq0, dq1, dkv, ggq, ggk = bwd(
        qh, kh, scales, qt, kt, kn, vn, dt_near, dt_far, ot0, ot1, linv, info, cos, sin, gq, gk
    )
    dq_sib, dkv_sib = sibling(dq1), sibling(dkv)
    *parts, dkv_total = qkv_grad(where, n1_t, dq0, dq1, dkv, dkv_sib)
    returned, dq0 = lax.optimization_barrier((returned, dq0))
    result = result_rows(expert_list, slot_list, gate_list, returned, hidden)
    blocks = normed_grad(wq_t, wq_ts, wkv, dq0, dq_sib, dkv_total, n1)
    gg1 = blocks[4][0] / g1[0]
    vector = jnp.concatenate([gg1, gg2[0], ggq[0], ggk[0]])
    per = vector.shape[0] // E
    wide = jnp.pad(vector.reshape(E, per), ((0, 0), (0, 128 - per))).reshape(E, 1, 128)
    blocks = [blocks[0]] + spread(blocks)
    mine = jnp.sum(exchange(wide), axis=0)

    parts = collect(parts, 0)
    parts, mine = lax.optimization_barrier((parts, mine))
    parts = collect(add_parts(parts), 1)
    parts, blocks = lax.optimization_barrier((parts, blocks))
    chunks = stack(share(add_last(parts), 1))
    chunks, mine, early_sums = lax.optimization_barrier((chunks, mine, early_sums))
    chunks = share(chunks, 0)
    first = mine.astype(bf16)
    second = (mine - first.astype(f32)).astype(bf16)
    router_part = lax.dynamic_slice(early_sums[1], (owner * SEG, 0), (SEG, E))
    small = jnp.concatenate([router_part, first, second, jnp.zeros((6, 128), bf16)], axis=0)
    everyone = exchange(jnp.broadcast_to(small[None], (E, SEG + 8, 128)))
    grad_input = final(blocks, block_input, ghid, g1)
    chunks, everyone, early_sums, grad_input, result = lax.optimization_barrier(
        (chunks, everyone, early_sums, grad_input, result)
    )
    vector = everyone[:, SEG, :per].astype(f32) + everyone[:, SEG + 1, :per].astype(f32)
    vector = vector.reshape(-1)
    grad_router = everyone[:, :SEG].reshape(16, 8, SEG, E).transpose(1, 0, 2, 3)
    grad_router = grad_router.reshape(D, E).astype(f32)
    grad_wout = early_sums[0].astype(f32)
    grad_wq, grad_wk, grad_wv = place(where, chunks)
    return (
        result,
        grad_input,
        vector[:D],
        grad_wq,
        grad_wk.T,
        grad_wv.T,
        vector[2 * D : 2 * D + HEAD],
        vector[2 * D + HEAD :],
        grad_wout,
        vector[D : 2 * D],
        grad_router,
        grad_wgate[None],
        grad_wup[None],
        grad_wdown[None],
    )


def solution(mesh):
    rows = P(("expert", "shard"), None)
    experts = P(("expert", "shard"), None, None)
    columns = P(None, "shard")
    return jax.shard_map(
        on_device,
        mesh=mesh,
        in_specs=(
            rows, rows, P(), columns, columns, columns, P(), P(), P("shard", None), P(), P(),
            experts, experts, experts, P("expert", None), P("expert", None), rows,
        ),
        out_specs=(
            rows, rows, P(), columns, columns, columns, P(), P(), P("shard", None), P(), P(),
            experts, experts, experts,
        ),
        check_vma=False,
    )
```

```python
import functools

import jax
import jax.numpy as jnp
from jax import lax
from jax.experimental import pallas as pl
from jax.experimental.pallas import tpu as pltpu
from jax.sharding import PartitionSpec as P

EPS = 1e-06
ROPE_BASE = 1000000.0
LOG2E = 1.4426950408889634
T = 128
D = 2048
HEAD = 128
LH = 4
E = 128
CAP = 5
SLOTS = E * CAP
SEG = D // 128
WIRE = CAP * SEG + 8
ROWS = 1024
HALF = 512
F = 768
bf16 = jnp.bfloat16
f32 = jnp.float32
ALL = ("expert", "shard")
COSTS = {
    "attend": 11,
    "out_projection": 5,
    "router": 6,
    "transpose_rows": 6,
    "expert_grad_rows": 8,
    "expert_main": 18,
    "expert_out": 7,
    "combine_grads": 7,
    "head_grad": 4,
    "out_projection_grad": 7,
}


def cost(micros):
    return pl.CostEstimate(
        flops=1, bytes_accessed=int(micros * 0.6e6) + 1, transcendentals=0
    )


def dot(a, b):
    return jnp.dot(a, b, preferred_element_type=f32)


def dot_t(a, b):
    return lax.dot_general(a, b, (((1,), (1,)), ((), ())), preferred_element_type=f32)


def call(kernel, name, outs, scratch, args, smem=()):
    in_specs = [
        pl.BlockSpec(memory_space=pltpu.SMEM if i in smem else pltpu.VMEM)
        for i in range(len(args))
    ]
    return pl.pallas_call(
        kernel,
        out_shape=outs,
        in_specs=in_specs,
        out_specs=[pl.BlockSpec(memory_space=pltpu.VMEM) for _ in outs],
        scratch_shapes=scratch,
        compiler_params=pltpu.CompilerParams(vmem_limit_bytes=63 * 1024 * 1024),
        cost_estimate=cost(COSTS.get(name, 0)),
        name=name,
    )(*args)


def grid_call(kernel, name, grid, in_specs, out_specs, outs, scratch, args, scalars=0):
    return pl.pallas_call(
        kernel,
        out_shape=outs,
        grid_spec=pltpu.PrefetchScalarGridSpec(
            num_scalar_prefetch=scalars,
            grid=grid,
            in_specs=in_specs,
            out_specs=out_specs,
            scratch_shapes=scratch,
        ),
        compiler_params=pltpu.CompilerParams(
            vmem_limit_bytes=63 * 1024 * 1024, dimension_semantics=("arbitrary",)
        ),
        cost_estimate=cost(COSTS.get(name, 0)),
        name=name,
    )(*args)


def whole(shape):
    return pl.BlockSpec(shape, lambda i, *_: (0,) * len(shape))


def rows_of(shape):
    return pl.BlockSpec(shape, lambda i, *_: (i, 0))


def cols_of(shape):
    return pl.BlockSpec(shape, lambda i, *_: (0, i))


def sds(shape, dtype):
    return jax.ShapeDtypeStruct(shape, dtype)


def split_rows(wire, dest):
    for s in range(CAP):
        for h in range(2):
            rows = slice(s * E + h * 64, s * E + (h + 1) * 64)
            block = wire[h * 64 : (h + 1) * 64, s * SEG : (s + 1) * SEG, :]
            dest[rows, :] = block.reshape(64, D)


def join_rows(source, wire):
    for s in range(CAP):
        for h in range(2):
            rows = slice(s * E + h * 64, s * E + (h + 1) * 64)
            wire[h * 64 : (h + 1) * 64, s * SEG : (s + 1) * SEG, :] = source[rows, :].reshape(
                64, SEG, 128
            )


def put_numbers(columns, wire):
    lane = lax.broadcasted_iota(jnp.int32, (E, 128), 1)
    plane = jnp.zeros((E, 128), f32)
    for s in range(CAP):
        plane = jnp.where(lane == s, columns[s], plane)
    first = plane.astype(bf16)
    rest = plane - first.astype(f32)
    second = rest.astype(bf16)
    third = (rest - second.astype(f32)).astype(bf16)
    none = jnp.zeros((E, 5 * 128), bf16)
    wide = jnp.concatenate([first, second, third, none], axis=1)
    wire[:, CAP * SEG :, :] = wide.reshape(E, 8, 128)


def get_numbers(wire):
    wide = wire[:, CAP * SEG :, :].reshape(E, 8 * 128)
    return (
        wide[:, :128].astype(f32) + wide[:, 128:256].astype(f32) + wide[:, 256:384].astype(f32)
    )


def pack_rows(x_ref, at_ref, wire, rows):
    slot = lax.broadcasted_iota(jnp.int32, (SLOTS, T), 0)
    hit = slot == at_ref[0:1, :]
    for k in range(1, 4):
        hit = hit | (slot == at_ref[k : k + 1, :])
    pick = jnp.where(hit, 1.0, 0.0).astype(bf16)
    for j in range(8):
        cols = slice(j * 256, (j + 1) * 256)
        rows[:, cols] = dot(pick, x_ref[:, cols]).astype(bf16)
    join_rows(rows, wire)


def pack_body(x_ref, at_ref, wire, rows):
    pack_rows(x_ref, at_ref, wire, rows)
    wire[:, CAP * SEG :, :] = jnp.zeros((E, 8, 128), bf16)


def pack(x, assign_t):
    return call(
        pack_body,
        "pack_rows",
        [sds((E, WIRE, 128), bf16)],
        [pltpu.VMEM((SLOTS, D), bf16)],
        (x, assign_t),
    )[0]


def sum_rows(wire, experts, slots, gates, out):
    def body(i, carry):
        for u in range(8):
            t = i * 8 + u
            total = None
            for k in range(4):
                p = t * 4 + k
                rows = pl.ds(pl.multiple_of(slots[p] * SEG, SEG), SEG)
                part = wire[experts[p], rows, :].astype(f32) * gates[p]
                total = part if total is None else total + part
            out[pl.ds(pl.multiple_of(t * SEG, SEG), SEG), :] = total
        return carry

    lax.fori_loop(0, T // 8, body, 0)


def column(row):
    return jnp.broadcast_to(row, (128, 128)).T[:, 0:1]


def qkv_body(pieces, *refs):
    count = len(pieces)
    core, blocks = refs[0], refs[1 : 1 + 2 * count]
    g1, wqt, wk, wks, wv, wvs, gq, gk, cos, sin = refs[1 + 2 * count : 11 + 2 * count]
    outs = refs[11 + 2 * count :]
    wkv = outs[-1]
    lower = core[0] == 0
    wkv[0:64, :] = jnp.where(lower, wk[...], wks[...])
    wkv[64:128, :] = jnp.where(lower, wks[...], wk[...])
    wkv[128:192, :] = jnp.where(lower, wv[...], wvs[...])
    wkv[192:256, :] = jnp.where(lower, wvs[...], wv[...])
    gain_q, gain_k = column(gq[...]), column(gk[...])
    for number, piece in enumerate(pieces):
        qn, qt, kn, kt, vt, scale, n1 = outs[7 * number : 7 * number + 7]
        for half in range(2):
            x = blocks[2 * number + half][...].astype(f32)
            r = lax.rsqrt(jnp.mean(x * x, axis=-1, keepdims=True) + EPS)
            n1[half * T : (half + 1) * T, :] = (x * r * g1[...]).astype(bf16)
        raw = dot_t(wqt[...], n1[...])
        raw_kv = dot_t(wkv[...], n1[...])
        first, second = piece * T, HALF + piece * T
        c = jnp.concatenate([cos[:, first : first + T], cos[:, second : second + T]], axis=1)
        s = jnp.concatenate([sin[:, first : first + T], sin[:, second : second + T]], axis=1)

        def path(v, gain, factor, keep, index):
            r = lax.rsqrt(jnp.mean(v * v, axis=0, keepdims=True) + EPS)
            scale[index : index + 1, :] = r
            v = v * r
            keep[...] = v.astype(bf16)
            v = v * gain
            low, high = v[:64], v[64:]
            return (
                ((low * c - high * s) * factor).astype(bf16),
                ((high * c + low * s) * factor).astype(bf16),
            )

        scale[...] = jnp.zeros_like(scale)
        for h in range(LH):
            heads = slice(h * HEAD, (h + 1) * HEAD)
            low, high = path(raw[heads], gain_q, HEAD ** (-0.5), qn.at[heads, :], h)
            qt[h * HEAD : h * HEAD + 64, :] = low
            qt[h * HEAD + 64 : (h + 1) * HEAD, :] = high
        key = raw_kv[:HEAD].astype(bf16)
        low, high = path(key.astype(f32), gain_k, 1.0, kn, LH)
        kt[:64, :] = low
        kt[64:, :] = high
        vt[...] = raw_kv[HEAD:].astype(bf16)


def qkv(pieces, core, blocks, *args):
    outs = [
        sds((LH * HEAD, 2 * T), bf16),
        sds((LH * HEAD, 2 * T), bf16),
        sds((HEAD, 2 * T), bf16),
        sds((HEAD, 2 * T), bf16),
        sds((HEAD, 2 * T), bf16),
        sds((8, 2 * T), f32),
        sds((2 * T, D), bf16),
    ] * len(pieces)
    keep = 0 in pieces
    return call(
        functools.partial(qkv_body, pieces),
        "qkv" + "".join(str(p) for p in pieces),
        outs + ([sds((2 * HEAD, D), bf16)] if keep else []),
        [] if keep else [pltpu.VMEM((2 * HEAD, D), bf16)],
        (core, *blocks, *args),
        smem=(0,),
    )


def build_mask(info, mask):
    for b in range(8):
        keys = jnp.broadcast_to(info[0:1, b * T : (b + 1) * T], (T, T)).T
        for j in range(8):
            cols = slice(j * T, (j + 1) * T)
            inside = (keys >= info[1:2, cols]) & (keys <= info[0:1, cols])
            mask[b * T : (b + 1) * T, cols] = jnp.where(inside, 1.0, 0.0)


def attend_body(*refs):
    q, k, v = refs[0:4], refs[4:8], refs[8:12]
    info, ot0, ot1, linv, qt, kt, kn, vn, mask, vt = refs[12:]
    for dy in range(4):
        for dc in range(2):
            to = slice(dc * HALF + dy * T, dc * HALF + (dy + 1) * T)
            src = slice(dc * T, (dc + 1) * T)
            qt[:, to] = q[dy][:, src]
            kt[:, to] = k[dy][:, src]
            vt[:, to] = v[dy][:, src]
    for b in range(8):
        rows = slice(b * T, (b + 1) * T)
        kn[rows, :] = kt[:, rows].astype(f32).T.astype(bf16)
        vn[rows, :] = vt[:, rows].astype(f32).T.astype(bf16)
    build_mask(info, mask)
    for half, out in ((1, ot1), (0, ot0)):

        def body(i, carry):
            local = pl.ds(pl.multiple_of(i * 256, 256), 256)
            cols = pl.ds(pl.multiple_of(half * HALF + i * 256, 256), 256)
            for h in range(LH):
                heads = slice(h * HEAD, (h + 1) * HEAD)
                scores = dot(kn[...], qt[heads, cols])
                weights = jnp.exp2(scores * LOG2E) * mask[:, cols]
                inverse = 1.0 / jnp.sum(weights, axis=0, keepdims=True)
                out[heads, local] = (dot(vt[...], weights.astype(bf16)) * inverse).astype(bf16)
                linv[h : h + 1, cols] = inverse
            return carry

        lax.fori_loop(0, 2, body, 0)


def attend(q, k, v, info):
    return call(
        attend_body,
        "attend",
        [
            sds((LH * HEAD, HALF), bf16),
            sds((LH * HEAD, HALF), bf16),
            sds((8, ROWS), f32),
            sds((LH * HEAD, ROWS), bf16),
            sds((HEAD, ROWS), bf16),
            sds((ROWS, HEAD), bf16),
            sds((ROWS, HEAD), bf16),
        ],
        [pltpu.VMEM((ROWS, ROWS), f32), pltpu.VMEM((HEAD, ROWS), bf16)],
        (*q, *k, *v, info),
    )


def flip(source, dest, row, col):
    height, width = source.shape
    for a in range(height // 128):
        for b in range(width // 128):
            block = source[a * 128 : (a + 1) * 128, b * 128 : (b + 1) * 128]
            rows = slice(row + b * 128, row + (b + 1) * 128)
            dest[rows, col + a * 128 : col + (a + 1) * 128] = block.astype(f32).T.astype(bf16)


def outproj_body(ot0, otr, wa, wb, b0, b1, b2, b3, heads):
    @pl.when(pl.program_id(0) == 0)
    def _():
        flip(ot0, heads, 0, 0)
        flip(otr, heads, 0, 512)

    total = dot(heads[:, :512], wa[...]) + dot(heads[:, 512:], wb[...])
    for dy, out in enumerate((b0, b1, b2, b3)):
        out[...] = total[dy * T : (dy + 1) * T, :].astype(bf16)


def outproj(ot0, otr, wa, wb):
    return grid_call(
        outproj_body,
        "out_projection",
        (4,),
        [whole((512, HALF)), whole((512, HALF)), cols_of((512, 512)), cols_of((512, 512))],
        [cols_of((T, 512))] * 4,
        [sds((T, D), bf16)] * 4,
        [pltpu.VMEM((HALF, 1024), bf16)],
        (ot0, otr, wa, wb),
    )


def transpose_body(n0, n1, n2, n3, out):
    for dy, piece in enumerate((n0, n1, n2, n3)):
        for dc in range(2):
            flip(piece.at[dc * T : (dc + 1) * T, :], out, 0, dc * HALF + dy * T)


def transpose_rows(pieces):
    return call(transpose_body, "transpose_rows", [sds((D, ROWS), bf16)], [], tuple(pieces))[0]


def route_body(rt, ids, ids_t):
    lane = lax.broadcasted_iota(jnp.int32, (T, E), 1)
    row = lax.broadcasted_iota(jnp.int32, (T, E), 0)
    wide = jnp.concatenate([rt[...].astype(f32), jnp.zeros((124, T), f32)], axis=0).T
    hot = [jnp.where(lane.astype(f32) == wide[:, k : k + 1], 1.0, 0.0) for k in range(4)]
    earlier = jnp.where(lane < row, 1.0, 0.0).astype(bf16)
    before = dot(earlier, (hot[0] + hot[1] + hot[2] + hot[3]).astype(bf16))
    table = wide
    for k in range(4):
        slot = jnp.sum(before * hot[k], axis=1, keepdims=True)
        table = jnp.where(lane == 4 + k, slot, table)
        table = jnp.where(lane == 8 + k, slot * E + wide[:, k : k + 1], table)
    ids[...] = table.astype(jnp.int32)
    ids_t[...] = table.T[0:16, :].astype(jnp.int32)


def route_tables(routes_t):
    return call(
        route_body,
        "route_tables",
        [sds((T, 128), jnp.int32), sds((16, T), jnp.int32)],
        [],
        (routes_t,),
    )


def router_body(b0, b1, b2, b3, x0, g2, wr, ids, at, hidden, n2, probs, gates, wire, rows):
    v = x0[...].astype(f32) + (
        (b0[...].astype(f32) + b1[...].astype(f32))
        + (b2[...].astype(f32) + b3[...].astype(f32))
    )
    hidden[...] = v
    r = lax.rsqrt(jnp.mean(v * v, axis=-1, keepdims=True) + EPS)
    n2[...] = (v * r * g2[...]).astype(bf16)
    logits = dot(n2[...], wr[...])
    pack_rows(n2, at, wire, rows)
    expo = jnp.exp(logits - jnp.max(logits, axis=-1, keepdims=True))
    p = expo / jnp.sum(expo, axis=-1, keepdims=True)
    probs[...] = p
    lane = lax.broadcasted_iota(jnp.int32, (T, E), 1)
    chosen = [
        jnp.sum(jnp.where(lane == ids[:, k : k + 1], p, 0.0), axis=-1, keepdims=True)
        for k in range(4)
    ]
    total = chosen[0] + chosen[1] + chosen[2] + chosen[3]
    packed = jnp.where(lane == 4, total, 0.0)
    for k in range(4):
        packed = jnp.where(lane == k, chosen[k] / total, packed)
    gates[...] = packed
    across = packed.T
    expert = lax.broadcasted_iota(jnp.int32, (E, T), 0)
    columns = []
    for s in range(CAP):
        mine = jnp.zeros((E, T), f32)
        for k in range(4):
            mine = jnp.where(expert + s * E == at[k : k + 1, :], across[k : k + 1, :], mine)
        columns.append(jnp.sum(mine, axis=1, keepdims=True))
    put_numbers(columns, wire)


def router(b, x0, g2, wr, ids, assign_t):
    return call(
        router_body,
        "router",
        [
            sds((T, D), f32),
            sds((T, D), bf16),
            sds((T, E), f32),
            sds((T, E), f32),
            sds((E, WIRE, 128), bf16),
        ],
        [pltpu.VMEM((SLOTS, D), bf16)],
        (*b, x0, g2, wr, ids, assign_t),
    )


def expert_grad_body(wire, wd, gr, ga):
    split_rows(wire, gr)

    def body(i, carry):
        cols = pl.ds(pl.multiple_of(i * 256, 256), 256)
        ga[:, cols] = dot_t(gr[...], wd[cols, :])
        return carry

    lax.fori_loop(0, F // 256, body, 0)


def expert_grad(wire, wd):
    return call(
        expert_grad_body,
        "expert_grad_rows",
        [sds((SLOTS, D), bf16), sds((SLOTS, F), f32)],
        [],
        (wire, wd),
    )


def expert_main_body(wire, wg, wu, ga, back, xs, act, acts, dg, du, xr, sc):
    split_rows(wire, xr)
    gates = get_numbers(wire)
    sc[...] = jnp.zeros_like(sc)

    def forward(i, carry):
        cols = pl.ds(pl.multiple_of(i * 256, 256), 256)
        gate = dot(xr[...], wg[:, cols])
        up = dot(xr[...], wu[:, cols])
        grad = ga[:, cols]
        s = 1.0 / (1.0 + jnp.exp(-gate))
        silu = gate * s
        a = silu * up
        act[:, cols] = a.astype(bf16)
        dg[:, cols] = (grad * up * s * (1.0 + gate * (1.0 - s))).astype(bf16)
        du[:, cols] = (grad * silu).astype(bf16)
        sc[...] += jnp.sum(a * grad, axis=1, keepdims=True)
        return carry

    lax.fori_loop(0, F // 256, forward, 0)
    for s in range(CAP):
        part = slice(s * E, (s + 1) * E)
        gate = gates[:, s : s + 1]
        xs[part, :] = (xr[part, :].astype(f32) * gate).astype(bf16)
        acts[part, :] = (act[part, :].astype(f32) * gate).astype(bf16)
    for j in range(8):
        part = slice(j * 256, (j + 1) * 256)
        xr[:, part] = (dot_t(dg[...], wg[part, :]) + dot_t(du[...], wu[part, :])).astype(bf16)
    join_rows(xr, back)
    put_numbers([sc[s * E : (s + 1) * E, :] for s in range(CAP)], back)


def expert_main(wire, wg, wu, ga):
    return call(
        expert_main_body,
        "expert_main",
        [
            sds((E, WIRE, 128), bf16),
            sds((SLOTS, D), bf16),
            sds((SLOTS, F), bf16),
            sds((SLOTS, F), bf16),
            sds((SLOTS, F), bf16),
            sds((SLOTS, F), bf16),
        ],
        [pltpu.VMEM((SLOTS, D), bf16), pltpu.VMEM((SLOTS, 1), f32)],
        (wire, wg, wu, ga),
    )


def expert_out_body(act, wd, wire, rows):
    for j in range(8):
        cols = slice(j * 256, (j + 1) * 256)
        rows[:, cols] = dot(act[...], wd[:, cols]).astype(bf16)
    join_rows(rows, wire)


def expert_out(act, wd):
    return call(
        expert_out_body,
        "expert_out",
        [sds((E, CAP * SEG, 128), bf16)],
        [pltpu.VMEM((SLOTS, D), bf16)],
        (act, wd),
    )[0]


def combine_body(
    where, experts, slots, gate_list, wire, hidden, n2, probs, gates, ids, og, g2, wr,
    ghid, gatt, router_own, router_sib, gg2, sums, gn2, parts,
):
    sum_rows(wire, experts, slots, gate_list, sums)
    scores = get_numbers(wire)
    lane = lax.broadcasted_iota(jnp.int32, (T, E), 1)
    grads = []
    for k in range(4):
        hot = jnp.where(lane == ids[:, k : k + 1], 1.0, 0.0)
        rows = lax.dot_general(
            hot, scores, (((1,), (0,)), ((), ())),
            precision=lax.Precision.HIGHEST, preferred_element_type=f32,
        )
        picked = jnp.where(lane == ids[:, 4 + k : 5 + k], rows, 0.0)
        grads.append(jnp.sum(picked, axis=-1, keepdims=True))
    inner = sum(grads[k] * gates[:, k : k + 1] for k in range(4))
    inverse = 1.0 / gates[:, 4:5]
    grad_probs = jnp.zeros((T, E), f32)
    for k in range(4):
        grad_probs = jnp.where(
            lane == ids[:, k : k + 1], (grads[k] - inner) * inverse, grad_probs
        )
    p = probs[...]
    gl = (p * (grad_probs - jnp.sum(p * grad_probs, axis=-1, keepdims=True))).astype(bf16)
    for h in range(2):
        tokens = slice(h * 64, (h + 1) * 64)
        gn2[tokens, :] = sums[h * 1024 : (h + 1) * 1024, :].reshape(64, D)
    gn2[...] += dot_t(gl, wr[...])
    c = gn2[...]
    v = hidden[...]
    r = lax.rsqrt(jnp.mean(v * v, axis=-1, keepdims=True) + EPS)
    u = c * g2[...]
    m = jnp.mean(u * v, axis=-1, keepdims=True)
    total = og[...].astype(f32) + r * u - v * (r * r * r * m)
    ghid[...] = total
    gatt[...] = total.astype(bf16)
    gg2[...] = jnp.sum(c * (v * r), axis=0, keepdims=True)
    for j in range(SEG):
        cols = slice(j * 128, (j + 1) * 128)
        owner = j // 2
        dy = lax.rem(owner // 2 + 4 - where[3], 4)
        dc = lax.rem(owner % 2 + where[2], 2)
        half = slice((j % 2) * 128, (j % 2 + 1) * 128)
        parts[dc * 4 + dy, half, :] = dot(n2[:, cols].astype(f32).T.astype(bf16), gl).astype(bf16)
    router_own[...] = parts[0:4]
    router_sib[...] = parts[4:8]


def combine(*args):
    return call(
        combine_body,
        "combine_grads",
        [
            sds((T, D), f32),
            sds((T, D), bf16),
            sds((4, 256, E), bf16),
            sds((4, 256, E), bf16),
            sds((1, D), f32),
        ],
        [
            pltpu.VMEM((T * SEG, 128), f32),
            pltpu.VMEM((T, D), f32),
            pltpu.VMEM((8, 256, E), bf16),
        ],
        args,
        smem=(0, 1, 2, 3),
    )


def result_body(experts, slots, gate_list, wire, hidden, out, sums):
    sum_rows(wire, experts, slots, gate_list, sums)
    for h in range(2):
        tokens = slice(h * 64, (h + 1) * 64)
        mixture = sums[h * 1024 : (h + 1) * 1024, :].reshape(64, D)
        out[tokens, :] = (hidden[tokens, :] + mixture).astype(bf16)


def result_rows(*args):
    return call(
        result_body,
        "result",
        [sds((T, D), bf16)],
        [pltpu.VMEM((T * SEG, 128), f32)],
        args,
        smem=(0, 1, 2),
    )[0]


def head_grad_body(*refs):
    blocks, (wo, dt, rows_all) = refs[:6], refs[6:]
    for b in range(6):
        rows_all[b * T : (b + 1) * T, :] = blocks[b][...]
    for b in range(3):
        rows = slice(b * 256, (b + 1) * 256)
        dt[:, rows] = dot_t(wo[...], rows_all[rows, :]).astype(bf16)


def head_grad(blocks, wo):
    return call(
        head_grad_body,
        "head_grad",
        [sds((LH * HEAD, 6 * T), bf16)],
        [pltpu.VMEM((6 * T, D), bf16)],
        (*blocks, wo),
    )[0]


def pre_body(where, *refs):
    blocks, routers = refs[:8], refs[8:12]
    ot0, ot1, wo, w0, w1, w2, w3, dt, rows_all, total = refs[12:]
    step = pl.program_id(0)
    for b in range(8):
        rows_all[b * T : (b + 1) * T, :] = blocks[b][...]
    grad = (dot(ot0[...], rows_all[:HALF, :]) + dot(ot1[...], rows_all[HALF:, :])).astype(bf16)
    for dx, out in enumerate((w0, w1, w2, w3)):

        @pl.when(step == dx)
        def _():
            for col in range(4):
                dz = lax.rem(col + 4 - where[0], 4)
                start = lax.rem(where[1] + dx, 4) * 64 + col * 16
                rows = pl.ds(pl.multiple_of(start, 16), 16)
                out[dz, :512, :] = grad[:, col * 128 : (col + 1) * 128]
                out[dz, 512:, :] = (
                    (routers[0][rows, :].astype(f32) + routers[1][rows, :].astype(f32))
                    + (routers[2][rows, :].astype(f32) + routers[3][rows, :].astype(f32))
                ).astype(bf16)

    last = jnp.concatenate([blocks[2][...], blocks[6][...]], axis=0)
    part = dot_t(wo[...], last)

    @pl.when(step == 0)
    def _():
        total[...] = part

    @pl.when(step > 0)
    def _():
        total[...] += part

    @pl.when(step == 3)
    def _():
        dt[...] = total[...].astype(bf16)


def pre(where, blocks, routers, ot0, ot1, wo):
    def turned(shape):
        return pl.BlockSpec(shape, lambda i, w: (0, lax.rem(i + w[1], 4)))

    return grid_call(
        pre_body,
        "out_projection_grad",
        (4,),
        [turned((T, 512))] * 8
        + [whole((256, E))] * 4
        + [whole((512, HALF))] * 2
        + [turned((512, 512))],
        [whole((4, 528, 128))] * 4 + [whole((512, 2 * T))],
        [sds((4, 528, 128), bf16)] * 4 + [sds((LH * HEAD, 2 * T), bf16)],
        [pltpu.VMEM((ROWS, 512), bf16), pltpu.VMEM((512, 2 * T), f32)],
        (where, *blocks, *routers, ot0, ot1, wo),
        scalars=1,
    )


def bwd_body(*refs):
    qh, kh, scales = refs[0:4], refs[4:8], refs[8:12]
    (qt, kt, kn, vn, dta, dtb, ot0, ot1, linv, info, cos, sin, gq, gk) = refs[12:26]
    dq0, dq1, dkv, ggq, ggk, mask, wb, sb, dqt, dk, dv, raw, dt, scale = refs[26:]
    for dc in range(2):
        for place, dy in enumerate((0, 1, 3)):
            to = slice(dc * HALF + dy * T, dc * HALF + (dy + 1) * T)
            dt[:, to] = dta[:, (place * 2 + dc) * T : (place * 2 + dc + 1) * T]
        dt[:, dc * HALF + 2 * T : dc * HALF + 3 * T] = dtb[:, dc * T : (dc + 1) * T]
        for dy in range(4):
            to = slice(dc * HALF + dy * T, dc * HALF + (dy + 1) * T)
            scale[:, to] = scales[dy][:, dc * T : (dc + 1) * T]
    build_mask(info, mask)
    dk[...] = jnp.zeros_like(dk)
    dv[...] = jnp.zeros_like(dv)
    for half, out in ((0, ot0), (1, ot1)):

        def body(i, carry):
            local = pl.ds(pl.multiple_of(i * 256, 256), 256)
            cols = pl.ds(pl.multiple_of(half * HALF + i * 256, 256), 256)
            for h in range(LH):
                heads = slice(h * HEAD, (h + 1) * HEAD)
                part = slice(h * 256, (h + 1) * 256)
                scores = dot(kn[...], qt[heads, cols])
                weights = jnp.exp2(scores * LOG2E) * (mask[:, cols] * linv[h : h + 1, cols])
                grad = dt[heads, cols]
                delta = jnp.sum(
                    grad.astype(f32) * out[heads, local].astype(f32), axis=0, keepdims=True
                )
                wb[:, part] = weights.astype(bf16)
                sb[:, part] = (weights * (dot(vn[...], grad) - delta)).astype(bf16)
                dqt[heads, cols] = dot(kt[...], sb[:, part])
            grads = jnp.concatenate(
                [dt[h * HEAD : (h + 1) * HEAD, cols] for h in range(LH)], axis=1
            )
            queries = jnp.concatenate(
                [qt[h * HEAD : (h + 1) * HEAD, cols] for h in range(LH)], axis=1
            )
            dv[...] += dot_t(wb[...], grads)
            dk[...] += dot_t(sb[...], queries)
            return carry

        lax.fori_loop(0, 2, body, 0)

    def unrope(v):
        low, high = v[:64], v[64:]
        c, s = cos[...], sin[...]
        return jnp.concatenate([low * c + high * s, high * c - low * s], axis=0)

    def norm_back(n, r, grad, gain):
        gain_grad = jnp.sum(grad * n, axis=1, keepdims=True)
        u = grad * gain
        return r * (u - n * jnp.mean(u * n, axis=0, keepdims=True)), gain_grad

    gain_q, gain_k = column(gq[...]), column(gk[...])
    total = jnp.zeros((HEAD, 1), f32)
    for h in range(LH):
        heads = slice(h * HEAD, (h + 1) * HEAD)
        for dy in range(4):
            for dc in range(2):
                to = slice(dc * HALF + dy * T, dc * HALF + (dy + 1) * T)
                raw[:, to] = qh[dy][heads, dc * T : (dc + 1) * T].astype(f32)
        grad, part = norm_back(raw[...], scale[h : h + 1, :], unrope(dqt[heads, :] * (HEAD ** (-0.5))), gain_q)
        total = total + part
        dq0[heads, :] = grad[:, :HALF].astype(bf16)
        dq1[heads, :] = grad[:, HALF:].astype(bf16)
    ggq[...] = jnp.broadcast_to(total, (HEAD, 128)).T[0:8, :]
    for dy in range(4):
        for dc in range(2):
            to = slice(dc * HALF + dy * T, dc * HALF + (dy + 1) * T)
            raw[:, to] = kh[dy][:, dc * T : (dc + 1) * T].astype(f32)
    grad, part = norm_back(raw[...], scale[LH : LH + 1, :], unrope(dk[...].T), gain_k)
    ggk[...] = jnp.broadcast_to(part, (HEAD, 128)).T[0:8, :]
    dkv[:HEAD, :] = grad.astype(bf16)
    dkv[HEAD:, :] = dv[...].T.astype(bf16)


def bwd(qh, kh, scales, *rest):
    return call(
        bwd_body,
        "attend_grad",
        [
            sds((LH * HEAD, HALF), bf16),
            sds((LH * HEAD, HALF), bf16),
            sds((2 * HEAD, ROWS), bf16),
            sds((8, HEAD), f32),
            sds((8, HEAD), f32),
        ],
        [
            pltpu.VMEM((ROWS, ROWS), f32),
            pltpu.VMEM((ROWS, LH * 256), bf16),
            pltpu.VMEM((ROWS, LH * 256), bf16),
            pltpu.VMEM((LH * HEAD, ROWS), f32),
            pltpu.VMEM((ROWS, HEAD), f32),
            pltpu.VMEM((ROWS, HEAD), f32),
            pltpu.VMEM((HEAD, ROWS), f32),
            pltpu.VMEM((LH * HEAD, ROWS), bf16),
            pltpu.VMEM((8, ROWS), f32),
        ],
        (*qh, *kh, *scales, *rest),
    )


def qkv_grad_body(where, n1t, dq0, dq1, own, sib, w0, w1, w2, w3, tot, dt):
    step = pl.program_id(0)

    @pl.when(step == 0)
    def _():
        tot[:, :HALF] = (own[:, :HALF].astype(f32) + sib[:, HALF:].astype(f32)).astype(bf16)
        tot[:, HALF:] = (own[:, HALF:].astype(f32) + sib[:, :HALF].astype(f32)).astype(bf16)
        dt[:512, :HALF] = dq0[...]
        dt[:512, HALF:] = dq1[...]
        upper = where[2] == 1
        dt[512:576, :] = jnp.where(upper, tot[64:128, :], tot[:64, :])
        dt[576:, :] = jnp.where(upper, tot[192:, :], tot[128:192, :])

    grad = dot_t(n1t[...], dt[...]).astype(bf16)
    for dz, out in enumerate((w0, w1, w2, w3)):

        @pl.when(step == dz)
        def _():
            for col in range(4):
                dx = lax.rem(col + 4 - where[1], 4)
                out[dx] = grad[col * 128 : (col + 1) * 128, :]


def qkv_grad(where, n1t, dq0, dq1, own, sib):
    return grid_call(
        qkv_grad_body,
        "qkv_weight_grad",
        (4,),
        [
            pl.BlockSpec((512, ROWS), lambda i, w: (lax.rem(i + w[0], 4), 0)),
            whole((512, HALF)),
            whole((512, HALF)),
            whole((2 * HEAD, ROWS)),
            whole((2 * HEAD, ROWS)),
        ],
        [whole((4, 128, 640))] * 4 + [whole((2 * HEAD, ROWS))],
        [sds((4, 128, 640), bf16)] * 4 + [sds((2 * HEAD, ROWS), bf16)],
        [pltpu.VMEM((640, ROWS), bf16)],
        (where, n1t, dq0, dq1, own, sib),
        scalars=1,
    )


def add_body(a, b, c, d, *outs):
    for i, out in enumerate(outs):
        out[...] = (
            (a[i].astype(f32) + b[i].astype(f32)) + (c[i].astype(f32) + d[i].astype(f32))
        ).astype(bf16)


def add_parts(parts):
    shape = parts[0].shape[1:]
    return call(add_body, "add_parts", [sds(shape, bf16)] * 4, [], tuple(parts))


def split_two(v):
    first = v.astype(bf16)
    return first, (v - first.astype(f32)).astype(bf16)


def normed_grad_body(
    wa, wb, wkv, dq0, dqr, tot, n0, n1, n2, n3, gg2, ggq, ggk, b0, b1, b2, b3, grads
):
    @pl.when(pl.program_id(0) == 0)
    def _():
        flip(dq0, grads, 0, 0)
        flip(dqr, grads, 0, 512)
        flip(tot, grads, 0, 1024)

    total = (
        dot(grads[:, :512], wa[...])
        + dot(grads[:, 512:1024], wb[...])
        + dot(grads[:, 1024:], wkv[...])
    )
    gain = jnp.zeros((1, 512), f32)
    outs = (b0, b1, b2, b3)
    for dy, (out, rows) in enumerate(zip(outs, (n0, n1, n2, n3))):
        part = total[dy * T : (dy + 1) * T, :]
        out[:T, :] = part.astype(bf16)
        gain = gain + jnp.sum(part * rows[...].astype(f32), axis=0, keepdims=True)
    heads = jnp.concatenate([ggq[0:1, :], ggk[0:1, :], jnp.zeros((1, 256), f32)], axis=1)
    numbers = [*split_two(gain), *split_two(gg2[...]), *split_two(heads)]
    extra = jnp.concatenate([n.astype(f32) for n in numbers] + [jnp.zeros((10, 512), f32)], axis=0)
    for out in outs:
        out[T:, :] = extra.astype(bf16)


def normed_grad(wa, wb, wkv, dq0, dqr, tot, n1, gg2, ggq, ggk):
    return grid_call(
        normed_grad_body,
        "normed_grad",
        (4,),
        [
            cols_of((512, 512)),
            cols_of((512, 512)),
            cols_of((256, 512)),
            whole((512, HALF)),
            whole((512, HALF)),
            whole((2 * HEAD, HALF)),
        ]
        + [cols_of((T, 512))] * 4
        + [cols_of((1, 512)), whole((8, HEAD)), whole((8, HEAD))],
        [cols_of((T + 16, 512))] * 4,
        [sds((T + 16, D), bf16)] * 4,
        [pltpu.VMEM((HALF, 1280), bf16)],
        (wa, wb, wkv, dq0, dqr, tot, *n1, gg2, ggq, ggk),
    )


def add_pair_body(a, b, *outs):
    for i, out in enumerate(outs):
        out[...] = (a[i].astype(f32) + b[i].astype(f32)).astype(bf16)


def add_pair(a, b):
    return call(add_pair_body, "add_pair", [sds(a.shape[1:], bf16)] * 4, [], (a, b))


def add_last_body(a, b, c, d, *outs):
    total = (
        (a[...].astype(f32) + b[...].astype(f32)) + (c[...].astype(f32) + d[...].astype(f32))
    ).astype(bf16)
    start = 0
    for out in outs:
        out[...] = total[start : start + out.shape[0]]
        start += out.shape[0]


def add_last(parts, *heights):
    outs = [sds((height, parts[0].shape[1]), bf16) for height in heights]
    return call(add_last_body, "add_last", outs, [], tuple(parts))


def stack_body(a, b, c, d, out):
    for i, part in enumerate((a, b, c, d)):
        out[i] = part[...]


def stack(parts):
    shape = (4, *parts[0].shape)
    return call(stack_body, "stack_parts", [sds(shape, bf16)], [], tuple(parts))[0]


def place_out_body(where, c0, c1, c2, c3, out):
    for dx, chunks in enumerate((c0, c1, c2, c3)):
        for dz in range(4):
            chunk = lax.rem(where[1] + dx, 4) * 4 + lax.rem(where[0] + dz, 4)
            cols = pl.ds(pl.multiple_of(chunk * 128, 128), 128)
            out[:, cols] = chunks[dz].astype(f32)


def place_out(where, chunks):
    return call(
        place_out_body,
        "place_output_grads",
        [sds((512, D), f32)],
        [],
        (where, *chunks),
        smem=(0,),
    )[0]


def place_body(where, c0, c1, c2, c3, gq, gkt, gvt):
    for dz, chunks in enumerate((c0, c1, c2, c3)):
        for dx in range(4):
            chunk = lax.rem(where[0] + dz, 4) * 4 + lax.rem(where[1] + dx, 4)
            rows = pl.ds(pl.multiple_of(chunk * 128, 128), 128)
            gq[rows, :] = chunks[dx, :, :512].astype(f32)
            both = chunks[dx, :, 512:].astype(f32).T
            gkt[:, rows] = both[:64]
            gvt[:, rows] = both[64:]


def place(where, chunks):
    return call(
        place_body,
        "place_weight_grads",
        [sds((D, 512), f32), sds((64, D), f32), sds((64, D), f32)],
        [],
        (where, *chunks),
        smem=(0,),
    )


def final_body(b0, b1, b2, b3, x0, ghid, g1, out, gains):
    whole_sum = (b0[...].astype(f32) + b1[...].astype(f32)) + (
        b2[...].astype(f32) + b3[...].astype(f32)
    )
    c = whole_sum[:T]
    v = x0[...].astype(f32)
    r = lax.rsqrt(jnp.mean(v * v, axis=-1, keepdims=True) + EPS)
    u = c * g1[...]
    m = jnp.mean(u * v, axis=-1, keepdims=True)
    out[...] = ghid[...] + r * u - v * (r * r * r * m)
    extra = whole_sum[T:]
    gains[...] = jnp.concatenate(
        [
            (extra[0:1] + extra[1:2]) / g1[...],
            extra[2:3] + extra[3:4],
            extra[4:5] + extra[5:6],
            jnp.zeros((5, D), f32),
        ],
        axis=0,
    )


def final(b, x0, ghid, g1):
    return call(
        final_body,
        "input_grad",
        [sds((T, D), f32), sds((8, D), f32)],
        [],
        (*b, x0, ghid, g1),
    )


def sibling(x):
    return lax.ppermute(x, "shard", [(i, i ^ 1) for i in range(8)])


def from_chip(x, dy):
    return lax.ppermute(x, "shard", [(i, (i - 2 * dy) % 8) for i in range(8)])


def to_chip(x, dy):
    return lax.ppermute(x, "shard", [(i, (i + 2 * dy) % 8) for i in range(8)])


def exchange(x):
    return lax.all_to_all(x, ALL, split_axis=0, concat_axis=0, tiled=True)


def spread(x):
    return [to_chip(x[d], d) for d in (1, 3, 2)]


def on_expert(x, dz, dx):
    pairs = [
        (z * 4 + c, ((z + dz) % 4) * 4 + (c + dx) % 4) for z in range(4) for c in range(4)
    ]
    return lax.ppermute(x, "expert", pairs)


def move(x, axis, distance):
    return on_expert(x, distance, 0) if axis == 0 else on_expert(x, 0, distance)


def collect(parts, axis):
    return [parts[0]] + [move(parts[d], axis, d) for d in (1, 3, 2)]


def share(x, axis):
    return [x] + [move(x, axis, (4 - d) % 4) for d in (1, 2, 3)]


def after(value, *others):
    return lax.optimization_barrier((value, *others))[0]


def on_device(
    block_input, out_grad, norm1_gain, w_query, w_key, w_value, query_gain, key_gain, w_out,
    norm2_gain, w_router, w_gate, w_up, w_down, seq_lengths, token_places, expert_routes,
):
    shard, owner = lax.axis_index("shard"), lax.axis_index("expert")
    chip, core = shard // 2, shard % 2
    where = jnp.stack([owner // 4, owner % 4, core, chip]).astype(jnp.int32)
    core_id = core.reshape(1)
    g1 = norm1_gain.astype(f32).reshape(1, D)
    g2 = norm2_gain.astype(f32).reshape(1, D)
    gq = query_gain.astype(f32).reshape(1, HEAD)
    gk = key_gain.astype(f32).reshape(1, HEAD)

    x_own = [block_input] + [from_chip(block_input, dy) for dy in (1, 2, 3)]
    x_sib = [sibling(block_input)]

    chips = (chip + jnp.arange(4)) % 4
    order = jnp.concatenate([chips * 2 + core, chips * 2 + 1 - core])
    places = token_places[0].reshape(8, T)[order].reshape(ROWS)
    lengths = seq_lengths[0]
    ends = jnp.cumsum(lengths)
    starts = jnp.sum(
        jnp.where(places[:, None] >= ends[None, :], lengths[None, :], 0), axis=1
    )
    positions = (places - starts).astype(f32)
    info = jnp.concatenate(
        [places[None].astype(f32), starts[None].astype(f32), jnp.zeros((6, ROWS), f32)], axis=0
    )
    inverse_freq = ROPE_BASE ** (-jnp.arange(0, HEAD, 2).astype(f32) / HEAD)
    angles = inverse_freq[:, None] * positions[None, :]
    cos, sin = jnp.cos(angles), jnp.sin(angles)

    ids, ids_t = route_tables(expert_routes.T)
    assign_t = ids_t[8:12]
    expert_list = ids[:, 0:4].reshape(-1)
    slot_list = ids[:, 4:8].reshape(-1)

    wk_t, wv_t = w_key.T, w_value.T
    wk_s, wv_s = sibling(wk_t), sibling(wv_t)
    wq_t = w_query.T
    wo_s = sibling(w_out)
    wq_ts = sibling(wq_t)

    weights = (g1, wq_t, wk_t, wk_s, wv_t, wv_s, gq, gk, cos, sin)
    zero = qkv((0,), core_id, (x_own[0], x_sib[0]), *weights)
    og_wire = pack(out_grad, assign_t)
    x_own[1], x_own[2], x_own[3], q_first, og_wire = lax.optimization_barrier(
        (x_own[1], x_own[2], x_own[3], zero[1], og_wire)
    )
    x_sib += [sibling(x_own[dy]) for dy in (1, 2, 3)]
    blocks = [side[dy] for dy in (1, 2, 3) for side in (x_own, x_sib)]
    others = qkv((1, 2, 3), core_id, blocks, *weights)
    wkv = zero[7]
    pieces = [zero[:7], others[:7], others[7:14], others[14:21]]
    qh, q, kh, k, v, scales, n1 = zip(*pieces)
    q = (q_first,) + q[1:]
    got_grads = exchange(og_wire)
    ot0, ot1, linv, qt, kt, kn, vn = attend(q, k, v, info)
    blocks = outproj(ot0, sibling(ot1), w_out, wo_s)
    blocks = [blocks[0]] + spread(blocks)
    hidden, n2, probs, gates, wire = router(blocks, block_input, g2, w_router, ids, assign_t)
    got_rows = exchange(wire)

    n1_t = transpose_rows(after(n1, wire))
    gate_list = gates[:, :4].reshape(-1)
    grad_rows, grad_act = expert_grad(after(got_grads, wire), w_down[0])
    got_rows, n1_t, grad_act, gate_list, wq_ts = lax.optimization_barrier(
        (got_rows, n1_t, grad_act, gate_list, wq_ts)
    )

    back, rows, act, scaled_act, dg, du = expert_main(got_rows, w_gate[0], w_up[0], grad_act)
    back_wire = exchange(back)

    rows, act, scaled_act, dg, du = after((rows, act, scaled_act, dg, du), back)
    out_wire = expert_out(act, w_down[0])

    def weight_grad(a, b):
        return lax.dot_general(a, b, (((0,), (0,)), ((), ())), preferred_element_type=f32)

    grad_wgate = weight_grad(rows, dg)
    grad_wup = weight_grad(rows, du)
    grad_wdown = weight_grad(scaled_act, grad_rows)
    back_wire, out_wire, grad_wgate, grad_wup, grad_wdown = lax.optimization_barrier(
        (back_wire, out_wire, grad_wgate, grad_wup, grad_wdown)
    )

    ghid, gatt, router_own, router_sib, gg2 = combine(
        where, expert_list, slot_list, gate_list, back_wire, hidden, n2, probs, gates, ids,
        out_grad, g2, w_router,
    )
    g_own = [gatt] + [from_chip(gatt, dy) for dy in (1, 2, 3)]
    router_parts = add_pair(router_own, sibling(router_sib))
    router_parts = [router_parts[0]] + spread(router_parts)
    g_sib = [sibling(block) for block in g_own]
    dt_near = head_grad(
        [g_own[0], g_sib[0], g_own[1], g_sib[1], g_own[3], g_sib[3]], w_out
    )
    g_far, dt_near = lax.optimization_barrier(((g_own[2], g_sib[2]), dt_near))
    g_own[2], g_sib[2] = g_far

    *out_parts, dt_far = pre(where, g_own + g_sib, router_parts, ot0, ot1, w_out)
    out_parts = collect(out_parts, 1)
    returned = exchange(after(out_wire, dt_far))

    dq0, dq1, dkv, ggq, ggk = bwd(
        qh, kh, scales, qt, kt, kn, vn, dt_near, dt_far, ot0, ot1, linv, info, cos, sin, gq, gk
    )
    dq1, dkv, out_parts = lax.optimization_barrier((dq1, dkv, out_parts))
    dq_sib, dkv_sib = sibling(dq1), sibling(dkv)
    *parts, dkv_total = qkv_grad(where, n1_t, dq0, dq1, dkv, dkv_sib)
    returned, dq0 = lax.optimization_barrier((returned, dq0))
    result = result_rows(expert_list, slot_list, gate_list, returned, hidden)
    blocks = normed_grad(wq_t, wq_ts, wkv, dq0, dq_sib, dkv_total, n1, gg2, ggq, ggk)
    blocks = [blocks[0]] + spread(blocks)
    out_parts = collect(add_parts(out_parts), 0)

    parts = collect(parts, 0)
    parts, out_parts = lax.optimization_barrier((parts, out_parts))
    out_chunk, router_chunk = add_last(out_parts, 512, SEG)
    out_chunks = share(out_chunk, 0)
    grad_router = exchange(jnp.broadcast_to(router_chunk[None], (E, SEG, E)))
    parts = collect(add_parts(parts), 1)
    parts, out_chunks, blocks = lax.optimization_barrier((parts, out_chunks, blocks))
    chunks = share(add_last(parts, 128)[0], 1)
    out_chunks = share(stack(out_chunks), 1)
    grad_input, gains = final(blocks, block_input, ghid, g1)
    gains = gains[:3]
    gains = gains + sibling(gains)
    chunks, gains = lax.optimization_barrier((stack(chunks), gains))
    chunks = share(chunks, 0)
    out_chunks = after(out_chunks, *chunks[1:])
    gains = jnp.sum(lax.all_gather(gains, "expert"), axis=0)
    grad_wout = place_out(where, out_chunks)
    grad_router = grad_router.reshape(4, 4, 8, SEG, E).transpose(2, 1, 0, 3, 4)
    grad_router = grad_router.reshape(D, E).astype(f32)
    chunks, gains, result, grad_wout, grad_router = lax.optimization_barrier(
        (chunks, gains, result, grad_wout, grad_router)
    )
    grad_wq, grad_wk, grad_wv = place(where, chunks)
    return (
        result,
        grad_input,
        gains[0],
        grad_wq,
        grad_wk.T,
        grad_wv.T,
        gains[2, :HEAD],
        gains[2, HEAD : 2 * HEAD],
        grad_wout,
        gains[1],
        grad_router,
        grad_wgate[None],
        grad_wup[None],
        grad_wdown[None],
    )


def solution(mesh):
    rows = P(("expert", "shard"), None)
    experts = P(("expert", "shard"), None, None)
    columns = P(None, "shard")
    return jax.shard_map(
        on_device,
        mesh=mesh,
        in_specs=(
            rows, rows, P(), columns, columns, columns, P(), P(), P("shard", None), P(), P(),
            experts, experts, experts, P("expert", None), P("expert", None), rows,
        ),
        out_specs=(
            rows, rows, P(), columns, columns, columns, P(), P(), P("shard", None), P(), P(),
            experts, experts, experts,
        ),
        check_vma=False,
    )
```

```python
import functools

import jax
import jax.numpy as jnp
from jax import lax
from jax.experimental import pallas as pl
from jax.experimental.pallas import tpu as pltpu
from jax.sharding import PartitionSpec as P

EPS = 1e-06
ROPE_BASE = 1000000.0
LOG2E = 1.4426950408889634
T = 128
D = 2048
HEAD = 128
LH = 4
E = 128
CAP = 5
SLOTS = E * CAP
SEG = D // 128
WIRE = CAP * SEG + 8
ROWS = 1024
HALF = 512
F = 768
bf16 = jnp.bfloat16
f32 = jnp.float32
ALL = ("expert", "shard")
COSTS = {
    "attend": 11,
    "out_projection": 5,
    "router": 6,
    "transpose_rows": 6,
    "expert_grad_rows": 8,
    "expert_main": 18,
    "expert_out": 7,
    "combine_grads": 7,
    "head_grad": 4,
    "out_projection_grad": 7,
}


def cost(micros):
    return pl.CostEstimate(
        flops=1, bytes_accessed=int(micros * 0.6e6) + 1, transcendentals=0
    )


def dot(a, b):
    return jnp.dot(a, b, preferred_element_type=f32)


def dot_t(a, b):
    return lax.dot_general(a, b, (((1,), (1,)), ((), ())), preferred_element_type=f32)


def call(kernel, name, outs, scratch, args, smem=()):
    in_specs = [
        pl.BlockSpec(memory_space=pltpu.SMEM if i in smem else pltpu.VMEM)
        for i in range(len(args))
    ]
    return pl.pallas_call(
        kernel,
        out_shape=outs,
        in_specs=in_specs,
        out_specs=[pl.BlockSpec(memory_space=pltpu.VMEM) for _ in outs],
        scratch_shapes=scratch,
        compiler_params=pltpu.CompilerParams(vmem_limit_bytes=63 * 1024 * 1024),
        cost_estimate=cost(COSTS.get(name, 0)),
        name=name,
    )(*args)


def grid_call(kernel, name, grid, in_specs, out_specs, outs, scratch, args, scalars=0):
    return pl.pallas_call(
        kernel,
        out_shape=outs,
        grid_spec=pltpu.PrefetchScalarGridSpec(
            num_scalar_prefetch=scalars,
            grid=grid,
            in_specs=in_specs,
            out_specs=out_specs,
            scratch_shapes=scratch,
        ),
        compiler_params=pltpu.CompilerParams(
            vmem_limit_bytes=63 * 1024 * 1024, dimension_semantics=("arbitrary",)
        ),
        cost_estimate=cost(COSTS.get(name, 0)),
        name=name,
    )(*args)


def whole(shape):
    return pl.BlockSpec(shape, lambda i, *_: (0,) * len(shape))


def rows_of(shape):
    return pl.BlockSpec(shape, lambda i, *_: (i, 0))


def cols_of(shape):
    return pl.BlockSpec(shape, lambda i, *_: (0, i))


def sds(shape, dtype):
    return jax.ShapeDtypeStruct(shape, dtype)


def split_rows(wire, dest):
    for s in range(CAP):
        for h in range(2):
            rows = slice(s * E + h * 64, s * E + (h + 1) * 64)
            block = wire[h * 64 : (h + 1) * 64, s * SEG : (s + 1) * SEG, :]
            dest[rows, :] = block.reshape(64, D)


def join_rows(source, wire):
    for s in range(CAP):
        for h in range(2):
            rows = slice(s * E + h * 64, s * E + (h + 1) * 64)
            wire[h * 64 : (h + 1) * 64, s * SEG : (s + 1) * SEG, :] = source[rows, :].reshape(
                64, SEG, 128
            )


def put_numbers(columns, wire):
    lane = lax.broadcasted_iota(jnp.int32, (E, 128), 1)
    plane = jnp.zeros((E, 128), f32)
    for s in range(CAP):
        plane = jnp.where(lane == s, columns[s], plane)
    first = plane.astype(bf16)
    rest = plane - first.astype(f32)
    second = rest.astype(bf16)
    third = (rest - second.astype(f32)).astype(bf16)
    none = jnp.zeros((E, 5 * 128), bf16)
    wide = jnp.concatenate([first, second, third, none], axis=1)
    wire[:, CAP * SEG :, :] = wide.reshape(E, 8, 128)


def get_numbers(wire):
    wide = wire[:, CAP * SEG :, :].reshape(E, 8 * 128)
    return (
        wide[:, :128].astype(f32) + wide[:, 128:256].astype(f32) + wide[:, 256:384].astype(f32)
    )


def pack_rows(x_ref, at_ref, wire, rows):
    slot = lax.broadcasted_iota(jnp.int32, (SLOTS, T), 0)
    hit = slot == at_ref[0:1, :]
    for k in range(1, 4):
        hit = hit | (slot == at_ref[k : k + 1, :])
    pick = jnp.where(hit, 1.0, 0.0).astype(bf16)
    for j in range(8):
        cols = slice(j * 256, (j + 1) * 256)
        rows[:, cols] = dot(pick, x_ref[:, cols]).astype(bf16)
    join_rows(rows, wire)


def pack_body(x_ref, at_ref, wire, rows):
    pack_rows(x_ref, at_ref, wire, rows)
    wire[:, CAP * SEG :, :] = jnp.zeros((E, 8, 128), bf16)


def pack(x, assign_t):
    return call(
        pack_body,
        "pack_rows",
        [sds((E, WIRE, 128), bf16)],
        [pltpu.VMEM((SLOTS, D), bf16)],
        (x, assign_t),
    )[0]


def sum_rows(wire, experts, slots, gates, out):
    def body(i, carry):
        for u in range(8):
            t = i * 8 + u
            total = None
            for k in range(4):
                p = t * 4 + k
                rows = pl.ds(pl.multiple_of(slots[p] * SEG, SEG), SEG)
                part = wire[experts[p], rows, :].astype(f32) * gates[p]
                total = part if total is None else total + part
            out[pl.ds(pl.multiple_of(t * SEG, SEG), SEG), :] = total
        return carry

    lax.fori_loop(0, T // 8, body, 0)


def column(row):
    return jnp.broadcast_to(row, (128, 128)).T[:, 0:1]


def qkv_body(pieces, *refs):
    count = len(pieces)
    core, blocks = refs[0], refs[1 : 1 + 2 * count]
    g1, wqt, wk, wks, wv, wvs, gq, gk, cos, sin = refs[1 + 2 * count : 11 + 2 * count]
    outs = refs[11 + 2 * count :]
    wkv = outs[-1]
    lower = core[0] == 0
    wkv[0:64, :] = jnp.where(lower, wk[...], wks[...])
    wkv[64:128, :] = jnp.where(lower, wks[...], wk[...])
    wkv[128:192, :] = jnp.where(lower, wv[...], wvs[...])
    wkv[192:256, :] = jnp.where(lower, wvs[...], wv[...])
    gain_q, gain_k = column(gq[...]), column(gk[...])
    for number, piece in enumerate(pieces):
        qn, qt, kn, kt, vt, scale, n1 = outs[7 * number : 7 * number + 7]
        for half in range(2):
            x = blocks[2 * number + half][...].astype(f32)
            r = lax.rsqrt(jnp.mean(x * x, axis=-1, keepdims=True) + EPS)
            n1[half * T : (half + 1) * T, :] = (x * r * g1[...]).astype(bf16)
        raw = dot_t(wqt[...], n1[...])
        raw_kv = dot_t(wkv[...], n1[...])
        first, second = piece * T, HALF + piece * T
        c = jnp.concatenate([cos[:, first : first + T], cos[:, second : second + T]], axis=1)
        s = jnp.concatenate([sin[:, first : first + T], sin[:, second : second + T]], axis=1)

        def path(v, gain, factor, keep, index):
            r = lax.rsqrt(jnp.mean(v * v, axis=0, keepdims=True) + EPS)
            scale[index : index + 1, :] = r
            v = v * r
            keep[...] = v.astype(bf16)
            v = v * gain
            low, high = v[:64], v[64:]
            return (
                ((low * c - high * s) * factor).astype(bf16),
                ((high * c + low * s) * factor).astype(bf16),
            )

        scale[...] = jnp.zeros_like(scale)
        for h in range(LH):
            heads = slice(h * HEAD, (h + 1) * HEAD)
            low, high = path(raw[heads], gain_q, HEAD ** (-0.5), qn.at[heads, :], h)
            qt[h * HEAD : h * HEAD + 64, :] = low
            qt[h * HEAD + 64 : (h + 1) * HEAD, :] = high
        key = raw_kv[:HEAD].astype(bf16)
        low, high = path(key.astype(f32), gain_k, 1.0, kn, LH)
        kt[:64, :] = low
        kt[64:, :] = high
        vt[...] = raw_kv[HEAD:].astype(bf16)


def qkv(pieces, core, blocks, *args):
    outs = [
        sds((LH * HEAD, 2 * T), bf16),
        sds((LH * HEAD, 2 * T), bf16),
        sds((HEAD, 2 * T), bf16),
        sds((HEAD, 2 * T), bf16),
        sds((HEAD, 2 * T), bf16),
        sds((8, 2 * T), f32),
        sds((2 * T, D), bf16),
    ] * len(pieces)
    keep = 0 in pieces
    return call(
        functools.partial(qkv_body, pieces),
        "qkv" + "".join(str(p) for p in pieces),
        outs + ([sds((2 * HEAD, D), bf16)] if keep else []),
        [] if keep else [pltpu.VMEM((2 * HEAD, D), bf16)],
        (core, *blocks, *args),
        smem=(0,),
    )


def build_mask(info, mask):
    for b in range(8):
        keys = jnp.broadcast_to(info[0:1, b * T : (b + 1) * T], (T, T)).T
        for j in range(8):
            cols = slice(j * T, (j + 1) * T)
            inside = (keys >= info[1:2, cols]) & (keys <= info[0:1, cols])
            mask[b * T : (b + 1) * T, cols] = jnp.where(inside, 1.0, 0.0)


def attend_body(*refs):
    q, k, v = refs[0:4], refs[4:8], refs[8:12]
    info, ot0, ot1, linv, qt, kt, kn, vn, mask, vt = refs[12:]
    for dy in range(4):
        for dc in range(2):
            to = slice(dc * HALF + dy * T, dc * HALF + (dy + 1) * T)
            src = slice(dc * T, (dc + 1) * T)
            qt[:, to] = q[dy][:, src]
            kt[:, to] = k[dy][:, src]
            vt[:, to] = v[dy][:, src]
    for b in range(8):
        rows = slice(b * T, (b + 1) * T)
        kn[rows, :] = kt[:, rows].astype(f32).T.astype(bf16)
        vn[rows, :] = vt[:, rows].astype(f32).T.astype(bf16)
    build_mask(info, mask)
    for half, out in ((1, ot1), (0, ot0)):
        cols = slice(half * HALF, (half + 1) * HALF)
        for h in range(LH):
            heads = slice(h * HEAD, (h + 1) * HEAD)
            scores = dot(kn[...], qt[heads, cols])
            weights = jnp.exp2(scores * LOG2E) * mask[:, cols]
            inverse = 1.0 / jnp.sum(weights, axis=0, keepdims=True)
            out[heads, :] = (dot(vt[...], weights.astype(bf16)) * inverse).astype(bf16)
            linv[h : h + 1, cols] = inverse


def attend(q, k, v, info):
    return call(
        attend_body,
        "attend",
        [
            sds((LH * HEAD, HALF), bf16),
            sds((LH * HEAD, HALF), bf16),
            sds((8, ROWS), f32),
            sds((LH * HEAD, ROWS), bf16),
            sds((HEAD, ROWS), bf16),
            sds((ROWS, HEAD), bf16),
            sds((ROWS, HEAD), bf16),
        ],
        [pltpu.VMEM((ROWS, ROWS), f32), pltpu.VMEM((HEAD, ROWS), bf16)],
        (*q, *k, *v, info),
    )


def flip(source, dest, row, col):
    height, width = source.shape
    for a in range(height // 128):
        for b in range(width // 128):
            block = source[a * 128 : (a + 1) * 128, b * 128 : (b + 1) * 128]
            rows = slice(row + b * 128, row + (b + 1) * 128)
            dest[rows, col + a * 128 : col + (a + 1) * 128] = block.astype(f32).T.astype(bf16)


def outproj_body(ot0, otr, wa, wb, b0, b1, b2, b3, heads):
    @pl.when(pl.program_id(0) == 0)
    def _():
        flip(ot0, heads, 0, 0)
        flip(otr, heads, 0, 512)

    total = dot(heads[:, :512], wa[...]) + dot(heads[:, 512:], wb[...])
    for dy, out in enumerate((b0, b1, b2, b3)):
        out[...] = total[dy * T : (dy + 1) * T, :].astype(bf16)


def outproj(ot0, otr, wa, wb):
    return grid_call(
        outproj_body,
        "out_projection",
        (4,),
        [whole((512, HALF)), whole((512, HALF)), cols_of((512, 512)), cols_of((512, 512))],
        [cols_of((T, 512))] * 4,
        [sds((T, D), bf16)] * 4,
        [pltpu.VMEM((HALF, 1024), bf16)],
        (ot0, otr, wa, wb),
    )


def transpose_body(n0, n1, n2, n3, out):
    for dy, piece in enumerate((n0, n1, n2, n3)):
        for dc in range(2):
            flip(piece.at[dc * T : (dc + 1) * T, :], out, 0, dc * HALF + dy * T)


def transpose_rows(pieces):
    return call(transpose_body, "transpose_rows", [sds((D, ROWS), bf16)], [], tuple(pieces))[0]


def route_body(rt, ids, ids_t):
    lane = lax.broadcasted_iota(jnp.int32, (T, E), 1)
    row = lax.broadcasted_iota(jnp.int32, (T, E), 0)
    wide = jnp.concatenate([rt[...].astype(f32), jnp.zeros((124, T), f32)], axis=0).T
    hot = [jnp.where(lane.astype(f32) == wide[:, k : k + 1], 1.0, 0.0) for k in range(4)]
    earlier = jnp.where(lane < row, 1.0, 0.0).astype(bf16)
    before = dot(earlier, (hot[0] + hot[1] + hot[2] + hot[3]).astype(bf16))
    table = wide
    for k in range(4):
        slot = jnp.sum(before * hot[k], axis=1, keepdims=True)
        table = jnp.where(lane == 4 + k, slot, table)
        table = jnp.where(lane == 8 + k, slot * E + wide[:, k : k + 1], table)
    ids[...] = table.astype(jnp.int32)
    ids_t[...] = table.T[0:16, :].astype(jnp.int32)


def route_tables(routes_t):
    return call(
        route_body,
        "route_tables",
        [sds((T, 128), jnp.int32), sds((16, T), jnp.int32)],
        [],
        (routes_t,),
    )


def router_body(b0, b1, b2, b3, x0, g2, wr, ids, at, hidden, n2, probs, gates, wire, rows):
    v = x0[...].astype(f32) + (
        (b0[...].astype(f32) + b1[...].astype(f32))
        + (b2[...].astype(f32) + b3[...].astype(f32))
    )
    hidden[...] = v
    r = lax.rsqrt(jnp.mean(v * v, axis=-1, keepdims=True) + EPS)
    n2[...] = (v * r * g2[...]).astype(bf16)
    logits = dot(n2[...], wr[...])
    pack_rows(n2, at, wire, rows)
    expo = jnp.exp(logits - jnp.max(logits, axis=-1, keepdims=True))
    p = expo / jnp.sum(expo, axis=-1, keepdims=True)
    probs[...] = p
    lane = lax.broadcasted_iota(jnp.int32, (T, E), 1)
    chosen = [
        jnp.sum(jnp.where(lane == ids[:, k : k + 1], p, 0.0), axis=-1, keepdims=True)
        for k in range(4)
    ]
    total = chosen[0] + chosen[1] + chosen[2] + chosen[3]
    packed = jnp.where(lane == 4, total, 0.0)
    for k in range(4):
        packed = jnp.where(lane == k, chosen[k] / total, packed)
    gates[...] = packed
    across = packed.T
    expert = lax.broadcasted_iota(jnp.int32, (E, T), 0)
    columns = []
    for s in range(CAP):
        mine = jnp.zeros((E, T), f32)
        for k in range(4):
            mine = jnp.where(expert + s * E == at[k : k + 1, :], across[k : k + 1, :], mine)
        columns.append(jnp.sum(mine, axis=1, keepdims=True))
    put_numbers(columns, wire)


def router(b, x0, g2, wr, ids, assign_t):
    return call(
        router_body,
        "router",
        [
            sds((T, D), f32),
            sds((T, D), bf16),
            sds((T, E), f32),
            sds((T, E), f32),
            sds((E, WIRE, 128), bf16),
        ],
        [pltpu.VMEM((SLOTS, D), bf16)],
        (*b, x0, g2, wr, ids, assign_t),
    )


def expert_grad_body(wire, wd, gr, ga):
    split_rows(wire, gr)

    def body(i, carry):
        cols = pl.ds(pl.multiple_of(i * 256, 256), 256)
        ga[:, cols] = dot_t(gr[...], wd[cols, :])
        return carry

    lax.fori_loop(0, F // 256, body, 0)


def expert_grad(wire, wd):
    return call(
        expert_grad_body,
        "expert_grad_rows",
        [sds((SLOTS, D), bf16), sds((SLOTS, F), f32)],
        [],
        (wire, wd),
    )


def expert_main_body(wire, wg, wu, ga, back, xs, act, acts, dg, du, xr, sc):
    split_rows(wire, xr)
    gates = get_numbers(wire)
    sc[...] = jnp.zeros_like(sc)

    def forward(i, carry):
        cols = pl.ds(pl.multiple_of(i * 384, 384), 384)
        gate = dot(xr[...], wg[:, cols])
        up = dot(xr[...], wu[:, cols])
        grad = ga[:, cols]
        s = 1.0 / (1.0 + jnp.exp(-gate))
        silu = gate * s
        a = silu * up
        act[:, cols] = a.astype(bf16)
        dg[:, cols] = (grad * up * s * (1.0 + gate * (1.0 - s))).astype(bf16)
        du[:, cols] = (grad * silu).astype(bf16)
        sc[...] += jnp.sum(a * grad, axis=1, keepdims=True)
        return carry

    lax.fori_loop(0, F // 384, forward, 0)
    for s in range(CAP):
        part = slice(s * E, (s + 1) * E)
        gate = gates[:, s : s + 1]
        xs[part, :] = (xr[part, :].astype(f32) * gate).astype(bf16)
        acts[part, :] = (act[part, :].astype(f32) * gate).astype(bf16)
    for j in range(4):
        part = slice(j * 512, (j + 1) * 512)
        xr[:, part] = (dot_t(dg[...], wg[part, :]) + dot_t(du[...], wu[part, :])).astype(bf16)
    join_rows(xr, back)
    put_numbers([sc[s * E : (s + 1) * E, :] for s in range(CAP)], back)


def expert_main(wire, wg, wu, ga):
    return call(
        expert_main_body,
        "expert_main",
        [
            sds((E, WIRE, 128), bf16),
            sds((SLOTS, D), bf16),
            sds((SLOTS, F), bf16),
            sds((SLOTS, F), bf16),
            sds((SLOTS, F), bf16),
            sds((SLOTS, F), bf16),
        ],
        [pltpu.VMEM((SLOTS, D), bf16), pltpu.VMEM((SLOTS, 1), f32)],
        (wire, wg, wu, ga),
    )


def expert_out_body(act, wd, wire, rows):
    for j in range(8):
        cols = slice(j * 256, (j + 1) * 256)
        rows[:, cols] = dot(act[...], wd[:, cols]).astype(bf16)
    join_rows(rows, wire)


def expert_out(act, wd):
    return call(
        expert_out_body,
        "expert_out",
        [sds((E, CAP * SEG, 128), bf16)],
        [pltpu.VMEM((SLOTS, D), bf16)],
        (act, wd),
    )[0]


def combine_body(
    where, experts, slots, gate_list, wire, hidden, n2, probs, gates, ids, og, g2, wr,
    ghid, gatt, router_own, router_sib, gg2, sums, gn2, parts,
):
    sum_rows(wire, experts, slots, gate_list, sums)
    scores = get_numbers(wire)
    lane = lax.broadcasted_iota(jnp.int32, (T, E), 1)
    grads = []
    for k in range(4):
        hot = jnp.where(lane == ids[:, k : k + 1], 1.0, 0.0)
        rows = lax.dot_general(
            hot, scores, (((1,), (0,)), ((), ())),
            precision=lax.Precision.HIGHEST, preferred_element_type=f32,
        )
        picked = jnp.where(lane == ids[:, 4 + k : 5 + k], rows, 0.0)
        grads.append(jnp.sum(picked, axis=-1, keepdims=True))
    inner = sum(grads[k] * gates[:, k : k + 1] for k in range(4))
    inverse = 1.0 / gates[:, 4:5]
    grad_probs = jnp.zeros((T, E), f32)
    for k in range(4):
        grad_probs = jnp.where(
            lane == ids[:, k : k + 1], (grads[k] - inner) * inverse, grad_probs
        )
    p = probs[...]
    gl = (p * (grad_probs - jnp.sum(p * grad_probs, axis=-1, keepdims=True))).astype(bf16)
    for h in range(2):
        tokens = slice(h * 64, (h + 1) * 64)
        gn2[tokens, :] = sums[h * 1024 : (h + 1) * 1024, :].reshape(64, D)
    gn2[...] += dot_t(gl, wr[...])
    c = gn2[...]
    v = hidden[...]
    r = lax.rsqrt(jnp.mean(v * v, axis=-1, keepdims=True) + EPS)
    u = c * g2[...]
    m = jnp.mean(u * v, axis=-1, keepdims=True)
    total = og[...].astype(f32) + r * u - v * (r * r * r * m)
    ghid[...] = total
    gatt[...] = total.astype(bf16)
    gg2[...] = jnp.sum(c * (v * r), axis=0, keepdims=True)
    for j in range(SEG):
        cols = slice(j * 128, (j + 1) * 128)
        owner = j // 2
        dy = lax.rem(owner // 2 + 4 - where[3], 4)
        dc = lax.rem(owner % 2 + where[2], 2)
        half = slice((j % 2) * 128, (j % 2 + 1) * 128)
        parts[dc * 4 + dy, half, :] = dot(n2[:, cols].astype(f32).T.astype(bf16), gl).astype(bf16)
    router_own[...] = parts[0:4]
    router_sib[...] = parts[4:8]


def combine(*args):
    return call(
        combine_body,
        "combine_grads",
        [
            sds((T, D), f32),
            sds((T, D), bf16),
            sds((4, 256, E), bf16),
            sds((4, 256, E), bf16),
            sds((1, D), f32),
        ],
        [
            pltpu.VMEM((T * SEG, 128), f32),
            pltpu.VMEM((T, D), f32),
            pltpu.VMEM((8, 256, E), bf16),
        ],
        args,
        smem=(0, 1, 2, 3),
    )


def result_body(experts, slots, gate_list, wire, hidden, out, sums):
    sum_rows(wire, experts, slots, gate_list, sums)
    for h in range(2):
        tokens = slice(h * 64, (h + 1) * 64)
        mixture = sums[h * 1024 : (h + 1) * 1024, :].reshape(64, D)
        out[tokens, :] = (hidden[tokens, :] + mixture).astype(bf16)


def result_rows(*args):
    return call(
        result_body,
        "result",
        [sds((T, D), bf16)],
        [pltpu.VMEM((T * SEG, 128), f32)],
        args,
        smem=(0, 1, 2),
    )[0]


def head_grad_body(*refs):
    blocks, (wo, dt, rows_all) = refs[:6], refs[6:]
    for b in range(6):
        rows_all[b * T : (b + 1) * T, :] = blocks[b][...]
    for b in range(3):
        rows = slice(b * 256, (b + 1) * 256)
        dt[:, rows] = dot_t(wo[...], rows_all[rows, :]).astype(bf16)


def head_grad(blocks, wo):
    return call(
        head_grad_body,
        "head_grad",
        [sds((LH * HEAD, 6 * T), bf16)],
        [pltpu.VMEM((6 * T, D), bf16)],
        (*blocks, wo),
    )[0]


def pre_body(*refs):
    blocks, (ot0, ot1, wo, gw, dt, rows_all, total) = refs[:8], refs[8:]
    step = pl.program_id(0)
    for b in range(8):
        rows_all[b * T : (b + 1) * T, :] = blocks[b][...]
    gw[...] = (dot(ot0[...], rows_all[:HALF, :]) + dot(ot1[...], rows_all[HALF:, :])).astype(bf16)
    last = jnp.concatenate([blocks[2][...], blocks[6][...]], axis=0)
    part = dot_t(wo[...], last)

    @pl.when(step == 0)
    def _():
        total[...] = part

    @pl.when(step > 0)
    def _():
        total[...] += part

    @pl.when(step == 3)
    def _():
        dt[...] = total[...].astype(bf16)


def pre(blocks, ot0, ot1, wo):
    return grid_call(
        pre_body,
        "out_projection_grad",
        (4,),
        [cols_of((T, 512))] * 8 + [whole((512, HALF))] * 2 + [cols_of((512, 512))],
        [cols_of((512, 512)), whole((512, 2 * T))],
        [sds((LH * HEAD, D), bf16), sds((LH * HEAD, 2 * T), bf16)],
        [pltpu.VMEM((ROWS, 512), bf16), pltpu.VMEM((512, 2 * T), f32)],
        (*blocks, ot0, ot1, wo),
    )


def bwd_body(*refs):
    qh, kh, scales = refs[0:4], refs[4:8], refs[8:12]
    (qt, kt, kn, vn, dta, dtb, ot0, ot1, linv, info, cos, sin, gq, gk) = refs[12:26]
    dq0, dq1, dkv, ggq, ggk, mask, wb, sb, dqt, dk, dv, raw, dt, scale = refs[26:]
    for dc in range(2):
        for place, dy in enumerate((0, 1, 3)):
            to = slice(dc * HALF + dy * T, dc * HALF + (dy + 1) * T)
            dt[:, to] = dta[:, (place * 2 + dc) * T : (place * 2 + dc + 1) * T]
        dt[:, dc * HALF + 2 * T : dc * HALF + 3 * T] = dtb[:, dc * T : (dc + 1) * T]
        for dy in range(4):
            to = slice(dc * HALF + dy * T, dc * HALF + (dy + 1) * T)
            scale[:, to] = scales[dy][:, dc * T : (dc + 1) * T]
    build_mask(info, mask)
    dk[...] = jnp.zeros_like(dk)
    dv[...] = jnp.zeros_like(dv)
    for half, out in ((0, ot0), (1, ot1)):
        cols = slice(half * HALF, (half + 1) * HALF)
        for h in range(LH):
            heads = slice(h * HEAD, (h + 1) * HEAD)
            part = slice(h * HALF, (h + 1) * HALF)
            scores = dot(kn[...], qt[heads, cols])
            weights = jnp.exp2(scores * LOG2E) * (mask[:, cols] * linv[h : h + 1, cols])
            grad = dt[heads, cols]
            delta = jnp.sum(
                grad.astype(f32) * out[heads, :].astype(f32), axis=0, keepdims=True
            )
            wb[:, part] = weights.astype(bf16)
            sb[:, part] = (weights * (dot(vn[...], grad) - delta)).astype(bf16)
            dqt[heads, cols] = dot(kt[...], sb[:, part])
        grads = jnp.concatenate([dt[h * HEAD : (h + 1) * HEAD, cols] for h in range(LH)], axis=1)
        queries = jnp.concatenate([qt[h * HEAD : (h + 1) * HEAD, cols] for h in range(LH)], axis=1)
        dv[...] += dot_t(wb[...], grads)
        dk[...] += dot_t(sb[...], queries)

    def unrope(v):
        low, high = v[:64], v[64:]
        c, s = cos[...], sin[...]
        return jnp.concatenate([low * c + high * s, high * c - low * s], axis=0)

    def norm_back(n, r, grad, gain):
        gain_grad = jnp.sum(grad * n, axis=1, keepdims=True)
        u = grad * gain
        return r * (u - n * jnp.mean(u * n, axis=0, keepdims=True)), gain_grad

    gain_q, gain_k = column(gq[...]), column(gk[...])
    total = jnp.zeros((HEAD, 1), f32)
    for h in range(LH):
        heads = slice(h * HEAD, (h + 1) * HEAD)
        for dy in range(4):
            for dc in range(2):
                to = slice(dc * HALF + dy * T, dc * HALF + (dy + 1) * T)
                raw[:, to] = qh[dy][heads, dc * T : (dc + 1) * T].astype(f32)
        grad, part = norm_back(raw[...], scale[h : h + 1, :], unrope(dqt[heads, :] * (HEAD ** (-0.5))), gain_q)
        total = total + part
        dq0[heads, :] = grad[:, :HALF].astype(bf16)
        dq1[heads, :] = grad[:, HALF:].astype(bf16)
    ggq[...] = jnp.broadcast_to(total, (HEAD, 128)).T[0:8, :]
    for dy in range(4):
        for dc in range(2):
            to = slice(dc * HALF + dy * T, dc * HALF + (dy + 1) * T)
            raw[:, to] = kh[dy][:, dc * T : (dc + 1) * T].astype(f32)
    grad, part = norm_back(raw[...], scale[LH : LH + 1, :], unrope(dk[...].T), gain_k)
    ggk[...] = jnp.broadcast_to(part, (HEAD, 128)).T[0:8, :]
    dkv[:HEAD, :] = grad.astype(bf16)
    dkv[HEAD:, :] = dv[...].T.astype(bf16)


def bwd(qh, kh, scales, *rest):
    return call(
        bwd_body,
        "attend_grad",
        [
            sds((LH * HEAD, HALF), bf16),
            sds((LH * HEAD, HALF), bf16),
            sds((2 * HEAD, ROWS), bf16),
            sds((8, HEAD), f32),
            sds((8, HEAD), f32),
        ],
        [
            pltpu.VMEM((ROWS, ROWS), f32),
            pltpu.VMEM((ROWS, LH * HALF), bf16),
            pltpu.VMEM((ROWS, LH * HALF), bf16),
            pltpu.VMEM((LH * HEAD, ROWS), f32),
            pltpu.VMEM((ROWS, HEAD), f32),
            pltpu.VMEM((ROWS, HEAD), f32),
            pltpu.VMEM((HEAD, ROWS), f32),
            pltpu.VMEM((LH * HEAD, ROWS), bf16),
            pltpu.VMEM((8, ROWS), f32),
        ],
        (*qh, *kh, *scales, *rest),
    )


def qkv_grad_body(where, n1t, dq0, dq1, own, sib, w0, w1, w2, w3, tot, dt):
    step = pl.program_id(0)

    @pl.when(step == 0)
    def _():
        tot[:, :HALF] = (own[:, :HALF].astype(f32) + sib[:, HALF:].astype(f32)).astype(bf16)
        tot[:, HALF:] = (own[:, HALF:].astype(f32) + sib[:, :HALF].astype(f32)).astype(bf16)
        dt[:512, :HALF] = dq0[...]
        dt[:512, HALF:] = dq1[...]
        upper = where[2] == 1
        dt[512:576, :] = jnp.where(upper, tot[64:128, :], tot[:64, :])
        dt[576:, :] = jnp.where(upper, tot[192:, :], tot[128:192, :])

    grad = dot_t(n1t[...], dt[...]).astype(bf16)
    for dz, out in enumerate((w0, w1, w2, w3)):

        @pl.when(step == dz)
        def _():
            for col in range(4):
                dx = lax.rem(col + 4 - where[1], 4)
                out[dx] = grad[col * 128 : (col + 1) * 128, :]


def qkv_grad(where, n1t, dq0, dq1, own, sib):
    return grid_call(
        qkv_grad_body,
        "qkv_weight_grad",
        (4,),
        [
            pl.BlockSpec((512, ROWS), lambda i, w: (lax.rem(i + w[0], 4), 0)),
            whole((512, HALF)),
            whole((512, HALF)),
            whole((2 * HEAD, ROWS)),
            whole((2 * HEAD, ROWS)),
        ],
        [whole((4, 128, 640))] * 4 + [whole((2 * HEAD, ROWS))],
        [sds((4, 128, 640), bf16)] * 4 + [sds((2 * HEAD, ROWS), bf16)],
        [pltpu.VMEM((640, ROWS), bf16)],
        (where, n1t, dq0, dq1, own, sib),
        scalars=1,
    )


def add_body(a, b, c, d, *outs):
    for i, out in enumerate(outs):
        out[...] = (
            (a[i].astype(f32) + b[i].astype(f32)) + (c[i].astype(f32) + d[i].astype(f32))
        ).astype(bf16)


def add_parts(parts):
    shape = parts[0].shape[1:]
    return call(add_body, "add_parts", [sds(shape, bf16)] * 4, [], tuple(parts))


def split_two(v):
    first = v.astype(bf16)
    return first, (v - first.astype(f32)).astype(bf16)


def normed_grad_body(
    wa, wb, wkv, dq0, dqr, tot, n0, n1, n2, n3, gg2, ggq, ggk, ra, rb, b0, b1, b2, b3, grads
):
    step = pl.program_id(0)

    @pl.when(step == 0)
    def _():
        flip(dq0, grads, 0, 0)
        flip(dqr, grads, 0, 512)
        flip(tot, grads, 0, 1024)

    total = (
        dot(grads[:, :512], wa[...])
        + dot(grads[:, 512:1024], wb[...])
        + dot(grads[:, 1024:], wkv[...])
    )
    gain = jnp.zeros((1, 512), f32)
    outs = (b0, b1, b2, b3)
    for dy, (out, rows) in enumerate(zip(outs, (n0, n1, n2, n3))):
        part = total[dy * T : (dy + 1) * T, :]
        out[:T, :] = part.astype(bf16)
        gain = gain + jnp.sum(part * rows[...].astype(f32), axis=0, keepdims=True)
    heads = jnp.concatenate([ggq[0:1, :], ggk[0:1, :], jnp.zeros((1, 256), f32)], axis=1)
    numbers = [*split_two(gain), *split_two(gg2[...]), *split_two(heads)]
    extra = jnp.concatenate([n.astype(f32) for n in numbers] + [jnp.zeros((10, 512), f32)], axis=0)
    for dy, out in enumerate(outs):
        out[T : T + 16, :] = extra.astype(bf16)
        for q in range(4):
            rows = pl.ds(pl.multiple_of(step * 64 + q * 16, 16), 16)
            both = ra[dy, rows, :].astype(f32) + rb[dy, rows, :].astype(f32)
            out[T + 16 :, q * 128 : (q + 1) * 128] = both.astype(bf16)


def normed_grad(wa, wb, wkv, dq0, dqr, tot, n1, gg2, ggq, ggk, ra, rb):
    return grid_call(
        normed_grad_body,
        "normed_grad",
        (4,),
        [
            cols_of((512, 512)),
            cols_of((512, 512)),
            cols_of((256, 512)),
            whole((512, HALF)),
            whole((512, HALF)),
            whole((2 * HEAD, HALF)),
        ]
        + [cols_of((T, 512))] * 4
        + [cols_of((1, 512)), whole((8, HEAD)), whole((8, HEAD))]
        + [whole((4, 256, E))] * 2,
        [cols_of((T + 32, 512))] * 4,
        [sds((T + 32, D), bf16)] * 4,
        [pltpu.VMEM((HALF, 1280), bf16)],
        (wa, wb, wkv, dq0, dqr, tot, *n1, gg2, ggq, ggk, ra, rb),
    )


def add_last_body(a, b, c, d, out):
    out[...] = (
        (a[...].astype(f32) + b[...].astype(f32)) + (c[...].astype(f32) + d[...].astype(f32))
    ).astype(bf16)


def add_last(parts):
    return call(add_last_body, "add_last", [sds(parts[0].shape, bf16)], [], tuple(parts))


def stack_body(a, b, c, d, out):
    for i, part in enumerate((a, b, c, d)):
        out[i] = part[...]


def stack(parts):
    shape = (4, *parts[0].shape)
    return call(stack_body, "stack_parts", [sds(shape, bf16)], [], tuple(parts))[0]


def place_body(where, c0, c1, c2, c3, gq, gkt, gvt):
    for dz, chunks in enumerate((c0, c1, c2, c3)):
        for dx in range(4):
            chunk = lax.rem(where[0] + dz, 4) * 4 + lax.rem(where[1] + dx, 4)
            rows = pl.ds(pl.multiple_of(chunk * 128, 128), 128)
            gq[rows, :] = chunks[dx, :, :512].astype(f32)
            both = chunks[dx, :, 512:].astype(f32).T
            gkt[:, rows] = both[:64]
            gvt[:, rows] = both[64:]


def place(where, chunks):
    return call(
        place_body,
        "place_weight_grads",
        [sds((D, 512), f32), sds((64, D), f32), sds((64, D), f32)],
        [],
        (where, *chunks),
        smem=(0,),
    )


def final_body(b0, b1, b2, b3, x0, ghid, g1, out, small):
    whole_sum = (b0[...].astype(f32) + b1[...].astype(f32)) + (
        b2[...].astype(f32) + b3[...].astype(f32)
    )
    c = whole_sum[:T]
    v = x0[...].astype(f32)
    r = lax.rsqrt(jnp.mean(v * v, axis=-1, keepdims=True) + EPS)
    u = c * g1[...]
    m = jnp.mean(u * v, axis=-1, keepdims=True)
    out[...] = ghid[...] + r * u - v * (r * r * r * m)
    extra = whole_sum[T : T + 16]
    numbers = [
        *split_two((extra[0:1] + extra[1:2]) / g1[...]),
        *split_two(extra[2:3] + extra[3:4]),
        *split_two(extra[4:5] + extra[5:6]),
    ]
    rows = jnp.concatenate(
        [whole_sum[T + 16 :]] + [n.astype(f32) for n in numbers] + [jnp.zeros((2, D), f32)],
        axis=0,
    ).astype(bf16)
    for e in range(16):
        small[e] = rows[:, e * 128 : (e + 1) * 128]


def final(b, x0, ghid, g1):
    return call(
        final_body,
        "input_grad",
        [sds((T, D), f32), sds((16, 24, 128), bf16)],
        [],
        (*b, x0, ghid, g1),
    )


def fold_body(parts, out):
    total = parts[0].astype(f32)
    for e in range(1, 16):
        total = total + parts[e].astype(f32)
    numbers = []
    for k in range(3):
        row = SEG + 2 * k
        numbers += split_two(total[row : row + 1] + total[row + 1 : row + 2])
    rows = jnp.concatenate(
        [total[:SEG]] + [n.astype(f32) for n in numbers] + [jnp.zeros((2, 128), f32)], axis=0
    ).astype(bf16)

    def body(i, carry):
        out[i] = rows
        return carry

    lax.fori_loop(0, E, body, 0)


def fold(parts):
    return call(fold_body, "fold_small", [sds((E, 24, 128), bf16)], [], (parts,))[0]


def sibling(x):
    return lax.ppermute(x, "shard", [(i, i ^ 1) for i in range(8)])


def from_chip(x, dy):
    return lax.ppermute(x, "shard", [(i, (i - 2 * dy) % 8) for i in range(8)])


def to_chip(x, dy):
    return lax.ppermute(x, "shard", [(i, (i + 2 * dy) % 8) for i in range(8)])


def exchange(x):
    return lax.all_to_all(x, ALL, split_axis=0, concat_axis=0, tiled=True)


def spread(x):
    return [to_chip(x[d], d) for d in (1, 3, 2)]


def on_expert(x, dz, dx):
    pairs = [
        (z * 4 + c, ((z + dz) % 4) * 4 + (c + dx) % 4) for z in range(4) for c in range(4)
    ]
    return lax.ppermute(x, "expert", pairs)


def move(x, axis, distance):
    return on_expert(x, distance, 0) if axis == 0 else on_expert(x, 0, distance)


def collect(parts, axis):
    return [parts[0]] + [move(parts[d], axis, d) for d in (1, 3, 2)]


def share(x, axis):
    return [x] + [move(x, axis, (4 - d) % 4) for d in (1, 2, 3)]


def after(value, *others):
    return lax.optimization_barrier((value, *others))[0]


def on_device(
    block_input, out_grad, norm1_gain, w_query, w_key, w_value, query_gain, key_gain, w_out,
    norm2_gain, w_router, w_gate, w_up, w_down, seq_lengths, token_places, expert_routes,
):
    shard, owner = lax.axis_index("shard"), lax.axis_index("expert")
    chip, core = shard // 2, shard % 2
    where = jnp.stack([owner // 4, owner % 4, core, chip]).astype(jnp.int32)
    core_id = core.reshape(1)
    g1 = norm1_gain.astype(f32).reshape(1, D)
    g2 = norm2_gain.astype(f32).reshape(1, D)
    gq = query_gain.astype(f32).reshape(1, HEAD)
    gk = key_gain.astype(f32).reshape(1, HEAD)

    x_own = [block_input] + [from_chip(block_input, dy) for dy in (1, 2, 3)]
    x_sib = [sibling(block_input)]

    chips = (chip + jnp.arange(4)) % 4
    order = jnp.concatenate([chips * 2 + core, chips * 2 + 1 - core])
    places = token_places[0].reshape(8, T)[order].reshape(ROWS)
    lengths = seq_lengths[0]
    ends = jnp.cumsum(lengths)
    starts = jnp.sum(
        jnp.where(places[:, None] >= ends[None, :], lengths[None, :], 0), axis=1
    )
    positions = (places - starts).astype(f32)
    info = jnp.concatenate(
        [places[None].astype(f32), starts[None].astype(f32), jnp.zeros((6, ROWS), f32)], axis=0
    )
    inverse_freq = ROPE_BASE ** (-jnp.arange(0, HEAD, 2).astype(f32) / HEAD)
    angles = inverse_freq[:, None] * positions[None, :]
    cos, sin = jnp.cos(angles), jnp.sin(angles)

    ids, ids_t = route_tables(expert_routes.T)
    assign_t = ids_t[8:12]
    expert_list = ids[:, 0:4].reshape(-1)
    slot_list = ids[:, 4:8].reshape(-1)

    wk_t, wv_t = w_key.T, w_value.T
    wk_s, wv_s = sibling(wk_t), sibling(wv_t)
    wq_t = w_query.T
    wo_s = sibling(w_out)
    wq_ts = sibling(wq_t)

    weights = (g1, wq_t, wk_t, wk_s, wv_t, wv_s, gq, gk, cos, sin)
    zero = qkv((0,), core_id, (x_own[0], x_sib[0]), *weights)
    og_wire = pack(out_grad, assign_t)
    x_own[1], x_own[2], x_own[3], q_first, og_wire = lax.optimization_barrier(
        (x_own[1], x_own[2], x_own[3], zero[1], og_wire)
    )
    x_sib += [sibling(x_own[dy]) for dy in (1, 2, 3)]
    blocks = [side[dy] for dy in (1, 2, 3) for side in (x_own, x_sib)]
    others = qkv((1, 2, 3), core_id, blocks, *weights)
    wkv = zero[7]
    pieces = [zero[:7], others[:7], others[7:14], others[14:21]]
    qh, q, kh, k, v, scales, n1 = zip(*pieces)
    q = (q_first,) + q[1:]
    got_grads = exchange(og_wire)
    ot0, ot1, linv, qt, kt, kn, vn = attend(q, k, v, info)
    blocks = outproj(ot0, sibling(ot1), w_out, wo_s)
    blocks = [blocks[0]] + spread(blocks)
    hidden, n2, probs, gates, wire = router(blocks, block_input, g2, w_router, ids, assign_t)
    got_rows = exchange(wire)

    n1_t = transpose_rows(after(n1, wire))
    gate_list = gates[:, :4].reshape(-1)
    grad_rows, grad_act = expert_grad(after(got_grads, wire), w_down[0])
    got_rows, n1_t, grad_act, gate_list, wq_ts = lax.optimization_barrier(
        (got_rows, n1_t, grad_act, gate_list, wq_ts)
    )

    back, rows, act, scaled_act, dg, du = expert_main(got_rows, w_gate[0], w_up[0], grad_act)
    back_wire = exchange(back)

    rows, act, scaled_act, dg, du = after((rows, act, scaled_act, dg, du), back)
    out_wire = expert_out(act, w_down[0])

    def weight_grad(a, b):
        return lax.dot_general(a, b, (((0,), (0,)), ((), ())), preferred_element_type=f32)

    grad_wgate = weight_grad(rows, dg)
    grad_wup = weight_grad(rows, du)
    grad_wdown = weight_grad(scaled_act, grad_rows)
    back_wire, out_wire, grad_wgate, grad_wup, grad_wdown = lax.optimization_barrier(
        (back_wire, out_wire, grad_wgate, grad_wup, grad_wdown)
    )

    ghid, gatt, router_own, router_sib, gg2 = combine(
        where, expert_list, slot_list, gate_list, back_wire, hidden, n2, probs, gates, ids,
        out_grad, g2, w_router,
    )
    g_own = [gatt] + [from_chip(gatt, dy) for dy in (1, 2, 3)]
    g_sib = [sibling(block) for block in g_own]
    dt_near = head_grad(
        [g_own[0], g_sib[0], g_own[1], g_sib[1], g_own[3], g_sib[3]], w_out
    )
    g_far, dt_near = lax.optimization_barrier(((g_own[2], g_sib[2]), dt_near))
    g_own[2], g_sib[2] = g_far

    returned = exchange(after(out_wire, g_own[2]))
    gwout, dt_far = pre(g_own + g_sib, ot0, ot1, w_out)
    grad_wout = lax.psum(gwout, "expert")

    dq0, dq1, dkv, ggq, ggk = bwd(
        qh, kh, scales, qt, kt, kn, vn, dt_near, dt_far, ot0, ot1, linv, info, cos, sin, gq, gk
    )
    router_sib = after(router_sib, dkv)
    dq_sib, dkv_sib = sibling(dq1), sibling(dkv)
    *parts, dkv_total = qkv_grad(where, n1_t, dq0, dq1, dkv, dkv_sib)
    returned, dq0 = lax.optimization_barrier((returned, dq0))
    result = result_rows(expert_list, slot_list, gate_list, returned, hidden)
    router_rec = sibling(router_sib)
    blocks = normed_grad(
        wq_t, wq_ts, wkv, dq0, dq_sib, dkv_total, n1, gg2, ggq, ggk, router_own, router_rec
    )
    blocks = [blocks[0]] + spread(blocks)

    parts = collect(add_parts(collect(parts, 0)), 1)
    parts, blocks = lax.optimization_barrier((parts, blocks))
    chunks = share(add_last(parts)[0], 1)
    grad_input, small = final(blocks, block_input, ghid, g1)
    small = lax.all_to_all(small, "expert", split_axis=0, concat_axis=0, tiled=True)
    chunks, small, grad_wout = lax.optimization_barrier((stack(chunks), small, grad_wout))
    chunks = share(chunks, 0)
    small = exchange(fold(small))
    grad_wout = grad_wout.astype(f32)
    chunks, small, grad_input, grad_wout, result = lax.optimization_barrier(
        (chunks, small, grad_input, grad_wout, result)
    )
    grad_wq, grad_wk, grad_wv = place(where, chunks)
    small = small.reshape(16, 8, 24, 128).astype(f32)
    grad_router = small[:, :, :SEG].transpose(1, 0, 2, 3).reshape(D, E)
    gains = small[:, 0, SEG:] + small[:, 1, SEG:]
    gains = [(gains[:, 2 * k] + gains[:, 2 * k + 1]).reshape(D) for k in range(3)]
    return (
        result,
        grad_input,
        gains[0],
        grad_wq,
        grad_wk.T,
        grad_wv.T,
        gains[2][:HEAD],
        gains[2][HEAD : 2 * HEAD],
        grad_wout,
        gains[1],
        grad_router,
        grad_wgate[None],
        grad_wup[None],
        grad_wdown[None],
    )


def solution(mesh):
    rows = P(("expert", "shard"), None)
    experts = P(("expert", "shard"), None, None)
    columns = P(None, "shard")
    return jax.shard_map(
        on_device,
        mesh=mesh,
        in_specs=(
            rows, rows, P(), columns, columns, columns, P(), P(), P("shard", None), P(), P(),
            experts, experts, experts, P("expert", None), P("expert", None), rows,
        ),
        out_specs=(
            rows, rows, P(), columns, columns, columns, P(), P(), P("shard", None), P(), P(),
            experts, experts, experts,
        ),
        check_vma=False,
    )
```

```python
import functools

import jax
import jax.numpy as jnp
from jax import lax
from jax.experimental import pallas as pl
from jax.experimental.pallas import tpu as pltpu
from jax.sharding import PartitionSpec as P

EPS = 1e-06
ROPE_BASE = 1000000.0
LOG2E = 1.4426950408889634
T = 128
D = 2048
HEAD = 128
LH = 4
E = 128
CAP = 5
SLOTS = E * CAP
SEG = D // 128
WIRE = CAP * SEG + 8
ROWS = 1024
HALF = 512
F = 768
bf16 = jnp.bfloat16
f32 = jnp.float32
ALL = ("expert", "shard")
COSTS = {
    "attend": 11,
    "out_projection": 5,
    "router": 6,
    "transpose_rows": 6,
    "expert_grad_rows": 8,
    "expert_main": 18,
    "expert_out": 7,
    "combine_grads": 7,
    "head_grad": 4,
    "out_projection_grad": 7,
}


def cost(micros):
    return pl.CostEstimate(
        flops=1, bytes_accessed=int(micros * 0.6e6) + 1, transcendentals=0
    )


def dot(a, b):
    return jnp.dot(a, b, preferred_element_type=f32)


def dot_t(a, b):
    return lax.dot_general(a, b, (((1,), (1,)), ((), ())), preferred_element_type=f32)


def call(kernel, name, outs, scratch, args, smem=()):
    in_specs = [
        pl.BlockSpec(memory_space=pltpu.SMEM if i in smem else pltpu.VMEM)
        for i in range(len(args))
    ]
    return pl.pallas_call(
        kernel,
        out_shape=outs,
        in_specs=in_specs,
        out_specs=[pl.BlockSpec(memory_space=pltpu.VMEM) for _ in outs],
        scratch_shapes=scratch,
        compiler_params=pltpu.CompilerParams(vmem_limit_bytes=63 * 1024 * 1024),
        cost_estimate=cost(COSTS.get(name, 0)),
        name=name,
    )(*args)


def grid_call(kernel, name, grid, in_specs, out_specs, outs, scratch, args, scalars=0):
    return pl.pallas_call(
        kernel,
        out_shape=outs,
        grid_spec=pltpu.PrefetchScalarGridSpec(
            num_scalar_prefetch=scalars,
            grid=grid,
            in_specs=in_specs,
            out_specs=out_specs,
            scratch_shapes=scratch,
        ),
        compiler_params=pltpu.CompilerParams(
            vmem_limit_bytes=63 * 1024 * 1024, dimension_semantics=("arbitrary",)
        ),
        cost_estimate=cost(COSTS.get(name, 0)),
        name=name,
    )(*args)


def whole(shape):
    return pl.BlockSpec(shape, lambda i, *_: (0,) * len(shape))


def rows_of(shape):
    return pl.BlockSpec(shape, lambda i, *_: (i, 0))


def cols_of(shape):
    return pl.BlockSpec(shape, lambda i, *_: (0, i))


def sds(shape, dtype):
    return jax.ShapeDtypeStruct(shape, dtype)


def split_rows(wire, dest):
    for s in range(CAP):
        for h in range(2):
            rows = slice(s * E + h * 64, s * E + (h + 1) * 64)
            block = wire[h * 64 : (h + 1) * 64, s * SEG : (s + 1) * SEG, :]
            dest[rows, :] = block.reshape(64, D)


def join_rows(source, wire):
    for s in range(CAP):
        for h in range(2):
            rows = slice(s * E + h * 64, s * E + (h + 1) * 64)
            wire[h * 64 : (h + 1) * 64, s * SEG : (s + 1) * SEG, :] = source[rows, :].reshape(
                64, SEG, 128
            )


def put_numbers(columns, wire):
    lane = lax.broadcasted_iota(jnp.int32, (E, 128), 1)
    plane = jnp.zeros((E, 128), f32)
    for s in range(CAP):
        plane = jnp.where(lane == s, columns[s], plane)
    first = plane.astype(bf16)
    rest = plane - first.astype(f32)
    second = rest.astype(bf16)
    third = (rest - second.astype(f32)).astype(bf16)
    none = jnp.zeros((E, 5 * 128), bf16)
    wide = jnp.concatenate([first, second, third, none], axis=1)
    wire[:, CAP * SEG :, :] = wide.reshape(E, 8, 128)


def get_numbers(wire):
    wide = wire[:, CAP * SEG :, :].reshape(E, 8 * 128)
    return (
        wide[:, :128].astype(f32) + wide[:, 128:256].astype(f32) + wide[:, 256:384].astype(f32)
    )


def pack_rows(x_ref, at_ref, wire, rows):
    slot = lax.broadcasted_iota(jnp.int32, (SLOTS, T), 0)
    hit = slot == at_ref[0:1, :]
    for k in range(1, 4):
        hit = hit | (slot == at_ref[k : k + 1, :])
    pick = jnp.where(hit, 1.0, 0.0).astype(bf16)
    for j in range(8):
        cols = slice(j * 256, (j + 1) * 256)
        rows[:, cols] = dot(pick, x_ref[:, cols]).astype(bf16)
    join_rows(rows, wire)


def pack_body(x_ref, at_ref, wire, rows):
    pack_rows(x_ref, at_ref, wire, rows)
    wire[:, CAP * SEG :, :] = jnp.zeros((E, 8, 128), bf16)


def pack(x, assign_t):
    return call(
        pack_body,
        "pack_rows",
        [sds((E, WIRE, 128), bf16)],
        [pltpu.VMEM((SLOTS, D), bf16)],
        (x, assign_t),
    )[0]


def sum_rows(wire, experts, slots, gates, out):
    def body(i, carry):
        for u in range(8):
            t = i * 8 + u
            total = None
            for k in range(4):
                p = t * 4 + k
                rows = pl.ds(pl.multiple_of(slots[p] * SEG, SEG), SEG)
                part = wire[experts[p], rows, :].astype(f32) * gates[p]
                total = part if total is None else total + part
            out[pl.ds(pl.multiple_of(t * SEG, SEG), SEG), :] = total
        return carry

    lax.fori_loop(0, T // 8, body, 0)


def column(row):
    return jnp.broadcast_to(row, (128, 128)).T[:, 0:1]


def qkv_body(pieces, *refs):
    count = len(pieces)
    core, blocks = refs[0], refs[1 : 1 + 2 * count]
    g1, wqt, wk, wks, wv, wvs, gq, gk, cos, sin = refs[1 + 2 * count : 11 + 2 * count]
    outs = refs[11 + 2 * count :]
    wkv = outs[-1]
    lower = core[0] == 0
    wkv[0:64, :] = jnp.where(lower, wk[...], wks[...])
    wkv[64:128, :] = jnp.where(lower, wks[...], wk[...])
    wkv[128:192, :] = jnp.where(lower, wv[...], wvs[...])
    wkv[192:256, :] = jnp.where(lower, wvs[...], wv[...])
    gain_q, gain_k = column(gq[...]), column(gk[...])
    for number, piece in enumerate(pieces):
        qn, qt, kn, kt, vt, scale, n1 = outs[7 * number : 7 * number + 7]
        for half in range(2):
            x = blocks[2 * number + half][...].astype(f32)
            r = lax.rsqrt(jnp.mean(x * x, axis=-1, keepdims=True) + EPS)
            n1[half * T : (half + 1) * T, :] = (x * r * g1[...]).astype(bf16)
        raw = dot_t(wqt[...], n1[...])
        raw_kv = dot_t(wkv[...], n1[...])
        first, second = piece * T, HALF + piece * T
        c = jnp.concatenate([cos[:, first : first + T], cos[:, second : second + T]], axis=1)
        s = jnp.concatenate([sin[:, first : first + T], sin[:, second : second + T]], axis=1)

        def path(v, gain, factor, keep, index):
            r = lax.rsqrt(jnp.mean(v * v, axis=0, keepdims=True) + EPS)
            scale[index : index + 1, :] = r
            v = v * r
            keep[...] = v.astype(bf16)
            v = v * gain
            low, high = v[:64], v[64:]
            return (
                ((low * c - high * s) * factor).astype(bf16),
                ((high * c + low * s) * factor).astype(bf16),
            )

        scale[...] = jnp.zeros_like(scale)
        for h in range(LH):
            heads = slice(h * HEAD, (h + 1) * HEAD)
            low, high = path(raw[heads], gain_q, HEAD ** (-0.5), qn.at[heads, :], h)
            qt[h * HEAD : h * HEAD + 64, :] = low
            qt[h * HEAD + 64 : (h + 1) * HEAD, :] = high
        key = raw_kv[:HEAD].astype(bf16)
        low, high = path(key.astype(f32), gain_k, 1.0, kn, LH)
        kt[:64, :] = low
        kt[64:, :] = high
        vt[...] = raw_kv[HEAD:].astype(bf16)


def qkv(pieces, core, blocks, *args):
    outs = [
        sds((LH * HEAD, 2 * T), bf16),
        sds((LH * HEAD, 2 * T), bf16),
        sds((HEAD, 2 * T), bf16),
        sds((HEAD, 2 * T), bf16),
        sds((HEAD, 2 * T), bf16),
        sds((8, 2 * T), f32),
        sds((2 * T, D), bf16),
    ] * len(pieces)
    keep = 0 in pieces
    return call(
        functools.partial(qkv_body, pieces),
        "qkv" + "".join(str(p) for p in pieces),
        outs + ([sds((2 * HEAD, D), bf16)] if keep else []),
        [] if keep else [pltpu.VMEM((2 * HEAD, D), bf16)],
        (core, *blocks, *args),
        smem=(0,),
    )


def build_mask(info, mask):
    for b in range(8):
        keys = jnp.broadcast_to(info[0:1, b * T : (b + 1) * T], (T, T)).T
        for j in range(8):
            cols = slice(j * T, (j + 1) * T)
            inside = (keys >= info[1:2, cols]) & (keys <= info[0:1, cols])
            mask[b * T : (b + 1) * T, cols] = jnp.where(inside, 1.0, 0.0)


def attend_body(*refs):
    q, k, v = refs[0:4], refs[4:8], refs[8:12]
    info, ot0, ot1, linv, qt, kt, kn, vn, mask, vt = refs[12:]
    for dy in range(4):
        for dc in range(2):
            to = slice(dc * HALF + dy * T, dc * HALF + (dy + 1) * T)
            src = slice(dc * T, (dc + 1) * T)
            qt[:, to] = q[dy][:, src]
            kt[:, to] = k[dy][:, src]
            vt[:, to] = v[dy][:, src]
    for b in range(8):
        rows = slice(b * T, (b + 1) * T)
        kn[rows, :] = kt[:, rows].astype(f32).T.astype(bf16)
        vn[rows, :] = vt[:, rows].astype(f32).T.astype(bf16)
    build_mask(info, mask)
    for half, out in ((1, ot1), (0, ot0)):
        cols = slice(half * HALF, (half + 1) * HALF)
        for h in range(LH):
            heads = slice(h * HEAD, (h + 1) * HEAD)
            scores = dot(kn[...], qt[heads, cols])
            weights = jnp.exp2(scores * LOG2E) * mask[:, cols]
            inverse = 1.0 / jnp.sum(weights, axis=0, keepdims=True)
            out[heads, :] = (dot(vt[...], weights.astype(bf16)) * inverse).astype(bf16)
            linv[h : h + 1, cols] = inverse


def attend(q, k, v, info):
    return call(
        attend_body,
        "attend",
        [
            sds((LH * HEAD, HALF), bf16),
            sds((LH * HEAD, HALF), bf16),
            sds((8, ROWS), f32),
            sds((LH * HEAD, ROWS), bf16),
            sds((HEAD, ROWS), bf16),
            sds((ROWS, HEAD), bf16),
            sds((ROWS, HEAD), bf16),
        ],
        [pltpu.VMEM((ROWS, ROWS), f32), pltpu.VMEM((HEAD, ROWS), bf16)],
        (*q, *k, *v, info),
    )


def flip(source, dest, row, col):
    height, width = source.shape
    for a in range(height // 128):
        for b in range(width // 128):
            block = source[a * 128 : (a + 1) * 128, b * 128 : (b + 1) * 128]
            rows = slice(row + b * 128, row + (b + 1) * 128)
            dest[rows, col + a * 128 : col + (a + 1) * 128] = block.astype(f32).T.astype(bf16)


def outproj_body(ot0, otr, wa, wb, b0, b1, b2, b3, heads):
    @pl.when(pl.program_id(0) == 0)
    def _():
        flip(ot0, heads, 0, 0)
        flip(otr, heads, 0, 512)

    total = dot(heads[:, :512], wa[...]) + dot(heads[:, 512:], wb[...])
    for dy, out in enumerate((b0, b1, b2, b3)):
        out[...] = total[dy * T : (dy + 1) * T, :].astype(bf16)


def outproj(ot0, otr, wa, wb):
    return grid_call(
        outproj_body,
        "out_projection",
        (4,),
        [whole((512, HALF)), whole((512, HALF)), cols_of((512, 512)), cols_of((512, 512))],
        [cols_of((T, 512))] * 4,
        [sds((T, D), bf16)] * 4,
        [pltpu.VMEM((HALF, 1024), bf16)],
        (ot0, otr, wa, wb),
    )


def transpose_body(n0, n1, n2, n3, out):
    for dy, piece in enumerate((n0, n1, n2, n3)):
        for dc in range(2):
            flip(piece.at[dc * T : (dc + 1) * T, :], out, 0, dc * HALF + dy * T)


def transpose_rows(pieces):
    return call(transpose_body, "transpose_rows", [sds((D, ROWS), bf16)], [], tuple(pieces))[0]


def route_body(rt, ids, ids_t):
    lane = lax.broadcasted_iota(jnp.int32, (T, E), 1)
    row = lax.broadcasted_iota(jnp.int32, (T, E), 0)
    wide = jnp.concatenate([rt[...].astype(f32), jnp.zeros((124, T), f32)], axis=0).T
    hot = [jnp.where(lane.astype(f32) == wide[:, k : k + 1], 1.0, 0.0) for k in range(4)]
    earlier = jnp.where(lane < row, 1.0, 0.0).astype(bf16)
    before = dot(earlier, (hot[0] + hot[1] + hot[2] + hot[3]).astype(bf16))
    table = wide
    for k in range(4):
        slot = jnp.sum(before * hot[k], axis=1, keepdims=True)
        table = jnp.where(lane == 4 + k, slot, table)
        table = jnp.where(lane == 8 + k, slot * E + wide[:, k : k + 1], table)
    ids[...] = table.astype(jnp.int32)
    ids_t[...] = table.T[0:16, :].astype(jnp.int32)


def route_tables(routes_t):
    return call(
        route_body,
        "route_tables",
        [sds((T, 128), jnp.int32), sds((16, T), jnp.int32)],
        [],
        (routes_t,),
    )


def router_body(b0, b1, b2, b3, x0, g2, wr, ids, at, hidden, n2, probs, gates, wire, rows):
    v = x0[...].astype(f32) + (
        (b0[...].astype(f32) + b1[...].astype(f32))
        + (b2[...].astype(f32) + b3[...].astype(f32))
    )
    hidden[...] = v
    r = lax.rsqrt(jnp.mean(v * v, axis=-1, keepdims=True) + EPS)
    n2[...] = (v * r * g2[...]).astype(bf16)
    logits = dot(n2[...], wr[...])
    pack_rows(n2, at, wire, rows)
    expo = jnp.exp(logits - jnp.max(logits, axis=-1, keepdims=True))
    p = expo / jnp.sum(expo, axis=-1, keepdims=True)
    probs[...] = p
    lane = lax.broadcasted_iota(jnp.int32, (T, E), 1)
    chosen = [
        jnp.sum(jnp.where(lane == ids[:, k : k + 1], p, 0.0), axis=-1, keepdims=True)
        for k in range(4)
    ]
    total = chosen[0] + chosen[1] + chosen[2] + chosen[3]
    packed = jnp.where(lane == 4, total, 0.0)
    for k in range(4):
        packed = jnp.where(lane == k, chosen[k] / total, packed)
    gates[...] = packed
    across = packed.T
    expert = lax.broadcasted_iota(jnp.int32, (E, T), 0)
    columns = []
    for s in range(CAP):
        mine = jnp.zeros((E, T), f32)
        for k in range(4):
            mine = jnp.where(expert + s * E == at[k : k + 1, :], across[k : k + 1, :], mine)
        columns.append(jnp.sum(mine, axis=1, keepdims=True))
    put_numbers(columns, wire)


def router(b, x0, g2, wr, ids, assign_t):
    return call(
        router_body,
        "router",
        [
            sds((T, D), f32),
            sds((T, D), bf16),
            sds((T, E), f32),
            sds((T, E), f32),
            sds((E, WIRE, 128), bf16),
        ],
        [pltpu.VMEM((SLOTS, D), bf16)],
        (*b, x0, g2, wr, ids, assign_t),
    )


def expert_grad_body(wire, wd, gr, ga):
    split_rows(wire, gr)

    def body(i, carry):
        cols = pl.ds(pl.multiple_of(i * 256, 256), 256)
        ga[:, cols] = dot_t(gr[...], wd[cols, :])
        return carry

    lax.fori_loop(0, F // 256, body, 0)


def expert_grad(wire, wd):
    return call(
        expert_grad_body,
        "expert_grad_rows",
        [sds((SLOTS, D), bf16), sds((SLOTS, F), f32)],
        [],
        (wire, wd),
    )


def expert_main_body(
    wire, wg, wu, ga, back, xs, act, acts, dg, du,
    wire_v, w_v, ga_v, xr, xs_v, act_v, acts_v, d_v, sc, sems,
):
    half = F // 2

    def copy(source, dest, number):
        return pltpu.make_async_copy(source, dest, sems.at[number])

    first = copy(wire, wire_v, 0)
    first.start()
    arrivals = []
    for c in range(2):
        cols = slice(c * half, (c + 1) * half)
        up_cols = slice(F + c * half, F + (c + 1) * half)
        group = [
            copy(wg.at[:, cols], w_v.at[:, cols], 1 + 3 * c),
            copy(wu.at[:, cols], w_v.at[:, up_cols], 2 + 3 * c),
            copy(ga.at[:, cols], ga_v.at[:, cols], 3 + 3 * c),
        ]
        for item in group:
            item.start()
        arrivals.append(group)
    first.wait()
    split_rows(wire_v, xr)
    gates = get_numbers(wire_v)
    sc[...] = jnp.zeros_like(sc)
    for c in range(2):
        for item in arrivals[c]:
            item.wait()
        cols = slice(c * half, (c + 1) * half)
        up_cols = slice(F + c * half, F + (c + 1) * half)
        gate = dot(xr[...], w_v[:, cols])
        up = dot(xr[...], w_v[:, up_cols])
        grad = ga_v[:, cols]
        s = 1.0 / (1.0 + jnp.exp(-gate))
        silu = gate * s
        a = silu * up
        act_v[:, cols] = a.astype(bf16)
        d_v[:, cols] = (grad * up * s * (1.0 + gate * (1.0 - s))).astype(bf16)
        d_v[:, up_cols] = (grad * silu).astype(bf16)
        sc[...] += jnp.sum(a * grad, axis=1, keepdims=True)
    departures = [copy(act_v, act, 7), copy(d_v.at[:, :F], dg, 8), copy(d_v.at[:, F:], du, 9)]
    for item in departures:
        item.start()
    for s in range(CAP):
        part = slice(s * E, (s + 1) * E)
        gate = gates[:, s : s + 1]
        xs_v[part, :] = (xr[part, :].astype(f32) * gate).astype(bf16)
        acts_v[part, :] = (act_v[part, :].astype(f32) * gate).astype(bf16)
    more = [copy(xs_v, xs, 10), copy(acts_v, acts, 11)]
    for item in more:
        item.start()
    for j in range(4):
        part = slice(j * 512, (j + 1) * 512)
        xr[:, part] = dot_t(d_v[...], w_v[part, :]).astype(bf16)
    join_rows(xr, wire_v)
    put_numbers([sc[s * E : (s + 1) * E, :] for s in range(CAP)], wire_v)
    last = copy(wire_v, back, 12)
    last.start()
    for item in departures + more + [last]:
        item.wait()


def expert_main(wire, wg, wu, ga):
    args = (wire, wg, wu, ga)
    outs = [
        sds((E, WIRE, 128), bf16),
        sds((SLOTS, D), bf16),
        sds((SLOTS, F), bf16),
        sds((SLOTS, F), bf16),
        sds((SLOTS, F), bf16),
        sds((SLOTS, F), bf16),
    ]
    return pl.pallas_call(
        expert_main_body,
        out_shape=outs,
        in_specs=[pl.BlockSpec(memory_space=pl.ANY)] * 4,
        out_specs=[pl.BlockSpec(memory_space=pl.ANY)] * 6,
        scratch_shapes=[
            pltpu.VMEM((E, WIRE, 128), bf16),
            pltpu.VMEM((D, 2 * F), bf16),
            pltpu.VMEM((SLOTS, F), f32),
            pltpu.VMEM((SLOTS, D), bf16),
            pltpu.VMEM((SLOTS, D), bf16),
            pltpu.VMEM((SLOTS, F), bf16),
            pltpu.VMEM((SLOTS, F), bf16),
            pltpu.VMEM((SLOTS, 2 * F), bf16),
            pltpu.VMEM((SLOTS, 1), f32),
            pltpu.SemaphoreType.DMA((13,)),
        ],
        compiler_params=pltpu.CompilerParams(vmem_limit_bytes=63 * 1024 * 1024),
        cost_estimate=cost(COSTS["expert_main"]),
        name="expert_main",
    )(*args)


def expert_out_body(act, wd, wire, rows):
    for j in range(8):
        cols = slice(j * 256, (j + 1) * 256)
        rows[:, cols] = dot(act[...], wd[:, cols]).astype(bf16)
    join_rows(rows, wire)


def expert_out(act, wd):
    return call(
        expert_out_body,
        "expert_out",
        [sds((E, CAP * SEG, 128), bf16)],
        [pltpu.VMEM((SLOTS, D), bf16)],
        (act, wd),
    )[0]


def combine_body(
    where, experts, slots, gate_list, wire, hidden, n2, probs, gates, ids, og, g2, wr,
    ghid, gatt, router_own, router_sib, gg2, sums, gn2, parts,
):
    sum_rows(wire, experts, slots, gate_list, sums)
    scores = get_numbers(wire)
    lane = lax.broadcasted_iota(jnp.int32, (T, E), 1)
    grads = []
    for k in range(4):
        hot = jnp.where(lane == ids[:, k : k + 1], 1.0, 0.0)
        rows = lax.dot_general(
            hot, scores, (((1,), (0,)), ((), ())),
            precision=lax.Precision.HIGHEST, preferred_element_type=f32,
        )
        picked = jnp.where(lane == ids[:, 4 + k : 5 + k], rows, 0.0)
        grads.append(jnp.sum(picked, axis=-1, keepdims=True))
    inner = sum(grads[k] * gates[:, k : k + 1] for k in range(4))
    inverse = 1.0 / gates[:, 4:5]
    grad_probs = jnp.zeros((T, E), f32)
    for k in range(4):
        grad_probs = jnp.where(
            lane == ids[:, k : k + 1], (grads[k] - inner) * inverse, grad_probs
        )
    p = probs[...]
    gl = (p * (grad_probs - jnp.sum(p * grad_probs, axis=-1, keepdims=True))).astype(bf16)
    for h in range(2):
        tokens = slice(h * 64, (h + 1) * 64)
        gn2[tokens, :] = sums[h * 1024 : (h + 1) * 1024, :].reshape(64, D)
    gn2[...] += dot_t(gl, wr[...])
    c = gn2[...]
    v = hidden[...]
    r = lax.rsqrt(jnp.mean(v * v, axis=-1, keepdims=True) + EPS)
    u = c * g2[...]
    m = jnp.mean(u * v, axis=-1, keepdims=True)
    total = og[...].astype(f32) + r * u - v * (r * r * r * m)
    ghid[...] = total
    gatt[...] = total.astype(bf16)
    gg2[...] = jnp.sum(c * (v * r), axis=0, keepdims=True)
    for j in range(SEG):
        cols = slice(j * 128, (j + 1) * 128)
        owner = j // 2
        dy = lax.rem(owner // 2 + 4 - where[3], 4)
        dc = lax.rem(owner % 2 + where[2], 2)
        half = slice((j % 2) * 128, (j % 2 + 1) * 128)
        parts[dc * 4 + dy, half, :] = dot(n2[:, cols].astype(f32).T.astype(bf16), gl).astype(bf16)
    router_own[...] = parts[0:4]
    router_sib[...] = parts[4:8]


def combine(*args):
    return call(
        combine_body,
        "combine_grads",
        [
            sds((T, D), f32),
            sds((T, D), bf16),
            sds((4, 256, E), bf16),
            sds((4, 256, E), bf16),
            sds((1, D), f32),
        ],
        [
            pltpu.VMEM((T * SEG, 128), f32),
            pltpu.VMEM((T, D), f32),
            pltpu.VMEM((8, 256, E), bf16),
        ],
        args,
        smem=(0, 1, 2, 3),
    )


def result_body(experts, slots, gate_list, wire, hidden, out, sums):
    sum_rows(wire, experts, slots, gate_list, sums)
    for h in range(2):
        tokens = slice(h * 64, (h + 1) * 64)
        mixture = sums[h * 1024 : (h + 1) * 1024, :].reshape(64, D)
        out[tokens, :] = (hidden[tokens, :] + mixture).astype(bf16)


def result_rows(*args):
    return call(
        result_body,
        "result",
        [sds((T, D), bf16)],
        [pltpu.VMEM((T * SEG, 128), f32)],
        args,
        smem=(0, 1, 2),
    )[0]


def pre_body(where, *refs):
    blocks, (ot0, ot1, wo, w0, w1, w2, w3, dt, rows_all, total) = refs[:8], refs[8:]
    step = pl.program_id(0)
    for b in range(8):
        rows_all[b * T : (b + 1) * T, :] = blocks[b][...]
    grad = (dot(ot0[...], rows_all[:HALF, :]) + dot(ot1[...], rows_all[HALF:, :])).astype(bf16)
    for dx, out in enumerate((w0, w1, w2, w3)):

        @pl.when(step == dx)
        def _():
            for col in range(4):
                out[lax.rem(col + 4 - where[0], 4)] = grad[:, col * 128 : (col + 1) * 128]

    part = dot_t(wo[...], rows_all[...])

    @pl.when(step == 0)
    def _():
        total[...] = part

    @pl.when(step > 0)
    def _():
        total[...] += part

    @pl.when(step == 3)
    def _():
        dt[...] = total[...].astype(bf16)


def pre(where, blocks, ot0, ot1, wo):
    def turned(shape):
        return pl.BlockSpec(shape, lambda i, w: (0, lax.rem(i + w[1], 4)))

    return grid_call(
        pre_body,
        "out_projection_grad",
        (4,),
        [turned((T, 512))] * 8 + [whole((512, HALF))] * 2 + [turned((512, 512))],
        [whole((4, 512, 128))] * 4 + [whole((512, ROWS))],
        [sds((4, 512, 128), bf16)] * 4 + [sds((LH * HEAD, ROWS), bf16)],
        [pltpu.VMEM((ROWS, 512), bf16), pltpu.VMEM((512, ROWS), f32)],
        (where, *blocks, ot0, ot1, wo),
        scalars=1,
    )


def bwd_body(*refs):
    qh, kh, scales = refs[0:4], refs[4:8], refs[8:12]
    (qt, kt, kn, vn, dt, ot0, ot1, linv, info, cos, sin, gq, gk) = refs[12:25]
    dq0, dq1, dkv, ggq, ggk, mask, wb, sb, dqt, dk, dv, raw, scale = refs[25:]
    for dc in range(2):
        for dy in range(4):
            to = slice(dc * HALF + dy * T, dc * HALF + (dy + 1) * T)
            scale[:, to] = scales[dy][:, dc * T : (dc + 1) * T]
    build_mask(info, mask)
    dk[...] = jnp.zeros_like(dk)
    dv[...] = jnp.zeros_like(dv)
    for half, out in ((0, ot0), (1, ot1)):
        cols = slice(half * HALF, (half + 1) * HALF)
        for h in range(LH):
            heads = slice(h * HEAD, (h + 1) * HEAD)
            part = slice(h * HALF, (h + 1) * HALF)
            scores = dot(kn[...], qt[heads, cols])
            weights = jnp.exp2(scores * LOG2E) * (mask[:, cols] * linv[h : h + 1, cols])
            grad = dt[heads, cols]
            delta = jnp.sum(
                grad.astype(f32) * out[heads, :].astype(f32), axis=0, keepdims=True
            )
            wb[:, part] = weights.astype(bf16)
            sb[:, part] = (weights * (dot(vn[...], grad) - delta)).astype(bf16)
            dqt[heads, cols] = dot(kt[...], sb[:, part])
        grads = jnp.concatenate([dt[h * HEAD : (h + 1) * HEAD, cols] for h in range(LH)], axis=1)
        queries = jnp.concatenate([qt[h * HEAD : (h + 1) * HEAD, cols] for h in range(LH)], axis=1)
        dv[...] += dot_t(wb[...], grads)
        dk[...] += dot_t(sb[...], queries)

    def unrope(v):
        low, high = v[:64], v[64:]
        c, s = cos[...], sin[...]
        return jnp.concatenate([low * c + high * s, high * c - low * s], axis=0)

    def norm_back(n, r, grad, gain):
        gain_grad = jnp.sum(grad * n, axis=1, keepdims=True)
        u = grad * gain
        return r * (u - n * jnp.mean(u * n, axis=0, keepdims=True)), gain_grad

    gain_q, gain_k = column(gq[...]), column(gk[...])
    total = jnp.zeros((HEAD, 1), f32)
    for h in range(LH):
        heads = slice(h * HEAD, (h + 1) * HEAD)
        for dy in range(4):
            for dc in range(2):
                to = slice(dc * HALF + dy * T, dc * HALF + (dy + 1) * T)
                raw[:, to] = qh[dy][heads, dc * T : (dc + 1) * T].astype(f32)
        grad, part = norm_back(raw[...], scale[h : h + 1, :], unrope(dqt[heads, :] * (HEAD ** (-0.5))), gain_q)
        total = total + part
        dq0[heads, :] = grad[:, :HALF].astype(bf16)
        dq1[heads, :] = grad[:, HALF:].astype(bf16)
    ggq[...] = jnp.broadcast_to(total, (HEAD, 128)).T[0:8, :]
    for dy in range(4):
        for dc in range(2):
            to = slice(dc * HALF + dy * T, dc * HALF + (dy + 1) * T)
            raw[:, to] = kh[dy][:, dc * T : (dc + 1) * T].astype(f32)
    grad, part = norm_back(raw[...], scale[LH : LH + 1, :], unrope(dk[...].T), gain_k)
    ggk[...] = jnp.broadcast_to(part, (HEAD, 128)).T[0:8, :]
    dkv[:HEAD, :] = grad.astype(bf16)
    dkv[HEAD:, :] = dv[...].T.astype(bf16)


def bwd(qh, kh, scales, *rest):
    return call(
        bwd_body,
        "attend_grad",
        [
            sds((LH * HEAD, HALF), bf16),
            sds((LH * HEAD, HALF), bf16),
            sds((2 * HEAD, ROWS), bf16),
            sds((8, HEAD), f32),
            sds((8, HEAD), f32),
        ],
        [
            pltpu.VMEM((ROWS, ROWS), f32),
            pltpu.VMEM((ROWS, LH * HALF), bf16),
            pltpu.VMEM((ROWS, LH * HALF), bf16),
            pltpu.VMEM((LH * HEAD, ROWS), f32),
            pltpu.VMEM((ROWS, HEAD), f32),
            pltpu.VMEM((ROWS, HEAD), f32),
            pltpu.VMEM((HEAD, ROWS), f32),
            pltpu.VMEM((8, ROWS), f32),
        ],
        (*qh, *kh, *scales, *rest),
    )


def qkv_grad_body(where, n1t, dq0, dq1, own, sib, out, tot, dt):
    @pl.when(pl.program_id(0) == 0)
    def _():
        tot[:, :HALF] = (own[:, :HALF].astype(f32) + sib[:, HALF:].astype(f32)).astype(bf16)
        tot[:, HALF:] = (own[:, HALF:].astype(f32) + sib[:, :HALF].astype(f32)).astype(bf16)
        dt[:512, :HALF] = dq0[...]
        dt[:512, HALF:] = dq1[...]
        upper = where[2] == 1
        dt[512:576, :] = jnp.where(upper, tot[64:128, :], tot[:64, :])
        dt[576:, :] = jnp.where(upper, tot[192:, :], tot[128:192, :])

    out[...] = dot_t(n1t[...], dt[...]).astype(bf16)


def qkv_grad(where, n1t, dq0, dq1, own, sib):
    return grid_call(
        qkv_grad_body,
        "qkv_weight_grad",
        (4,),
        [
            rows_of((512, ROWS)),
            whole((512, HALF)),
            whole((512, HALF)),
            whole((2 * HEAD, ROWS)),
            whole((2 * HEAD, ROWS)),
        ],
        [rows_of((512, 640)), whole((2 * HEAD, ROWS))],
        [sds((D, 640), bf16), sds((2 * HEAD, ROWS), bf16)],
        [pltpu.VMEM((640, ROWS), bf16)],
        (where, n1t, dq0, dq1, own, sib),
        scalars=1,
    )


def widen_body(grads, gq, gkt, gvt):
    gq[...] = grads[:, :512].astype(f32)
    both = grads[:, 512:].astype(f32).T
    gkt[...] = both[:64]
    gvt[...] = both[64:]


def widen(grads):
    return grid_call(
        widen_body,
        "widen_grads",
        (4,),
        [rows_of((512, 640))],
        [rows_of((512, 512)), cols_of((64, 512)), cols_of((64, 512))],
        [sds((D, 512), f32), sds((64, D), f32), sds((64, D), f32)],
        [],
        (grads,),
    )


def add_body(a, b, c, d, *outs):
    for i, out in enumerate(outs):
        out[...] = (
            (a[i].astype(f32) + b[i].astype(f32)) + (c[i].astype(f32) + d[i].astype(f32))
        ).astype(bf16)


def add_parts(parts):
    shape = parts[0].shape[1:]
    return call(add_body, "add_parts", [sds(shape, bf16)] * 4, [], tuple(parts))


def split_two(v):
    first = v.astype(bf16)
    return first, (v - first.astype(f32)).astype(bf16)


def normed_grad_body(
    wa, wb, wkv, dq0, dqr, tot, n0, n1, n2, n3, gg2, ggq, ggk, ra, rb, b0, b1, b2, b3, grads
):
    step = pl.program_id(0)

    @pl.when(step == 0)
    def _():
        flip(dq0, grads, 0, 0)
        flip(dqr, grads, 0, 512)
        flip(tot, grads, 0, 1024)

    total = (
        dot(grads[:, :512], wa[...])
        + dot(grads[:, 512:1024], wb[...])
        + dot(grads[:, 1024:], wkv[...])
    )
    gain = jnp.zeros((1, 512), f32)
    outs = (b0, b1, b2, b3)
    for dy, (out, rows) in enumerate(zip(outs, (n0, n1, n2, n3))):
        part = total[dy * T : (dy + 1) * T, :]
        out[:T, :] = part.astype(bf16)
        gain = gain + jnp.sum(part * rows[...].astype(f32), axis=0, keepdims=True)
    heads = jnp.concatenate([ggq[0:1, :], ggk[0:1, :], jnp.zeros((1, 256), f32)], axis=1)
    numbers = [*split_two(gain), *split_two(gg2[...]), *split_two(heads)]
    extra = jnp.concatenate([n.astype(f32) for n in numbers] + [jnp.zeros((10, 512), f32)], axis=0)
    for dy, out in enumerate(outs):
        out[T : T + 16, :] = extra.astype(bf16)
        for q in range(4):
            rows = pl.ds(pl.multiple_of(step * 64 + q * 16, 16), 16)
            both = ra[dy, rows, :].astype(f32) + rb[dy, rows, :].astype(f32)
            out[T + 16 :, q * 128 : (q + 1) * 128] = both.astype(bf16)


def normed_grad(wa, wb, wkv, dq0, dqr, tot, n1, gg2, ggq, ggk, ra, rb):
    return grid_call(
        normed_grad_body,
        "normed_grad",
        (4,),
        [
            cols_of((512, 512)),
            cols_of((512, 512)),
            cols_of((256, 512)),
            whole((512, HALF)),
            whole((512, HALF)),
            whole((2 * HEAD, HALF)),
        ]
        + [cols_of((T, 512))] * 4
        + [cols_of((1, 512)), whole((8, HEAD)), whole((8, HEAD))]
        + [whole((4, 256, E))] * 2,
        [cols_of((T + 32, 512))] * 4,
        [sds((T + 32, D), bf16)] * 4,
        [pltpu.VMEM((HALF, 1280), bf16)],
        (wa, wb, wkv, dq0, dqr, tot, *n1, gg2, ggq, ggk, ra, rb),
    )


def add_last_body(a, b, c, d, out):
    out[...] = (
        (a[...].astype(f32) + b[...].astype(f32)) + (c[...].astype(f32) + d[...].astype(f32))
    ).astype(bf16)


def add_last(parts):
    return call(add_last_body, "add_last", [sds(parts[0].shape, bf16)], [], tuple(parts))


def stack_body(a, b, c, d, out):
    for i, part in enumerate((a, b, c, d)):
        out[i] = part[...]


def stack(parts):
    shape = (4, *parts[0].shape)
    return call(stack_body, "stack_parts", [sds(shape, bf16)], [], tuple(parts))[0]


def place_out_body(where, c0, c1, c2, c3, out):
    for dx, chunks in enumerate((c0, c1, c2, c3)):
        for dz in range(4):
            chunk = lax.rem(where[1] + dx, 4) * 4 + lax.rem(where[0] + dz, 4)
            cols = pl.ds(pl.multiple_of(chunk * 128, 128), 128)
            out[:, cols] = chunks[dz].astype(f32)


def place_out(where, chunks):
    return call(
        place_out_body,
        "place_output_grads",
        [sds((512, D), f32)],
        [],
        (where, *chunks),
        smem=(0,),
    )[0]


def final_body(b0, b1, b2, b3, x0, ghid, g1, out, small):
    whole_sum = (b0[...].astype(f32) + b1[...].astype(f32)) + (
        b2[...].astype(f32) + b3[...].astype(f32)
    )
    c = whole_sum[:T]
    v = x0[...].astype(f32)
    r = lax.rsqrt(jnp.mean(v * v, axis=-1, keepdims=True) + EPS)
    u = c * g1[...]
    m = jnp.mean(u * v, axis=-1, keepdims=True)
    out[...] = ghid[...] + r * u - v * (r * r * r * m)
    extra = whole_sum[T : T + 16]
    numbers = [
        *split_two((extra[0:1] + extra[1:2]) / g1[...]),
        *split_two(extra[2:3] + extra[3:4]),
        *split_two(extra[4:5] + extra[5:6]),
    ]
    rows = jnp.concatenate(
        [whole_sum[T + 16 :]] + [n.astype(f32) for n in numbers] + [jnp.zeros((2, D), f32)],
        axis=0,
    ).astype(bf16)
    for e in range(16):
        small[e] = rows[:, e * 128 : (e + 1) * 128]


def final(b, x0, ghid, g1):
    return call(
        final_body,
        "input_grad",
        [sds((T, D), f32), sds((16, 24, 128), bf16)],
        [],
        (*b, x0, ghid, g1),
    )


def fold_body(parts, out):
    total = parts[0].astype(f32)
    for e in range(1, 16):
        total = total + parts[e].astype(f32)
    numbers = []
    for k in range(3):
        row = SEG + 2 * k
        numbers += split_two(total[row : row + 1] + total[row + 1 : row + 2])
    rows = jnp.concatenate(
        [total[:SEG]] + [n.astype(f32) for n in numbers] + [jnp.zeros((2, 128), f32)], axis=0
    ).astype(bf16)

    def body(i, carry):
        out[i] = rows
        return carry

    lax.fori_loop(0, E, body, 0)


def fold(parts):
    return call(fold_body, "fold_small", [sds((E, 24, 128), bf16)], [], (parts,))[0]


def sibling(x):
    return lax.ppermute(x, "shard", [(i, i ^ 1) for i in range(8)])


def from_chip(x, dy):
    return lax.ppermute(x, "shard", [(i, (i - 2 * dy) % 8) for i in range(8)])


def to_chip(x, dy):
    return lax.ppermute(x, "shard", [(i, (i + 2 * dy) % 8) for i in range(8)])


def exchange(x):
    return lax.all_to_all(x, ALL, split_axis=0, concat_axis=0, tiled=True)


def spread(x):
    return [to_chip(x[d], d) for d in (1, 3, 2)]


def on_expert(x, dz, dx):
    pairs = [
        (z * 4 + c, ((z + dz) % 4) * 4 + (c + dx) % 4) for z in range(4) for c in range(4)
    ]
    return lax.ppermute(x, "expert", pairs)


def move(x, axis, distance):
    return on_expert(x, distance, 0) if axis == 0 else on_expert(x, 0, distance)


def collect(parts, axis):
    return [parts[0]] + [move(parts[d], axis, d) for d in (1, 3, 2)]


def share(x, axis):
    return [x] + [move(x, axis, (4 - d) % 4) for d in (1, 2, 3)]


def after(value, *others):
    return lax.optimization_barrier((value, *others))[0]


def on_device(
    block_input, out_grad, norm1_gain, w_query, w_key, w_value, query_gain, key_gain, w_out,
    norm2_gain, w_router, w_gate, w_up, w_down, seq_lengths, token_places, expert_routes,
):
    shard, owner = lax.axis_index("shard"), lax.axis_index("expert")
    chip, core = shard // 2, shard % 2
    where = jnp.stack([owner // 4, owner % 4, core, chip]).astype(jnp.int32)
    core_id = core.reshape(1)
    g1 = norm1_gain.astype(f32).reshape(1, D)
    g2 = norm2_gain.astype(f32).reshape(1, D)
    gq = query_gain.astype(f32).reshape(1, HEAD)
    gk = key_gain.astype(f32).reshape(1, HEAD)

    x_own = [block_input] + [from_chip(block_input, dy) for dy in (1, 2, 3)]
    x_sib = [sibling(block_input)]

    chips = (chip + jnp.arange(4)) % 4
    order = jnp.concatenate([chips * 2 + core, chips * 2 + 1 - core])
    places = token_places[0].reshape(8, T)[order].reshape(ROWS)
    lengths = seq_lengths[0]
    ends = jnp.cumsum(lengths)
    starts = jnp.sum(
        jnp.where(places[:, None] >= ends[None, :], lengths[None, :], 0), axis=1
    )
    positions = (places - starts).astype(f32)
    info = jnp.concatenate(
        [places[None].astype(f32), starts[None].astype(f32), jnp.zeros((6, ROWS), f32)], axis=0
    )
    inverse_freq = ROPE_BASE ** (-jnp.arange(0, HEAD, 2).astype(f32) / HEAD)
    angles = inverse_freq[:, None] * positions[None, :]
    cos, sin = jnp.cos(angles), jnp.sin(angles)

    ids, ids_t = route_tables(expert_routes.T)
    assign_t = ids_t[8:12]
    expert_list = ids[:, 0:4].reshape(-1)
    slot_list = ids[:, 4:8].reshape(-1)

    wk_t, wv_t = w_key.T, w_value.T
    wk_s, wv_s = sibling(wk_t), sibling(wv_t)
    wq_t = w_query.T
    wo_s = sibling(w_out)
    wq_ts = sibling(wq_t)

    weights = (g1, wq_t, wk_t, wk_s, wv_t, wv_s, gq, gk, cos, sin)
    zero = qkv((0,), core_id, (x_own[0], x_sib[0]), *weights)
    og_wire = pack(out_grad, assign_t)
    x_own[1], x_own[2], x_own[3], q_first, og_wire = lax.optimization_barrier(
        (x_own[1], x_own[2], x_own[3], zero[1], og_wire)
    )
    x_sib += [sibling(x_own[dy]) for dy in (1, 2, 3)]
    blocks = [side[dy] for dy in (1, 2, 3) for side in (x_own, x_sib)]
    others = qkv((1, 2, 3), core_id, blocks, *weights)
    wkv = zero[7]
    pieces = [zero[:7], others[:7], others[7:14], others[14:21]]
    qh, q, kh, k, v, scales, n1 = zip(*pieces)
    q = (q_first,) + q[1:]
    got_grads = exchange(og_wire)
    ot0, ot1, linv, qt, kt, kn, vn = attend(q, k, v, info)
    blocks = outproj(ot0, sibling(ot1), w_out, wo_s)
    blocks = [blocks[0]] + spread(blocks)
    hidden, n2, probs, gates, wire = router(blocks, block_input, g2, w_router, ids, assign_t)
    got_rows = exchange(wire)

    n1_t = transpose_rows(after(n1, wire))
    gate_list = gates[:, :4].reshape(-1)
    grad_rows, grad_act = expert_grad(after(got_grads, wire), w_down[0])
    got_rows, n1_t, grad_act, gate_list, wq_ts = lax.optimization_barrier(
        (got_rows, n1_t, grad_act, gate_list, wq_ts)
    )

    back, rows, act, scaled_act, dg, du = expert_main(got_rows, w_gate[0], w_up[0], grad_act)
    back_wire = exchange(back)

    rows, act, scaled_act, dg, du = after((rows, act, scaled_act, dg, du), back)
    out_wire = expert_out(act, w_down[0])

    def weight_grad(a, b):
        return lax.dot_general(a, b, (((0,), (0,)), ((), ())), preferred_element_type=f32)

    grad_wgate = weight_grad(rows, dg)
    grad_wup = weight_grad(rows, du)
    grad_wdown = weight_grad(scaled_act, grad_rows)
    back_wire, out_wire, grad_wgate, grad_wup, grad_wdown = lax.optimization_barrier(
        (back_wire, out_wire, grad_wgate, grad_wup, grad_wdown)
    )

    ghid, gatt, router_own, router_sib, gg2 = combine(
        where, expert_list, slot_list, gate_list, back_wire, hidden, n2, probs, gates, ids,
        out_grad, g2, w_router,
    )
    g_own = [gatt] + [from_chip(gatt, dy) for dy in (1, 2, 3)]
    g_sib = [sibling(block) for block in g_own]
    returned = exchange(after(out_wire, *g_sib))
    *out_parts, dt = pre(where, g_own + g_sib, ot0, ot1, w_out)

    dq0, dq1, dkv, ggq, ggk = bwd(
        qh, kh, scales, qt, kt, kn, vn, dt, ot0, ot1, linv, info, cos, sin, gq, gk
    )
    router_sib = after(router_sib, dkv)
    dq_sib, dkv_sib = sibling(dq1), sibling(dkv)
    gw, dkv_total = qkv_grad(where, n1_t, dq0, dq1, dkv, dkv_sib)
    returned, dq0 = lax.optimization_barrier((returned, dq0))
    result = result_rows(expert_list, slot_list, gate_list, returned, hidden)
    router_rec = sibling(router_sib)
    blocks = normed_grad(
        wq_t, wq_ts, wkv, dq0, dq_sib, dkv_total, n1, gg2, ggq, ggk, router_own, router_rec
    )
    blocks = [blocks[0]] + spread(blocks)

    gw = lax.psum(gw, "expert")
    out_parts = collect(add_parts(collect(out_parts, 1)), 0)
    chunks = stack(share(add_last(out_parts)[0], 0))
    grad_input, small = final(blocks, block_input, ghid, g1)
    small = lax.all_to_all(small, "expert", split_axis=0, concat_axis=0, tiled=True)
    small = exchange(fold(small))
    grad_wout = place_out(where, share(chunks, 1))
    gw, small, grad_input, grad_wout, result = lax.optimization_barrier(
        (gw, small, grad_input, grad_wout, result)
    )
    grad_wq, grad_wk, grad_wv = widen(gw)
    small = small.reshape(16, 8, 24, 128).astype(f32)
    grad_router = small[:, :, :SEG].transpose(1, 0, 2, 3).reshape(D, E)
    gains = small[:, 0, SEG:] + small[:, 1, SEG:]
    gains = [(gains[:, 2 * k] + gains[:, 2 * k + 1]).reshape(D) for k in range(3)]
    return (
        result,
        grad_input,
        gains[0],
        grad_wq,
        grad_wk.T,
        grad_wv.T,
        gains[2][:HEAD],
        gains[2][HEAD : 2 * HEAD],
        grad_wout,
        gains[1],
        grad_router,
        grad_wgate[None],
        grad_wup[None],
        grad_wdown[None],
    )


def solution(mesh):
    rows = P(("expert", "shard"), None)
    experts = P(("expert", "shard"), None, None)
    columns = P(None, "shard")
    return jax.shard_map(
        on_device,
        mesh=mesh,
        in_specs=(
            rows, rows, P(), columns, columns, columns, P(), P(), P("shard", None), P(), P(),
            experts, experts, experts, P("expert", None), P("expert", None), rows,
        ),
        out_specs=(
            rows, rows, P(), columns, columns, columns, P(), P(), P("shard", None), P(), P(),
            experts, experts, experts,
        ),
        check_vma=False,
    )
```

```python
import functools

import jax
import jax.numpy as jnp
from jax import lax
from jax.experimental import pallas as pl
from jax.experimental.pallas import tpu as pltpu
from jax.sharding import PartitionSpec as P

EPS = 1e-06
ROPE_BASE = 1000000.0
LOG2E = 1.4426950408889634
T = 128
D = 2048
HEAD = 128
LH = 4
E = 128
CAP = 5
SLOTS = E * CAP
SEG = D // 128
WIRE = CAP * SEG + 8
ROWS = 1024
HALF = 512
F = 768
bf16 = jnp.bfloat16
f32 = jnp.float32
ALL = ("expert", "shard")
COSTS = {
    "attend": 11,
    "out_projection": 5,
    "router": 6,
    "transpose_rows": 6,
    "expert_grad_rows": 8,
    "expert_main": 18,
    "expert_out": 7,
    "combine_grads": 7,
    "head_grad": 4,
    "out_projection_grad": 7,
}


def cost(micros):
    return pl.CostEstimate(
        flops=1, bytes_accessed=int(micros * 0.6e6) + 1, transcendentals=0
    )


def dot(a, b):
    return jnp.dot(a, b, preferred_element_type=f32)


def dot_t(a, b):
    return lax.dot_general(a, b, (((1,), (1,)), ((), ())), preferred_element_type=f32)


def call(kernel, name, outs, scratch, args, smem=()):
    in_specs = [
        pl.BlockSpec(memory_space=pltpu.SMEM if i in smem else pltpu.VMEM)
        for i in range(len(args))
    ]
    return pl.pallas_call(
        kernel,
        out_shape=outs,
        in_specs=in_specs,
        out_specs=[pl.BlockSpec(memory_space=pltpu.VMEM) for _ in outs],
        scratch_shapes=scratch,
        compiler_params=pltpu.CompilerParams(vmem_limit_bytes=63 * 1024 * 1024),
        cost_estimate=cost(COSTS.get(name, 0)),
        name=name,
    )(*args)


def grid_call(kernel, name, grid, in_specs, out_specs, outs, scratch, args, scalars=0):
    return pl.pallas_call(
        kernel,
        out_shape=outs,
        grid_spec=pltpu.PrefetchScalarGridSpec(
            num_scalar_prefetch=scalars,
            grid=grid,
            in_specs=in_specs,
            out_specs=out_specs,
            scratch_shapes=scratch,
        ),
        compiler_params=pltpu.CompilerParams(
            vmem_limit_bytes=63 * 1024 * 1024, dimension_semantics=("arbitrary",)
        ),
        cost_estimate=cost(COSTS.get(name, 0)),
        name=name,
    )(*args)


def copy_call(kernel, name, outs, scratch, copies, args, smem=()):
    return pl.pallas_call(
        kernel,
        out_shape=outs,
        in_specs=[
            pl.BlockSpec(memory_space=pltpu.SMEM if i in smem else pl.ANY)
            for i in range(len(args))
        ],
        out_specs=[pl.BlockSpec(memory_space=pl.ANY)] * len(outs),
        scratch_shapes=[*scratch, pltpu.SemaphoreType.DMA((copies,))],
        compiler_params=pltpu.CompilerParams(vmem_limit_bytes=63 * 1024 * 1024),
        cost_estimate=cost(COSTS.get(name, 0)),
        name=name,
    )(*args)


class Copies:
    def __init__(self, sems):
        self.sems, self.count, self.leaving = sems, 0, []

    def bring(self, source, dest):
        item = pltpu.make_async_copy(source, dest, self.sems.at[self.count])
        self.count += 1
        item.start()
        return item

    def take(self, source, dest):
        self.leaving.append(self.bring(source, dest))

    def finish(self):
        for item in self.leaving:
            item.wait()


def whole(shape):
    return pl.BlockSpec(shape, lambda i, *_: (0,) * len(shape))


def rows_of(shape):
    return pl.BlockSpec(shape, lambda i, *_: (i, 0))


def cols_of(shape):
    return pl.BlockSpec(shape, lambda i, *_: (0, i))


def sds(shape, dtype):
    return jax.ShapeDtypeStruct(shape, dtype)


def split_rows(wire, dest):
    for s in range(CAP):
        for h in range(2):
            rows = slice(s * E + h * 64, s * E + (h + 1) * 64)
            block = wire[h * 64 : (h + 1) * 64, s * SEG : (s + 1) * SEG, :]
            dest[rows, :] = block.reshape(64, D)


def join_rows(source, wire):
    for s in range(CAP):
        for h in range(2):
            rows = slice(s * E + h * 64, s * E + (h + 1) * 64)
            wire[h * 64 : (h + 1) * 64, s * SEG : (s + 1) * SEG, :] = source[rows, :].reshape(
                64, SEG, 128
            )


def put_numbers(columns, wire):
    lane = lax.broadcasted_iota(jnp.int32, (E, 128), 1)
    plane = jnp.zeros((E, 128), f32)
    for s in range(CAP):
        plane = jnp.where(lane == s, columns[s], plane)
    first = plane.astype(bf16)
    rest = plane - first.astype(f32)
    second = rest.astype(bf16)
    third = (rest - second.astype(f32)).astype(bf16)
    none = jnp.zeros((E, 5 * 128), bf16)
    wide = jnp.concatenate([first, second, third, none], axis=1)
    wire[:, CAP * SEG :, :] = wide.reshape(E, 8, 128)


def get_numbers(wire):
    wide = wire[:, CAP * SEG :, :].reshape(E, 8 * 128)
    return (
        wide[:, :128].astype(f32) + wide[:, 128:256].astype(f32) + wide[:, 256:384].astype(f32)
    )


def pack_rows(x_ref, at_ref, wire, rows):
    slot = lax.broadcasted_iota(jnp.int32, (SLOTS, T), 0)
    hit = slot == at_ref[0:1, :]
    for k in range(1, 4):
        hit = hit | (slot == at_ref[k : k + 1, :])
    pick = jnp.where(hit, 1.0, 0.0).astype(bf16)
    for j in range(8):
        cols = slice(j * 256, (j + 1) * 256)
        rows[:, cols] = dot(pick, x_ref[:, cols]).astype(bf16)
    join_rows(rows, wire)


def pack_body(x_ref, at_ref, wire, rows):
    pack_rows(x_ref, at_ref, wire, rows)
    wire[:, CAP * SEG :, :] = jnp.zeros((E, 8, 128), bf16)


def pack(x, assign_t):
    return call(
        pack_body,
        "pack_rows",
        [sds((E, WIRE, 128), bf16)],
        [pltpu.VMEM((SLOTS, D), bf16)],
        (x, assign_t),
    )[0]


def sum_rows(wire, experts, slots, gates, out):
    def body(i, carry):
        for u in range(8):
            t = i * 8 + u
            total = None
            for k in range(4):
                p = t * 4 + k
                rows = pl.ds(pl.multiple_of(slots[p] * SEG, SEG), SEG)
                part = wire[experts[p], rows, :].astype(f32) * gates[p]
                total = part if total is None else total + part
            out[pl.ds(pl.multiple_of(t * SEG, SEG), SEG), :] = total
        return carry

    lax.fori_loop(0, T // 8, body, 0)


def column(row):
    return jnp.broadcast_to(row, (128, 128)).T[:, 0:1]


def qkv_body(pieces, *refs):
    count = len(pieces)
    core, blocks = refs[0], refs[1 : 1 + 2 * count]
    g1, wqt, wk, wks, wv, wvs, gq, gk, cos, sin = refs[1 + 2 * count : 11 + 2 * count]
    outs = refs[11 + 2 * count :]
    wkv = outs[-1]
    lower = core[0] == 0
    wkv[0:64, :] = jnp.where(lower, wk[...], wks[...])
    wkv[64:128, :] = jnp.where(lower, wks[...], wk[...])
    wkv[128:192, :] = jnp.where(lower, wv[...], wvs[...])
    wkv[192:256, :] = jnp.where(lower, wvs[...], wv[...])
    gain_q, gain_k = column(gq[...]), column(gk[...])
    for number, piece in enumerate(pieces):
        qn, qt, kn, kt, vt, scale, n1 = outs[7 * number : 7 * number + 7]
        for half in range(2):
            x = blocks[2 * number + half][...].astype(f32)
            r = lax.rsqrt(jnp.mean(x * x, axis=-1, keepdims=True) + EPS)
            n1[half * T : (half + 1) * T, :] = (x * r * g1[...]).astype(bf16)
        raw = dot_t(wqt[...], n1[...])
        raw_kv = dot_t(wkv[...], n1[...])
        first, second = piece * T, HALF + piece * T
        c = jnp.concatenate([cos[:, first : first + T], cos[:, second : second + T]], axis=1)
        s = jnp.concatenate([sin[:, first : first + T], sin[:, second : second + T]], axis=1)

        def path(v, gain, factor, keep, index):
            r = lax.rsqrt(jnp.mean(v * v, axis=0, keepdims=True) + EPS)
            scale[index : index + 1, :] = r
            v = v * r
            keep[...] = v.astype(bf16)
            v = v * gain
            low, high = v[:64], v[64:]
            return (
                ((low * c - high * s) * factor).astype(bf16),
                ((high * c + low * s) * factor).astype(bf16),
            )

        scale[...] = jnp.zeros_like(scale)
        for h in range(LH):
            heads = slice(h * HEAD, (h + 1) * HEAD)
            low, high = path(raw[heads], gain_q, HEAD ** (-0.5), qn.at[heads, :], h)
            qt[h * HEAD : h * HEAD + 64, :] = low
            qt[h * HEAD + 64 : (h + 1) * HEAD, :] = high
        key = raw_kv[:HEAD].astype(bf16)
        low, high = path(key.astype(f32), gain_k, 1.0, kn, LH)
        kt[:64, :] = low
        kt[64:, :] = high
        vt[...] = raw_kv[HEAD:].astype(bf16)


def qkv(pieces, core, blocks, *args):
    outs = [
        sds((LH * HEAD, 2 * T), bf16),
        sds((LH * HEAD, 2 * T), bf16),
        sds((HEAD, 2 * T), bf16),
        sds((HEAD, 2 * T), bf16),
        sds((HEAD, 2 * T), bf16),
        sds((8, 2 * T), f32),
        sds((2 * T, D), bf16),
    ] * len(pieces)
    keep = 0 in pieces
    return call(
        functools.partial(qkv_body, pieces),
        "qkv" + "".join(str(p) for p in pieces),
        outs + ([sds((2 * HEAD, D), bf16)] if keep else []),
        [] if keep else [pltpu.VMEM((2 * HEAD, D), bf16)],
        (core, *blocks, *args),
        smem=(0,),
    )


def build_mask(info, mask):
    for b in range(8):
        keys = jnp.broadcast_to(info[0:1, b * T : (b + 1) * T], (T, T)).T
        for j in range(8):
            cols = slice(j * T, (j + 1) * T)
            inside = (keys >= info[1:2, cols]) & (keys <= info[0:1, cols])
            mask[b * T : (b + 1) * T, cols] = jnp.where(inside, 1.0, 0.0)


def attend_body(*refs):
    q, k, v = refs[0:4], refs[4:8], refs[8:12]
    info, ot0, ot1, linv, qt, kt, kn, vn, mask, vt = refs[12:]
    for dy in range(4):
        for dc in range(2):
            to = slice(dc * HALF + dy * T, dc * HALF + (dy + 1) * T)
            src = slice(dc * T, (dc + 1) * T)
            qt[:, to] = q[dy][:, src]
            kt[:, to] = k[dy][:, src]
            vt[:, to] = v[dy][:, src]
    for b in range(8):
        rows = slice(b * T, (b + 1) * T)
        kn[rows, :] = kt[:, rows].astype(f32).T.astype(bf16)
        vn[rows, :] = vt[:, rows].astype(f32).T.astype(bf16)
    build_mask(info, mask)
    for half, out in ((1, ot1), (0, ot0)):
        cols = slice(half * HALF, (half + 1) * HALF)
        for h in range(LH):
            heads = slice(h * HEAD, (h + 1) * HEAD)
            scores = dot(kn[...], qt[heads, cols])
            weights = jnp.exp2(scores * LOG2E) * mask[:, cols]
            inverse = 1.0 / jnp.sum(weights, axis=0, keepdims=True)
            out[heads, :] = (dot(vt[...], weights.astype(bf16)) * inverse).astype(bf16)
            linv[h : h + 1, cols] = inverse


def attend(q, k, v, info):
    return call(
        attend_body,
        "attend",
        [
            sds((LH * HEAD, HALF), bf16),
            sds((LH * HEAD, HALF), bf16),
            sds((8, ROWS), f32),
            sds((LH * HEAD, ROWS), bf16),
            sds((HEAD, ROWS), bf16),
            sds((ROWS, HEAD), bf16),
            sds((ROWS, HEAD), bf16),
        ],
        [pltpu.VMEM((ROWS, ROWS), f32), pltpu.VMEM((HEAD, ROWS), bf16)],
        (*q, *k, *v, info),
    )


def flip(source, dest, row, col):
    height, width = source.shape
    for a in range(height // 128):
        for b in range(width // 128):
            block = source[a * 128 : (a + 1) * 128, b * 128 : (b + 1) * 128]
            rows = slice(row + b * 128, row + (b + 1) * 128)
            dest[rows, col + a * 128 : col + (a + 1) * 128] = block.astype(f32).T.astype(bf16)


def outproj_body(ot0, otr, wa, wb, b0, b1, b2, b3, heads):
    @pl.when(pl.program_id(0) == 0)
    def _():
        flip(ot0, heads, 0, 0)
        flip(otr, heads, 0, 512)

    total = dot(heads[:, :512], wa[...]) + dot(heads[:, 512:], wb[...])
    for dy, out in enumerate((b0, b1, b2, b3)):
        out[...] = total[dy * T : (dy + 1) * T, :].astype(bf16)


def outproj(ot0, otr, wa, wb):
    return grid_call(
        outproj_body,
        "out_projection",
        (2,),
        [whole((512, HALF)), whole((512, HALF)), cols_of((512, 1024)), cols_of((512, 1024))],
        [cols_of((T, 1024))] * 4,
        [sds((T, D), bf16)] * 4,
        [pltpu.VMEM((HALF, 1024), bf16)],
        (ot0, otr, wa, wb),
    )


def transpose_body(n0, n1, n2, n3, out):
    for dy, piece in enumerate((n0, n1, n2, n3)):
        for dc in range(2):
            flip(piece.at[dc * T : (dc + 1) * T, :], out, 0, dc * HALF + dy * T)


def transpose_rows(pieces):
    return call(transpose_body, "transpose_rows", [sds((D, ROWS), bf16)], [], tuple(pieces))[0]


def route_body(rt, ids, ids_t):
    lane = lax.broadcasted_iota(jnp.int32, (T, E), 1)
    row = lax.broadcasted_iota(jnp.int32, (T, E), 0)
    wide = jnp.concatenate([rt[...].astype(f32), jnp.zeros((124, T), f32)], axis=0).T
    hot = [jnp.where(lane.astype(f32) == wide[:, k : k + 1], 1.0, 0.0) for k in range(4)]
    earlier = jnp.where(lane < row, 1.0, 0.0).astype(bf16)
    before = dot(earlier, (hot[0] + hot[1] + hot[2] + hot[3]).astype(bf16))
    table = wide
    for k in range(4):
        slot = jnp.sum(before * hot[k], axis=1, keepdims=True)
        table = jnp.where(lane == 4 + k, slot, table)
        table = jnp.where(lane == 8 + k, slot * E + wide[:, k : k + 1], table)
    ids[...] = table.astype(jnp.int32)
    ids_t[...] = table.T[0:16, :].astype(jnp.int32)


def route_tables(routes_t):
    return call(
        route_body,
        "route_tables",
        [sds((T, 128), jnp.int32), sds((16, T), jnp.int32)],
        [],
        (routes_t,),
    )


def router_body(b0, b1, b2, b3, x0, g2, wr, ids, at, hidden, n2, probs, gates, wire, rows):
    v = x0[...].astype(f32) + (
        (b0[...].astype(f32) + b1[...].astype(f32))
        + (b2[...].astype(f32) + b3[...].astype(f32))
    )
    hidden[...] = v
    r = lax.rsqrt(jnp.mean(v * v, axis=-1, keepdims=True) + EPS)
    n2[...] = (v * r * g2[...]).astype(bf16)
    logits = dot(n2[...], wr[...])
    pack_rows(n2, at, wire, rows)
    expo = jnp.exp(logits - jnp.max(logits, axis=-1, keepdims=True))
    p = expo / jnp.sum(expo, axis=-1, keepdims=True)
    probs[...] = p
    lane = lax.broadcasted_iota(jnp.int32, (T, E), 1)
    chosen = [
        jnp.sum(jnp.where(lane == ids[:, k : k + 1], p, 0.0), axis=-1, keepdims=True)
        for k in range(4)
    ]
    total = chosen[0] + chosen[1] + chosen[2] + chosen[3]
    packed = jnp.where(lane == 4, total, 0.0)
    for k in range(4):
        packed = jnp.where(lane == k, chosen[k] / total, packed)
    gates[...] = packed
    across = packed.T
    expert = lax.broadcasted_iota(jnp.int32, (E, T), 0)
    columns = []
    for s in range(CAP):
        mine = jnp.zeros((E, T), f32)
        for k in range(4):
            mine = jnp.where(expert + s * E == at[k : k + 1, :], across[k : k + 1, :], mine)
        columns.append(jnp.sum(mine, axis=1, keepdims=True))
    put_numbers(columns, wire)


def router(b, x0, g2, wr, ids, assign_t):
    return call(
        router_body,
        "router",
        [
            sds((T, D), f32),
            sds((T, D), bf16),
            sds((T, E), f32),
            sds((T, E), f32),
            sds((E, WIRE, 128), bf16),
        ],
        [pltpu.VMEM((SLOTS, D), bf16)],
        (*b, x0, g2, wr, ids, assign_t),
    )


def expert_grad_body(wire, wd, gr, ga):
    split_rows(wire, gr)

    def body(i, carry):
        cols = pl.ds(pl.multiple_of(i * 256, 256), 256)
        ga[:, cols] = dot_t(gr[...], wd[cols, :])
        return carry

    lax.fori_loop(0, F // 256, body, 0)


def expert_grad(wire, wd):
    return call(
        expert_grad_body,
        "expert_grad_rows",
        [sds((SLOTS, D), bf16), sds((SLOTS, F), f32)],
        [],
        (wire, wd),
    )


def expert_main_body(
    wire, wg, wu, ga, back, xs, act, acts, dg, du,
    wire_v, w_v, ga_v, xr, xs_v, act_v, acts_v, d_v, sc, sems,
):
    half = F // 2

    def copy(source, dest, number):
        return pltpu.make_async_copy(source, dest, sems.at[number])

    first = copy(wire, wire_v, 0)
    first.start()
    arrivals = []
    for c in range(2):
        cols = slice(c * half, (c + 1) * half)
        up_cols = slice(F + c * half, F + (c + 1) * half)
        group = [
            copy(wg.at[:, cols], w_v.at[:, cols], 1 + 3 * c),
            copy(wu.at[:, cols], w_v.at[:, up_cols], 2 + 3 * c),
            copy(ga.at[:, cols], ga_v.at[:, cols], 3 + 3 * c),
        ]
        for item in group:
            item.start()
        arrivals.append(group)
    first.wait()
    split_rows(wire_v, xr)
    gates = get_numbers(wire_v)
    sc[...] = jnp.zeros_like(sc)
    for c in range(2):
        for item in arrivals[c]:
            item.wait()
        cols = slice(c * half, (c + 1) * half)
        up_cols = slice(F + c * half, F + (c + 1) * half)
        gate = dot(xr[...], w_v[:, cols])
        up = dot(xr[...], w_v[:, up_cols])
        grad = ga_v[:, cols]
        s = 1.0 / (1.0 + jnp.exp(-gate))
        silu = gate * s
        a = silu * up
        act_v[:, cols] = a.astype(bf16)
        d_v[:, cols] = (grad * up * s * (1.0 + gate * (1.0 - s))).astype(bf16)
        d_v[:, up_cols] = (grad * silu).astype(bf16)
        sc[...] += jnp.sum(a * grad, axis=1, keepdims=True)
    departures = [copy(act_v, act, 7), copy(d_v.at[:, :F], dg, 8), copy(d_v.at[:, F:], du, 9)]
    for item in departures:
        item.start()
    for s in range(CAP):
        part = slice(s * E, (s + 1) * E)
        gate = gates[:, s : s + 1]
        xs_v[part, :] = (xr[part, :].astype(f32) * gate).astype(bf16)
        acts_v[part, :] = (act_v[part, :].astype(f32) * gate).astype(bf16)
    more = [copy(xs_v, xs, 10), copy(acts_v, acts, 11)]
    for item in more:
        item.start()
    for j in range(4):
        part = slice(j * 512, (j + 1) * 512)
        xr[:, part] = dot_t(d_v[...], w_v[part, :]).astype(bf16)
    join_rows(xr, wire_v)
    put_numbers([sc[s * E : (s + 1) * E, :] for s in range(CAP)], wire_v)
    last = copy(wire_v, back, 12)
    last.start()
    for item in departures + more + [last]:
        item.wait()


def expert_main(wire, wg, wu, ga):
    args = (wire, wg, wu, ga)
    outs = [
        sds((E, WIRE, 128), bf16),
        sds((SLOTS, D), bf16),
        sds((SLOTS, F), bf16),
        sds((SLOTS, F), bf16),
        sds((SLOTS, F), bf16),
        sds((SLOTS, F), bf16),
    ]
    return pl.pallas_call(
        expert_main_body,
        out_shape=outs,
        in_specs=[pl.BlockSpec(memory_space=pl.ANY)] * 4,
        out_specs=[pl.BlockSpec(memory_space=pl.ANY)] * 6,
        scratch_shapes=[
            pltpu.VMEM((E, WIRE, 128), bf16),
            pltpu.VMEM((D, 2 * F), bf16),
            pltpu.VMEM((SLOTS, F), f32),
            pltpu.VMEM((SLOTS, D), bf16),
            pltpu.VMEM((SLOTS, D), bf16),
            pltpu.VMEM((SLOTS, F), bf16),
            pltpu.VMEM((SLOTS, F), bf16),
            pltpu.VMEM((SLOTS, 2 * F), bf16),
            pltpu.VMEM((SLOTS, 1), f32),
            pltpu.SemaphoreType.DMA((13,)),
        ],
        compiler_params=pltpu.CompilerParams(vmem_limit_bytes=63 * 1024 * 1024),
        cost_estimate=cost(COSTS["expert_main"]),
        name="expert_main",
    )(*args)


def expert_out_body(act, wd, wire, rows):
    for j in range(8):
        cols = slice(j * 256, (j + 1) * 256)
        rows[:, cols] = dot(act[...], wd[:, cols]).astype(bf16)
    join_rows(rows, wire)


def expert_out(act, wd):
    return call(
        expert_out_body,
        "expert_out",
        [sds((E, CAP * SEG, 128), bf16)],
        [pltpu.VMEM((SLOTS, D), bf16)],
        (act, wd),
    )[0]


def combine_body(
    where, experts, slots, gate_list, wire, hidden, n2, probs, gates, ids, og, g2, wr,
    ghid, gatt, router_own, router_sib, gg2, sums, gn2, parts,
):
    sum_rows(wire, experts, slots, gate_list, sums)
    scores = get_numbers(wire)
    lane = lax.broadcasted_iota(jnp.int32, (T, E), 1)
    grads = []
    for k in range(4):
        hot = jnp.where(lane == ids[:, k : k + 1], 1.0, 0.0)
        rows = lax.dot_general(
            hot, scores, (((1,), (0,)), ((), ())),
            precision=lax.Precision.HIGHEST, preferred_element_type=f32,
        )
        picked = jnp.where(lane == ids[:, 4 + k : 5 + k], rows, 0.0)
        grads.append(jnp.sum(picked, axis=-1, keepdims=True))
    inner = sum(grads[k] * gates[:, k : k + 1] for k in range(4))
    inverse = 1.0 / gates[:, 4:5]
    grad_probs = jnp.zeros((T, E), f32)
    for k in range(4):
        grad_probs = jnp.where(
            lane == ids[:, k : k + 1], (grads[k] - inner) * inverse, grad_probs
        )
    p = probs[...]
    gl = (p * (grad_probs - jnp.sum(p * grad_probs, axis=-1, keepdims=True))).astype(bf16)
    for h in range(2):
        tokens = slice(h * 64, (h + 1) * 64)
        gn2[tokens, :] = sums[h * 1024 : (h + 1) * 1024, :].reshape(64, D)
    gn2[...] += dot_t(gl, wr[...])
    c = gn2[...]
    v = hidden[...]
    r = lax.rsqrt(jnp.mean(v * v, axis=-1, keepdims=True) + EPS)
    u = c * g2[...]
    m = jnp.mean(u * v, axis=-1, keepdims=True)
    total = og[...].astype(f32) + r * u - v * (r * r * r * m)
    ghid[...] = total
    gatt[...] = total.astype(bf16)
    gg2[...] = jnp.sum(c * (v * r), axis=0, keepdims=True)
    for j in range(SEG):
        cols = slice(j * 128, (j + 1) * 128)
        owner = j // 2
        dy = lax.rem(owner // 2 + 4 - where[3], 4)
        dc = lax.rem(owner % 2 + where[2], 2)
        half = slice((j % 2) * 128, (j % 2 + 1) * 128)
        parts[dc * 4 + dy, half, :] = dot(n2[:, cols].astype(f32).T.astype(bf16), gl).astype(bf16)
    router_own[...] = parts[0:4]
    router_sib[...] = parts[4:8]


def combine(*args):
    return call(
        combine_body,
        "combine_grads",
        [
            sds((T, D), f32),
            sds((T, D), bf16),
            sds((4, 256, E), bf16),
            sds((4, 256, E), bf16),
            sds((1, D), f32),
        ],
        [
            pltpu.VMEM((T * SEG, 128), f32),
            pltpu.VMEM((T, D), f32),
            pltpu.VMEM((8, 256, E), bf16),
        ],
        args,
        smem=(0, 1, 2, 3),
    )


def result_body(experts, slots, gate_list, wire, hidden, out, sums):
    sum_rows(wire, experts, slots, gate_list, sums)
    for h in range(2):
        tokens = slice(h * 64, (h + 1) * 64)
        mixture = sums[h * 1024 : (h + 1) * 1024, :].reshape(64, D)
        out[tokens, :] = (hidden[tokens, :] + mixture).astype(bf16)


def result_rows(*args):
    return call(
        result_body,
        "result",
        [sds((T, D), bf16)],
        [pltpu.VMEM((T * SEG, 128), f32)],
        args,
        smem=(0, 1, 2),
    )[0]


def pre_body(where, *refs):
    blocks, (ot0, ot1, wo, *outs) = refs[:8], refs[8:16]
    dt, (heads, rows_all, wo_v, grads, dt_v, sems) = refs[15], refs[16:]
    copies = Copies(sems)
    arrivals = [copies.bring(ot0, heads.at[:, :HALF]), copies.bring(ot1, heads.at[:, HALF:])]
    columns = []
    waits = []
    for step in range(4):
        start = lax.rem(where[1] + step, 4) * 512
        columns.append(pl.ds(pl.multiple_of(start, 512), 512))
        waits.append(
            [
                copies.bring(
                    blocks[b].at[:, columns[step]],
                    rows_all.at[b * T : (b + 1) * T, columns[step]],
                )
                for b in range(8)
            ]
        )
    last = copies.bring(wo, wo_v)
    for item in arrivals:
        item.wait()
    for step in range(4):
        for item in waits[step]:
            item.wait()
        grad = dot(heads[...], rows_all[:, columns[step]]).astype(bf16)
        for col in range(4):
            grads[step, lax.rem(col + 4 - where[0], 4)] = grad[:, col * 128 : (col + 1) * 128]
        copies.take(grads.at[step], outs[step])
    last.wait()
    dt_v[...] = dot_t(wo_v[...], rows_all[...]).astype(bf16)
    copies.take(dt_v, dt)
    copies.finish()


def pre(where, blocks, ot0, ot1, wo):
    return copy_call(
        pre_body,
        "out_projection_grad",
        [sds((4, 512, 128), bf16)] * 4 + [sds((LH * HEAD, ROWS), bf16)],
        [
            pltpu.VMEM((512, ROWS), bf16),
            pltpu.VMEM((ROWS, D), bf16),
            pltpu.VMEM((512, D), bf16),
            pltpu.VMEM((4, 4, 512, 128), bf16),
            pltpu.VMEM((512, ROWS), bf16),
        ],
        2 + 32 + 1 + 5,
        (where, *blocks, ot0, ot1, wo),
        smem=(0,),
    )


def bwd_body(*refs):
    qh, kh, scales = refs[0:4], refs[4:8], refs[8:12]
    (qt, kt, kn, vn, dt, ot0, ot1, linv, info, cos, sin, gq, gk) = refs[12:25]
    dq0, dq1, dkv, ggq, ggk, mask, wb, sb, dqt, dk, dv, raw, scale = refs[25:]
    for dc in range(2):
        for dy in range(4):
            to = slice(dc * HALF + dy * T, dc * HALF + (dy + 1) * T)
            scale[:, to] = scales[dy][:, dc * T : (dc + 1) * T]
    build_mask(info, mask)
    dk[...] = jnp.zeros_like(dk)
    dv[...] = jnp.zeros_like(dv)
    for half, out in ((0, ot0), (1, ot1)):
        cols = slice(half * HALF, (half + 1) * HALF)
        for h in range(LH):
            heads = slice(h * HEAD, (h + 1) * HEAD)
            part = slice(h * HALF, (h + 1) * HALF)
            scores = dot(kn[...], qt[heads, cols])
            weights = jnp.exp2(scores * LOG2E) * (mask[:, cols] * linv[h : h + 1, cols])
            grad = dt[heads, cols]
            delta = jnp.sum(
                grad.astype(f32) * out[heads, :].astype(f32), axis=0, keepdims=True
            )
            wb[:, part] = weights.astype(bf16)
            sb[:, part] = (weights * (dot(vn[...], grad) - delta)).astype(bf16)
            dqt[heads, cols] = dot(kt[...], sb[:, part])
        grads = jnp.concatenate([dt[h * HEAD : (h + 1) * HEAD, cols] for h in range(LH)], axis=1)
        queries = jnp.concatenate([qt[h * HEAD : (h + 1) * HEAD, cols] for h in range(LH)], axis=1)
        dv[...] += dot_t(wb[...], grads)
        dk[...] += dot_t(sb[...], queries)

    def unrope(v):
        low, high = v[:64], v[64:]
        c, s = cos[...], sin[...]
        return jnp.concatenate([low * c + high * s, high * c - low * s], axis=0)

    def norm_back(n, r, grad, gain):
        gain_grad = jnp.sum(grad * n, axis=1, keepdims=True)
        u = grad * gain
        return r * (u - n * jnp.mean(u * n, axis=0, keepdims=True)), gain_grad

    gain_q, gain_k = column(gq[...]), column(gk[...])
    total = jnp.zeros((HEAD, 1), f32)
    for h in range(LH):
        heads = slice(h * HEAD, (h + 1) * HEAD)
        for dy in range(4):
            for dc in range(2):
                to = slice(dc * HALF + dy * T, dc * HALF + (dy + 1) * T)
                raw[:, to] = qh[dy][heads, dc * T : (dc + 1) * T].astype(f32)
        grad, part = norm_back(raw[...], scale[h : h + 1, :], unrope(dqt[heads, :] * (HEAD ** (-0.5))), gain_q)
        total = total + part
        dq0[heads, :] = grad[:, :HALF].astype(bf16)
        dq1[heads, :] = grad[:, HALF:].astype(bf16)
    ggq[...] = jnp.broadcast_to(total, (HEAD, 128)).T[0:8, :]
    for dy in range(4):
        for dc in range(2):
            to = slice(dc * HALF + dy * T, dc * HALF + (dy + 1) * T)
            raw[:, to] = kh[dy][:, dc * T : (dc + 1) * T].astype(f32)
    grad, part = norm_back(raw[...], scale[LH : LH + 1, :], unrope(dk[...].T), gain_k)
    ggk[...] = jnp.broadcast_to(part, (HEAD, 128)).T[0:8, :]
    dkv[:HEAD, :] = grad.astype(bf16)
    dkv[HEAD:, :] = dv[...].T.astype(bf16)


def bwd(qh, kh, scales, *rest):
    return call(
        bwd_body,
        "attend_grad",
        [
            sds((LH * HEAD, HALF), bf16),
            sds((LH * HEAD, HALF), bf16),
            sds((2 * HEAD, ROWS), bf16),
            sds((8, HEAD), f32),
            sds((8, HEAD), f32),
        ],
        [
            pltpu.VMEM((ROWS, ROWS), f32),
            pltpu.VMEM((ROWS, LH * HALF), bf16),
            pltpu.VMEM((ROWS, LH * HALF), bf16),
            pltpu.VMEM((LH * HEAD, ROWS), f32),
            pltpu.VMEM((ROWS, HEAD), f32),
            pltpu.VMEM((ROWS, HEAD), f32),
            pltpu.VMEM((HEAD, ROWS), f32),
            pltpu.VMEM((8, ROWS), f32),
        ],
        (*qh, *kh, *scales, *rest),
    )


def qkv_grad_body(where, n1t, dq0, dq1, own, sib, out, tot, dt):
    @pl.when(pl.program_id(0) == 0)
    def _():
        tot[:, :HALF] = (own[:, :HALF].astype(f32) + sib[:, HALF:].astype(f32)).astype(bf16)
        tot[:, HALF:] = (own[:, HALF:].astype(f32) + sib[:, :HALF].astype(f32)).astype(bf16)
        dt[:512, :HALF] = dq0[...]
        dt[:512, HALF:] = dq1[...]
        upper = where[2] == 1
        dt[512:576, :] = jnp.where(upper, tot[64:128, :], tot[:64, :])
        dt[576:, :] = jnp.where(upper, tot[192:, :], tot[128:192, :])

    out[...] = dot_t(n1t[...], dt[...]).astype(bf16)


def qkv_grad(where, n1t, dq0, dq1, own, sib):
    return grid_call(
        qkv_grad_body,
        "qkv_weight_grad",
        (2,),
        [
            rows_of((1024, ROWS)),
            whole((512, HALF)),
            whole((512, HALF)),
            whole((2 * HEAD, ROWS)),
            whole((2 * HEAD, ROWS)),
        ],
        [rows_of((1024, 640)), whole((2 * HEAD, ROWS))],
        [sds((D, 640), bf16), sds((2 * HEAD, ROWS), bf16)],
        [pltpu.VMEM((640, ROWS), bf16)],
        (where, n1t, dq0, dq1, own, sib),
        scalars=1,
    )


def widen_body(grads, gq, gkt, gvt):
    gq[...] = grads[:, :512].astype(f32)
    both = grads[:, 512:].astype(f32).T
    gkt[...] = both[:64]
    gvt[...] = both[64:]


def widen(grads):
    return grid_call(
        widen_body,
        "widen_grads",
        (4,),
        [rows_of((512, 640))],
        [rows_of((512, 512)), cols_of((64, 512)), cols_of((64, 512))],
        [sds((D, 512), f32), sds((64, D), f32), sds((64, D), f32)],
        [],
        (grads,),
    )


def add_body(a, b, c, d, *outs):
    for i, out in enumerate(outs):
        out[...] = (
            (a[i].astype(f32) + b[i].astype(f32)) + (c[i].astype(f32) + d[i].astype(f32))
        ).astype(bf16)


def add_parts(parts):
    shape = parts[0].shape[1:]
    return call(add_body, "add_parts", [sds(shape, bf16)] * 4, [], tuple(parts))


def split_two(v):
    first = v.astype(bf16)
    return first, (v - first.astype(f32)).astype(bf16)


def normed_grad_body(
    wa, wb, wkv, dq0, dqr, tot, n0, n1, n2, n3, gg2, ggq, ggk, ra, rb, b0, b1, b2, b3, grads
):
    step = pl.program_id(0)

    @pl.when(step == 0)
    def _():
        flip(dq0, grads, 0, 0)
        flip(dqr, grads, 0, 512)
        flip(tot, grads, 0, 1024)

    total = (
        dot(grads[:, :512], wa[...])
        + dot(grads[:, 512:1024], wb[...])
        + dot(grads[:, 1024:], wkv[...])
    )
    gain = jnp.zeros((1, 512), f32)
    outs = (b0, b1, b2, b3)
    for dy, (out, rows) in enumerate(zip(outs, (n0, n1, n2, n3))):
        part = total[dy * T : (dy + 1) * T, :]
        out[:T, :] = part.astype(bf16)
        gain = gain + jnp.sum(part * rows[...].astype(f32), axis=0, keepdims=True)
    heads = jnp.concatenate([ggq[0:1, :], ggk[0:1, :], jnp.zeros((1, 256), f32)], axis=1)
    numbers = [*split_two(gain), *split_two(gg2[...]), *split_two(heads)]
    extra = jnp.concatenate([n.astype(f32) for n in numbers] + [jnp.zeros((10, 512), f32)], axis=0)
    for dy, out in enumerate(outs):
        out[T : T + 16, :] = extra.astype(bf16)
        for q in range(4):
            rows = pl.ds(pl.multiple_of(step * 64 + q * 16, 16), 16)
            both = ra[dy, rows, :].astype(f32) + rb[dy, rows, :].astype(f32)
            out[T + 16 :, q * 128 : (q + 1) * 128] = both.astype(bf16)


def normed_grad(wa, wb, wkv, dq0, dqr, tot, n1, gg2, ggq, ggk, ra, rb):
    return grid_call(
        normed_grad_body,
        "normed_grad",
        (4,),
        [
            cols_of((512, 512)),
            cols_of((512, 512)),
            cols_of((256, 512)),
            whole((512, HALF)),
            whole((512, HALF)),
            whole((2 * HEAD, HALF)),
        ]
        + [cols_of((T, 512))] * 4
        + [cols_of((1, 512)), whole((8, HEAD)), whole((8, HEAD))]
        + [whole((4, 256, E))] * 2,
        [cols_of((T + 32, 512))] * 4,
        [sds((T + 32, D), bf16)] * 4,
        [pltpu.VMEM((HALF, 1280), bf16)],
        (wa, wb, wkv, dq0, dqr, tot, *n1, gg2, ggq, ggk, ra, rb),
    )


def add_last_body(a, b, c, d, out):
    out[...] = (
        (a[...].astype(f32) + b[...].astype(f32)) + (c[...].astype(f32) + d[...].astype(f32))
    ).astype(bf16)


def add_last(parts):
    return call(add_last_body, "add_last", [sds(parts[0].shape, bf16)], [], tuple(parts))


def stack_body(a, b, c, d, out):
    for i, part in enumerate((a, b, c, d)):
        out[i] = part[...]


def stack(parts):
    shape = (4, *parts[0].shape)
    return call(stack_body, "stack_parts", [sds(shape, bf16)], [], tuple(parts))[0]


def place_out_body(where, c0, c1, c2, c3, out):
    for dx, chunks in enumerate((c0, c1, c2, c3)):
        for dz in range(4):
            chunk = lax.rem(where[1] + dx, 4) * 4 + lax.rem(where[0] + dz, 4)
            cols = pl.ds(pl.multiple_of(chunk * 128, 128), 128)
            out[:, cols] = chunks[dz].astype(f32)


def place_out(where, chunks):
    return call(
        place_out_body,
        "place_output_grads",
        [sds((512, D), f32)],
        [],
        (where, *chunks),
        smem=(0,),
    )[0]


def final_body(b0, b1, b2, b3, x0, ghid, g1, out, small):
    whole_sum = (b0[...].astype(f32) + b1[...].astype(f32)) + (
        b2[...].astype(f32) + b3[...].astype(f32)
    )
    c = whole_sum[:T]
    v = x0[...].astype(f32)
    r = lax.rsqrt(jnp.mean(v * v, axis=-1, keepdims=True) + EPS)
    u = c * g1[...]
    m = jnp.mean(u * v, axis=-1, keepdims=True)
    out[...] = ghid[...] + r * u - v * (r * r * r * m)
    extra = whole_sum[T : T + 16]
    numbers = [
        *split_two((extra[0:1] + extra[1:2]) / g1[...]),
        *split_two(extra[2:3] + extra[3:4]),
        *split_two(extra[4:5] + extra[5:6]),
    ]
    rows = jnp.concatenate(
        [whole_sum[T + 16 :]] + [n.astype(f32) for n in numbers] + [jnp.zeros((2, D), f32)],
        axis=0,
    ).astype(bf16)
    for e in range(16):
        small[e] = rows[:, e * 128 : (e + 1) * 128]


def final(b, x0, ghid, g1):
    return call(
        final_body,
        "input_grad",
        [sds((T, D), f32), sds((16, 24, 128), bf16)],
        [],
        (*b, x0, ghid, g1),
    )


def fold_body(parts, out):
    total = parts[0].astype(f32)
    for e in range(1, 16):
        total = total + parts[e].astype(f32)
    numbers = []
    for k in range(3):
        row = SEG + 2 * k
        numbers += split_two(total[row : row + 1] + total[row + 1 : row + 2])
    rows = jnp.concatenate(
        [total[:SEG]] + [n.astype(f32) for n in numbers] + [jnp.zeros((2, 128), f32)], axis=0
    ).astype(bf16)

    def body(i, carry):
        out[i] = rows
        return carry

    lax.fori_loop(0, E, body, 0)


def fold(parts):
    return call(fold_body, "fold_small", [sds((E, 24, 128), bf16)], [], (parts,))[0]


def sibling(x):
    return lax.ppermute(x, "shard", [(i, i ^ 1) for i in range(8)])


def from_chip(x, dy):
    return lax.ppermute(x, "shard", [(i, (i - 2 * dy) % 8) for i in range(8)])


def to_chip(x, dy):
    return lax.ppermute(x, "shard", [(i, (i + 2 * dy) % 8) for i in range(8)])


def exchange(x):
    return lax.all_to_all(x, ALL, split_axis=0, concat_axis=0, tiled=True)


def spread(x):
    return [to_chip(x[d], d) for d in (1, 3, 2)]


def on_expert(x, dz, dx):
    pairs = [
        (z * 4 + c, ((z + dz) % 4) * 4 + (c + dx) % 4) for z in range(4) for c in range(4)
    ]
    return lax.ppermute(x, "expert", pairs)


def move(x, axis, distance):
    return on_expert(x, distance, 0) if axis == 0 else on_expert(x, 0, distance)


def collect(parts, axis):
    return [parts[0]] + [move(parts[d], axis, d) for d in (1, 3, 2)]


def share(x, axis):
    return [x] + [move(x, axis, (4 - d) % 4) for d in (1, 2, 3)]


def after(value, *others):
    return lax.optimization_barrier((value, *others))[0]


def on_device(
    block_input, out_grad, norm1_gain, w_query, w_key, w_value, query_gain, key_gain, w_out,
    norm2_gain, w_router, w_gate, w_up, w_down, seq_lengths, token_places, expert_routes,
):
    shard, owner = lax.axis_index("shard"), lax.axis_index("expert")
    chip, core = shard // 2, shard % 2
    where = jnp.stack([owner // 4, owner % 4, core, chip]).astype(jnp.int32)
    core_id = core.reshape(1)
    g1 = norm1_gain.astype(f32).reshape(1, D)
    g2 = norm2_gain.astype(f32).reshape(1, D)
    gq = query_gain.astype(f32).reshape(1, HEAD)
    gk = key_gain.astype(f32).reshape(1, HEAD)

    x_own = [block_input] + [from_chip(block_input, dy) for dy in (1, 2, 3)]
    x_sib = [sibling(block_input)]

    chips = (chip + jnp.arange(4)) % 4
    order = jnp.concatenate([chips * 2 + core, chips * 2 + 1 - core])
    places = token_places[0].reshape(8, T)[order].reshape(ROWS)
    lengths = seq_lengths[0]
    ends = jnp.cumsum(lengths)
    starts = jnp.sum(
        jnp.where(places[:, None] >= ends[None, :], lengths[None, :], 0), axis=1
    )
    positions = (places - starts).astype(f32)
    info = jnp.concatenate(
        [places[None].astype(f32), starts[None].astype(f32), jnp.zeros((6, ROWS), f32)], axis=0
    )
    inverse_freq = ROPE_BASE ** (-jnp.arange(0, HEAD, 2).astype(f32) / HEAD)
    angles = inverse_freq[:, None] * positions[None, :]
    cos, sin = jnp.cos(angles), jnp.sin(angles)

    ids, ids_t = route_tables(expert_routes.T)
    assign_t = ids_t[8:12]
    expert_list = ids[:, 0:4].reshape(-1)
    slot_list = ids[:, 4:8].reshape(-1)

    wk_t, wv_t = w_key.T, w_value.T
    wk_s, wv_s = sibling(wk_t), sibling(wv_t)
    wq_t = w_query.T
    wo_s = sibling(w_out)
    wq_ts = sibling(wq_t)

    weights = (g1, wq_t, wk_t, wk_s, wv_t, wv_s, gq, gk, cos, sin)
    zero = qkv((0,), core_id, (x_own[0], x_sib[0]), *weights)
    og_wire = pack(out_grad, assign_t)
    x_own[1], x_own[2], x_own[3], q_first, og_wire = lax.optimization_barrier(
        (x_own[1], x_own[2], x_own[3], zero[1], og_wire)
    )
    x_sib += [sibling(x_own[dy]) for dy in (1, 2, 3)]
    blocks = [side[dy] for dy in (1, 2, 3) for side in (x_own, x_sib)]
    others = qkv((1, 2, 3), core_id, blocks, *weights)
    wkv = zero[7]
    pieces = [zero[:7], others[:7], others[7:14], others[14:21]]
    qh, q, kh, k, v, scales, n1 = zip(*pieces)
    q = (q_first,) + q[1:]
    got_grads = exchange(og_wire)
    ot0, ot1, linv, qt, kt, kn, vn = attend(q, k, v, info)
    blocks = outproj(ot0, sibling(ot1), w_out, wo_s)
    blocks = [blocks[0]] + spread(blocks)
    hidden, n2, probs, gates, wire = router(blocks, block_input, g2, w_router, ids, assign_t)
    got_rows = exchange(wire)

    n1_t = transpose_rows(after(n1, wire))
    gate_list = gates[:, :4].reshape(-1)
    grad_rows, grad_act = expert_grad(after(got_grads, wire), w_down[0])
    got_rows, n1_t, grad_act, gate_list, wq_ts = lax.optimization_barrier(
        (got_rows, n1_t, grad_act, gate_list, wq_ts)
    )

    back, rows, act, scaled_act, dg, du = expert_main(got_rows, w_gate[0], w_up[0], grad_act)
    back_wire = exchange(back)

    rows, act, scaled_act, dg, du = after((rows, act, scaled_act, dg, du), back)
    out_wire = expert_out(act, w_down[0])

    def weight_grad(a, b):
        return lax.dot_general(a, b, (((0,), (0,)), ((), ())), preferred_element_type=f32)

    grad_wgate = weight_grad(rows, dg)
    grad_wup = weight_grad(rows, du)
    grad_wdown = weight_grad(scaled_act, grad_rows)
    back_wire, out_wire, grad_wgate, grad_wup, grad_wdown = lax.optimization_barrier(
        (back_wire, out_wire, grad_wgate, grad_wup, grad_wdown)
    )

    ghid, gatt, router_own, router_sib, gg2 = combine(
        where, expert_list, slot_list, gate_list, back_wire, hidden, n2, probs, gates, ids,
        out_grad, g2, w_router,
    )
    g_own = [gatt] + [from_chip(gatt, dy) for dy in (1, 2, 3)]
    g_sib = [sibling(block) for block in g_own]
    *out_parts, dt = pre(where, g_own + g_sib, ot0, ot1, w_out)

    dq0, dq1, dkv, ggq, ggk = bwd(
        qh, kh, scales, qt, kt, kn, vn, dt, ot0, ot1, linv, info, cos, sin, gq, gk
    )
    out_parts, dq1, dkv = lax.optimization_barrier((collect(out_parts, 1), dq1, dkv))
    router_sib = after(router_sib, dkv)
    dq_sib, dkv_sib = sibling(dq1), sibling(dkv)
    gw, dkv_total = qkv_grad(where, n1_t, dq0, dq1, dkv, dkv_sib)
    returned = exchange(after(out_wire, dkv_total))
    router_rec = sibling(router_sib)
    blocks = normed_grad(
        wq_t, wq_ts, wkv, dq0, dq_sib, dkv_total, n1, gg2, ggq, ggk, router_own, router_rec
    )
    blocks = [blocks[0]] + spread(blocks)

    gw = lax.psum(gw, "expert")
    out_parts = collect(add_parts(out_parts), 0)
    chunks = share(add_last(out_parts)[0], 0)
    chunks, blocks = lax.optimization_barrier((chunks, blocks))
    chunks = share(stack(chunks), 1)
    grad_input, small = final(blocks, block_input, ghid, g1)
    small, returned = lax.optimization_barrier((small, returned))
    result = result_rows(expert_list, slot_list, gate_list, returned, hidden)
    small = lax.all_to_all(small, "expert", split_axis=0, concat_axis=0, tiled=True)
    small, chunks = lax.optimization_barrier((small, chunks))
    small = exchange(fold(small))
    grad_wout = place_out(where, chunks)
    gw, small, grad_input, grad_wout, result = lax.optimization_barrier(
        (gw, small, grad_input, grad_wout, result)
    )
    grad_wq, grad_wk, grad_wv = widen(gw)
    small = small.reshape(16, 8, 24, 128).astype(f32)
    grad_router = small[:, :, :SEG].transpose(1, 0, 2, 3).reshape(D, E)
    gains = small[:, 0, SEG:] + small[:, 1, SEG:]
    gains = [(gains[:, 2 * k] + gains[:, 2 * k + 1]).reshape(D) for k in range(3)]
    return (
        result,
        grad_input,
        gains[0],
        grad_wq,
        grad_wk.T,
        grad_wv.T,
        gains[2][:HEAD],
        gains[2][HEAD : 2 * HEAD],
        grad_wout,
        gains[1],
        grad_router,
        grad_wgate[None],
        grad_wup[None],
        grad_wdown[None],
    )


def solution(mesh):
    rows = P(("expert", "shard"), None)
    experts = P(("expert", "shard"), None, None)
    columns = P(None, "shard")
    return jax.shard_map(
        on_device,
        mesh=mesh,
        in_specs=(
            rows, rows, P(), columns, columns, columns, P(), P(), P("shard", None), P(), P(),
            experts, experts, experts, P("expert", None), P("expert", None), rows,
        ),
        out_specs=(
            rows, rows, P(), columns, columns, columns, P(), P(), P("shard", None), P(), P(),
            experts, experts, experts,
        ),
        check_vma=False,
    )
```

```python
import functools

import jax
import jax.numpy as jnp
from jax import lax
from jax.experimental import pallas as pl
from jax.experimental.pallas import tpu as pltpu
from jax.sharding import PartitionSpec as P

EPS = 1e-06
ROPE_BASE = 1000000.0
LOG2E = 1.4426950408889634
T = 128
D = 2048
HEAD = 128
LH = 4
E = 128
CAP = 5
SLOTS = E * CAP
SEG = D // 128
WIRE = CAP * SEG + 8
ROWS = 1024
HALF = 512
F = 768
bf16 = jnp.bfloat16
f32 = jnp.float32
ALL = ("expert", "shard")
COSTS = {
    "attend": 11,
    "out_projection": 5,
    "router": 6,
    "transpose_rows": 6,
    "expert_grad_rows": 8,
    "expert_main": 18,
    "expert_out": 7,
    "combine_grads": 7,
    "head_grad": 4,
    "out_projection_grad": 7,
}


def cost(micros):
    return pl.CostEstimate(
        flops=1, bytes_accessed=int(micros * 0.6e6) + 1, transcendentals=0
    )


def dot(a, b):
    return jnp.dot(a, b, preferred_element_type=f32)


def dot_t(a, b):
    return lax.dot_general(a, b, (((1,), (1,)), ((), ())), preferred_element_type=f32)


def call(kernel, name, outs, scratch, args, smem=()):
    in_specs = [
        pl.BlockSpec(memory_space=pltpu.SMEM if i in smem else pltpu.VMEM)
        for i in range(len(args))
    ]
    return pl.pallas_call(
        kernel,
        out_shape=outs,
        in_specs=in_specs,
        out_specs=[pl.BlockSpec(memory_space=pltpu.VMEM) for _ in outs],
        scratch_shapes=scratch,
        compiler_params=pltpu.CompilerParams(vmem_limit_bytes=63 * 1024 * 1024),
        cost_estimate=cost(COSTS.get(name, 0)),
        name=name,
    )(*args)


def grid_call(kernel, name, grid, in_specs, out_specs, outs, scratch, args, scalars=0):
    return pl.pallas_call(
        kernel,
        out_shape=outs,
        grid_spec=pltpu.PrefetchScalarGridSpec(
            num_scalar_prefetch=scalars,
            grid=grid,
            in_specs=in_specs,
            out_specs=out_specs,
            scratch_shapes=scratch,
        ),
        compiler_params=pltpu.CompilerParams(
            vmem_limit_bytes=63 * 1024 * 1024, dimension_semantics=("arbitrary",)
        ),
        cost_estimate=cost(COSTS.get(name, 0)),
        name=name,
    )(*args)


def copy_call(kernel, name, outs, scratch, copies, args, smem=()):
    return pl.pallas_call(
        kernel,
        out_shape=outs,
        in_specs=[
            pl.BlockSpec(memory_space=pltpu.SMEM if i in smem else pl.ANY)
            for i in range(len(args))
        ],
        out_specs=[pl.BlockSpec(memory_space=pl.ANY)] * len(outs),
        scratch_shapes=[*scratch, pltpu.SemaphoreType.DMA((copies,))],
        compiler_params=pltpu.CompilerParams(vmem_limit_bytes=63 * 1024 * 1024),
        cost_estimate=cost(COSTS.get(name, 0)),
        name=name,
    )(*args)


class Copies:
    def __init__(self, sems):
        self.sems, self.count, self.leaving = sems, 0, []

    def bring(self, source, dest):
        item = pltpu.make_async_copy(source, dest, self.sems.at[self.count])
        self.count += 1
        item.start()
        return item

    def take(self, source, dest):
        self.leaving.append(self.bring(source, dest))

    def finish(self):
        for item in self.leaving:
            item.wait()


def whole(shape):
    return pl.BlockSpec(shape, lambda i, *_: (0,) * len(shape))


def rows_of(shape):
    return pl.BlockSpec(shape, lambda i, *_: (i, 0))


def cols_of(shape):
    return pl.BlockSpec(shape, lambda i, *_: (0, i))


def sds(shape, dtype):
    return jax.ShapeDtypeStruct(shape, dtype)


def split_rows(wire, dest):
    for s in range(CAP):
        for h in range(2):
            rows = slice(s * E + h * 64, s * E + (h + 1) * 64)
            block = wire[h * 64 : (h + 1) * 64, s * SEG : (s + 1) * SEG, :]
            dest[rows, :] = block.reshape(64, D)


def join_rows(source, wire):
    for s in range(CAP):
        for h in range(2):
            rows = slice(s * E + h * 64, s * E + (h + 1) * 64)
            wire[h * 64 : (h + 1) * 64, s * SEG : (s + 1) * SEG, :] = source[rows, :].reshape(
                64, SEG, 128
            )


def put_numbers(columns, wire):
    lane = lax.broadcasted_iota(jnp.int32, (E, 128), 1)
    plane = jnp.zeros((E, 128), f32)
    for s in range(CAP):
        plane = jnp.where(lane == s, columns[s], plane)
    first = plane.astype(bf16)
    rest = plane - first.astype(f32)
    second = rest.astype(bf16)
    third = (rest - second.astype(f32)).astype(bf16)
    none = jnp.zeros((E, 5 * 128), bf16)
    wide = jnp.concatenate([first, second, third, none], axis=1)
    wire[:, CAP * SEG :, :] = wide.reshape(E, 8, 128)


def get_numbers(wire):
    wide = wire[:, CAP * SEG :, :].reshape(E, 8 * 128)
    return (
        wide[:, :128].astype(f32) + wide[:, 128:256].astype(f32) + wide[:, 256:384].astype(f32)
    )


def pack_rows(x_ref, at_ref, wire, rows):
    slot = lax.broadcasted_iota(jnp.int32, (SLOTS, T), 0)
    hit = slot == at_ref[0:1, :]
    for k in range(1, 4):
        hit = hit | (slot == at_ref[k : k + 1, :])
    pick = jnp.where(hit, 1.0, 0.0).astype(bf16)
    for j in range(8):
        cols = slice(j * 256, (j + 1) * 256)
        rows[:, cols] = dot(pick, x_ref[:, cols]).astype(bf16)
    join_rows(rows, wire)


def pack_body(x_ref, at_ref, wire, rows):
    pack_rows(x_ref, at_ref, wire, rows)
    wire[:, CAP * SEG :, :] = jnp.zeros((E, 8, 128), bf16)


def pack(x, assign_t):
    return call(
        pack_body,
        "pack_rows",
        [sds((E, WIRE, 128), bf16)],
        [pltpu.VMEM((SLOTS, D), bf16)],
        (x, assign_t),
    )[0]


def sum_rows(wire, experts, slots, gates, out):
    def body(i, carry):
        for u in range(8):
            t = i * 8 + u
            total = None
            for k in range(4):
                p = t * 4 + k
                rows = pl.ds(pl.multiple_of(slots[p] * SEG, SEG), SEG)
                part = wire[experts[p], rows, :].astype(f32) * gates[p]
                total = part if total is None else total + part
            out[pl.ds(pl.multiple_of(t * SEG, SEG), SEG), :] = total
        return carry

    lax.fori_loop(0, T // 8, body, 0)


def column(row):
    return jnp.broadcast_to(row, (128, 128)).T[:, 0:1]


def qkv_body(pieces, *refs):
    count = len(pieces)
    core, blocks = refs[0], refs[1 : 1 + 2 * count]
    g1, wqt, wk, wks, wv, wvs, gq, gk, cos, sin = refs[1 + 2 * count : 11 + 2 * count]
    outs = refs[11 + 2 * count :]
    wkv = outs[-1]
    lower = core[0] == 0
    wkv[0:64, :] = jnp.where(lower, wk[...], wks[...])
    wkv[64:128, :] = jnp.where(lower, wks[...], wk[...])
    wkv[128:192, :] = jnp.where(lower, wv[...], wvs[...])
    wkv[192:256, :] = jnp.where(lower, wvs[...], wv[...])
    gain_q, gain_k = column(gq[...]), column(gk[...])
    for number, piece in enumerate(pieces):
        qn, qt, kn, kt, vt, scale, n1 = outs[7 * number : 7 * number + 7]
        for half in range(2):
            x = blocks[2 * number + half][...].astype(f32)
            r = lax.rsqrt(jnp.mean(x * x, axis=-1, keepdims=True) + EPS)
            n1[half * T : (half + 1) * T, :] = (x * r * g1[...]).astype(bf16)
        raw = dot_t(wqt[...], n1[...])
        raw_kv = dot_t(wkv[...], n1[...])
        first, second = piece * T, HALF + piece * T
        c = jnp.concatenate([cos[:, first : first + T], cos[:, second : second + T]], axis=1)
        s = jnp.concatenate([sin[:, first : first + T], sin[:, second : second + T]], axis=1)

        def path(v, gain, factor, keep, index):
            r = lax.rsqrt(jnp.mean(v * v, axis=0, keepdims=True) + EPS)
            scale[index : index + 1, :] = r
            v = v * r
            keep[...] = v.astype(bf16)
            v = v * gain
            low, high = v[:64], v[64:]
            return (
                ((low * c - high * s) * factor).astype(bf16),
                ((high * c + low * s) * factor).astype(bf16),
            )

        scale[...] = jnp.zeros_like(scale)
        for h in range(LH):
            heads = slice(h * HEAD, (h + 1) * HEAD)
            low, high = path(raw[heads], gain_q, HEAD ** (-0.5), qn.at[heads, :], h)
            qt[h * HEAD : h * HEAD + 64, :] = low
            qt[h * HEAD + 64 : (h + 1) * HEAD, :] = high
        key = raw_kv[:HEAD].astype(bf16)
        low, high = path(key.astype(f32), gain_k, 1.0, kn, LH)
        kt[:64, :] = low
        kt[64:, :] = high
        vt[...] = raw_kv[HEAD:].astype(bf16)


def qkv(pieces, core, blocks, *args):
    outs = [
        sds((LH * HEAD, 2 * T), bf16),
        sds((LH * HEAD, 2 * T), bf16),
        sds((HEAD, 2 * T), bf16),
        sds((HEAD, 2 * T), bf16),
        sds((HEAD, 2 * T), bf16),
        sds((8, 2 * T), f32),
        sds((2 * T, D), bf16),
    ] * len(pieces)
    keep = 0 in pieces
    return call(
        functools.partial(qkv_body, pieces),
        "qkv" + "".join(str(p) for p in pieces),
        outs + ([sds((2 * HEAD, D), bf16)] if keep else []),
        [] if keep else [pltpu.VMEM((2 * HEAD, D), bf16)],
        (core, *blocks, *args),
        smem=(0,),
    )


def build_mask(info, mask):
    for b in range(8):
        keys = jnp.broadcast_to(info[0:1, b * T : (b + 1) * T], (T, T)).T
        for j in range(8):
            cols = slice(j * T, (j + 1) * T)
            inside = (keys >= info[1:2, cols]) & (keys <= info[0:1, cols])
            mask[b * T : (b + 1) * T, cols] = jnp.where(inside, 1.0, 0.0)


def attend_body(*refs):
    q, k, v = refs[0:4], refs[4:8], refs[8:12]
    info, ot0, ot1, linv, qt, kt, kn, vn, mask, vt = refs[12:]
    for dy in range(4):
        for dc in range(2):
            to = slice(dc * HALF + dy * T, dc * HALF + (dy + 1) * T)
            src = slice(dc * T, (dc + 1) * T)
            qt[:, to] = q[dy][:, src]
            kt[:, to] = k[dy][:, src]
            vt[:, to] = v[dy][:, src]
    for b in range(8):
        rows = slice(b * T, (b + 1) * T)
        kn[rows, :] = kt[:, rows].astype(f32).T.astype(bf16)
        vn[rows, :] = vt[:, rows].astype(f32).T.astype(bf16)
    build_mask(info, mask)
    for half, out in ((1, ot1), (0, ot0)):
        cols = slice(half * HALF, (half + 1) * HALF)
        for h in range(LH):
            heads = slice(h * HEAD, (h + 1) * HEAD)
            scores = dot(kn[...], qt[heads, cols])
            weights = jnp.exp2(scores * LOG2E) * mask[:, cols]
            inverse = 1.0 / jnp.sum(weights, axis=0, keepdims=True)
            out[heads, :] = (dot(vt[...], weights.astype(bf16)) * inverse).astype(bf16)
            linv[h : h + 1, cols] = inverse


def attend(q, k, v, info):
    return call(
        attend_body,
        "attend",
        [
            sds((LH * HEAD, HALF), bf16),
            sds((LH * HEAD, HALF), bf16),
            sds((8, ROWS), f32),
            sds((LH * HEAD, ROWS), bf16),
            sds((HEAD, ROWS), bf16),
            sds((ROWS, HEAD), bf16),
            sds((ROWS, HEAD), bf16),
        ],
        [pltpu.VMEM((ROWS, ROWS), f32), pltpu.VMEM((HEAD, ROWS), bf16)],
        (*q, *k, *v, info),
    )


def flip(source, dest, row, col):
    height, width = source.shape
    for a in range(height // 128):
        for b in range(width // 128):
            block = source[a * 128 : (a + 1) * 128, b * 128 : (b + 1) * 128]
            rows = slice(row + b * 128, row + (b + 1) * 128)
            dest[rows, col + a * 128 : col + (a + 1) * 128] = block.astype(f32).T.astype(bf16)


def outproj_body(ot0, otr, wa, wb, b0, b1, b2, b3, heads):
    @pl.when(pl.program_id(0) == 0)
    def _():
        flip(ot0, heads, 0, 0)
        flip(otr, heads, 0, 512)

    total = dot(heads[:, :512], wa[...]) + dot(heads[:, 512:], wb[...])
    for dy, out in enumerate((b0, b1, b2, b3)):
        out[...] = total[dy * T : (dy + 1) * T, :].astype(bf16)


def outproj(ot0, otr, wa, wb):
    return grid_call(
        outproj_body,
        "out_projection",
        (2,),
        [whole((512, HALF)), whole((512, HALF)), cols_of((512, 1024)), cols_of((512, 1024))],
        [cols_of((T, 1024))] * 4,
        [sds((T, D), bf16)] * 4,
        [pltpu.VMEM((HALF, 1024), bf16)],
        (ot0, otr, wa, wb),
    )


def transpose_body(n0, n1, n2, n3, out):
    for dy, piece in enumerate((n0, n1, n2, n3)):
        for dc in range(2):
            flip(piece.at[dc * T : (dc + 1) * T, :], out, 0, dc * HALF + dy * T)


def transpose_rows(pieces):
    return call(transpose_body, "transpose_rows", [sds((D, ROWS), bf16)], [], tuple(pieces))[0]


def route_body(rt, ids, ids_t):
    lane = lax.broadcasted_iota(jnp.int32, (T, E), 1)
    row = lax.broadcasted_iota(jnp.int32, (T, E), 0)
    wide = jnp.concatenate([rt[...].astype(f32), jnp.zeros((124, T), f32)], axis=0).T
    hot = [jnp.where(lane.astype(f32) == wide[:, k : k + 1], 1.0, 0.0) for k in range(4)]
    earlier = jnp.where(lane < row, 1.0, 0.0).astype(bf16)
    before = dot(earlier, (hot[0] + hot[1] + hot[2] + hot[3]).astype(bf16))
    table = wide
    for k in range(4):
        slot = jnp.sum(before * hot[k], axis=1, keepdims=True)
        table = jnp.where(lane == 4 + k, slot, table)
        table = jnp.where(lane == 8 + k, slot * E + wide[:, k : k + 1], table)
    ids[...] = table.astype(jnp.int32)
    ids_t[...] = table.T[0:16, :].astype(jnp.int32)


def route_tables(routes_t):
    return call(
        route_body,
        "route_tables",
        [sds((T, 128), jnp.int32), sds((16, T), jnp.int32)],
        [],
        (routes_t,),
    )


def router_body(b0, b1, b2, b3, x0, g2, wr, ids, at, hidden, n2, probs, gates, wire, rows):
    v = x0[...].astype(f32) + (
        (b0[...].astype(f32) + b1[...].astype(f32))
        + (b2[...].astype(f32) + b3[...].astype(f32))
    )
    hidden[...] = v
    r = lax.rsqrt(jnp.mean(v * v, axis=-1, keepdims=True) + EPS)
    n2[...] = (v * r * g2[...]).astype(bf16)
    logits = dot(n2[...], wr[...])
    pack_rows(n2, at, wire, rows)
    expo = jnp.exp(logits - jnp.max(logits, axis=-1, keepdims=True))
    p = expo / jnp.sum(expo, axis=-1, keepdims=True)
    probs[...] = p
    lane = lax.broadcasted_iota(jnp.int32, (T, E), 1)
    chosen = [
        jnp.sum(jnp.where(lane == ids[:, k : k + 1], p, 0.0), axis=-1, keepdims=True)
        for k in range(4)
    ]
    total = chosen[0] + chosen[1] + chosen[2] + chosen[3]
    packed = jnp.where(lane == 4, total, 0.0)
    for k in range(4):
        packed = jnp.where(lane == k, chosen[k] / total, packed)
    gates[...] = packed
    across = packed.T
    expert = lax.broadcasted_iota(jnp.int32, (E, T), 0)
    columns = []
    for s in range(CAP):
        mine = jnp.zeros((E, T), f32)
        for k in range(4):
            mine = jnp.where(expert + s * E == at[k : k + 1, :], across[k : k + 1, :], mine)
        columns.append(jnp.sum(mine, axis=1, keepdims=True))
    put_numbers(columns, wire)


def router(b, x0, g2, wr, ids, assign_t):
    return call(
        router_body,
        "router",
        [
            sds((T, D), f32),
            sds((T, D), bf16),
            sds((T, E), f32),
            sds((T, E), f32),
            sds((E, WIRE, 128), bf16),
        ],
        [pltpu.VMEM((SLOTS, D), bf16)],
        (*b, x0, g2, wr, ids, assign_t),
    )


def expert_grad_body(wire, wd, gr, ga):
    split_rows(wire, gr)

    def body(i, carry):
        cols = pl.ds(pl.multiple_of(i * 256, 256), 256)
        ga[:, cols] = dot_t(gr[...], wd[cols, :])
        return carry

    lax.fori_loop(0, F // 256, body, 0)


def expert_grad(wire, wd):
    return call(
        expert_grad_body,
        "expert_grad_rows",
        [sds((SLOTS, D), bf16), sds((SLOTS, F), f32)],
        [],
        (wire, wd),
    )


def expert_main_body(
    wire, wg, wu, ga, back, xs, act, acts, dg, du,
    wire_v, w_v, ga_v, xr, xs_v, act_v, acts_v, d_v, sc, sems,
):
    half = F // 2

    def copy(source, dest, number):
        return pltpu.make_async_copy(source, dest, sems.at[number])

    first = copy(wire, wire_v, 0)
    first.start()
    arrivals = []
    for c in range(2):
        cols = slice(c * half, (c + 1) * half)
        up_cols = slice(F + c * half, F + (c + 1) * half)
        group = [
            copy(wg.at[:, cols], w_v.at[:, cols], 1 + 3 * c),
            copy(wu.at[:, cols], w_v.at[:, up_cols], 2 + 3 * c),
            copy(ga.at[:, cols], ga_v.at[:, cols], 3 + 3 * c),
        ]
        for item in group:
            item.start()
        arrivals.append(group)
    first.wait()
    split_rows(wire_v, xr)
    gates = get_numbers(wire_v)
    sc[...] = jnp.zeros_like(sc)
    for c in range(2):
        for item in arrivals[c]:
            item.wait()
        cols = slice(c * half, (c + 1) * half)
        up_cols = slice(F + c * half, F + (c + 1) * half)
        gate = dot(xr[...], w_v[:, cols])
        up = dot(xr[...], w_v[:, up_cols])
        grad = ga_v[:, cols]
        s = 1.0 / (1.0 + jnp.exp(-gate))
        silu = gate * s
        a = silu * up
        act_v[:, cols] = a.astype(bf16)
        d_v[:, cols] = (grad * up * s * (1.0 + gate * (1.0 - s))).astype(bf16)
        d_v[:, up_cols] = (grad * silu).astype(bf16)
        sc[...] += jnp.sum(a * grad, axis=1, keepdims=True)
    departures = [copy(act_v, act, 7), copy(d_v.at[:, :F], dg, 8), copy(d_v.at[:, F:], du, 9)]
    for item in departures:
        item.start()
    for s in range(CAP):
        part = slice(s * E, (s + 1) * E)
        gate = gates[:, s : s + 1]
        xs_v[part, :] = (xr[part, :].astype(f32) * gate).astype(bf16)
        acts_v[part, :] = (act_v[part, :].astype(f32) * gate).astype(bf16)
    more = [copy(xs_v, xs, 10), copy(acts_v, acts, 11)]
    for item in more:
        item.start()
    for j in range(4):
        part = slice(j * 512, (j + 1) * 512)
        xr[:, part] = dot_t(d_v[...], w_v[part, :]).astype(bf16)
    join_rows(xr, wire_v)
    put_numbers([sc[s * E : (s + 1) * E, :] for s in range(CAP)], wire_v)
    last = copy(wire_v, back, 12)
    last.start()
    for item in departures + more + [last]:
        item.wait()


def expert_main(wire, wg, wu, ga):
    args = (wire, wg, wu, ga)
    outs = [
        sds((E, WIRE, 128), bf16),
        sds((SLOTS, D), bf16),
        sds((SLOTS, F), bf16),
        sds((SLOTS, F), bf16),
        sds((SLOTS, F), bf16),
        sds((SLOTS, F), bf16),
    ]
    return pl.pallas_call(
        expert_main_body,
        out_shape=outs,
        in_specs=[pl.BlockSpec(memory_space=pl.ANY)] * 4,
        out_specs=[pl.BlockSpec(memory_space=pl.ANY)] * 6,
        scratch_shapes=[
            pltpu.VMEM((E, WIRE, 128), bf16),
            pltpu.VMEM((D, 2 * F), bf16),
            pltpu.VMEM((SLOTS, F), f32),
            pltpu.VMEM((SLOTS, D), bf16),
            pltpu.VMEM((SLOTS, D), bf16),
            pltpu.VMEM((SLOTS, F), bf16),
            pltpu.VMEM((SLOTS, F), bf16),
            pltpu.VMEM((SLOTS, 2 * F), bf16),
            pltpu.VMEM((SLOTS, 1), f32),
            pltpu.SemaphoreType.DMA((13,)),
        ],
        compiler_params=pltpu.CompilerParams(vmem_limit_bytes=63 * 1024 * 1024),
        cost_estimate=cost(COSTS["expert_main"]),
        name="expert_main",
    )(*args)


def expert_out_body(act, wd, wire, rows):
    for j in range(8):
        cols = slice(j * 256, (j + 1) * 256)
        rows[:, cols] = dot(act[...], wd[:, cols]).astype(bf16)
    join_rows(rows, wire)


def expert_out(act, wd):
    return call(
        expert_out_body,
        "expert_out",
        [sds((E, CAP * SEG, 128), bf16)],
        [pltpu.VMEM((SLOTS, D), bf16)],
        (act, wd),
    )[0]


def combine_body(
    where, experts, slots, gate_list, wire, hidden, n2, probs, gates, ids, og, g2, wr,
    ghid, gatt, router_own, router_sib, gg2, sums, gn2, parts,
):
    sum_rows(wire, experts, slots, gate_list, sums)
    scores = get_numbers(wire)
    lane = lax.broadcasted_iota(jnp.int32, (T, E), 1)
    grads = []
    for k in range(4):
        hot = jnp.where(lane == ids[:, k : k + 1], 1.0, 0.0)
        rows = lax.dot_general(
            hot, scores, (((1,), (0,)), ((), ())),
            precision=lax.Precision.HIGHEST, preferred_element_type=f32,
        )
        picked = jnp.where(lane == ids[:, 4 + k : 5 + k], rows, 0.0)
        grads.append(jnp.sum(picked, axis=-1, keepdims=True))
    inner = sum(grads[k] * gates[:, k : k + 1] for k in range(4))
    inverse = 1.0 / gates[:, 4:5]
    grad_probs = jnp.zeros((T, E), f32)
    for k in range(4):
        grad_probs = jnp.where(
            lane == ids[:, k : k + 1], (grads[k] - inner) * inverse, grad_probs
        )
    p = probs[...]
    gl = (p * (grad_probs - jnp.sum(p * grad_probs, axis=-1, keepdims=True))).astype(bf16)
    for h in range(2):
        tokens = slice(h * 64, (h + 1) * 64)
        gn2[tokens, :] = sums[h * 1024 : (h + 1) * 1024, :].reshape(64, D)
    gn2[...] += dot_t(gl, wr[...])
    c = gn2[...]
    v = hidden[...]
    r = lax.rsqrt(jnp.mean(v * v, axis=-1, keepdims=True) + EPS)
    u = c * g2[...]
    m = jnp.mean(u * v, axis=-1, keepdims=True)
    total = og[...].astype(f32) + r * u - v * (r * r * r * m)
    ghid[...] = total
    gatt[...] = total.astype(bf16)
    gg2[...] = jnp.sum(c * (v * r), axis=0, keepdims=True)
    for j in range(SEG):
        cols = slice(j * 128, (j + 1) * 128)
        owner = j // 2
        dy = lax.rem(owner // 2 + 4 - where[3], 4)
        dc = lax.rem(owner % 2 + where[2], 2)
        half = slice((j % 2) * 128, (j % 2 + 1) * 128)
        parts[dc * 4 + dy, half, :] = dot(n2[:, cols].astype(f32).T.astype(bf16), gl).astype(bf16)
    router_own[...] = parts[0:4]
    router_sib[...] = parts[4:8]


def combine(*args):
    return call(
        combine_body,
        "combine_grads",
        [
            sds((T, D), f32),
            sds((T, D), bf16),
            sds((4, 256, E), bf16),
            sds((4, 256, E), bf16),
            sds((1, D), f32),
        ],
        [
            pltpu.VMEM((T * SEG, 128), f32),
            pltpu.VMEM((T, D), f32),
            pltpu.VMEM((8, 256, E), bf16),
        ],
        args,
        smem=(0, 1, 2, 3),
    )


def result_body(experts, slots, gate_list, wire, hidden, out, sums):
    sum_rows(wire, experts, slots, gate_list, sums)
    for h in range(2):
        tokens = slice(h * 64, (h + 1) * 64)
        mixture = sums[h * 1024 : (h + 1) * 1024, :].reshape(64, D)
        out[tokens, :] = (hidden[tokens, :] + mixture).astype(bf16)


def result_rows(*args):
    return call(
        result_body,
        "result",
        [sds((T, D), bf16)],
        [pltpu.VMEM((T * SEG, 128), f32)],
        args,
        smem=(0, 1, 2),
    )[0]


def pre_body(where, *refs):
    blocks, (ot0, ot1, wo, *outs) = refs[:8], refs[8:16]
    dt, (heads, rows_all, wo_v, grads, dt_v, sems) = refs[15], refs[16:]
    copies = Copies(sems)
    arrivals = [copies.bring(ot0, heads.at[:, :HALF]), copies.bring(ot1, heads.at[:, HALF:])]
    columns = []
    waits = []
    for step in range(4):
        start = lax.rem(where[1] + step, 4) * 512
        columns.append(pl.ds(pl.multiple_of(start, 512), 512))
        waits.append(
            [
                copies.bring(
                    blocks[b].at[:, columns[step]],
                    rows_all.at[b * T : (b + 1) * T, columns[step]],
                )
                for b in range(8)
            ]
        )
    last = copies.bring(wo, wo_v)
    for item in arrivals:
        item.wait()
    for step in range(4):
        for item in waits[step]:
            item.wait()
        grad = dot(heads[...], rows_all[:, columns[step]]).astype(bf16)
        for col in range(4):
            grads[step, lax.rem(col + 4 - where[0], 4)] = grad[:, col * 128 : (col + 1) * 128]
        copies.take(grads.at[step], outs[step])
    last.wait()
    dt_v[...] = dot_t(wo_v[...], rows_all[...]).astype(bf16)
    copies.take(dt_v, dt)
    copies.finish()


def pre(where, blocks, ot0, ot1, wo):
    return copy_call(
        pre_body,
        "out_projection_grad",
        [sds((4, 512, 128), bf16)] * 4 + [sds((LH * HEAD, ROWS), bf16)],
        [
            pltpu.VMEM((512, ROWS), bf16),
            pltpu.VMEM((ROWS, D), bf16),
            pltpu.VMEM((512, D), bf16),
            pltpu.VMEM((4, 4, 512, 128), bf16),
            pltpu.VMEM((512, ROWS), bf16),
        ],
        2 + 32 + 1 + 5,
        (where, *blocks, ot0, ot1, wo),
        smem=(0,),
    )


def bwd_body(*refs):
    qh, kh, scales = refs[0:4], refs[4:8], refs[8:12]
    (qt, kt, kn, vn, dt, ot0, ot1, linv, info, cos, sin, gq, gk) = refs[12:25]
    dq0, dq1, dkv, ggq, ggk, mask, wb, sb, dqt, dk, dv, raw, scale = refs[25:]
    for dc in range(2):
        for dy in range(4):
            to = slice(dc * HALF + dy * T, dc * HALF + (dy + 1) * T)
            scale[:, to] = scales[dy][:, dc * T : (dc + 1) * T]
    build_mask(info, mask)
    dk[...] = jnp.zeros_like(dk)
    dv[...] = jnp.zeros_like(dv)
    for half, out in ((0, ot0), (1, ot1)):
        cols = slice(half * HALF, (half + 1) * HALF)
        for h in range(LH):
            heads = slice(h * HEAD, (h + 1) * HEAD)
            part = slice(h * HALF, (h + 1) * HALF)
            scores = dot(kn[...], qt[heads, cols])
            weights = jnp.exp2(scores * LOG2E) * (mask[:, cols] * linv[h : h + 1, cols])
            grad = dt[heads, cols]
            delta = jnp.sum(
                grad.astype(f32) * out[heads, :].astype(f32), axis=0, keepdims=True
            )
            wb[:, part] = weights.astype(bf16)
            sb[:, part] = (weights * (dot(vn[...], grad) - delta)).astype(bf16)
            dqt[heads, cols] = dot(kt[...], sb[:, part])
        grads = jnp.concatenate([dt[h * HEAD : (h + 1) * HEAD, cols] for h in range(LH)], axis=1)
        queries = jnp.concatenate([qt[h * HEAD : (h + 1) * HEAD, cols] for h in range(LH)], axis=1)
        dv[...] += dot_t(wb[...], grads)
        dk[...] += dot_t(sb[...], queries)

    def unrope(v):
        low, high = v[:64], v[64:]
        c, s = cos[...], sin[...]
        return jnp.concatenate([low * c + high * s, high * c - low * s], axis=0)

    def norm_back(n, r, grad, gain):
        gain_grad = jnp.sum(grad * n, axis=1, keepdims=True)
        u = grad * gain
        return r * (u - n * jnp.mean(u * n, axis=0, keepdims=True)), gain_grad

    gain_q, gain_k = column(gq[...]), column(gk[...])
    total = jnp.zeros((HEAD, 1), f32)
    for h in range(LH):
        heads = slice(h * HEAD, (h + 1) * HEAD)
        for dy in range(4):
            for dc in range(2):
                to = slice(dc * HALF + dy * T, dc * HALF + (dy + 1) * T)
                raw[:, to] = qh[dy][heads, dc * T : (dc + 1) * T].astype(f32)
        grad, part = norm_back(raw[...], scale[h : h + 1, :], unrope(dqt[heads, :] * (HEAD ** (-0.5))), gain_q)
        total = total + part
        dq0[heads, :] = grad[:, :HALF].astype(bf16)
        dq1[heads, :] = grad[:, HALF:].astype(bf16)
    ggq[...] = jnp.broadcast_to(total, (HEAD, 128)).T[0:8, :]
    for dy in range(4):
        for dc in range(2):
            to = slice(dc * HALF + dy * T, dc * HALF + (dy + 1) * T)
            raw[:, to] = kh[dy][:, dc * T : (dc + 1) * T].astype(f32)
    grad, part = norm_back(raw[...], scale[LH : LH + 1, :], unrope(dk[...].T), gain_k)
    ggk[...] = jnp.broadcast_to(part, (HEAD, 128)).T[0:8, :]
    dkv[:HEAD, :] = grad.astype(bf16)
    dkv[HEAD:, :] = dv[...].T.astype(bf16)


def bwd(qh, kh, scales, *rest):
    return call(
        bwd_body,
        "attend_grad",
        [
            sds((LH * HEAD, HALF), bf16),
            sds((LH * HEAD, HALF), bf16),
            sds((2 * HEAD, ROWS), bf16),
            sds((8, HEAD), f32),
            sds((8, HEAD), f32),
        ],
        [
            pltpu.VMEM((ROWS, ROWS), f32),
            pltpu.VMEM((ROWS, LH * HALF), bf16),
            pltpu.VMEM((ROWS, LH * HALF), bf16),
            pltpu.VMEM((LH * HEAD, ROWS), f32),
            pltpu.VMEM((ROWS, HEAD), f32),
            pltpu.VMEM((ROWS, HEAD), f32),
            pltpu.VMEM((HEAD, ROWS), f32),
            pltpu.VMEM((8, ROWS), f32),
        ],
        (*qh, *kh, *scales, *rest),
    )


def qkv_grad_body(where, n1t, dq0, dq1, own, sib, out, tot, dt):
    @pl.when(pl.program_id(0) == 0)
    def _():
        tot[:, :HALF] = (own[:, :HALF].astype(f32) + sib[:, HALF:].astype(f32)).astype(bf16)
        tot[:, HALF:] = (own[:, HALF:].astype(f32) + sib[:, :HALF].astype(f32)).astype(bf16)
        dt[:512, :HALF] = dq0[...]
        dt[:512, HALF:] = dq1[...]
        upper = where[2] == 1
        dt[512:576, :] = jnp.where(upper, tot[64:128, :], tot[:64, :])
        dt[576:, :] = jnp.where(upper, tot[192:, :], tot[128:192, :])

    out[...] = dot_t(n1t[...], dt[...]).astype(bf16)


def qkv_grad(where, n1t, dq0, dq1, own, sib):
    return grid_call(
        qkv_grad_body,
        "qkv_weight_grad",
        (2,),
        [
            rows_of((1024, ROWS)),
            whole((512, HALF)),
            whole((512, HALF)),
            whole((2 * HEAD, ROWS)),
            whole((2 * HEAD, ROWS)),
        ],
        [rows_of((1024, 640)), whole((2 * HEAD, ROWS))],
        [sds((D, 640), bf16), sds((2 * HEAD, ROWS), bf16)],
        [pltpu.VMEM((640, ROWS), bf16)],
        (where, n1t, dq0, dq1, own, sib),
        scalars=1,
    )


def widen_body(grads, gq, gkt, gvt):
    gq[...] = grads[:, :512].astype(f32)
    both = grads[:, 512:].astype(f32).T
    gkt[...] = both[:64]
    gvt[...] = both[64:]


def widen(grads):
    return grid_call(
        widen_body,
        "widen_grads",
        (4,),
        [rows_of((512, 640))],
        [rows_of((512, 512)), cols_of((64, 512)), cols_of((64, 512))],
        [sds((D, 512), f32), sds((64, D), f32), sds((64, D), f32)],
        [],
        (grads,),
    )


def add_body(a, b, c, d, *outs):
    for i, out in enumerate(outs):
        out[...] = (
            (a[i].astype(f32) + b[i].astype(f32)) + (c[i].astype(f32) + d[i].astype(f32))
        ).astype(bf16)


def add_parts(parts):
    shape = parts[0].shape[1:]
    return call(add_body, "add_parts", [sds(shape, bf16)] * 4, [], tuple(parts))


def split_two(v):
    first = v.astype(bf16)
    return first, (v - first.astype(f32)).astype(bf16)


def normed_grad_body(
    wa, wb, wkv, dq0, dqr, tot, n0, n1, n2, n3, gg2, ggq, ggk, ra, rb, b0, b1, b2, b3, grads
):
    step = pl.program_id(0)

    @pl.when(step == 0)
    def _():
        flip(dq0, grads, 0, 0)
        flip(dqr, grads, 0, 512)
        flip(tot, grads, 0, 1024)

    total = (
        dot(grads[:, :512], wa[...])
        + dot(grads[:, 512:1024], wb[...])
        + dot(grads[:, 1024:], wkv[...])
    )
    gain = jnp.zeros((1, 512), f32)
    outs = (b0, b1, b2, b3)
    for dy, (out, rows) in enumerate(zip(outs, (n0, n1, n2, n3))):
        part = total[dy * T : (dy + 1) * T, :]
        out[:T, :] = part.astype(bf16)
        gain = gain + jnp.sum(part * rows[...].astype(f32), axis=0, keepdims=True)
    heads = jnp.concatenate([ggq[0:1, :], ggk[0:1, :], jnp.zeros((1, 256), f32)], axis=1)
    numbers = [*split_two(gain), *split_two(gg2[...]), *split_two(heads)]
    extra = jnp.concatenate([n.astype(f32) for n in numbers] + [jnp.zeros((10, 512), f32)], axis=0)
    for dy, out in enumerate(outs):
        out[T : T + 16, :] = extra.astype(bf16)
        for q in range(4):
            rows = pl.ds(pl.multiple_of(step * 64 + q * 16, 16), 16)
            both = ra[dy, rows, :].astype(f32) + rb[dy, rows, :].astype(f32)
            out[T + 16 :, q * 128 : (q + 1) * 128] = both.astype(bf16)


def normed_grad(wa, wb, wkv, dq0, dqr, tot, n1, gg2, ggq, ggk, ra, rb):
    return grid_call(
        normed_grad_body,
        "normed_grad",
        (4,),
        [
            cols_of((512, 512)),
            cols_of((512, 512)),
            cols_of((256, 512)),
            whole((512, HALF)),
            whole((512, HALF)),
            whole((2 * HEAD, HALF)),
        ]
        + [cols_of((T, 512))] * 4
        + [cols_of((1, 512)), whole((8, HEAD)), whole((8, HEAD))]
        + [whole((4, 256, E))] * 2,
        [cols_of((T + 32, 512))] * 4,
        [sds((T + 32, D), bf16)] * 4,
        [pltpu.VMEM((HALF, 1280), bf16)],
        (wa, wb, wkv, dq0, dqr, tot, *n1, gg2, ggq, ggk, ra, rb),
    )


def add_last_body(a, b, c, d, out):
    out[...] = (
        (a[...].astype(f32) + b[...].astype(f32)) + (c[...].astype(f32) + d[...].astype(f32))
    ).astype(bf16)


def add_last(parts):
    return call(add_last_body, "add_last", [sds(parts[0].shape, bf16)], [], tuple(parts))


def stack_body(a, b, c, d, out):
    for i, part in enumerate((a, b, c, d)):
        out[i] = part[...]


def stack(parts):
    shape = (4, *parts[0].shape)
    return call(stack_body, "stack_parts", [sds(shape, bf16)], [], tuple(parts))[0]


def place_out_body(where, c0, c1, c2, c3, out):
    for dx, chunks in enumerate((c0, c1, c2, c3)):
        for dz in range(4):
            chunk = lax.rem(where[1] + dx, 4) * 4 + lax.rem(where[0] + dz, 4)
            cols = pl.ds(pl.multiple_of(chunk * 128, 128), 128)
            out[:, cols] = chunks[dz].astype(f32)


def place_out(where, chunks):
    return call(
        place_out_body,
        "place_output_grads",
        [sds((512, D), f32)],
        [],
        (where, *chunks),
        smem=(0,),
    )[0]


def final_body(b0, b1, b2, b3, x0, ghid, g1, out, small):
    whole_sum = (b0[...].astype(f32) + b1[...].astype(f32)) + (
        b2[...].astype(f32) + b3[...].astype(f32)
    )
    c = whole_sum[:T]
    v = x0[...].astype(f32)
    r = lax.rsqrt(jnp.mean(v * v, axis=-1, keepdims=True) + EPS)
    u = c * g1[...]
    m = jnp.mean(u * v, axis=-1, keepdims=True)
    out[...] = ghid[...] + r * u - v * (r * r * r * m)
    extra = whole_sum[T : T + 16]
    numbers = [
        *split_two((extra[0:1] + extra[1:2]) / g1[...]),
        *split_two(extra[2:3] + extra[3:4]),
        *split_two(extra[4:5] + extra[5:6]),
    ]
    rows = jnp.concatenate(
        [whole_sum[T + 16 :]] + [n.astype(f32) for n in numbers] + [jnp.zeros((2, D), f32)],
        axis=0,
    ).astype(bf16)
    for e in range(16):
        small[e] = rows[:, e * 128 : (e + 1) * 128]


def final(b, x0, ghid, g1):
    return call(
        final_body,
        "input_grad",
        [sds((T, D), f32), sds((16, 24, 128), bf16)],
        [],
        (*b, x0, ghid, g1),
    )


def fold_body(parts, out):
    total = parts[0].astype(f32)
    for e in range(1, 16):
        total = total + parts[e].astype(f32)
    numbers = []
    for k in range(3):
        row = SEG + 2 * k
        numbers += split_two(total[row : row + 1] + total[row + 1 : row + 2])
    rows = jnp.concatenate(
        [total[:SEG]] + [n.astype(f32) for n in numbers] + [jnp.zeros((2, 128), f32)], axis=0
    ).astype(bf16)

    def body(i, carry):
        out[i] = rows
        return carry

    lax.fori_loop(0, E, body, 0)


def fold(parts):
    return call(fold_body, "fold_small", [sds((E, 24, 128), bf16)], [], (parts,))[0]


def sibling(x):
    return lax.ppermute(x, "shard", [(i, i ^ 1) for i in range(8)])


def from_chip(x, dy):
    return lax.ppermute(x, "shard", [(i, (i - 2 * dy) % 8) for i in range(8)])


def to_chip(x, dy):
    return lax.ppermute(x, "shard", [(i, (i + 2 * dy) % 8) for i in range(8)])


def exchange(x):
    return lax.all_to_all(x, ALL, split_axis=0, concat_axis=0, tiled=True)


def spread(x):
    return [to_chip(x[d], d) for d in (1, 3, 2)]


def on_expert(x, dz, dx):
    pairs = [
        (z * 4 + c, ((z + dz) % 4) * 4 + (c + dx) % 4) for z in range(4) for c in range(4)
    ]
    return lax.ppermute(x, "expert", pairs)


def move(x, axis, distance):
    return on_expert(x, distance, 0) if axis == 0 else on_expert(x, 0, distance)


def collect(parts, axis):
    return [parts[0]] + [move(parts[d], axis, d) for d in (1, 3, 2)]


def share(x, axis):
    return [x] + [move(x, axis, (4 - d) % 4) for d in (1, 2, 3)]


def after(value, *others):
    return lax.optimization_barrier((value, *others))[0]


def on_device(
    block_input, out_grad, norm1_gain, w_query, w_key, w_value, query_gain, key_gain, w_out,
    norm2_gain, w_router, w_gate, w_up, w_down, seq_lengths, token_places, expert_routes,
):
    shard, owner = lax.axis_index("shard"), lax.axis_index("expert")
    chip, core = shard // 2, shard % 2
    where = jnp.stack([owner // 4, owner % 4, core, chip]).astype(jnp.int32)
    core_id = core.reshape(1)
    g1 = norm1_gain.astype(f32).reshape(1, D)
    g2 = norm2_gain.astype(f32).reshape(1, D)
    gq = query_gain.astype(f32).reshape(1, HEAD)
    gk = key_gain.astype(f32).reshape(1, HEAD)

    x_own = [block_input] + [from_chip(block_input, dy) for dy in (1, 2, 3)]
    x_sib = [sibling(block_input)]

    chips = (chip + jnp.arange(4)) % 4
    order = jnp.concatenate([chips * 2 + core, chips * 2 + 1 - core])
    places = token_places[0].reshape(8, T)[order].reshape(ROWS)
    lengths = seq_lengths[0]
    ends = jnp.cumsum(lengths)
    starts = jnp.sum(
        jnp.where(places[:, None] >= ends[None, :], lengths[None, :], 0), axis=1
    )
    positions = (places - starts).astype(f32)
    info = jnp.concatenate(
        [places[None].astype(f32), starts[None].astype(f32), jnp.zeros((6, ROWS), f32)], axis=0
    )
    inverse_freq = ROPE_BASE ** (-jnp.arange(0, HEAD, 2).astype(f32) / HEAD)
    angles = inverse_freq[:, None] * positions[None, :]
    cos, sin = jnp.cos(angles), jnp.sin(angles)

    ids, ids_t = route_tables(expert_routes.T)
    assign_t = ids_t[8:12]
    expert_list = ids[:, 0:4].reshape(-1)
    slot_list = ids[:, 4:8].reshape(-1)

    wk_t, wv_t = w_key.T, w_value.T
    wk_s, wv_s = sibling(wk_t), sibling(wv_t)
    wq_t = w_query.T
    wq_ts = sibling(wq_t)

    og_wire = pack(out_grad, assign_t)
    x_own, x_sib, og_wire, wq_t, cos, sin, info, wk_s, wv_s = lax.optimization_barrier(
        (x_own, x_sib, og_wire, wq_t, cos, sin, info, wk_s, wv_s)
    )
    x_sib += [sibling(x_own[dy]) for dy in (1, 2, 3)]
    blocks = [side[dy] for dy in range(4) for side in (x_own, x_sib)]
    weights = (g1, wq_t, wk_t, wk_s, wv_t, wv_s, gq, gk, cos, sin)
    *pieces, wkv = qkv((0, 1, 2, 3), core_id, blocks, *weights)
    pieces = [pieces[7 * dy : 7 * dy + 7] for dy in range(4)]
    qh, q, kh, k, v, scales, n1 = zip(*pieces)
    got_grads = exchange(og_wire)
    wo_s = sibling(after(w_out, q[0]))
    ot0, ot1, linv, qt, kt, kn, vn = attend(q, k, v, info)
    blocks = outproj(ot0, sibling(ot1), w_out, wo_s)
    blocks = [blocks[0]] + spread(blocks)
    hidden, n2, probs, gates, wire = router(blocks, block_input, g2, w_router, ids, assign_t)
    got_rows = exchange(wire)

    n1_t = transpose_rows(after(n1, wire))
    gate_list = gates[:, :4].reshape(-1)
    grad_rows, grad_act = expert_grad(after(got_grads, wire), w_down[0])
    got_rows, n1_t, grad_act, gate_list, wq_ts = lax.optimization_barrier(
        (got_rows, n1_t, grad_act, gate_list, wq_ts)
    )

    back, rows, act, scaled_act, dg, du = expert_main(got_rows, w_gate[0], w_up[0], grad_act)
    back_wire = exchange(back)

    rows, act, scaled_act, dg, du = after((rows, act, scaled_act, dg, du), back)
    out_wire = expert_out(act, w_down[0])

    def weight_grad(a, b):
        return lax.dot_general(a, b, (((0,), (0,)), ((), ())), preferred_element_type=f32)

    grad_wgate = weight_grad(rows, dg)
    grad_wup = weight_grad(rows, du)
    grad_wdown = weight_grad(scaled_act, grad_rows)
    back_wire, out_wire, grad_wgate, grad_wup, grad_wdown = lax.optimization_barrier(
        (back_wire, out_wire, grad_wgate, grad_wup, grad_wdown)
    )

    ghid, gatt, router_own, router_sib, gg2 = combine(
        where, expert_list, slot_list, gate_list, back_wire, hidden, n2, probs, gates, ids,
        out_grad, g2, w_router,
    )
    g_own = [gatt] + [from_chip(gatt, dy) for dy in (1, 2, 3)]
    g_sib = [sibling(block) for block in g_own]
    returned = exchange(after(out_wire, *g_sib))
    *out_parts, dt = pre(where, g_own + g_sib, ot0, ot1, w_out)

    dq0, dq1, dkv, ggq, ggk = bwd(
        qh, kh, scales, qt, kt, kn, vn, dt, ot0, ot1, linv, info, cos, sin, gq, gk
    )
    out_parts = collect(out_parts, 1)
    router_sib = after(router_sib, dkv)
    dq_sib, dkv_sib = sibling(dq1), sibling(dkv)
    gw, dkv_total = qkv_grad(where, n1_t, dq0, dq1, dkv, dkv_sib)
    returned, dq0, out_parts = lax.optimization_barrier((returned, dq0, out_parts))
    router_rec = sibling(router_sib)
    blocks = normed_grad(
        wq_t, wq_ts, wkv, dq0, dq_sib, dkv_total, n1, gg2, ggq, ggk, router_own, router_rec
    )
    blocks = [blocks[0]] + spread(blocks)

    gw = lax.psum(gw, "expert")
    out_parts = collect(add_parts(out_parts), 0)
    chunks = share(add_last(out_parts)[0], 0)
    chunks, blocks = lax.optimization_barrier((chunks, blocks))
    chunks = share(stack(chunks), 1)
    grad_input, small = final(blocks, block_input, ghid, g1)
    result = result_rows(expert_list, slot_list, gate_list, returned, hidden)
    small = lax.all_to_all(small, "expert", split_axis=0, concat_axis=0, tiled=True)
    small, chunks = lax.optimization_barrier((small, chunks))
    small = exchange(fold(small))
    grad_wout = place_out(where, chunks)
    gw, small, grad_input, grad_wout, result = lax.optimization_barrier(
        (gw, small, grad_input, grad_wout, result)
    )
    grad_wq, grad_wk, grad_wv = widen(gw)
    small = small.reshape(16, 8, 24, 128).astype(f32)
    grad_router = small[:, :, :SEG].transpose(1, 0, 2, 3).reshape(D, E)
    gains = small[:, 0, SEG:] + small[:, 1, SEG:]
    gains = [(gains[:, 2 * k] + gains[:, 2 * k + 1]).reshape(D) for k in range(3)]
    return (
        result,
        grad_input,
        gains[0],
        grad_wq,
        grad_wk.T,
        grad_wv.T,
        gains[2][:HEAD],
        gains[2][HEAD : 2 * HEAD],
        grad_wout,
        gains[1],
        grad_router,
        grad_wgate[None],
        grad_wup[None],
        grad_wdown[None],
    )


def solution(mesh):
    rows = P(("expert", "shard"), None)
    experts = P(("expert", "shard"), None, None)
    columns = P(None, "shard")
    return jax.shard_map(
        on_device,
        mesh=mesh,
        in_specs=(
            rows, rows, P(), columns, columns, columns, P(), P(), P("shard", None), P(), P(),
            experts, experts, experts, P("expert", None), P("expert", None), rows,
        ),
        out_specs=(
            rows, rows, P(), columns, columns, columns, P(), P(), P("shard", None), P(), P(),
            experts, experts, experts,
        ),
        check_vma=False,
    )
```

```python
import functools

import jax
import jax.numpy as jnp
from jax import lax
from jax.experimental import pallas as pl
from jax.experimental.pallas import tpu as pltpu
from jax.sharding import PartitionSpec as P

EPS = 1e-06
ROPE_BASE = 1000000.0
LOG2E = 1.4426950408889634
T = 128
D = 2048
HEAD = 128
LH = 4
E = 128
CAP = 5
SLOTS = E * CAP
SEG = D // 128
WIRE = CAP * SEG + 8
ROWS = 1024
HALF = 512
F = 768
bf16 = jnp.bfloat16
f32 = jnp.float32
ALL = ("expert", "shard")
COSTS = {
    "attend": 11,
    "out_projection": 5,
    "router": 6,
    "transpose_rows": 6,
    "expert_grad_rows": 8,
    "expert_main": 18,
    "expert_out": 7,
    "combine_grads": 7,
    "head_grad": 4,
    "out_projection_grad": 7,
}


def cost(micros):
    return pl.CostEstimate(
        flops=1, bytes_accessed=int(micros * 0.6e6) + 1, transcendentals=0
    )


def dot(a, b):
    return jnp.dot(a, b, preferred_element_type=f32)


def dot_t(a, b):
    return lax.dot_general(a, b, (((1,), (1,)), ((), ())), preferred_element_type=f32)


def call(kernel, name, outs, scratch, args, smem=()):
    in_specs = [
        pl.BlockSpec(memory_space=pltpu.SMEM if i in smem else pltpu.VMEM)
        for i in range(len(args))
    ]
    return pl.pallas_call(
        kernel,
        out_shape=outs,
        in_specs=in_specs,
        out_specs=[pl.BlockSpec(memory_space=pltpu.VMEM) for _ in outs],
        scratch_shapes=scratch,
        compiler_params=pltpu.CompilerParams(vmem_limit_bytes=63 * 1024 * 1024),
        cost_estimate=cost(COSTS.get(name, 0)),
        name=name,
    )(*args)


def grid_call(kernel, name, grid, in_specs, out_specs, outs, scratch, args, scalars=0):
    return pl.pallas_call(
        kernel,
        out_shape=outs,
        grid_spec=pltpu.PrefetchScalarGridSpec(
            num_scalar_prefetch=scalars,
            grid=grid,
            in_specs=in_specs,
            out_specs=out_specs,
            scratch_shapes=scratch,
        ),
        compiler_params=pltpu.CompilerParams(
            vmem_limit_bytes=63 * 1024 * 1024, dimension_semantics=("arbitrary",)
        ),
        cost_estimate=cost(COSTS.get(name, 0)),
        name=name,
    )(*args)


def copy_call(kernel, name, outs, scratch, copies, args, smem=()):
    return pl.pallas_call(
        kernel,
        out_shape=outs,
        in_specs=[
            pl.BlockSpec(memory_space=pltpu.SMEM if i in smem else pl.ANY)
            for i in range(len(args))
        ],
        out_specs=[pl.BlockSpec(memory_space=pl.ANY)] * len(outs),
        scratch_shapes=[*scratch, pltpu.SemaphoreType.DMA((copies,))],
        compiler_params=pltpu.CompilerParams(vmem_limit_bytes=63 * 1024 * 1024),
        cost_estimate=cost(COSTS.get(name, 0)),
        name=name,
    )(*args)


class Copies:
    def __init__(self, sems):
        self.sems, self.count, self.leaving = sems, 0, []

    def bring(self, source, dest):
        item = pltpu.make_async_copy(source, dest, self.sems.at[self.count])
        self.count += 1
        item.start()
        return item

    def take(self, source, dest):
        self.leaving.append(self.bring(source, dest))

    def finish(self):
        for item in self.leaving:
            item.wait()


def whole(shape):
    return pl.BlockSpec(shape, lambda i, *_: (0,) * len(shape))


def rows_of(shape):
    return pl.BlockSpec(shape, lambda i, *_: (i, 0))


def cols_of(shape):
    return pl.BlockSpec(shape, lambda i, *_: (0, i))


def sds(shape, dtype):
    return jax.ShapeDtypeStruct(shape, dtype)


def split_rows(wire, dest):
    for s in range(CAP):
        for h in range(2):
            rows = slice(s * E + h * 64, s * E + (h + 1) * 64)
            block = wire[h * 64 : (h + 1) * 64, s * SEG : (s + 1) * SEG, :]
            dest[rows, :] = block.reshape(64, D)


def join_rows(source, wire):
    for s in range(CAP):
        for h in range(2):
            rows = slice(s * E + h * 64, s * E + (h + 1) * 64)
            wire[h * 64 : (h + 1) * 64, s * SEG : (s + 1) * SEG, :] = source[rows, :].reshape(
                64, SEG, 128
            )


def put_numbers(columns, wire):
    lane = lax.broadcasted_iota(jnp.int32, (E, 128), 1)
    plane = jnp.zeros((E, 128), f32)
    for s in range(CAP):
        plane = jnp.where(lane == s, columns[s], plane)
    first = plane.astype(bf16)
    rest = plane - first.astype(f32)
    second = rest.astype(bf16)
    third = (rest - second.astype(f32)).astype(bf16)
    none = jnp.zeros((E, 5 * 128), bf16)
    wide = jnp.concatenate([first, second, third, none], axis=1)
    wire[:, CAP * SEG :, :] = wide.reshape(E, 8, 128)


def get_numbers(wire):
    wide = wire[:, CAP * SEG :, :].reshape(E, 8 * 128)
    return (
        wide[:, :128].astype(f32) + wide[:, 128:256].astype(f32) + wide[:, 256:384].astype(f32)
    )


def pack_rows(x_ref, at_ref, wire, rows):
    slot = lax.broadcasted_iota(jnp.int32, (SLOTS, T), 0)
    hit = slot == at_ref[0:1, :]
    for k in range(1, 4):
        hit = hit | (slot == at_ref[k : k + 1, :])
    pick = jnp.where(hit, 1.0, 0.0).astype(bf16)
    for j in range(8):
        cols = slice(j * 256, (j + 1) * 256)
        rows[:, cols] = dot(pick, x_ref[:, cols]).astype(bf16)
    join_rows(rows, wire)


def pack_body(x_ref, at_ref, wire, rows):
    pack_rows(x_ref, at_ref, wire, rows)
    wire[:, CAP * SEG :, :] = jnp.zeros((E, 8, 128), bf16)


def pack(x, assign_t):
    return call(
        pack_body,
        "pack_rows",
        [sds((E, WIRE, 128), bf16)],
        [pltpu.VMEM((SLOTS, D), bf16)],
        (x, assign_t),
    )[0]


def sum_rows(wire, experts, slots, gates, out):
    def body(i, carry):
        for u in range(8):
            t = i * 8 + u
            total = None
            for k in range(4):
                p = t * 4 + k
                rows = pl.ds(pl.multiple_of(slots[p] * SEG, SEG), SEG)
                part = wire[experts[p], rows, :].astype(f32) * gates[p]
                total = part if total is None else total + part
            out[pl.ds(pl.multiple_of(t * SEG, SEG), SEG), :] = total
        return carry

    lax.fori_loop(0, T // 8, body, 0)


def column(row):
    return jnp.broadcast_to(row, (128, 128)).T[:, 0:1]


def qkv_body(pieces, *refs):
    count = len(pieces)
    core, blocks = refs[0], refs[1 : 1 + 2 * count]
    g1, wqt, wk, wks, wv, wvs, gq, gk, cos, sin = refs[1 + 2 * count : 11 + 2 * count]
    outs = refs[11 + 2 * count :]
    wkv = outs[-1]
    lower = core[0] == 0
    wkv[0:64, :] = jnp.where(lower, wk[...], wks[...])
    wkv[64:128, :] = jnp.where(lower, wks[...], wk[...])
    wkv[128:192, :] = jnp.where(lower, wv[...], wvs[...])
    wkv[192:256, :] = jnp.where(lower, wvs[...], wv[...])
    gain_q, gain_k = column(gq[...]), column(gk[...])
    for number, piece in enumerate(pieces):
        qn, qt, kn, kt, vt, scale, n1 = outs[7 * number : 7 * number + 7]
        for half in range(2):
            x = blocks[2 * number + half][...].astype(f32)
            r = lax.rsqrt(jnp.mean(x * x, axis=-1, keepdims=True) + EPS)
            n1[half * T : (half + 1) * T, :] = (x * r * g1[...]).astype(bf16)
        raw = dot_t(wqt[...], n1[...])
        raw_kv = dot_t(wkv[...], n1[...])
        first, second = piece * T, HALF + piece * T
        c = jnp.concatenate([cos[:, first : first + T], cos[:, second : second + T]], axis=1)
        s = jnp.concatenate([sin[:, first : first + T], sin[:, second : second + T]], axis=1)

        def path(v, gain, factor, keep, index):
            r = lax.rsqrt(jnp.mean(v * v, axis=0, keepdims=True) + EPS)
            scale[index : index + 1, :] = r
            v = v * r
            keep[...] = v.astype(bf16)
            v = v * gain
            low, high = v[:64], v[64:]
            return (
                ((low * c - high * s) * factor).astype(bf16),
                ((high * c + low * s) * factor).astype(bf16),
            )

        scale[...] = jnp.zeros_like(scale)
        for h in range(LH):
            heads = slice(h * HEAD, (h + 1) * HEAD)
            low, high = path(raw[heads], gain_q, HEAD ** (-0.5), qn.at[heads, :], h)
            qt[h * HEAD : h * HEAD + 64, :] = low
            qt[h * HEAD + 64 : (h + 1) * HEAD, :] = high
        key = raw_kv[:HEAD].astype(bf16)
        low, high = path(key.astype(f32), gain_k, 1.0, kn, LH)
        kt[:64, :] = low
        kt[64:, :] = high
        vt[...] = raw_kv[HEAD:].astype(bf16)


def qkv(pieces, core, blocks, *args):
    outs = [
        sds((LH * HEAD, 2 * T), bf16),
        sds((LH * HEAD, 2 * T), bf16),
        sds((HEAD, 2 * T), bf16),
        sds((HEAD, 2 * T), bf16),
        sds((HEAD, 2 * T), bf16),
        sds((8, 2 * T), f32),
        sds((2 * T, D), bf16),
    ] * len(pieces)
    keep = 0 in pieces
    return call(
        functools.partial(qkv_body, pieces),
        "qkv" + "".join(str(p) for p in pieces),
        outs + ([sds((2 * HEAD, D), bf16)] if keep else []),
        [] if keep else [pltpu.VMEM((2 * HEAD, D), bf16)],
        (core, *blocks, *args),
        smem=(0,),
    )


def build_mask(info, mask):
    for b in range(8):
        keys = jnp.broadcast_to(info[0:1, b * T : (b + 1) * T], (T, T)).T
        for j in range(8):
            cols = slice(j * T, (j + 1) * T)
            inside = (keys >= info[1:2, cols]) & (keys <= info[0:1, cols])
            mask[b * T : (b + 1) * T, cols] = jnp.where(inside, 1.0, 0.0)


def attend_body(*refs):
    q, k, v = refs[0:4], refs[4:8], refs[8:12]
    info, ot0, ot1, linv, qt, kt, kn, vn, mask, vt = refs[12:]
    for dy in range(4):
        for dc in range(2):
            to = slice(dc * HALF + dy * T, dc * HALF + (dy + 1) * T)
            src = slice(dc * T, (dc + 1) * T)
            qt[:, to] = q[dy][:, src]
            kt[:, to] = k[dy][:, src]
            vt[:, to] = v[dy][:, src]
    for b in range(8):
        rows = slice(b * T, (b + 1) * T)
        kn[rows, :] = kt[:, rows].astype(f32).T.astype(bf16)
        vn[rows, :] = vt[:, rows].astype(f32).T.astype(bf16)
    build_mask(info, mask)
    for half, out in ((1, ot1), (0, ot0)):
        cols = slice(half * HALF, (half + 1) * HALF)
        for h in range(LH):
            heads = slice(h * HEAD, (h + 1) * HEAD)
            scores = dot(kn[...], qt[heads, cols])
            weights = jnp.exp2(scores * LOG2E) * mask[:, cols]
            inverse = 1.0 / jnp.sum(weights, axis=0, keepdims=True)
            out[heads, :] = (dot(vt[...], weights.astype(bf16)) * inverse).astype(bf16)
            linv[h : h + 1, cols] = inverse


def attend(q, k, v, info):
    return call(
        attend_body,
        "attend",
        [
            sds((LH * HEAD, HALF), bf16),
            sds((LH * HEAD, HALF), bf16),
            sds((8, ROWS), f32),
            sds((LH * HEAD, ROWS), bf16),
            sds((HEAD, ROWS), bf16),
            sds((ROWS, HEAD), bf16),
            sds((ROWS, HEAD), bf16),
        ],
        [pltpu.VMEM((ROWS, ROWS), f32), pltpu.VMEM((HEAD, ROWS), bf16)],
        (*q, *k, *v, info),
    )


def flip(source, dest, row, col):
    height, width = source.shape
    for a in range(height // 128):
        for b in range(width // 128):
            block = source[a * 128 : (a + 1) * 128, b * 128 : (b + 1) * 128]
            rows = slice(row + b * 128, row + (b + 1) * 128)
            dest[rows, col + a * 128 : col + (a + 1) * 128] = block.astype(f32).T.astype(bf16)


def outproj_body(ot0, otr, wa, wb, b0, b1, b2, b3, heads):
    @pl.when(pl.program_id(0) == 0)
    def _():
        flip(ot0, heads, 0, 0)
        flip(otr, heads, 0, 512)

    total = dot(heads[:, :512], wa[...]) + dot(heads[:, 512:], wb[...])
    for dy, out in enumerate((b0, b1, b2, b3)):
        out[...] = total[dy * T : (dy + 1) * T, :].astype(bf16)


def outproj(ot0, otr, wa, wb):
    return grid_call(
        outproj_body,
        "out_projection",
        (2,),
        [whole((512, HALF)), whole((512, HALF)), cols_of((512, 1024)), cols_of((512, 1024))],
        [cols_of((T, 1024))] * 4,
        [sds((T, D), bf16)] * 4,
        [pltpu.VMEM((HALF, 1024), bf16)],
        (ot0, otr, wa, wb),
    )


def transpose_body(n0, n1, n2, n3, out):
    for dy, piece in enumerate((n0, n1, n2, n3)):
        for dc in range(2):
            flip(piece.at[dc * T : (dc + 1) * T, :], out, 0, dc * HALF + dy * T)


def transpose_rows(pieces):
    return call(transpose_body, "transpose_rows", [sds((D, ROWS), bf16)], [], tuple(pieces))[0]


def route_body(rt, ids, ids_t):
    lane = lax.broadcasted_iota(jnp.int32, (T, E), 1)
    row = lax.broadcasted_iota(jnp.int32, (T, E), 0)
    wide = jnp.concatenate([rt[...].astype(f32), jnp.zeros((124, T), f32)], axis=0).T
    hot = [jnp.where(lane.astype(f32) == wide[:, k : k + 1], 1.0, 0.0) for k in range(4)]
    earlier = jnp.where(lane < row, 1.0, 0.0).astype(bf16)
    before = dot(earlier, (hot[0] + hot[1] + hot[2] + hot[3]).astype(bf16))
    table = wide
    for k in range(4):
        slot = jnp.sum(before * hot[k], axis=1, keepdims=True)
        table = jnp.where(lane == 4 + k, slot, table)
        table = jnp.where(lane == 8 + k, slot * E + wide[:, k : k + 1], table)
    ids[...] = table.astype(jnp.int32)
    ids_t[...] = table.T[0:16, :].astype(jnp.int32)


def route_tables(routes_t):
    return call(
        route_body,
        "route_tables",
        [sds((T, 128), jnp.int32), sds((16, T), jnp.int32)],
        [],
        (routes_t,),
    )


def router_body(b0, b1, b2, b3, x0, g2, wr, ids, at, hidden, n2, probs, gates, wire, rows):
    v = x0[...].astype(f32) + (
        (b0[...].astype(f32) + b1[...].astype(f32))
        + (b2[...].astype(f32) + b3[...].astype(f32))
    )
    hidden[...] = v
    r = lax.rsqrt(jnp.mean(v * v, axis=-1, keepdims=True) + EPS)
    n2[...] = (v * r * g2[...]).astype(bf16)
    logits = dot(n2[...], wr[...])
    pack_rows(n2, at, wire, rows)
    expo = jnp.exp(logits - jnp.max(logits, axis=-1, keepdims=True))
    p = expo / jnp.sum(expo, axis=-1, keepdims=True)
    probs[...] = p
    lane = lax.broadcasted_iota(jnp.int32, (T, E), 1)
    chosen = [
        jnp.sum(jnp.where(lane == ids[:, k : k + 1], p, 0.0), axis=-1, keepdims=True)
        for k in range(4)
    ]
    total = chosen[0] + chosen[1] + chosen[2] + chosen[3]
    packed = jnp.where(lane == 4, total, 0.0)
    for k in range(4):
        packed = jnp.where(lane == k, chosen[k] / total, packed)
    gates[...] = packed
    across = packed.T
    expert = lax.broadcasted_iota(jnp.int32, (E, T), 0)
    columns = []
    for s in range(CAP):
        mine = jnp.zeros((E, T), f32)
        for k in range(4):
            mine = jnp.where(expert + s * E == at[k : k + 1, :], across[k : k + 1, :], mine)
        columns.append(jnp.sum(mine, axis=1, keepdims=True))
    put_numbers(columns, wire)


def router(b, x0, g2, wr, ids, assign_t):
    return call(
        router_body,
        "router",
        [
            sds((T, D), f32),
            sds((T, D), bf16),
            sds((T, E), f32),
            sds((T, E), f32),
            sds((E, WIRE, 128), bf16),
        ],
        [pltpu.VMEM((SLOTS, D), bf16)],
        (*b, x0, g2, wr, ids, assign_t),
    )


def expert_grad_body(wire, wd, gr, ga):
    split_rows(wire, gr)

    def body(i, carry):
        cols = pl.ds(pl.multiple_of(i * 256, 256), 256)
        ga[:, cols] = dot_t(gr[...], wd[cols, :])
        return carry

    lax.fori_loop(0, F // 256, body, 0)


def expert_grad(wire, wd):
    return call(
        expert_grad_body,
        "expert_grad_rows",
        [sds((SLOTS, D), bf16), sds((SLOTS, F), f32)],
        [],
        (wire, wd),
    )


def expert_main_body(
    wire, wg, wu, ga, back, xs, act, acts, dg, du,
    wire_v, w_v, ga_v, xr, xs_v, act_v, acts_v, d_v, sc, sems,
):
    half = F // 2

    def copy(source, dest, number):
        return pltpu.make_async_copy(source, dest, sems.at[number])

    first = copy(wire, wire_v, 0)
    first.start()
    arrivals = []
    for c in range(2):
        cols = slice(c * half, (c + 1) * half)
        up_cols = slice(F + c * half, F + (c + 1) * half)
        group = [
            copy(wg.at[:, cols], w_v.at[:, cols], 1 + 3 * c),
            copy(wu.at[:, cols], w_v.at[:, up_cols], 2 + 3 * c),
            copy(ga.at[:, cols], ga_v.at[:, cols], 3 + 3 * c),
        ]
        for item in group:
            item.start()
        arrivals.append(group)
    first.wait()
    split_rows(wire_v, xr)
    gates = get_numbers(wire_v)
    sc[...] = jnp.zeros_like(sc)
    for c in range(2):
        for item in arrivals[c]:
            item.wait()
        cols = slice(c * half, (c + 1) * half)
        up_cols = slice(F + c * half, F + (c + 1) * half)
        gate = dot(xr[...], w_v[:, cols])
        up = dot(xr[...], w_v[:, up_cols])
        grad = ga_v[:, cols]
        s = 1.0 / (1.0 + jnp.exp(-gate))
        silu = gate * s
        a = silu * up
        act_v[:, cols] = a.astype(bf16)
        d_v[:, cols] = (grad * up * s * (1.0 + gate * (1.0 - s))).astype(bf16)
        d_v[:, up_cols] = (grad * silu).astype(bf16)
        sc[...] += jnp.sum(a * grad, axis=1, keepdims=True)
    departures = [copy(act_v, act, 7), copy(d_v.at[:, :F], dg, 8), copy(d_v.at[:, F:], du, 9)]
    for item in departures:
        item.start()
    for s in range(CAP):
        part = slice(s * E, (s + 1) * E)
        gate = gates[:, s : s + 1]
        xs_v[part, :] = (xr[part, :].astype(f32) * gate).astype(bf16)
        acts_v[part, :] = (act_v[part, :].astype(f32) * gate).astype(bf16)
    more = [copy(xs_v, xs, 10), copy(acts_v, acts, 11)]
    for item in more:
        item.start()
    for j in range(4):
        part = slice(j * 512, (j + 1) * 512)
        xr[:, part] = dot_t(d_v[...], w_v[part, :]).astype(bf16)
    join_rows(xr, wire_v)
    put_numbers([sc[s * E : (s + 1) * E, :] for s in range(CAP)], wire_v)
    last = copy(wire_v, back, 12)
    last.start()
    for item in departures + more + [last]:
        item.wait()


def expert_main(wire, wg, wu, ga):
    args = (wire, wg, wu, ga)
    outs = [
        sds((E, WIRE, 128), bf16),
        sds((SLOTS, D), bf16),
        sds((SLOTS, F), bf16),
        sds((SLOTS, F), bf16),
        sds((SLOTS, F), bf16),
        sds((SLOTS, F), bf16),
    ]
    return pl.pallas_call(
        expert_main_body,
        out_shape=outs,
        in_specs=[pl.BlockSpec(memory_space=pl.ANY)] * 4,
        out_specs=[pl.BlockSpec(memory_space=pl.ANY)] * 6,
        scratch_shapes=[
            pltpu.VMEM((E, WIRE, 128), bf16),
            pltpu.VMEM((D, 2 * F), bf16),
            pltpu.VMEM((SLOTS, F), f32),
            pltpu.VMEM((SLOTS, D), bf16),
            pltpu.VMEM((SLOTS, D), bf16),
            pltpu.VMEM((SLOTS, F), bf16),
            pltpu.VMEM((SLOTS, F), bf16),
            pltpu.VMEM((SLOTS, 2 * F), bf16),
            pltpu.VMEM((SLOTS, 1), f32),
            pltpu.SemaphoreType.DMA((13,)),
        ],
        compiler_params=pltpu.CompilerParams(vmem_limit_bytes=63 * 1024 * 1024),
        cost_estimate=cost(COSTS["expert_main"]),
        name="expert_main",
    )(*args)


def expert_out_body(act, wd, wire, rows):
    for j in range(8):
        cols = slice(j * 256, (j + 1) * 256)
        rows[:, cols] = dot(act[...], wd[:, cols]).astype(bf16)
    join_rows(rows, wire)


def expert_out(act, wd):
    return call(
        expert_out_body,
        "expert_out",
        [sds((E, CAP * SEG, 128), bf16)],
        [pltpu.VMEM((SLOTS, D), bf16)],
        (act, wd),
    )[0]


def combine_body(
    where, experts, slots, gate_list, wire, hidden, n2, probs, gates, ids, og, g2, wr,
    ghid, gatt, grouter, gg2, sums, gn2,
):
    sum_rows(wire, experts, slots, gate_list, sums)
    scores = get_numbers(wire)
    lane = lax.broadcasted_iota(jnp.int32, (T, E), 1)
    grads = []
    for k in range(4):
        hot = jnp.where(lane == ids[:, k : k + 1], 1.0, 0.0)
        rows = lax.dot_general(
            hot, scores, (((1,), (0,)), ((), ())),
            precision=lax.Precision.HIGHEST, preferred_element_type=f32,
        )
        picked = jnp.where(lane == ids[:, 4 + k : 5 + k], rows, 0.0)
        grads.append(jnp.sum(picked, axis=-1, keepdims=True))
    inner = sum(grads[k] * gates[:, k : k + 1] for k in range(4))
    inverse = 1.0 / gates[:, 4:5]
    grad_probs = jnp.zeros((T, E), f32)
    for k in range(4):
        grad_probs = jnp.where(
            lane == ids[:, k : k + 1], (grads[k] - inner) * inverse, grad_probs
        )
    p = probs[...]
    gl = (p * (grad_probs - jnp.sum(p * grad_probs, axis=-1, keepdims=True))).astype(bf16)
    for h in range(2):
        tokens = slice(h * 64, (h + 1) * 64)
        gn2[tokens, :] = sums[h * 1024 : (h + 1) * 1024, :].reshape(64, D)
    gn2[...] += dot_t(gl, wr[...])
    c = gn2[...]
    v = hidden[...]
    r = lax.rsqrt(jnp.mean(v * v, axis=-1, keepdims=True) + EPS)
    u = c * g2[...]
    m = jnp.mean(u * v, axis=-1, keepdims=True)
    total = og[...].astype(f32) + r * u - v * (r * r * r * m)
    ghid[...] = total
    gatt[...] = total.astype(bf16)
    gg2[...] = jnp.sum(c * (v * r), axis=0, keepdims=True)
    for j in range(SEG):
        cols = slice(j * 128, (j + 1) * 128)
        grouter[cols, :] = dot(n2[:, cols].astype(f32).T.astype(bf16), gl).astype(bf16)


def combine(*args):
    return call(
        combine_body,
        "combine_grads",
        [sds((T, D), f32), sds((T, D), bf16), sds((D, E), bf16), sds((1, D), f32)],
        [pltpu.VMEM((T * SEG, 128), f32), pltpu.VMEM((T, D), f32)],
        args,
        smem=(0, 1, 2, 3),
    )


def result_body(experts, slots, gate_list, wire, hidden, out, sums):
    sum_rows(wire, experts, slots, gate_list, sums)
    for h in range(2):
        tokens = slice(h * 64, (h + 1) * 64)
        mixture = sums[h * 1024 : (h + 1) * 1024, :].reshape(64, D)
        out[tokens, :] = (hidden[tokens, :] + mixture).astype(bf16)


def result_rows(*args):
    return call(
        result_body,
        "result",
        [sds((T, D), bf16)],
        [pltpu.VMEM((T * SEG, 128), f32)],
        args,
        smem=(0, 1, 2),
    )[0]


def pre_body(where, *refs):
    blocks, (ot0, ot1, wo, *outs) = refs[:8], refs[8:16]
    dt, (heads, rows_all, wo_v, grads, dt_v, sems) = refs[15], refs[16:]
    copies = Copies(sems)
    arrivals = [copies.bring(ot0, heads.at[:, :HALF]), copies.bring(ot1, heads.at[:, HALF:])]
    columns = []
    waits = []
    for step in range(4):
        start = lax.rem(where[1] + step, 4) * 512
        columns.append(pl.ds(pl.multiple_of(start, 512), 512))
        waits.append(
            [
                copies.bring(
                    blocks[b].at[:, columns[step]],
                    rows_all.at[b * T : (b + 1) * T, columns[step]],
                )
                for b in range(8)
            ]
        )
    last = copies.bring(wo, wo_v)
    for item in arrivals:
        item.wait()
    for step in range(4):
        for item in waits[step]:
            item.wait()
        grad = dot(heads[...], rows_all[:, columns[step]]).astype(bf16)
        for col in range(4):
            grads[step, lax.rem(col + 4 - where[0], 4)] = grad[:, col * 128 : (col + 1) * 128]
        copies.take(grads.at[step], outs[step])
    last.wait()
    dt_v[...] = dot_t(wo_v[...], rows_all[...]).astype(bf16)
    copies.take(dt_v, dt)
    copies.finish()


def pre(where, blocks, ot0, ot1, wo):
    return copy_call(
        pre_body,
        "out_projection_grad",
        [sds((4, 512, 128), bf16)] * 4 + [sds((LH * HEAD, ROWS), bf16)],
        [
            pltpu.VMEM((512, ROWS), bf16),
            pltpu.VMEM((ROWS, D), bf16),
            pltpu.VMEM((512, D), bf16),
            pltpu.VMEM((4, 4, 512, 128), bf16),
            pltpu.VMEM((512, ROWS), bf16),
        ],
        2 + 32 + 1 + 5,
        (where, *blocks, ot0, ot1, wo),
        smem=(0,),
    )


def bwd_body(*refs):
    qh, kh, scales = refs[0:4], refs[4:8], refs[8:12]
    (qt, kt, kn, vn, dt, ot0, ot1, linv, info, cos, sin, gq, gk) = refs[12:25]
    dq0, dq1, dkv, ggq, ggk, mask, wb, sb, dqt, dk, dv, raw, scale = refs[25:]
    for dc in range(2):
        for dy in range(4):
            to = slice(dc * HALF + dy * T, dc * HALF + (dy + 1) * T)
            scale[:, to] = scales[dy][:, dc * T : (dc + 1) * T]
    build_mask(info, mask)
    dk[...] = jnp.zeros_like(dk)
    dv[...] = jnp.zeros_like(dv)
    for half, out in ((0, ot0), (1, ot1)):
        cols = slice(half * HALF, (half + 1) * HALF)
        for h in range(LH):
            heads = slice(h * HEAD, (h + 1) * HEAD)
            part = slice(h * HALF, (h + 1) * HALF)
            scores = dot(kn[...], qt[heads, cols])
            weights = jnp.exp2(scores * LOG2E) * (mask[:, cols] * linv[h : h + 1, cols])
            grad = dt[heads, cols]
            delta = jnp.sum(
                grad.astype(f32) * out[heads, :].astype(f32), axis=0, keepdims=True
            )
            wb[:, part] = weights.astype(bf16)
            sb[:, part] = (weights * (dot(vn[...], grad) - delta)).astype(bf16)
            dqt[heads, cols] = dot(kt[...], sb[:, part])
        grads = jnp.concatenate([dt[h * HEAD : (h + 1) * HEAD, cols] for h in range(LH)], axis=1)
        queries = jnp.concatenate([qt[h * HEAD : (h + 1) * HEAD, cols] for h in range(LH)], axis=1)
        dv[...] += dot_t(wb[...], grads)
        dk[...] += dot_t(sb[...], queries)

    def unrope(v):
        low, high = v[:64], v[64:]
        c, s = cos[...], sin[...]
        return jnp.concatenate([low * c + high * s, high * c - low * s], axis=0)

    def norm_back(n, r, grad, gain):
        gain_grad = jnp.sum(grad * n, axis=1, keepdims=True)
        u = grad * gain
        return r * (u - n * jnp.mean(u * n, axis=0, keepdims=True)), gain_grad

    gain_q, gain_k = column(gq[...]), column(gk[...])
    total = jnp.zeros((HEAD, 1), f32)
    for h in range(LH):
        heads = slice(h * HEAD, (h + 1) * HEAD)
        for dy in range(4):
            for dc in range(2):
                to = slice(dc * HALF + dy * T, dc * HALF + (dy + 1) * T)
                raw[:, to] = qh[dy][heads, dc * T : (dc + 1) * T].astype(f32)
        grad, part = norm_back(raw[...], scale[h : h + 1, :], unrope(dqt[heads, :] * (HEAD ** (-0.5))), gain_q)
        total = total + part
        dq0[heads, :] = grad[:, :HALF].astype(bf16)
        dq1[heads, :] = grad[:, HALF:].astype(bf16)
    ggq[...] = jnp.broadcast_to(total, (HEAD, 128)).T[0:8, :]
    for dy in range(4):
        for dc in range(2):
            to = slice(dc * HALF + dy * T, dc * HALF + (dy + 1) * T)
            raw[:, to] = kh[dy][:, dc * T : (dc + 1) * T].astype(f32)
    grad, part = norm_back(raw[...], scale[LH : LH + 1, :], unrope(dk[...].T), gain_k)
    ggk[...] = jnp.broadcast_to(part, (HEAD, 128)).T[0:8, :]
    dkv[:HEAD, :] = grad.astype(bf16)
    dkv[HEAD:, :] = dv[...].T.astype(bf16)


def bwd(qh, kh, scales, *rest):
    return call(
        bwd_body,
        "attend_grad",
        [
            sds((LH * HEAD, HALF), bf16),
            sds((LH * HEAD, HALF), bf16),
            sds((2 * HEAD, ROWS), bf16),
            sds((8, HEAD), f32),
            sds((8, HEAD), f32),
        ],
        [
            pltpu.VMEM((ROWS, ROWS), f32),
            pltpu.VMEM((ROWS, LH * HALF), bf16),
            pltpu.VMEM((ROWS, LH * HALF), bf16),
            pltpu.VMEM((LH * HEAD, ROWS), f32),
            pltpu.VMEM((ROWS, HEAD), f32),
            pltpu.VMEM((ROWS, HEAD), f32),
            pltpu.VMEM((HEAD, ROWS), f32),
            pltpu.VMEM((8, ROWS), f32),
        ],
        (*qh, *kh, *scales, *rest),
    )


def qkv_grad_body(where, n1t, dq0, dq1, own, sib, out, tot, dt):
    @pl.when(pl.program_id(0) == 0)
    def _():
        tot[:, :HALF] = (own[:, :HALF].astype(f32) + sib[:, HALF:].astype(f32)).astype(bf16)
        tot[:, HALF:] = (own[:, HALF:].astype(f32) + sib[:, :HALF].astype(f32)).astype(bf16)
        dt[:512, :HALF] = dq0[...]
        dt[:512, HALF:] = dq1[...]
        upper = where[2] == 1
        dt[512:576, :] = jnp.where(upper, tot[64:128, :], tot[:64, :])
        dt[576:, :] = jnp.where(upper, tot[192:, :], tot[128:192, :])

    out[...] = dot_t(n1t[...], dt[...]).astype(bf16)


def qkv_grad(where, n1t, dq0, dq1, own, sib):
    return grid_call(
        qkv_grad_body,
        "qkv_weight_grad",
        (2,),
        [
            rows_of((1024, ROWS)),
            whole((512, HALF)),
            whole((512, HALF)),
            whole((2 * HEAD, ROWS)),
            whole((2 * HEAD, ROWS)),
        ],
        [rows_of((1024, 640)), whole((2 * HEAD, ROWS))],
        [sds((D, 640), bf16), sds((2 * HEAD, ROWS), bf16)],
        [pltpu.VMEM((640, ROWS), bf16)],
        (where, n1t, dq0, dq1, own, sib),
        scalars=1,
    )


def widen_body(grads, gq, gkt, gvt):
    gq[...] = grads[:, :512].astype(f32)
    both = grads[:, 512:].astype(f32).T
    gkt[...] = both[:64]
    gvt[...] = both[64:]


def widen(grads):
    return grid_call(
        widen_body,
        "widen_grads",
        (4,),
        [rows_of((512, 640))],
        [rows_of((512, 512)), cols_of((64, 512)), cols_of((64, 512))],
        [sds((D, 512), f32), sds((64, D), f32), sds((64, D), f32)],
        [],
        (grads,),
    )


def add_body(a, b, c, d, *outs):
    for i, out in enumerate(outs):
        out[...] = (
            (a[i].astype(f32) + b[i].astype(f32)) + (c[i].astype(f32) + d[i].astype(f32))
        ).astype(bf16)


def add_parts(parts):
    shape = parts[0].shape[1:]
    return call(add_body, "add_parts", [sds(shape, bf16)] * 4, [], tuple(parts))


def normed_grad_body(wa, wb, wkv, dq0, dqr, tot, n0, n1, n2, n3, b0, b1, b2, b3, gg1, grads):
    @pl.when(pl.program_id(0) == 0)
    def _():
        flip(dq0, grads, 0, 0)
        flip(dqr, grads, 0, 512)
        flip(tot, grads, 0, 1024)

    total = (
        dot(grads[:, :512], wa[...])
        + dot(grads[:, 512:1024], wb[...])
        + dot(grads[:, 1024:], wkv[...])
    )
    gain = jnp.zeros((1, 512), f32)
    for dy, (out, rows) in enumerate(((b0, n0), (b1, n1), (b2, n2), (b3, n3))):
        part = total[dy * T : (dy + 1) * T, :]
        out[...] = part.astype(bf16)
        gain = gain + jnp.sum(part * rows[...].astype(f32), axis=0, keepdims=True)
    gg1[...] = jnp.broadcast_to(gain, (8, 512))


def normed_grad(wa, wb, wkv, dq0, dqr, tot, n1):
    return grid_call(
        normed_grad_body,
        "normed_grad",
        (4,),
        [
            cols_of((512, 512)),
            cols_of((512, 512)),
            cols_of((256, 512)),
            whole((512, HALF)),
            whole((512, HALF)),
            whole((2 * HEAD, HALF)),
        ]
        + [cols_of((T, 512))] * 4,
        [cols_of((T, 512))] * 4 + [cols_of((8, 512))],
        [sds((T, D), bf16)] * 4 + [sds((8, D), f32)],
        [pltpu.VMEM((HALF, 1280), bf16)],
        (wa, wb, wkv, dq0, dqr, tot, *n1),
    )


def add_last_body(a, b, c, d, out):
    out[...] = (
        (a[...].astype(f32) + b[...].astype(f32)) + (c[...].astype(f32) + d[...].astype(f32))
    ).astype(bf16)


def add_last(parts):
    return call(add_last_body, "add_last", [sds(parts[0].shape, bf16)], [], tuple(parts))


def stack_body(a, b, c, d, out):
    for i, part in enumerate((a, b, c, d)):
        out[i] = part[...]


def stack(parts):
    shape = (4, *parts[0].shape)
    return call(stack_body, "stack_parts", [sds(shape, bf16)], [], tuple(parts))[0]


def place_out_body(where, c0, c1, c2, c3, out):
    for dx, chunks in enumerate((c0, c1, c2, c3)):
        for dz in range(4):
            chunk = lax.rem(where[1] + dx, 4) * 4 + lax.rem(where[0] + dz, 4)
            cols = pl.ds(pl.multiple_of(chunk * 128, 128), 128)
            out[:, cols] = chunks[dz].astype(f32)


def place_out(where, chunks):
    return call(
        place_out_body,
        "place_output_grads",
        [sds((512, D), f32)],
        [],
        (where, *chunks),
        smem=(0,),
    )[0]


def final_body(b0, b1, b2, b3, x0, ghid, g1, out):
    c = (b0[...].astype(f32) + b1[...].astype(f32)) + (b2[...].astype(f32) + b3[...].astype(f32))
    v = x0[...].astype(f32)
    r = lax.rsqrt(jnp.mean(v * v, axis=-1, keepdims=True) + EPS)
    u = c * g1[...]
    m = jnp.mean(u * v, axis=-1, keepdims=True)
    out[...] = ghid[...] + r * u - v * (r * r * r * m)


def final(b, x0, ghid, g1):
    return call(final_body, "input_grad", [sds((T, D), f32)], [], (*b, x0, ghid, g1))[0]


def fold_body(parts, out):
    def add(i, total):
        return total + parts[i].astype(f32)

    total = lax.fori_loop(0, E, add, jnp.zeros((24, 128), f32))
    numbers = total[SEG : SEG + 1] + total[SEG + 1 : SEG + 2]
    first = numbers.astype(bf16).astype(f32)
    rows = jnp.concatenate(
        [total[:SEG], first, numbers - first, jnp.zeros((6, 128), f32)], axis=0
    ).astype(bf16)

    def put(i, carry):
        out[i] = rows
        return carry

    lax.fori_loop(0, E, put, 0)


def fold(parts):
    return call(fold_body, "fold_small", [sds((E, 24, 128), bf16)], [], (parts,))[0]


def sibling(x):
    return lax.ppermute(x, "shard", [(i, i ^ 1) for i in range(8)])


def from_chip(x, dy):
    return lax.ppermute(x, "shard", [(i, (i - 2 * dy) % 8) for i in range(8)])


def to_chip(x, dy):
    return lax.ppermute(x, "shard", [(i, (i + 2 * dy) % 8) for i in range(8)])


def exchange(x):
    return lax.all_to_all(x, ALL, split_axis=0, concat_axis=0, tiled=True)


def spread(x):
    return [to_chip(x[d], d) for d in (1, 3, 2)]


def on_expert(x, dz, dx):
    pairs = [
        (z * 4 + c, ((z + dz) % 4) * 4 + (c + dx) % 4) for z in range(4) for c in range(4)
    ]
    return lax.ppermute(x, "expert", pairs)


def move(x, axis, distance):
    return on_expert(x, distance, 0) if axis == 0 else on_expert(x, 0, distance)


def collect(parts, axis):
    return [parts[0]] + [move(parts[d], axis, d) for d in (1, 3, 2)]


def share(x, axis):
    return [x] + [move(x, axis, (4 - d) % 4) for d in (1, 2, 3)]


def after(value, *others):
    return lax.optimization_barrier((value, *others))[0]


def on_device(
    block_input, out_grad, norm1_gain, w_query, w_key, w_value, query_gain, key_gain, w_out,
    norm2_gain, w_router, w_gate, w_up, w_down, seq_lengths, token_places, expert_routes,
):
    shard, owner = lax.axis_index("shard"), lax.axis_index("expert")
    chip, core = shard // 2, shard % 2
    where = jnp.stack([owner // 4, owner % 4, core, chip]).astype(jnp.int32)
    core_id = core.reshape(1)
    g1 = norm1_gain.astype(f32).reshape(1, D)
    g2 = norm2_gain.astype(f32).reshape(1, D)
    gq = query_gain.astype(f32).reshape(1, HEAD)
    gk = key_gain.astype(f32).reshape(1, HEAD)

    x_own = [block_input] + [from_chip(block_input, dy) for dy in (1, 2, 3)]
    x_sib = [sibling(block_input)]

    chips = (chip + jnp.arange(4)) % 4
    order = jnp.concatenate([chips * 2 + core, chips * 2 + 1 - core])
    places = token_places[0].reshape(8, T)[order].reshape(ROWS)
    lengths = seq_lengths[0]
    ends = jnp.cumsum(lengths)
    starts = jnp.sum(
        jnp.where(places[:, None] >= ends[None, :], lengths[None, :], 0), axis=1
    )
    positions = (places - starts).astype(f32)
    info = jnp.concatenate(
        [places[None].astype(f32), starts[None].astype(f32), jnp.zeros((6, ROWS), f32)], axis=0
    )
    inverse_freq = ROPE_BASE ** (-jnp.arange(0, HEAD, 2).astype(f32) / HEAD)
    angles = inverse_freq[:, None] * positions[None, :]
    cos, sin = jnp.cos(angles), jnp.sin(angles)

    ids, ids_t = route_tables(expert_routes.T)
    assign_t = ids_t[8:12]
    expert_list = ids[:, 0:4].reshape(-1)
    slot_list = ids[:, 4:8].reshape(-1)

    wk_t, wv_t = w_key.T, w_value.T
    wk_s, wv_s = sibling(wk_t), sibling(wv_t)
    wq_t = w_query.T
    wq_ts = sibling(wq_t)

    og_wire = pack(out_grad, assign_t)
    x_own, x_sib, og_wire, wq_t, cos, sin, info, wk_s, wv_s = lax.optimization_barrier(
        (x_own, x_sib, og_wire, wq_t, cos, sin, info, wk_s, wv_s)
    )
    x_sib += [sibling(x_own[dy]) for dy in (1, 2, 3)]
    blocks = [side[dy] for dy in range(4) for side in (x_own, x_sib)]
    weights = (g1, wq_t, wk_t, wk_s, wv_t, wv_s, gq, gk, cos, sin)
    *pieces, wkv = qkv((0, 1, 2, 3), core_id, blocks, *weights)
    pieces = [pieces[7 * dy : 7 * dy + 7] for dy in range(4)]
    qh, q, kh, k, v, scales, n1 = zip(*pieces)
    got_grads = exchange(og_wire)
    wo_s = sibling(after(w_out, q[0]))
    ot0, ot1, linv, qt, kt, kn, vn = attend(q, k, v, info)
    blocks = outproj(ot0, sibling(ot1), w_out, wo_s)
    blocks = [blocks[0]] + spread(blocks)
    hidden, n2, probs, gates, wire = router(blocks, block_input, g2, w_router, ids, assign_t)
    got_rows = exchange(wire)

    n1_t = transpose_rows(after(n1, wire))
    gate_list = gates[:, :4].reshape(-1)
    grad_rows, grad_act = expert_grad(after(got_grads, wire), w_down[0])
    got_rows, n1_t, grad_act, gate_list, wq_ts = lax.optimization_barrier(
        (got_rows, n1_t, grad_act, gate_list, wq_ts)
    )

    back, rows, act, scaled_act, dg, du = expert_main(got_rows, w_gate[0], w_up[0], grad_act)
    back_wire = exchange(back)

    rows, act, scaled_act, dg, du = after((rows, act, scaled_act, dg, du), back)
    out_wire = expert_out(act, w_down[0])

    def weight_grad(a, b):
        return lax.dot_general(a, b, (((0,), (0,)), ((), ())), preferred_element_type=f32)

    grad_wgate = weight_grad(rows, dg)
    grad_wup = weight_grad(rows, du)
    grad_wdown = weight_grad(scaled_act, grad_rows)
    back_wire, out_wire, grad_wgate, grad_wup, grad_wdown = lax.optimization_barrier(
        (back_wire, out_wire, grad_wgate, grad_wup, grad_wdown)
    )

    ghid, gatt, grouter, gg2 = combine(
        where, expert_list, slot_list, gate_list, back_wire, hidden, n2, probs, gates, ids,
        out_grad, g2, w_router,
    )
    g_own = [gatt] + [from_chip(gatt, dy) for dy in (1, 2, 3)]
    g_sib = [sibling(block) for block in g_own]
    returned = exchange(after(out_wire, *g_sib))
    *out_parts, dt = pre(where, g_own + g_sib, ot0, ot1, w_out)

    dq0, dq1, dkv, ggq, ggk = bwd(
        qh, kh, scales, qt, kt, kn, vn, dt, ot0, ot1, linv, info, cos, sin, gq, gk
    )
    out_parts = collect(out_parts, 1)
    dq_sib, dkv_sib = sibling(dq1), sibling(dkv)
    gw, dkv_total = qkv_grad(where, n1_t, dq0, dq1, dkv, dkv_sib)
    returned, dq0 = lax.optimization_barrier((returned, dq0))
    blocks = normed_grad(wq_t, wq_ts, wkv, dq0, dq_sib, dkv_total, n1)
    vector = jnp.concatenate([blocks[4][0] / g1[0], gg2[0], ggq[0], ggk[0]])
    per = vector.shape[0] // E
    vector = jnp.pad(vector.reshape(E, 1, per), ((0, 0), (0, 0), (0, 128 - per)))
    first = vector.astype(bf16)
    second = (vector - first.astype(f32)).astype(bf16)
    small = jnp.concatenate(
        [grouter.reshape(E, SEG, E), first, second, jnp.zeros((E, 6, 128), bf16)], axis=1
    )
    small = exchange(fold(exchange(small)))
    blocks = [blocks[0]] + spread(blocks)
    gw = lax.psum(gw, "expert")
    out_parts = collect(add_parts(out_parts), 0)
    out_parts, blocks = lax.optimization_barrier((out_parts, blocks))
    chunks = share(stack(share(add_last(out_parts)[0], 0)), 1)
    grad_input = final(blocks, block_input, ghid, g1)
    result = result_rows(expert_list, slot_list, gate_list, returned, hidden)
    grad_wout = place_out(where, chunks)
    gw, small, grad_input, grad_wout, result = lax.optimization_barrier(
        (gw, small, grad_input, grad_wout, result)
    )
    grad_wq, grad_wk, grad_wv = widen(gw)
    grad_router = small[:, :SEG].reshape(D, E).astype(f32)
    vector = small[:, SEG, :per].astype(f32) + small[:, SEG + 1, :per].astype(f32)
    vector = vector.reshape(-1)
    return (
        result,
        grad_input,
        vector[:D],
        grad_wq,
        grad_wk.T,
        grad_wv.T,
        vector[2 * D : 2 * D + HEAD],
        vector[2 * D + HEAD :],
        grad_wout,
        vector[D : 2 * D],
        grad_router,
        grad_wgate[None],
        grad_wup[None],
        grad_wdown[None],
    )


def solution(mesh):
    rows = P(("expert", "shard"), None)
    experts = P(("expert", "shard"), None, None)
    columns = P(None, "shard")
    return jax.shard_map(
        on_device,
        mesh=mesh,
        in_specs=(
            rows, rows, P(), columns, columns, columns, P(), P(), P("shard", None), P(), P(),
            experts, experts, experts, P("expert", None), P("expert", None), rows,
        ),
        out_specs=(
            rows, rows, P(), columns, columns, columns, P(), P(), P("shard", None), P(), P(),
            experts, experts, experts,
        ),
        check_vma=False,
    )
```

```python
import functools

import jax
import jax.numpy as jnp
from jax import lax
from jax.experimental import pallas as pl
from jax.experimental.pallas import tpu as pltpu
from jax.sharding import PartitionSpec as P

EPS = 1e-06
ROPE_BASE = 1000000.0
LOG2E = 1.4426950408889634
T = 128
D = 2048
HEAD = 128
LH = 4
E = 128
CAP = 5
SLOTS = E * CAP
SEG = D // 128
WIRE = CAP * SEG + 8
ROWS = 1024
HALF = 512
F = 768
bf16 = jnp.bfloat16
f32 = jnp.float32
ALL = ("expert", "shard")
COSTS = {
    "attend": 11,
    "out_projection": 5,
    "router": 6,
    "transpose_rows": 6,
    "expert_grad_rows": 8,
    "expert_main": 18,
    "expert_out": 7,
    "combine_grads": 7,
    "head_grad": 4,
    "out_projection_grad": 7,
}


def cost(micros):
    return pl.CostEstimate(
        flops=1, bytes_accessed=int(micros * 0.6e6) + 1, transcendentals=0
    )


def dot(a, b):
    return jnp.dot(a, b, preferred_element_type=f32)


def dot_t(a, b):
    return lax.dot_general(a, b, (((1,), (1,)), ((), ())), preferred_element_type=f32)


def call(kernel, name, outs, scratch, args, smem=()):
    in_specs = [
        pl.BlockSpec(memory_space=pltpu.SMEM if i in smem else pltpu.VMEM)
        for i in range(len(args))
    ]
    return pl.pallas_call(
        kernel,
        out_shape=outs,
        in_specs=in_specs,
        out_specs=[pl.BlockSpec(memory_space=pltpu.VMEM) for _ in outs],
        scratch_shapes=scratch,
        compiler_params=pltpu.CompilerParams(vmem_limit_bytes=63 * 1024 * 1024),
        cost_estimate=cost(COSTS.get(name, 0)),
        name=name,
    )(*args)


def grid_call(kernel, name, grid, in_specs, out_specs, outs, scratch, args, scalars=0):
    return pl.pallas_call(
        kernel,
        out_shape=outs,
        grid_spec=pltpu.PrefetchScalarGridSpec(
            num_scalar_prefetch=scalars,
            grid=grid,
            in_specs=in_specs,
            out_specs=out_specs,
            scratch_shapes=scratch,
        ),
        compiler_params=pltpu.CompilerParams(
            vmem_limit_bytes=63 * 1024 * 1024, dimension_semantics=("arbitrary",)
        ),
        cost_estimate=cost(COSTS.get(name, 0)),
        name=name,
    )(*args)


def copy_call(kernel, name, outs, scratch, copies, args, smem=()):
    return pl.pallas_call(
        kernel,
        out_shape=outs,
        in_specs=[
            pl.BlockSpec(memory_space=pltpu.SMEM if i in smem else pl.ANY)
            for i in range(len(args))
        ],
        out_specs=[pl.BlockSpec(memory_space=pl.ANY)] * len(outs),
        scratch_shapes=[*scratch, pltpu.SemaphoreType.DMA((copies,))],
        compiler_params=pltpu.CompilerParams(vmem_limit_bytes=63 * 1024 * 1024),
        cost_estimate=cost(COSTS.get(name, 0)),
        name=name,
    )(*args)


class Copies:
    def __init__(self, sems):
        self.sems, self.count, self.leaving = sems, 0, []

    def bring(self, source, dest):
        item = pltpu.make_async_copy(source, dest, self.sems.at[self.count])
        self.count += 1
        item.start()
        return item

    def take(self, source, dest):
        self.leaving.append(self.bring(source, dest))

    def finish(self):
        for item in self.leaving:
            item.wait()


def whole(shape):
    return pl.BlockSpec(shape, lambda i, *_: (0,) * len(shape))


def rows_of(shape):
    return pl.BlockSpec(shape, lambda i, *_: (i, 0))


def cols_of(shape):
    return pl.BlockSpec(shape, lambda i, *_: (0, i))


def sds(shape, dtype):
    return jax.ShapeDtypeStruct(shape, dtype)


def split_rows(wire, dest):
    for s in range(CAP):
        for h in range(2):
            rows = slice(s * E + h * 64, s * E + (h + 1) * 64)
            block = wire[h * 64 : (h + 1) * 64, s * SEG : (s + 1) * SEG, :]
            dest[rows, :] = block.reshape(64, D)


def join_rows(source, wire):
    for s in range(CAP):
        for h in range(2):
            rows = slice(s * E + h * 64, s * E + (h + 1) * 64)
            wire[h * 64 : (h + 1) * 64, s * SEG : (s + 1) * SEG, :] = source[rows, :].reshape(
                64, SEG, 128
            )


def put_numbers(columns, wire):
    lane = lax.broadcasted_iota(jnp.int32, (E, 128), 1)
    plane = jnp.zeros((E, 128), f32)
    for s in range(CAP):
        plane = jnp.where(lane == s, columns[s], plane)
    first = plane.astype(bf16)
    rest = plane - first.astype(f32)
    second = rest.astype(bf16)
    third = (rest - second.astype(f32)).astype(bf16)
    none = jnp.zeros((E, 5 * 128), bf16)
    wide = jnp.concatenate([first, second, third, none], axis=1)
    wire[:, CAP * SEG :, :] = wide.reshape(E, 8, 128)


def get_numbers(wire):
    wide = wire[:, CAP * SEG :, :].reshape(E, 8 * 128)
    return (
        wide[:, :128].astype(f32) + wide[:, 128:256].astype(f32) + wide[:, 256:384].astype(f32)
    )


def pack_rows(x_ref, at_ref, wire, rows):
    slot = lax.broadcasted_iota(jnp.int32, (SLOTS, T), 0)
    hit = slot == at_ref[0:1, :]
    for k in range(1, 4):
        hit = hit | (slot == at_ref[k : k + 1, :])
    pick = jnp.where(hit, 1.0, 0.0).astype(bf16)
    for j in range(8):
        cols = slice(j * 256, (j + 1) * 256)
        rows[:, cols] = dot(pick, x_ref[:, cols]).astype(bf16)
    join_rows(rows, wire)


def pack_body(x_ref, at_ref, wire, rows):
    pack_rows(x_ref, at_ref, wire, rows)
    wire[:, CAP * SEG :, :] = jnp.zeros((E, 8, 128), bf16)


def pack(x, assign_t):
    return call(
        pack_body,
        "pack_rows",
        [sds((E, WIRE, 128), bf16)],
        [pltpu.VMEM((SLOTS, D), bf16)],
        (x, assign_t),
    )[0]


def sum_rows(wire, experts, slots, gates, out):
    def body(i, carry):
        for u in range(8):
            t = i * 8 + u
            total = None
            for k in range(4):
                p = t * 4 + k
                rows = pl.ds(pl.multiple_of(slots[p] * SEG, SEG), SEG)
                part = wire[experts[p], rows, :].astype(f32) * gates[p]
                total = part if total is None else total + part
            out[pl.ds(pl.multiple_of(t * SEG, SEG), SEG), :] = total
        return carry

    lax.fori_loop(0, T // 8, body, 0)


def column(row):
    return jnp.broadcast_to(row, (128, 128)).T[:, 0:1]


def qkv_body(pieces, *refs):
    count = len(pieces)
    core, blocks = refs[0], refs[1 : 1 + 2 * count]
    g1, wqt, wk, wks, wv, wvs, gq, gk, cos, sin = refs[1 + 2 * count : 11 + 2 * count]
    outs = refs[11 + 2 * count :]
    wkv = outs[-1]
    lower = core[0] == 0
    wkv[0:64, :] = jnp.where(lower, wk[...], wks[...])
    wkv[64:128, :] = jnp.where(lower, wks[...], wk[...])
    wkv[128:192, :] = jnp.where(lower, wv[...], wvs[...])
    wkv[192:256, :] = jnp.where(lower, wvs[...], wv[...])
    gain_q, gain_k = column(gq[...]), column(gk[...])
    for number, piece in enumerate(pieces):
        qn, qt, kn, kt, vt, scale, n1 = outs[7 * number : 7 * number + 7]
        for half in range(2):
            x = blocks[2 * number + half][...].astype(f32)
            r = lax.rsqrt(jnp.mean(x * x, axis=-1, keepdims=True) + EPS)
            n1[half * T : (half + 1) * T, :] = (x * r * g1[...]).astype(bf16)
        raw = dot_t(wqt[...], n1[...])
        raw_kv = dot_t(wkv[...], n1[...])
        first, second = piece * T, HALF + piece * T
        c = jnp.concatenate([cos[:, first : first + T], cos[:, second : second + T]], axis=1)
        s = jnp.concatenate([sin[:, first : first + T], sin[:, second : second + T]], axis=1)

        def path(v, gain, factor, keep, index):
            r = lax.rsqrt(jnp.mean(v * v, axis=0, keepdims=True) + EPS)
            scale[index : index + 1, :] = r
            v = v * r
            keep[...] = v.astype(bf16)
            v = v * gain
            low, high = v[:64], v[64:]
            return (
                ((low * c - high * s) * factor).astype(bf16),
                ((high * c + low * s) * factor).astype(bf16),
            )

        scale[...] = jnp.zeros_like(scale)
        for h in range(LH):
            heads = slice(h * HEAD, (h + 1) * HEAD)
            low, high = path(raw[heads], gain_q, HEAD ** (-0.5), qn.at[heads, :], h)
            qt[h * HEAD : h * HEAD + 64, :] = low
            qt[h * HEAD + 64 : (h + 1) * HEAD, :] = high
        key = raw_kv[:HEAD].astype(bf16)
        low, high = path(key.astype(f32), gain_k, 1.0, kn, LH)
        kt[:64, :] = low
        kt[64:, :] = high
        vt[...] = raw_kv[HEAD:].astype(bf16)


def qkv(pieces, core, blocks, *args):
    outs = [
        sds((LH * HEAD, 2 * T), bf16),
        sds((LH * HEAD, 2 * T), bf16),
        sds((HEAD, 2 * T), bf16),
        sds((HEAD, 2 * T), bf16),
        sds((HEAD, 2 * T), bf16),
        sds((8, 2 * T), f32),
        sds((2 * T, D), bf16),
    ] * len(pieces)
    keep = 0 in pieces
    return call(
        functools.partial(qkv_body, pieces),
        "qkv" + "".join(str(p) for p in pieces),
        outs + ([sds((2 * HEAD, D), bf16)] if keep else []),
        [] if keep else [pltpu.VMEM((2 * HEAD, D), bf16)],
        (core, *blocks, *args),
        smem=(0,),
    )


def build_mask(info, mask):
    for b in range(8):
        keys = jnp.broadcast_to(info[0:1, b * T : (b + 1) * T], (T, T)).T
        for j in range(8):
            cols = slice(j * T, (j + 1) * T)
            inside = (keys >= info[1:2, cols]) & (keys <= info[0:1, cols])
            mask[b * T : (b + 1) * T, cols] = jnp.where(inside, 1.0, 0.0)


def attend_body(*refs):
    q, k, v = refs[0:4], refs[4:8], refs[8:12]
    info, ot0, ot1, linv, qt, kt, kn, vn, mask, vt = refs[12:]
    for dy in range(4):
        for dc in range(2):
            to = slice(dc * HALF + dy * T, dc * HALF + (dy + 1) * T)
            src = slice(dc * T, (dc + 1) * T)
            qt[:, to] = q[dy][:, src]
            kt[:, to] = k[dy][:, src]
            vt[:, to] = v[dy][:, src]
    for b in range(8):
        rows = slice(b * T, (b + 1) * T)
        kn[rows, :] = kt[:, rows].astype(f32).T.astype(bf16)
        vn[rows, :] = vt[:, rows].astype(f32).T.astype(bf16)
    build_mask(info, mask)
    for half, out in ((1, ot1), (0, ot0)):
        cols = slice(half * HALF, (half + 1) * HALF)
        for h in range(LH):
            heads = slice(h * HEAD, (h + 1) * HEAD)
            scores = dot(kn[...], qt[heads, cols])
            weights = jnp.exp2(scores * LOG2E) * mask[:, cols]
            inverse = 1.0 / jnp.sum(weights, axis=0, keepdims=True)
            out[heads, :] = (dot(vt[...], weights.astype(bf16)) * inverse).astype(bf16)
            linv[h : h + 1, cols] = inverse


def attend(q, k, v, info):
    return call(
        attend_body,
        "attend",
        [
            sds((LH * HEAD, HALF), bf16),
            sds((LH * HEAD, HALF), bf16),
            sds((8, ROWS), f32),
            sds((LH * HEAD, ROWS), bf16),
            sds((HEAD, ROWS), bf16),
            sds((ROWS, HEAD), bf16),
            sds((ROWS, HEAD), bf16),
        ],
        [pltpu.VMEM((ROWS, ROWS), f32), pltpu.VMEM((HEAD, ROWS), bf16)],
        (*q, *k, *v, info),
    )


def flip(source, dest, row, col):
    height, width = source.shape
    for a in range(height // 128):
        for b in range(width // 128):
            block = source[a * 128 : (a + 1) * 128, b * 128 : (b + 1) * 128]
            rows = slice(row + b * 128, row + (b + 1) * 128)
            dest[rows, col + a * 128 : col + (a + 1) * 128] = block.astype(f32).T.astype(bf16)


def outproj_body(ot0, otr, wa, wb, b0, b1, b2, b3, heads):
    @pl.when(pl.program_id(0) == 0)
    def _():
        flip(ot0, heads, 0, 0)
        flip(otr, heads, 0, 512)

    total = dot(heads[:, :512], wa[...]) + dot(heads[:, 512:], wb[...])
    for dy, out in enumerate((b0, b1, b2, b3)):
        out[...] = total[dy * T : (dy + 1) * T, :].astype(bf16)


def outproj(ot0, otr, wa, wb):
    return grid_call(
        outproj_body,
        "out_projection",
        (2,),
        [whole((512, HALF)), whole((512, HALF)), cols_of((512, 1024)), cols_of((512, 1024))],
        [cols_of((T, 1024))] * 4,
        [sds((T, D), bf16)] * 4,
        [pltpu.VMEM((HALF, 1024), bf16)],
        (ot0, otr, wa, wb),
    )


def transpose_body(n0, n1, n2, n3, out):
    for dy, piece in enumerate((n0, n1, n2, n3)):
        for dc in range(2):
            flip(piece.at[dc * T : (dc + 1) * T, :], out, 0, dc * HALF + dy * T)


def transpose_rows(pieces):
    return call(transpose_body, "transpose_rows", [sds((D, ROWS), bf16)], [], tuple(pieces))[0]


def route_body(rt, ids, ids_t):
    lane = lax.broadcasted_iota(jnp.int32, (T, E), 1)
    row = lax.broadcasted_iota(jnp.int32, (T, E), 0)
    wide = jnp.concatenate([rt[...].astype(f32), jnp.zeros((124, T), f32)], axis=0).T
    hot = [jnp.where(lane.astype(f32) == wide[:, k : k + 1], 1.0, 0.0) for k in range(4)]
    earlier = jnp.where(lane < row, 1.0, 0.0).astype(bf16)
    before = dot(earlier, (hot[0] + hot[1] + hot[2] + hot[3]).astype(bf16))
    table = wide
    for k in range(4):
        slot = jnp.sum(before * hot[k], axis=1, keepdims=True)
        table = jnp.where(lane == 4 + k, slot, table)
        table = jnp.where(lane == 8 + k, slot * E + wide[:, k : k + 1], table)
    ids[...] = table.astype(jnp.int32)
    ids_t[...] = table.T[0:16, :].astype(jnp.int32)


def route_tables(routes_t):
    return call(
        route_body,
        "route_tables",
        [sds((T, 128), jnp.int32), sds((16, T), jnp.int32)],
        [],
        (routes_t,),
    )


def router_body(b0, b1, b2, b3, x0, g2, wr, ids, at, hidden, n2, probs, gates, wire, rows):
    v = x0[...].astype(f32) + (
        (b0[...].astype(f32) + b1[...].astype(f32))
        + (b2[...].astype(f32) + b3[...].astype(f32))
    )
    hidden[...] = v
    r = lax.rsqrt(jnp.mean(v * v, axis=-1, keepdims=True) + EPS)
    n2[...] = (v * r * g2[...]).astype(bf16)
    logits = dot(n2[...], wr[...])
    pack_rows(n2, at, wire, rows)
    expo = jnp.exp(logits - jnp.max(logits, axis=-1, keepdims=True))
    p = expo / jnp.sum(expo, axis=-1, keepdims=True)
    probs[...] = p
    lane = lax.broadcasted_iota(jnp.int32, (T, E), 1)
    chosen = [
        jnp.sum(jnp.where(lane == ids[:, k : k + 1], p, 0.0), axis=-1, keepdims=True)
        for k in range(4)
    ]
    total = chosen[0] + chosen[1] + chosen[2] + chosen[3]
    packed = jnp.where(lane == 4, total, 0.0)
    for k in range(4):
        packed = jnp.where(lane == k, chosen[k] / total, packed)
    gates[...] = packed
    across = packed.T
    expert = lax.broadcasted_iota(jnp.int32, (E, T), 0)
    columns = []
    for s in range(CAP):
        mine = jnp.zeros((E, T), f32)
        for k in range(4):
            mine = jnp.where(expert + s * E == at[k : k + 1, :], across[k : k + 1, :], mine)
        columns.append(jnp.sum(mine, axis=1, keepdims=True))
    put_numbers(columns, wire)


def router(b, x0, g2, wr, ids, assign_t):
    return call(
        router_body,
        "router",
        [
            sds((T, D), f32),
            sds((T, D), bf16),
            sds((T, E), f32),
            sds((T, E), f32),
            sds((E, WIRE, 128), bf16),
        ],
        [pltpu.VMEM((SLOTS, D), bf16)],
        (*b, x0, g2, wr, ids, assign_t),
    )


def expert_grad_body(wire, wd, gr, ga):
    split_rows(wire, gr)

    def body(i, carry):
        cols = pl.ds(pl.multiple_of(i * 256, 256), 256)
        ga[:, cols] = dot_t(gr[...], wd[cols, :])
        return carry

    lax.fori_loop(0, F // 256, body, 0)


def expert_grad(wire, wd):
    return call(
        expert_grad_body,
        "expert_grad_rows",
        [sds((SLOTS, D), bf16), sds((SLOTS, F), f32)],
        [],
        (wire, wd),
    )


def expert_main_body(
    wire, wg, wu, ga, back, xs, act, acts, dg, du,
    wire_v, w_v, ga_v, xr, xs_v, act_v, acts_v, d_v, sc, sems,
):
    half = F // 2

    def copy(source, dest, number):
        return pltpu.make_async_copy(source, dest, sems.at[number])

    first = copy(wire, wire_v, 0)
    first.start()
    arrivals = []
    for c in range(2):
        cols = slice(c * half, (c + 1) * half)
        up_cols = slice(F + c * half, F + (c + 1) * half)
        group = [
            copy(wg.at[:, cols], w_v.at[:, cols], 1 + 3 * c),
            copy(wu.at[:, cols], w_v.at[:, up_cols], 2 + 3 * c),
            copy(ga.at[:, cols], ga_v.at[:, cols], 3 + 3 * c),
        ]
        for item in group:
            item.start()
        arrivals.append(group)
    first.wait()
    split_rows(wire_v, xr)
    gates = get_numbers(wire_v)
    sc[...] = jnp.zeros_like(sc)
    for c in range(2):
        for item in arrivals[c]:
            item.wait()
        cols = slice(c * half, (c + 1) * half)
        up_cols = slice(F + c * half, F + (c + 1) * half)
        gate = dot(xr[...], w_v[:, cols])
        up = dot(xr[...], w_v[:, up_cols])
        grad = ga_v[:, cols]
        s = 1.0 / (1.0 + jnp.exp(-gate))
        silu = gate * s
        a = silu * up
        act_v[:, cols] = a.astype(bf16)
        d_v[:, cols] = (grad * up * s * (1.0 + gate * (1.0 - s))).astype(bf16)
        d_v[:, up_cols] = (grad * silu).astype(bf16)
        sc[...] += jnp.sum(a * grad, axis=1, keepdims=True)
    departures = [copy(act_v, act, 7), copy(d_v.at[:, :F], dg, 8), copy(d_v.at[:, F:], du, 9)]
    for item in departures:
        item.start()
    for s in range(CAP):
        part = slice(s * E, (s + 1) * E)
        gate = gates[:, s : s + 1]
        xs_v[part, :] = (xr[part, :].astype(f32) * gate).astype(bf16)
        acts_v[part, :] = (act_v[part, :].astype(f32) * gate).astype(bf16)
    more = [copy(xs_v, xs, 10), copy(acts_v, acts, 11)]
    for item in more:
        item.start()
    for j in range(4):
        part = slice(j * 512, (j + 1) * 512)
        xr[:, part] = dot_t(d_v[...], w_v[part, :]).astype(bf16)
    join_rows(xr, wire_v)
    put_numbers([sc[s * E : (s + 1) * E, :] for s in range(CAP)], wire_v)
    last = copy(wire_v, back, 12)
    last.start()
    for item in departures + more + [last]:
        item.wait()


def expert_main(wire, wg, wu, ga):
    args = (wire, wg, wu, ga)
    outs = [
        sds((E, WIRE, 128), bf16),
        sds((SLOTS, D), bf16),
        sds((SLOTS, F), bf16),
        sds((SLOTS, F), bf16),
        sds((SLOTS, F), bf16),
        sds((SLOTS, F), bf16),
    ]
    return pl.pallas_call(
        expert_main_body,
        out_shape=outs,
        in_specs=[pl.BlockSpec(memory_space=pl.ANY)] * 4,
        out_specs=[pl.BlockSpec(memory_space=pl.ANY)] * 6,
        scratch_shapes=[
            pltpu.VMEM((E, WIRE, 128), bf16),
            pltpu.VMEM((D, 2 * F), bf16),
            pltpu.VMEM((SLOTS, F), f32),
            pltpu.VMEM((SLOTS, D), bf16),
            pltpu.VMEM((SLOTS, D), bf16),
            pltpu.VMEM((SLOTS, F), bf16),
            pltpu.VMEM((SLOTS, F), bf16),
            pltpu.VMEM((SLOTS, 2 * F), bf16),
            pltpu.VMEM((SLOTS, 1), f32),
            pltpu.SemaphoreType.DMA((13,)),
        ],
        compiler_params=pltpu.CompilerParams(vmem_limit_bytes=63 * 1024 * 1024),
        cost_estimate=cost(COSTS["expert_main"]),
        name="expert_main",
    )(*args)


def expert_out_body(act, wd, wire, rows):
    for j in range(8):
        cols = slice(j * 256, (j + 1) * 256)
        rows[:, cols] = dot(act[...], wd[:, cols]).astype(bf16)
    join_rows(rows, wire)


def expert_out(act, wd):
    return call(
        expert_out_body,
        "expert_out",
        [sds((E, CAP * SEG, 128), bf16)],
        [pltpu.VMEM((SLOTS, D), bf16)],
        (act, wd),
    )[0]


def combine_body(
    where, experts, slots, gate_list, wire, hidden, n2, probs, gates, ids, og, g2, wr,
    ghid, gatt, grouter, gg2, sums, gn2,
):
    sum_rows(wire, experts, slots, gate_list, sums)
    scores = get_numbers(wire)
    lane = lax.broadcasted_iota(jnp.int32, (T, E), 1)
    grads = []
    for k in range(4):
        hot = jnp.where(lane == ids[:, k : k + 1], 1.0, 0.0)
        rows = lax.dot_general(
            hot, scores, (((1,), (0,)), ((), ())),
            precision=lax.Precision.HIGHEST, preferred_element_type=f32,
        )
        picked = jnp.where(lane == ids[:, 4 + k : 5 + k], rows, 0.0)
        grads.append(jnp.sum(picked, axis=-1, keepdims=True))
    inner = sum(grads[k] * gates[:, k : k + 1] for k in range(4))
    inverse = 1.0 / gates[:, 4:5]
    grad_probs = jnp.zeros((T, E), f32)
    for k in range(4):
        grad_probs = jnp.where(
            lane == ids[:, k : k + 1], (grads[k] - inner) * inverse, grad_probs
        )
    p = probs[...]
    gl = (p * (grad_probs - jnp.sum(p * grad_probs, axis=-1, keepdims=True))).astype(bf16)
    for h in range(2):
        tokens = slice(h * 64, (h + 1) * 64)
        gn2[tokens, :] = sums[h * 1024 : (h + 1) * 1024, :].reshape(64, D)
    gn2[...] += dot_t(gl, wr[...])
    c = gn2[...]
    v = hidden[...]
    r = lax.rsqrt(jnp.mean(v * v, axis=-1, keepdims=True) + EPS)
    u = c * g2[...]
    m = jnp.mean(u * v, axis=-1, keepdims=True)
    total = og[...].astype(f32) + r * u - v * (r * r * r * m)
    ghid[...] = total
    gatt[...] = total.astype(bf16)
    gg2[...] = jnp.sum(c * (v * r), axis=0, keepdims=True)
    for j in range(SEG):
        cols = slice(j * 128, (j + 1) * 128)
        grouter[cols, :] = dot(n2[:, cols].astype(f32).T.astype(bf16), gl).astype(bf16)


def combine(*args):
    return call(
        combine_body,
        "combine_grads",
        [sds((T, D), f32), sds((T, D), bf16), sds((D, E), bf16), sds((1, D), f32)],
        [pltpu.VMEM((T * SEG, 128), f32), pltpu.VMEM((T, D), f32)],
        args,
        smem=(0, 1, 2, 3),
    )


def result_body(experts, slots, gate_list, wire, hidden, out, sums):
    sum_rows(wire, experts, slots, gate_list, sums)
    for h in range(2):
        tokens = slice(h * 64, (h + 1) * 64)
        mixture = sums[h * 1024 : (h + 1) * 1024, :].reshape(64, D)
        out[tokens, :] = (hidden[tokens, :] + mixture).astype(bf16)


def result_rows(*args):
    return call(
        result_body,
        "result",
        [sds((T, D), bf16)],
        [pltpu.VMEM((T * SEG, 128), f32)],
        args,
        smem=(0, 1, 2),
    )[0]


def pre_body(where, *refs):
    blocks, (ot0, ot1, wo, *outs) = refs[:8], refs[8:16]
    dt, (heads, rows_all, wo_v, grads, dt_v, sems) = refs[15], refs[16:]
    copies = Copies(sems)
    arrivals = [copies.bring(ot0, heads.at[:, :HALF]), copies.bring(ot1, heads.at[:, HALF:])]
    columns = []
    waits = []
    for step in range(4):
        start = lax.rem(where[1] + step, 4) * 512
        columns.append(pl.ds(pl.multiple_of(start, 512), 512))
        waits.append(
            [
                copies.bring(
                    blocks[b].at[:, columns[step]],
                    rows_all.at[b * T : (b + 1) * T, columns[step]],
                )
                for b in range(8)
            ]
        )
    last = copies.bring(wo, wo_v)
    for item in arrivals:
        item.wait()
    for step in range(4):
        for item in waits[step]:
            item.wait()
        grad = dot(heads[...], rows_all[:, columns[step]]).astype(bf16)
        for col in range(4):
            grads[step, lax.rem(col + 4 - where[0], 4)] = grad[:, col * 128 : (col + 1) * 128]
        copies.take(grads.at[step], outs[step])
    last.wait()
    dt_v[...] = dot_t(wo_v[...], rows_all[...]).astype(bf16)
    copies.take(dt_v, dt)
    copies.finish()


def pre(where, blocks, ot0, ot1, wo):
    return copy_call(
        pre_body,
        "out_projection_grad",
        [sds((4, 512, 128), bf16)] * 4 + [sds((LH * HEAD, ROWS), bf16)],
        [
            pltpu.VMEM((512, ROWS), bf16),
            pltpu.VMEM((ROWS, D), bf16),
            pltpu.VMEM((512, D), bf16),
            pltpu.VMEM((4, 4, 512, 128), bf16),
            pltpu.VMEM((512, ROWS), bf16),
        ],
        2 + 32 + 1 + 5,
        (where, *blocks, ot0, ot1, wo),
        smem=(0,),
    )


def bwd_body(*refs):
    qh, kh, scales = refs[0:4], refs[4:8], refs[8:12]
    (qt, kt, kn, vn, dt, ot0, ot1, linv, info, cos, sin, gq, gk) = refs[12:25]
    dq0, dq1, dkv, ggq, ggk, mask, wb, sb, dqt, dk, dv, raw, scale = refs[25:]
    for dc in range(2):
        for dy in range(4):
            to = slice(dc * HALF + dy * T, dc * HALF + (dy + 1) * T)
            scale[:, to] = scales[dy][:, dc * T : (dc + 1) * T]
    build_mask(info, mask)
    dk[...] = jnp.zeros_like(dk)
    dv[...] = jnp.zeros_like(dv)
    for half, out in ((0, ot0), (1, ot1)):
        cols = slice(half * HALF, (half + 1) * HALF)
        for h in range(LH):
            heads = slice(h * HEAD, (h + 1) * HEAD)
            part = slice(h * HALF, (h + 1) * HALF)
            scores = dot(kn[...], qt[heads, cols])
            weights = jnp.exp2(scores * LOG2E) * (mask[:, cols] * linv[h : h + 1, cols])
            grad = dt[heads, cols]
            delta = jnp.sum(
                grad.astype(f32) * out[heads, :].astype(f32), axis=0, keepdims=True
            )
            wb[:, part] = weights.astype(bf16)
            sb[:, part] = (weights * (dot(vn[...], grad) - delta)).astype(bf16)
            dqt[heads, cols] = dot(kt[...], sb[:, part])
        grads = jnp.concatenate([dt[h * HEAD : (h + 1) * HEAD, cols] for h in range(LH)], axis=1)
        queries = jnp.concatenate([qt[h * HEAD : (h + 1) * HEAD, cols] for h in range(LH)], axis=1)
        dv[...] += dot_t(wb[...], grads)
        dk[...] += dot_t(sb[...], queries)

    def unrope(v):
        low, high = v[:64], v[64:]
        c, s = cos[...], sin[...]
        return jnp.concatenate([low * c + high * s, high * c - low * s], axis=0)

    def norm_back(n, r, grad, gain):
        gain_grad = jnp.sum(grad * n, axis=1, keepdims=True)
        u = grad * gain
        return r * (u - n * jnp.mean(u * n, axis=0, keepdims=True)), gain_grad

    gain_q, gain_k = column(gq[...]), column(gk[...])
    total = jnp.zeros((HEAD, 1), f32)
    for h in range(LH):
        heads = slice(h * HEAD, (h + 1) * HEAD)
        for dy in range(4):
            for dc in range(2):
                to = slice(dc * HALF + dy * T, dc * HALF + (dy + 1) * T)
                raw[:, to] = qh[dy][heads, dc * T : (dc + 1) * T].astype(f32)
        grad, part = norm_back(raw[...], scale[h : h + 1, :], unrope(dqt[heads, :] * (HEAD ** (-0.5))), gain_q)
        total = total + part
        dq0[heads, :] = grad[:, :HALF].astype(bf16)
        dq1[heads, :] = grad[:, HALF:].astype(bf16)
    ggq[...] = jnp.broadcast_to(total, (HEAD, 128)).T[0:8, :]
    for dy in range(4):
        for dc in range(2):
            to = slice(dc * HALF + dy * T, dc * HALF + (dy + 1) * T)
            raw[:, to] = kh[dy][:, dc * T : (dc + 1) * T].astype(f32)
    grad, part = norm_back(raw[...], scale[LH : LH + 1, :], unrope(dk[...].T), gain_k)
    ggk[...] = jnp.broadcast_to(part, (HEAD, 128)).T[0:8, :]
    dkv[:HEAD, :] = grad.astype(bf16)
    dkv[HEAD:, :] = dv[...].T.astype(bf16)


def bwd(qh, kh, scales, *rest):
    return call(
        bwd_body,
        "attend_grad",
        [
            sds((LH * HEAD, HALF), bf16),
            sds((LH * HEAD, HALF), bf16),
            sds((2 * HEAD, ROWS), bf16),
            sds((8, HEAD), f32),
            sds((8, HEAD), f32),
        ],
        [
            pltpu.VMEM((ROWS, ROWS), f32),
            pltpu.VMEM((ROWS, LH * HALF), bf16),
            pltpu.VMEM((ROWS, LH * HALF), bf16),
            pltpu.VMEM((LH * HEAD, ROWS), f32),
            pltpu.VMEM((ROWS, HEAD), f32),
            pltpu.VMEM((ROWS, HEAD), f32),
            pltpu.VMEM((HEAD, ROWS), f32),
            pltpu.VMEM((8, ROWS), f32),
        ],
        (*qh, *kh, *scales, *rest),
    )


def qkv_grad_body(where, n1t, dq0, dq1, own, sib, out, tot, dt):
    @pl.when(pl.program_id(0) == 0)
    def _():
        tot[:, :HALF] = (own[:, :HALF].astype(f32) + sib[:, HALF:].astype(f32)).astype(bf16)
        tot[:, HALF:] = (own[:, HALF:].astype(f32) + sib[:, :HALF].astype(f32)).astype(bf16)
        dt[:512, :HALF] = dq0[...]
        dt[:512, HALF:] = dq1[...]
        upper = where[2] == 1
        dt[512:576, :] = jnp.where(upper, tot[64:128, :], tot[:64, :])
        dt[576:, :] = jnp.where(upper, tot[192:, :], tot[128:192, :])

    out[...] = dot_t(n1t[...], dt[...]).astype(bf16)


def qkv_grad(where, n1t, dq0, dq1, own, sib):
    return grid_call(
        qkv_grad_body,
        "qkv_weight_grad",
        (2,),
        [
            rows_of((1024, ROWS)),
            whole((512, HALF)),
            whole((512, HALF)),
            whole((2 * HEAD, ROWS)),
            whole((2 * HEAD, ROWS)),
        ],
        [rows_of((1024, 640)), whole((2 * HEAD, ROWS))],
        [sds((D, 640), bf16), sds((2 * HEAD, ROWS), bf16)],
        [pltpu.VMEM((640, ROWS), bf16)],
        (where, n1t, dq0, dq1, own, sib),
        scalars=1,
    )


def widen_body(grads, gq, gkt, gvt):
    gq[...] = grads[:, :512].astype(f32)
    both = grads[:, 512:].astype(f32).T
    gkt[...] = both[:64]
    gvt[...] = both[64:]


def widen(grads):
    return grid_call(
        widen_body,
        "widen_grads",
        (4,),
        [rows_of((512, 640))],
        [rows_of((512, 512)), cols_of((64, 512)), cols_of((64, 512))],
        [sds((D, 512), f32), sds((64, D), f32), sds((64, D), f32)],
        [],
        (grads,),
    )


def add_body(a, b, c, d, *outs):
    for i, out in enumerate(outs):
        out[...] = (
            (a[i].astype(f32) + b[i].astype(f32)) + (c[i].astype(f32) + d[i].astype(f32))
        ).astype(bf16)


def add_parts(parts):
    shape = parts[0].shape[1:]
    return call(add_body, "add_parts", [sds(shape, bf16)] * 4, [], tuple(parts))


def normed_grad_body(wa, wb, wkv, dq0, dqr, tot, n0, n1, n2, n3, b0, b1, b2, b3, gg1, grads):
    @pl.when(pl.program_id(0) == 0)
    def _():
        flip(dq0, grads, 0, 0)
        flip(dqr, grads, 0, 512)
        flip(tot, grads, 0, 1024)

    total = (
        dot(grads[:, :512], wa[...])
        + dot(grads[:, 512:1024], wb[...])
        + dot(grads[:, 1024:], wkv[...])
    )
    gain = jnp.zeros((1, 512), f32)
    for dy, (out, rows) in enumerate(((b0, n0), (b1, n1), (b2, n2), (b3, n3))):
        part = total[dy * T : (dy + 1) * T, :]
        out[...] = part.astype(bf16)
        gain = gain + jnp.sum(part * rows[...].astype(f32), axis=0, keepdims=True)
    gg1[...] = jnp.broadcast_to(gain, (8, 512))


def normed_grad(wa, wb, wkv, dq0, dqr, tot, n1):
    return grid_call(
        normed_grad_body,
        "normed_grad",
        (4,),
        [
            cols_of((512, 512)),
            cols_of((512, 512)),
            cols_of((256, 512)),
            whole((512, HALF)),
            whole((512, HALF)),
            whole((2 * HEAD, HALF)),
        ]
        + [cols_of((T, 512))] * 4,
        [cols_of((T, 512))] * 4 + [cols_of((8, 512))],
        [sds((T, D), bf16)] * 4 + [sds((8, D), f32)],
        [pltpu.VMEM((HALF, 1280), bf16)],
        (wa, wb, wkv, dq0, dqr, tot, *n1),
    )


def add_last_body(a, b, c, d, small, out):
    out[:512, :] = (
        (a[...].astype(f32) + b[...].astype(f32)) + (c[...].astype(f32) + d[...].astype(f32))
    ).astype(bf16)

    def add(i, total):
        return total + small[i].astype(f32)

    total = lax.fori_loop(0, E, add, jnp.zeros((24, 128), f32))
    numbers = total[SEG : SEG + 1] + total[SEG + 1 : SEG + 2]
    first = numbers.astype(bf16).astype(f32)
    out[512:, :] = jnp.concatenate(
        [total[:SEG], first, numbers - first, jnp.zeros((14, 128), f32)], axis=0
    ).astype(bf16)


def add_last(parts, small):
    args = (*parts, small)
    return call(add_last_body, "add_last", [sds((544, 128), bf16)], [], args)[0]


def stack_body(a, b, c, d, out):
    for i, part in enumerate((a, b, c, d)):
        out[i] = part[...]


def stack(parts):
    shape = (4, *parts[0].shape)
    return call(stack_body, "stack_parts", [sds(shape, bf16)], [], tuple(parts))[0]


def place_out_body(where, c0, c1, c2, c3, out):
    for dx, chunks in enumerate((c0, c1, c2, c3)):
        for dz in range(4):
            chunk = lax.rem(where[1] + dx, 4) * 4 + lax.rem(where[0] + dz, 4)
            cols = pl.ds(pl.multiple_of(chunk * 128, 128), 128)
            out[:, cols] = chunks[dz, :512, :].astype(f32)


def place_out(where, chunks):
    return call(
        place_out_body,
        "place_output_grads",
        [sds((512, D), f32)],
        [],
        (where, *chunks),
        smem=(0,),
    )[0]


def final_body(b0, b1, b2, b3, x0, ghid, g1, out):
    c = (b0[...].astype(f32) + b1[...].astype(f32)) + (b2[...].astype(f32) + b3[...].astype(f32))
    v = x0[...].astype(f32)
    r = lax.rsqrt(jnp.mean(v * v, axis=-1, keepdims=True) + EPS)
    u = c * g1[...]
    m = jnp.mean(u * v, axis=-1, keepdims=True)
    out[...] = ghid[...] + r * u - v * (r * r * r * m)


def final(b, x0, ghid, g1):
    return call(final_body, "input_grad", [sds((T, D), f32)], [], (*b, x0, ghid, g1))[0]


def gather_small_body(c0, c1, c2, c3, out):
    for dx, chunks in enumerate((c0, c1, c2, c3)):
        for dz in range(4):
            out[dx * 4 + dz] = chunks[dz, 512:, :]


def gather_small(chunks):
    return call(
        gather_small_body, "gather_small", [sds((16, 32, 128), bf16)], [], tuple(chunks)
    )[0]


def place_small_body(where, a0, a1, a2, a3, b, router, numbers):
    for dy, own in enumerate((a0, a1, a2, a3)):
        for dc in range(2):
            shard = lax.rem(where[3] + dy, 4) * 2 + lax.rem(where[2] + dc, 2)
            for dx in range(4):
                for dz in range(4):
                    expert = lax.rem(where[0] + dz, 4) * 4 + lax.rem(where[1] + dx, 4)
                    index = expert * 8 + shard
                    part = own[dx * 4 + dz] if dc == 0 else b[dy, dx * 4 + dz]
                    part = part.astype(f32)
                    rows = pl.ds(pl.multiple_of(index * SEG, SEG), SEG)
                    router[rows, :] = part[:SEG]
                    numbers[pl.ds(index, 1), :] = part[SEG : SEG + 1] + part[SEG + 1 : SEG + 2]


def place_small(where, own, sib):
    return call(
        place_small_body,
        "place_small",
        [sds((D, E), f32), sds((E, 128), f32)],
        [],
        (where, *own, sib),
        smem=(0,),
    )


def sibling(x):
    return lax.ppermute(x, "shard", [(i, i ^ 1) for i in range(8)])


def from_chip(x, dy):
    return lax.ppermute(x, "shard", [(i, (i - 2 * dy) % 8) for i in range(8)])


def to_chip(x, dy):
    return lax.ppermute(x, "shard", [(i, (i + 2 * dy) % 8) for i in range(8)])


def exchange(x):
    return lax.all_to_all(x, ALL, split_axis=0, concat_axis=0, tiled=True)


def spread(x):
    return [to_chip(x[d], d) for d in (1, 3, 2)]


def on_expert(x, dz, dx):
    pairs = [
        (z * 4 + c, ((z + dz) % 4) * 4 + (c + dx) % 4) for z in range(4) for c in range(4)
    ]
    return lax.ppermute(x, "expert", pairs)


def move(x, axis, distance):
    return on_expert(x, distance, 0) if axis == 0 else on_expert(x, 0, distance)


def collect(parts, axis):
    return [parts[0]] + [move(parts[d], axis, d) for d in (1, 3, 2)]


def share(x, axis):
    return [x] + [move(x, axis, (4 - d) % 4) for d in (1, 2, 3)]


def after(value, *others):
    return lax.optimization_barrier((value, *others))[0]


def on_device(
    block_input, out_grad, norm1_gain, w_query, w_key, w_value, query_gain, key_gain, w_out,
    norm2_gain, w_router, w_gate, w_up, w_down, seq_lengths, token_places, expert_routes,
):
    shard, owner = lax.axis_index("shard"), lax.axis_index("expert")
    chip, core = shard // 2, shard % 2
    where = jnp.stack([owner // 4, owner % 4, core, chip]).astype(jnp.int32)
    core_id = core.reshape(1)
    g1 = norm1_gain.astype(f32).reshape(1, D)
    g2 = norm2_gain.astype(f32).reshape(1, D)
    gq = query_gain.astype(f32).reshape(1, HEAD)
    gk = key_gain.astype(f32).reshape(1, HEAD)

    x_own = [block_input] + [from_chip(block_input, dy) for dy in (1, 2, 3)]
    x_sib = [sibling(block_input)]

    chips = (chip + jnp.arange(4)) % 4
    order = jnp.concatenate([chips * 2 + core, chips * 2 + 1 - core])
    places = token_places[0].reshape(8, T)[order].reshape(ROWS)
    lengths = seq_lengths[0]
    ends = jnp.cumsum(lengths)
    starts = jnp.sum(
        jnp.where(places[:, None] >= ends[None, :], lengths[None, :], 0), axis=1
    )
    positions = (places - starts).astype(f32)
    info = jnp.concatenate(
        [places[None].astype(f32), starts[None].astype(f32), jnp.zeros((6, ROWS), f32)], axis=0
    )
    inverse_freq = ROPE_BASE ** (-jnp.arange(0, HEAD, 2).astype(f32) / HEAD)
    angles = inverse_freq[:, None] * positions[None, :]
    cos, sin = jnp.cos(angles), jnp.sin(angles)

    ids, ids_t = route_tables(expert_routes.T)
    assign_t = ids_t[8:12]
    expert_list = ids[:, 0:4].reshape(-1)
    slot_list = ids[:, 4:8].reshape(-1)

    wk_t, wv_t = w_key.T, w_value.T
    wk_s, wv_s = sibling(wk_t), sibling(wv_t)
    wq_t = w_query.T
    wq_ts = sibling(wq_t)

    og_wire = pack(out_grad, assign_t)
    x_own, x_sib, og_wire, wq_t, cos, sin, info, wk_s, wv_s = lax.optimization_barrier(
        (x_own, x_sib, og_wire, wq_t, cos, sin, info, wk_s, wv_s)
    )
    x_sib += [sibling(x_own[dy]) for dy in (1, 2, 3)]
    blocks = [side[dy] for dy in range(4) for side in (x_own, x_sib)]
    weights = (g1, wq_t, wk_t, wk_s, wv_t, wv_s, gq, gk, cos, sin)
    *pieces, wkv = qkv((0, 1, 2, 3), core_id, blocks, *weights)
    pieces = [pieces[7 * dy : 7 * dy + 7] for dy in range(4)]
    qh, q, kh, k, v, scales, n1 = zip(*pieces)
    got_grads = exchange(og_wire)
    wo_s = sibling(after(w_out, q[0]))
    ot0, ot1, linv, qt, kt, kn, vn = attend(q, k, v, info)
    blocks = outproj(ot0, sibling(ot1), w_out, wo_s)
    blocks = [blocks[0]] + spread(blocks)
    hidden, n2, probs, gates, wire = router(blocks, block_input, g2, w_router, ids, assign_t)
    got_rows = exchange(wire)

    n1_t = transpose_rows(after(n1, wire))
    gate_list = gates[:, :4].reshape(-1)
    grad_rows, grad_act = expert_grad(after(got_grads, wire), w_down[0])
    got_rows, n1_t, grad_act, gate_list, wq_ts = lax.optimization_barrier(
        (got_rows, n1_t, grad_act, gate_list, wq_ts)
    )

    back, rows, act, scaled_act, dg, du = expert_main(got_rows, w_gate[0], w_up[0], grad_act)
    back_wire = exchange(back)

    rows, act, scaled_act, dg, du = after((rows, act, scaled_act, dg, du), back)
    out_wire = expert_out(act, w_down[0])

    def weight_grad(a, b):
        return lax.dot_general(a, b, (((0,), (0,)), ((), ())), preferred_element_type=f32)

    grad_wgate = weight_grad(rows, dg)
    grad_wup = weight_grad(rows, du)
    grad_wdown = weight_grad(scaled_act, grad_rows)
    back_wire, out_wire, grad_wgate, grad_wup, grad_wdown = lax.optimization_barrier(
        (back_wire, out_wire, grad_wgate, grad_wup, grad_wdown)
    )

    ghid, gatt, grouter, gg2 = combine(
        where, expert_list, slot_list, gate_list, back_wire, hidden, n2, probs, gates, ids,
        out_grad, g2, w_router,
    )
    g_own = [gatt] + [from_chip(gatt, dy) for dy in (1, 2, 3)]
    g_sib = [sibling(block) for block in g_own]
    returned = exchange(after(out_wire, *g_sib))
    *out_parts, dt = pre(where, g_own + g_sib, ot0, ot1, w_out)

    dq0, dq1, dkv, ggq, ggk = bwd(
        qh, kh, scales, qt, kt, kn, vn, dt, ot0, ot1, linv, info, cos, sin, gq, gk
    )
    out_parts = collect(out_parts, 1)
    dq_sib, dkv_sib = sibling(dq1), sibling(dkv)
    gw, dkv_total = qkv_grad(where, n1_t, dq0, dq1, dkv, dkv_sib)
    returned, dq0 = lax.optimization_barrier((returned, dq0))
    blocks = normed_grad(wq_t, wq_ts, wkv, dq0, dq_sib, dkv_total, n1)
    vector = jnp.concatenate([blocks[4][0] / g1[0], gg2[0], ggq[0], ggk[0]])
    per = vector.shape[0] // E
    vector = jnp.pad(vector.reshape(E, 1, per), ((0, 0), (0, 0), (0, 128 - per)))
    first = vector.astype(bf16)
    second = (vector - first.astype(f32)).astype(bf16)
    small = jnp.concatenate(
        [grouter.reshape(E, SEG, E), first, second, jnp.zeros((E, 6, 128), bf16)], axis=1
    )
    small = exchange(small)
    blocks = [blocks[0]] + spread(blocks)
    gw = lax.psum(gw, "expert")
    out_parts = collect(add_parts(out_parts), 0)
    out_parts, blocks = lax.optimization_barrier((out_parts, blocks))
    chunks = share(stack(share(add_last(out_parts, small), 0)), 1)
    grad_input = final(blocks, block_input, ghid, g1)
    result = result_rows(expert_list, slot_list, gate_list, returned, hidden)
    chunks, grad_input, result = lax.optimization_barrier((chunks, grad_input, result))
    small = gather_small(chunks)
    small = [small] + [from_chip(small, dy) for dy in (1, 2, 3)]
    grad_router, numbers = place_small(where, small, sibling(jnp.stack(small)))
    grad_wout = place_out(where, chunks)
    gw, grad_wout = lax.optimization_barrier((gw, grad_wout))
    grad_wq, grad_wk, grad_wv = widen(gw)
    vector = numbers[:, :per].reshape(-1)
    return (
        result,
        grad_input,
        vector[:D],
        grad_wq,
        grad_wk.T,
        grad_wv.T,
        vector[2 * D : 2 * D + HEAD],
        vector[2 * D + HEAD :],
        grad_wout,
        vector[D : 2 * D],
        grad_router,
        grad_wgate[None],
        grad_wup[None],
        grad_wdown[None],
    )


def solution(mesh):
    rows = P(("expert", "shard"), None)
    experts = P(("expert", "shard"), None, None)
    columns = P(None, "shard")
    return jax.shard_map(
        on_device,
        mesh=mesh,
        in_specs=(
            rows, rows, P(), columns, columns, columns, P(), P(), P("shard", None), P(), P(),
            experts, experts, experts, P("expert", None), P("expert", None), rows,
        ),
        out_specs=(
            rows, rows, P(), columns, columns, columns, P(), P(), P("shard", None), P(), P(),
            experts, experts, experts,
        ),
        check_vma=False,
    )
```

```python
import functools

import jax
import jax.numpy as jnp
from jax import lax
from jax.experimental import pallas as pl
from jax.experimental.pallas import tpu as pltpu
from jax.sharding import PartitionSpec as P

EPS = 1e-06
ROPE_BASE = 1000000.0
LOG2E = 1.4426950408889634
T = 128
D = 2048
HEAD = 128
LH = 4
E = 128
CAP = 5
SLOTS = E * CAP
SEG = D // 128
WIRE = CAP * SEG + 8
ROWS = 1024
HALF = 512
F = 768
bf16 = jnp.bfloat16
f32 = jnp.float32
ALL = ("expert", "shard")
COSTS = {
    "attend": 11,
    "out_projection": 5,
    "router": 6,
    "transpose_rows": 6,
    "expert_grad_rows": 8,
    "expert_main": 18,
    "expert_out": 7,
    "combine_grads": 7,
    "widen_grads": 10,
    "place_output_grads": 10,
    "head_grad": 4,
    "out_projection_grad": 7,
}


def cost(micros):
    return pl.CostEstimate(
        flops=1, bytes_accessed=int(micros * 0.6e6) + 1, transcendentals=0
    )


def dot(a, b):
    return jnp.dot(a, b, preferred_element_type=f32)


def dot_t(a, b):
    return lax.dot_general(a, b, (((1,), (1,)), ((), ())), preferred_element_type=f32)


def call(kernel, name, outs, scratch, args, smem=()):
    in_specs = [
        pl.BlockSpec(memory_space=pltpu.SMEM if i in smem else pltpu.VMEM)
        for i in range(len(args))
    ]
    return pl.pallas_call(
        kernel,
        out_shape=outs,
        in_specs=in_specs,
        out_specs=[pl.BlockSpec(memory_space=pltpu.VMEM) for _ in outs],
        scratch_shapes=scratch,
        compiler_params=pltpu.CompilerParams(vmem_limit_bytes=63 * 1024 * 1024),
        cost_estimate=cost(COSTS.get(name, 0)),
        name=name,
    )(*args)


def grid_call(kernel, name, grid, in_specs, out_specs, outs, scratch, args, scalars=0):
    return pl.pallas_call(
        kernel,
        out_shape=outs,
        grid_spec=pltpu.PrefetchScalarGridSpec(
            num_scalar_prefetch=scalars,
            grid=grid,
            in_specs=in_specs,
            out_specs=out_specs,
            scratch_shapes=scratch,
        ),
        compiler_params=pltpu.CompilerParams(
            vmem_limit_bytes=63 * 1024 * 1024, dimension_semantics=("arbitrary",)
        ),
        cost_estimate=cost(COSTS.get(name, 0)),
        name=name,
    )(*args)


def copy_call(kernel, name, outs, scratch, copies, args, smem=()):
    return pl.pallas_call(
        kernel,
        out_shape=outs,
        in_specs=[
            pl.BlockSpec(memory_space=pltpu.SMEM if i in smem else pl.ANY)
            for i in range(len(args))
        ],
        out_specs=[pl.BlockSpec(memory_space=pl.ANY)] * len(outs),
        scratch_shapes=[*scratch, pltpu.SemaphoreType.DMA((copies,))],
        compiler_params=pltpu.CompilerParams(vmem_limit_bytes=63 * 1024 * 1024),
        cost_estimate=cost(COSTS.get(name, 0)),
        name=name,
    )(*args)


class Copies:
    def __init__(self, sems):
        self.sems, self.count, self.leaving = sems, 0, []

    def bring(self, source, dest):
        item = pltpu.make_async_copy(source, dest, self.sems.at[self.count])
        self.count += 1
        item.start()
        return item

    def take(self, source, dest):
        self.leaving.append(self.bring(source, dest))

    def finish(self):
        for item in self.leaving:
            item.wait()


def whole(shape):
    return pl.BlockSpec(shape, lambda i, *_: (0,) * len(shape))


def rows_of(shape):
    return pl.BlockSpec(shape, lambda i, *_: (i, 0))


def cols_of(shape):
    return pl.BlockSpec(shape, lambda i, *_: (0, i))


def sds(shape, dtype):
    return jax.ShapeDtypeStruct(shape, dtype)


def split_rows(wire, dest):
    for s in range(CAP):
        for h in range(2):
            rows = slice(s * E + h * 64, s * E + (h + 1) * 64)
            block = wire[h * 64 : (h + 1) * 64, s * SEG : (s + 1) * SEG, :]
            dest[rows, :] = block.reshape(64, D)


def join_rows(source, wire):
    for s in range(CAP):
        for h in range(2):
            rows = slice(s * E + h * 64, s * E + (h + 1) * 64)
            wire[h * 64 : (h + 1) * 64, s * SEG : (s + 1) * SEG, :] = source[rows, :].reshape(
                64, SEG, 128
            )


def put_numbers(columns, wire):
    lane = lax.broadcasted_iota(jnp.int32, (E, 128), 1)
    plane = jnp.zeros((E, 128), f32)
    for s in range(CAP):
        plane = jnp.where(lane == s, columns[s], plane)
    first = plane.astype(bf16)
    rest = plane - first.astype(f32)
    second = rest.astype(bf16)
    third = (rest - second.astype(f32)).astype(bf16)
    none = jnp.zeros((E, 5 * 128), bf16)
    wide = jnp.concatenate([first, second, third, none], axis=1)
    wire[:, CAP * SEG :, :] = wide.reshape(E, 8, 128)


def get_numbers(wire):
    wide = wire[:, CAP * SEG :, :].reshape(E, 8 * 128)
    return (
        wide[:, :128].astype(f32) + wide[:, 128:256].astype(f32) + wide[:, 256:384].astype(f32)
    )


def pack_rows(x_ref, at_ref, wire, rows):
    slot = lax.broadcasted_iota(jnp.int32, (SLOTS, T), 0)
    hit = slot == at_ref[0:1, :]
    for k in range(1, 4):
        hit = hit | (slot == at_ref[k : k + 1, :])
    pick = jnp.where(hit, 1.0, 0.0).astype(bf16)
    for j in range(8):
        cols = slice(j * 256, (j + 1) * 256)
        rows[:, cols] = dot(pick, x_ref[:, cols]).astype(bf16)
    join_rows(rows, wire)


def pack_body(x_ref, at_ref, wire, rows):
    pack_rows(x_ref, at_ref, wire, rows)
    wire[:, CAP * SEG :, :] = jnp.zeros((E, 8, 128), bf16)


def pack(x, assign_t):
    return call(
        pack_body,
        "pack_rows",
        [sds((E, WIRE, 128), bf16)],
        [pltpu.VMEM((SLOTS, D), bf16)],
        (x, assign_t),
    )[0]


def sum_rows(wire, experts, slots, gates, out):
    def body(i, carry):
        for u in range(8):
            t = i * 8 + u
            total = None
            for k in range(4):
                p = t * 4 + k
                rows = pl.ds(pl.multiple_of(slots[p] * SEG, SEG), SEG)
                part = wire[experts[p], rows, :].astype(f32) * gates[p]
                total = part if total is None else total + part
            out[pl.ds(pl.multiple_of(t * SEG, SEG), SEG), :] = total
        return carry

    lax.fori_loop(0, T // 8, body, 0)


def column(row):
    return jnp.broadcast_to(row, (128, 128)).T[:, 0:1]


def qkv_body(pieces, *refs):
    count = len(pieces)
    core, blocks = refs[0], refs[1 : 1 + 2 * count]
    g1, wqt, wk, wks, wv, wvs, gq, gk, cos, sin = refs[1 + 2 * count : 11 + 2 * count]
    outs = refs[11 + 2 * count :]
    wkv = outs[-1]
    lower = core[0] == 0
    wkv[0:64, :] = jnp.where(lower, wk[...], wks[...])
    wkv[64:128, :] = jnp.where(lower, wks[...], wk[...])
    wkv[128:192, :] = jnp.where(lower, wv[...], wvs[...])
    wkv[192:256, :] = jnp.where(lower, wvs[...], wv[...])
    gain_q, gain_k = column(gq[...]), column(gk[...])
    for number, piece in enumerate(pieces):
        qn, qt, kn, kt, vt, scale, n1 = outs[7 * number : 7 * number + 7]
        for half in range(2):
            x = blocks[2 * number + half][...].astype(f32)
            r = lax.rsqrt(jnp.mean(x * x, axis=-1, keepdims=True) + EPS)
            n1[half * T : (half + 1) * T, :] = (x * r * g1[...]).astype(bf16)
        raw = dot_t(wqt[...], n1[...])
        raw_kv = dot_t(wkv[...], n1[...])
        first, second = piece * T, HALF + piece * T
        c = jnp.concatenate([cos[:, first : first + T], cos[:, second : second + T]], axis=1)
        s = jnp.concatenate([sin[:, first : first + T], sin[:, second : second + T]], axis=1)

        def path(v, gain, factor, keep, index):
            r = lax.rsqrt(jnp.mean(v * v, axis=0, keepdims=True) + EPS)
            scale[index : index + 1, :] = r
            v = v * r
            keep[...] = v.astype(bf16)
            v = v * gain
            low, high = v[:64], v[64:]
            return (
                ((low * c - high * s) * factor).astype(bf16),
                ((high * c + low * s) * factor).astype(bf16),
            )

        scale[...] = jnp.zeros_like(scale)
        for h in range(LH):
            heads = slice(h * HEAD, (h + 1) * HEAD)
            low, high = path(raw[heads], gain_q, HEAD ** (-0.5), qn.at[heads, :], h)
            qt[h * HEAD : h * HEAD + 64, :] = low
            qt[h * HEAD + 64 : (h + 1) * HEAD, :] = high
        key = raw_kv[:HEAD].astype(bf16)
        low, high = path(key.astype(f32), gain_k, 1.0, kn, LH)
        kt[:64, :] = low
        kt[64:, :] = high
        vt[...] = raw_kv[HEAD:].astype(bf16)


def qkv(pieces, core, blocks, *args):
    outs = [
        sds((LH * HEAD, 2 * T), bf16),
        sds((LH * HEAD, 2 * T), bf16),
        sds((HEAD, 2 * T), bf16),
        sds((HEAD, 2 * T), bf16),
        sds((HEAD, 2 * T), bf16),
        sds((8, 2 * T), f32),
        sds((2 * T, D), bf16),
    ] * len(pieces)
    keep = 0 in pieces
    return call(
        functools.partial(qkv_body, pieces),
        "qkv" + "".join(str(p) for p in pieces),
        outs + ([sds((2 * HEAD, D), bf16)] if keep else []),
        [] if keep else [pltpu.VMEM((2 * HEAD, D), bf16)],
        (core, *blocks, *args),
        smem=(0,),
    )


def build_mask(info, mask):
    for b in range(8):
        keys = jnp.broadcast_to(info[0:1, b * T : (b + 1) * T], (T, T)).T
        for j in range(8):
            cols = slice(j * T, (j + 1) * T)
            inside = (keys >= info[1:2, cols]) & (keys <= info[0:1, cols])
            mask[b * T : (b + 1) * T, cols] = jnp.where(inside, 1.0, 0.0)


def attend_body(*refs):
    q, k, v = refs[0:4], refs[4:8], refs[8:12]
    info, ot0, ot1, linv, qt, kt, kn, vn, mask, vt = refs[12:]
    for dy in range(4):
        for dc in range(2):
            to = slice(dc * HALF + dy * T, dc * HALF + (dy + 1) * T)
            src = slice(dc * T, (dc + 1) * T)
            qt[:, to] = q[dy][:, src]
            kt[:, to] = k[dy][:, src]
            vt[:, to] = v[dy][:, src]
    for b in range(8):
        rows = slice(b * T, (b + 1) * T)
        kn[rows, :] = kt[:, rows].astype(f32).T.astype(bf16)
        vn[rows, :] = vt[:, rows].astype(f32).T.astype(bf16)
    build_mask(info, mask)
    for half, out in ((1, ot1), (0, ot0)):
        cols = slice(half * HALF, (half + 1) * HALF)
        for h in range(LH):
            heads = slice(h * HEAD, (h + 1) * HEAD)
            scores = dot(kn[...], qt[heads, cols])
            weights = jnp.exp2(scores * LOG2E) * mask[:, cols]
            inverse = 1.0 / jnp.sum(weights, axis=0, keepdims=True)
            out[heads, :] = (dot(vt[...], weights.astype(bf16)) * inverse).astype(bf16)
            linv[h : h + 1, cols] = inverse


def attend(q, k, v, info):
    return call(
        attend_body,
        "attend",
        [
            sds((LH * HEAD, HALF), bf16),
            sds((LH * HEAD, HALF), bf16),
            sds((8, ROWS), f32),
            sds((LH * HEAD, ROWS), bf16),
            sds((HEAD, ROWS), bf16),
            sds((ROWS, HEAD), bf16),
            sds((ROWS, HEAD), bf16),
        ],
        [pltpu.VMEM((ROWS, ROWS), f32), pltpu.VMEM((HEAD, ROWS), bf16)],
        (*q, *k, *v, info),
    )


def flip(source, dest, row, col):
    height, width = source.shape
    for a in range(height // 128):
        for b in range(width // 128):
            block = source[a * 128 : (a + 1) * 128, b * 128 : (b + 1) * 128]
            rows = slice(row + b * 128, row + (b + 1) * 128)
            dest[rows, col + a * 128 : col + (a + 1) * 128] = block.astype(f32).T.astype(bf16)


def outproj_body(ot0, otr, wa, wb, b0, b1, b2, b3, heads):
    @pl.when(pl.program_id(0) == 0)
    def _():
        flip(ot0, heads, 0, 0)
        flip(otr, heads, 0, 512)

    total = dot(heads[:, :512], wa[...]) + dot(heads[:, 512:], wb[...])
    for dy, out in enumerate((b0, b1, b2, b3)):
        out[...] = total[dy * T : (dy + 1) * T, :].astype(bf16)


def outproj(ot0, otr, wa, wb):
    return grid_call(
        outproj_body,
        "out_projection",
        (2,),
        [whole((512, HALF)), whole((512, HALF)), cols_of((512, 1024)), cols_of((512, 1024))],
        [cols_of((T, 1024))] * 4,
        [sds((T, D), bf16)] * 4,
        [pltpu.VMEM((HALF, 1024), bf16)],
        (ot0, otr, wa, wb),
    )


def transpose_body(n0, n1, n2, n3, out):
    for dy, piece in enumerate((n0, n1, n2, n3)):
        for dc in range(2):
            flip(piece.at[dc * T : (dc + 1) * T, :], out, 0, dc * HALF + dy * T)


def transpose_rows(pieces):
    return call(transpose_body, "transpose_rows", [sds((D, ROWS), bf16)], [], tuple(pieces))[0]


def route_body(rt, ids, ids_t):
    lane = lax.broadcasted_iota(jnp.int32, (T, E), 1)
    row = lax.broadcasted_iota(jnp.int32, (T, E), 0)
    wide = jnp.concatenate([rt[...].astype(f32), jnp.zeros((124, T), f32)], axis=0).T
    hot = [jnp.where(lane.astype(f32) == wide[:, k : k + 1], 1.0, 0.0) for k in range(4)]
    earlier = jnp.where(lane < row, 1.0, 0.0).astype(bf16)
    before = dot(earlier, (hot[0] + hot[1] + hot[2] + hot[3]).astype(bf16))
    table = wide
    for k in range(4):
        slot = jnp.sum(before * hot[k], axis=1, keepdims=True)
        table = jnp.where(lane == 4 + k, slot, table)
        table = jnp.where(lane == 8 + k, slot * E + wide[:, k : k + 1], table)
    ids[...] = table.astype(jnp.int32)
    ids_t[...] = table.T[0:16, :].astype(jnp.int32)


def route_tables(routes_t):
    return call(
        route_body,
        "route_tables",
        [sds((T, 128), jnp.int32), sds((16, T), jnp.int32)],
        [],
        (routes_t,),
    )


def router_body(b0, b1, b2, b3, x0, g2, wr, ids, at, hidden, n2, probs, gates, wire, rows):
    v = x0[...].astype(f32) + (
        (b0[...].astype(f32) + b1[...].astype(f32))
        + (b2[...].astype(f32) + b3[...].astype(f32))
    )
    hidden[...] = v
    r = lax.rsqrt(jnp.mean(v * v, axis=-1, keepdims=True) + EPS)
    n2[...] = (v * r * g2[...]).astype(bf16)
    logits = dot(n2[...], wr[...])
    pack_rows(n2, at, wire, rows)
    expo = jnp.exp(logits - jnp.max(logits, axis=-1, keepdims=True))
    p = expo / jnp.sum(expo, axis=-1, keepdims=True)
    probs[...] = p
    lane = lax.broadcasted_iota(jnp.int32, (T, E), 1)
    chosen = [
        jnp.sum(jnp.where(lane == ids[:, k : k + 1], p, 0.0), axis=-1, keepdims=True)
        for k in range(4)
    ]
    total = chosen[0] + chosen[1] + chosen[2] + chosen[3]
    packed = jnp.where(lane == 4, total, 0.0)
    for k in range(4):
        packed = jnp.where(lane == k, chosen[k] / total, packed)
    gates[...] = packed
    across = packed.T
    expert = lax.broadcasted_iota(jnp.int32, (E, T), 0)
    columns = []
    for s in range(CAP):
        mine = jnp.zeros((E, T), f32)
        for k in range(4):
            mine = jnp.where(expert + s * E == at[k : k + 1, :], across[k : k + 1, :], mine)
        columns.append(jnp.sum(mine, axis=1, keepdims=True))
    put_numbers(columns, wire)


def router(b, x0, g2, wr, ids, assign_t):
    return call(
        router_body,
        "router",
        [
            sds((T, D), f32),
            sds((T, D), bf16),
            sds((T, E), f32),
            sds((T, E), f32),
            sds((E, WIRE, 128), bf16),
        ],
        [pltpu.VMEM((SLOTS, D), bf16)],
        (*b, x0, g2, wr, ids, assign_t),
    )


def expert_grad_body(wire, wd, gr, ga):
    split_rows(wire, gr)

    def body(i, carry):
        cols = pl.ds(pl.multiple_of(i * 256, 256), 256)
        ga[:, cols] = dot_t(gr[...], wd[cols, :])
        return carry

    lax.fori_loop(0, F // 256, body, 0)


def expert_grad(wire, wd):
    return call(
        expert_grad_body,
        "expert_grad_rows",
        [sds((SLOTS, D), bf16), sds((SLOTS, F), f32)],
        [],
        (wire, wd),
    )


def expert_main_body(
    wire, wg, wu, ga, back, xs, act, acts, dg, du,
    wire_v, w_v, ga_v, xr, xs_v, act_v, acts_v, d_v, sc, sems,
):
    half = F // 2

    def copy(source, dest, number):
        return pltpu.make_async_copy(source, dest, sems.at[number])

    first = copy(wire, wire_v, 0)
    first.start()
    arrivals = []
    for c in range(2):
        cols = slice(c * half, (c + 1) * half)
        up_cols = slice(F + c * half, F + (c + 1) * half)
        group = [
            copy(wg.at[:, cols], w_v.at[:, cols], 1 + 3 * c),
            copy(wu.at[:, cols], w_v.at[:, up_cols], 2 + 3 * c),
            copy(ga.at[:, cols], ga_v.at[:, cols], 3 + 3 * c),
        ]
        for item in group:
            item.start()
        arrivals.append(group)
    first.wait()
    split_rows(wire_v, xr)
    gates = get_numbers(wire_v)
    sc[...] = jnp.zeros_like(sc)
    for c in range(2):
        for item in arrivals[c]:
            item.wait()
        cols = slice(c * half, (c + 1) * half)
        up_cols = slice(F + c * half, F + (c + 1) * half)
        gate = dot(xr[...], w_v[:, cols])
        up = dot(xr[...], w_v[:, up_cols])
        grad = ga_v[:, cols]
        s = 1.0 / (1.0 + jnp.exp(-gate))
        silu = gate * s
        a = silu * up
        act_v[:, cols] = a.astype(bf16)
        d_v[:, cols] = (grad * up * s * (1.0 + gate * (1.0 - s))).astype(bf16)
        d_v[:, up_cols] = (grad * silu).astype(bf16)
        sc[...] += jnp.sum(a * grad, axis=1, keepdims=True)
    departures = [copy(act_v, act, 7), copy(d_v.at[:, :F], dg, 8), copy(d_v.at[:, F:], du, 9)]
    for item in departures:
        item.start()
    for s in range(CAP):
        part = slice(s * E, (s + 1) * E)
        gate = gates[:, s : s + 1]
        xs_v[part, :] = (xr[part, :].astype(f32) * gate).astype(bf16)
        acts_v[part, :] = (act_v[part, :].astype(f32) * gate).astype(bf16)
    more = [copy(xs_v, xs, 10), copy(acts_v, acts, 11)]
    for item in more:
        item.start()
    for j in range(4):
        part = slice(j * 512, (j + 1) * 512)
        xr[:, part] = dot_t(d_v[...], w_v[part, :]).astype(bf16)
    join_rows(xr, wire_v)
    put_numbers([sc[s * E : (s + 1) * E, :] for s in range(CAP)], wire_v)
    last = copy(wire_v, back, 12)
    last.start()
    for item in departures + more + [last]:
        item.wait()


def expert_main(wire, wg, wu, ga):
    args = (wire, wg, wu, ga)
    outs = [
        sds((E, WIRE, 128), bf16),
        sds((SLOTS, D), bf16),
        sds((SLOTS, F), bf16),
        sds((SLOTS, F), bf16),
        sds((SLOTS, F), bf16),
        sds((SLOTS, F), bf16),
    ]
    return pl.pallas_call(
        expert_main_body,
        out_shape=outs,
        in_specs=[pl.BlockSpec(memory_space=pl.ANY)] * 4,
        out_specs=[pl.BlockSpec(memory_space=pl.ANY)] * 6,
        scratch_shapes=[
            pltpu.VMEM((E, WIRE, 128), bf16),
            pltpu.VMEM((D, 2 * F), bf16),
            pltpu.VMEM((SLOTS, F), f32),
            pltpu.VMEM((SLOTS, D), bf16),
            pltpu.VMEM((SLOTS, D), bf16),
            pltpu.VMEM((SLOTS, F), bf16),
            pltpu.VMEM((SLOTS, F), bf16),
            pltpu.VMEM((SLOTS, 2 * F), bf16),
            pltpu.VMEM((SLOTS, 1), f32),
            pltpu.SemaphoreType.DMA((13,)),
        ],
        compiler_params=pltpu.CompilerParams(vmem_limit_bytes=63 * 1024 * 1024),
        cost_estimate=cost(COSTS["expert_main"]),
        name="expert_main",
    )(*args)


def expert_out_body(act, wd, wire, rows):
    for j in range(8):
        cols = slice(j * 256, (j + 1) * 256)
        rows[:, cols] = dot(act[...], wd[:, cols]).astype(bf16)
    join_rows(rows, wire)


def expert_out(act, wd):
    return call(
        expert_out_body,
        "expert_out",
        [sds((E, CAP * SEG, 128), bf16)],
        [pltpu.VMEM((SLOTS, D), bf16)],
        (act, wd),
    )[0]


def combine_body(
    where, experts, slots, gate_list, wire, hidden, n2, probs, gates, ids, og, g2, wr,
    ghid, gatt, grouter, gg2, sums, gn2,
):
    sum_rows(wire, experts, slots, gate_list, sums)
    scores = get_numbers(wire)
    lane = lax.broadcasted_iota(jnp.int32, (T, E), 1)
    grads = []
    for k in range(4):
        hot = jnp.where(lane == ids[:, k : k + 1], 1.0, 0.0)
        rows = lax.dot_general(
            hot, scores, (((1,), (0,)), ((), ())),
            precision=lax.Precision.HIGHEST, preferred_element_type=f32,
        )
        picked = jnp.where(lane == ids[:, 4 + k : 5 + k], rows, 0.0)
        grads.append(jnp.sum(picked, axis=-1, keepdims=True))
    inner = sum(grads[k] * gates[:, k : k + 1] for k in range(4))
    inverse = 1.0 / gates[:, 4:5]
    grad_probs = jnp.zeros((T, E), f32)
    for k in range(4):
        grad_probs = jnp.where(
            lane == ids[:, k : k + 1], (grads[k] - inner) * inverse, grad_probs
        )
    p = probs[...]
    gl = (p * (grad_probs - jnp.sum(p * grad_probs, axis=-1, keepdims=True))).astype(bf16)
    for h in range(2):
        tokens = slice(h * 64, (h + 1) * 64)
        gn2[tokens, :] = sums[h * 1024 : (h + 1) * 1024, :].reshape(64, D)
    gn2[...] += dot_t(gl, wr[...])
    c = gn2[...]
    v = hidden[...]
    r = lax.rsqrt(jnp.mean(v * v, axis=-1, keepdims=True) + EPS)
    u = c * g2[...]
    m = jnp.mean(u * v, axis=-1, keepdims=True)
    total = og[...].astype(f32) + r * u - v * (r * r * r * m)
    ghid[...] = total
    gatt[...] = total.astype(bf16)
    gg2[...] = jnp.sum(c * (v * r), axis=0, keepdims=True)
    for j in range(SEG):
        cols = slice(j * 128, (j + 1) * 128)
        grouter[cols, :] = dot(n2[:, cols].astype(f32).T.astype(bf16), gl).astype(bf16)


def combine(*args):
    return call(
        combine_body,
        "combine_grads",
        [sds((T, D), f32), sds((T, D), bf16), sds((D, E), bf16), sds((1, D), f32)],
        [pltpu.VMEM((T * SEG, 128), f32), pltpu.VMEM((T, D), f32)],
        args,
        smem=(0, 1, 2, 3),
    )


def result_body(experts, slots, gate_list, wire, hidden, out, sums):
    sum_rows(wire, experts, slots, gate_list, sums)
    for h in range(2):
        tokens = slice(h * 64, (h + 1) * 64)
        mixture = sums[h * 1024 : (h + 1) * 1024, :].reshape(64, D)
        out[tokens, :] = (hidden[tokens, :] + mixture).astype(bf16)


def result_rows(*args):
    return call(
        result_body,
        "result",
        [sds((T, D), bf16)],
        [pltpu.VMEM((T * SEG, 128), f32)],
        args,
        smem=(0, 1, 2),
    )[0]


def pre_body(where, *refs):
    blocks, (ot0, ot1, wo, *outs) = refs[:8], refs[8:16]
    dt, (heads, rows_all, wo_v, grads, dt_v, sems) = refs[15], refs[16:]
    copies = Copies(sems)
    arrivals = [copies.bring(ot0, heads.at[:, :HALF]), copies.bring(ot1, heads.at[:, HALF:])]
    columns = []
    waits = []
    for step in range(4):
        start = lax.rem(where[1] + step, 4) * 512
        columns.append(pl.ds(pl.multiple_of(start, 512), 512))
        waits.append(
            [
                copies.bring(
                    blocks[b].at[:, columns[step]],
                    rows_all.at[b * T : (b + 1) * T, columns[step]],
                )
                for b in range(8)
            ]
        )
    last = copies.bring(wo, wo_v)
    for item in arrivals:
        item.wait()
    for step in range(4):
        for item in waits[step]:
            item.wait()
        grad = dot(heads[...], rows_all[:, columns[step]]).astype(bf16)
        for col in range(4):
            grads[step, lax.rem(col + 4 - where[0], 4)] = grad[:, col * 128 : (col + 1) * 128]
        copies.take(grads.at[step], outs[step])
    last.wait()
    dt_v[...] = dot_t(wo_v[...], rows_all[...]).astype(bf16)
    copies.take(dt_v, dt)
    copies.finish()


def pre(where, blocks, ot0, ot1, wo):
    return copy_call(
        pre_body,
        "out_projection_grad",
        [sds((4, 512, 128), bf16)] * 4 + [sds((LH * HEAD, ROWS), bf16)],
        [
            pltpu.VMEM((512, ROWS), bf16),
            pltpu.VMEM((ROWS, D), bf16),
            pltpu.VMEM((512, D), bf16),
            pltpu.VMEM((4, 4, 512, 128), bf16),
            pltpu.VMEM((512, ROWS), bf16),
        ],
        2 + 32 + 1 + 5,
        (where, *blocks, ot0, ot1, wo),
        smem=(0,),
    )


def bwd_body(*refs):
    qh, kh, scales = refs[0:4], refs[4:8], refs[8:12]
    (qt, kt, kn, vn, dt, ot0, ot1, linv, info, cos, sin, gq, gk) = refs[12:25]
    dq0, dq1, dkv, ggq, ggk, mask, wb, sb, dqt, dk, dv, raw, scale = refs[25:]
    for dc in range(2):
        for dy in range(4):
            to = slice(dc * HALF + dy * T, dc * HALF + (dy + 1) * T)
            scale[:, to] = scales[dy][:, dc * T : (dc + 1) * T]
    build_mask(info, mask)
    dk[...] = jnp.zeros_like(dk)
    dv[...] = jnp.zeros_like(dv)
    for half, out in ((0, ot0), (1, ot1)):
        cols = slice(half * HALF, (half + 1) * HALF)
        for h in range(LH):
            heads = slice(h * HEAD, (h + 1) * HEAD)
            part = slice(h * HALF, (h + 1) * HALF)
            scores = dot(kn[...], qt[heads, cols])
            weights = jnp.exp2(scores * LOG2E) * (mask[:, cols] * linv[h : h + 1, cols])
            grad = dt[heads, cols]
            delta = jnp.sum(
                grad.astype(f32) * out[heads, :].astype(f32), axis=0, keepdims=True
            )
            wb[:, part] = weights.astype(bf16)
            sb[:, part] = (weights * (dot(vn[...], grad) - delta)).astype(bf16)
            dqt[heads, cols] = dot(kt[...], sb[:, part])
        grads = jnp.concatenate([dt[h * HEAD : (h + 1) * HEAD, cols] for h in range(LH)], axis=1)
        queries = jnp.concatenate([qt[h * HEAD : (h + 1) * HEAD, cols] for h in range(LH)], axis=1)
        dv[...] += dot_t(wb[...], grads)
        dk[...] += dot_t(sb[...], queries)

    def unrope(v):
        low, high = v[:64], v[64:]
        c, s = cos[...], sin[...]
        return jnp.concatenate([low * c + high * s, high * c - low * s], axis=0)

    def norm_back(n, r, grad, gain):
        gain_grad = jnp.sum(grad * n, axis=1, keepdims=True)
        u = grad * gain
        return r * (u - n * jnp.mean(u * n, axis=0, keepdims=True)), gain_grad

    gain_q, gain_k = column(gq[...]), column(gk[...])
    total = jnp.zeros((HEAD, 1), f32)
    for h in range(LH):
        heads = slice(h * HEAD, (h + 1) * HEAD)
        for dy in range(4):
            for dc in range(2):
                to = slice(dc * HALF + dy * T, dc * HALF + (dy + 1) * T)
                raw[:, to] = qh[dy][heads, dc * T : (dc + 1) * T].astype(f32)
        grad, part = norm_back(raw[...], scale[h : h + 1, :], unrope(dqt[heads, :] * (HEAD ** (-0.5))), gain_q)
        total = total + part
        dq0[heads, :] = grad[:, :HALF].astype(bf16)
        dq1[heads, :] = grad[:, HALF:].astype(bf16)
    ggq[...] = jnp.broadcast_to(total, (HEAD, 128)).T[0:8, :]
    for dy in range(4):
        for dc in range(2):
            to = slice(dc * HALF + dy * T, dc * HALF + (dy + 1) * T)
            raw[:, to] = kh[dy][:, dc * T : (dc + 1) * T].astype(f32)
    grad, part = norm_back(raw[...], scale[LH : LH + 1, :], unrope(dk[...].T), gain_k)
    ggk[...] = jnp.broadcast_to(part, (HEAD, 128)).T[0:8, :]
    dkv[:HEAD, :] = grad.astype(bf16)
    dkv[HEAD:, :] = dv[...].T.astype(bf16)


def bwd(qh, kh, scales, *rest):
    return call(
        bwd_body,
        "attend_grad",
        [
            sds((LH * HEAD, HALF), bf16),
            sds((LH * HEAD, HALF), bf16),
            sds((2 * HEAD, ROWS), bf16),
            sds((8, HEAD), f32),
            sds((8, HEAD), f32),
        ],
        [
            pltpu.VMEM((ROWS, ROWS), f32),
            pltpu.VMEM((ROWS, LH * HALF), bf16),
            pltpu.VMEM((ROWS, LH * HALF), bf16),
            pltpu.VMEM((LH * HEAD, ROWS), f32),
            pltpu.VMEM((ROWS, HEAD), f32),
            pltpu.VMEM((ROWS, HEAD), f32),
            pltpu.VMEM((HEAD, ROWS), f32),
            pltpu.VMEM((8, ROWS), f32),
        ],
        (*qh, *kh, *scales, *rest),
    )


def qkv_grad_body(where, n1t, dq0, dq1, own, sib, out, tot, dt):
    @pl.when(pl.program_id(0) == 0)
    def _():
        tot[:, :HALF] = (own[:, :HALF].astype(f32) + sib[:, HALF:].astype(f32)).astype(bf16)
        tot[:, HALF:] = (own[:, HALF:].astype(f32) + sib[:, :HALF].astype(f32)).astype(bf16)
        dt[:512, :HALF] = dq0[...]
        dt[:512, HALF:] = dq1[...]
        upper = where[2] == 1
        dt[512:576, :] = jnp.where(upper, tot[64:128, :], tot[:64, :])
        dt[576:, :] = jnp.where(upper, tot[192:, :], tot[128:192, :])

    out[...] = dot_t(n1t[...], dt[...]).astype(bf16)


def qkv_grad(where, n1t, dq0, dq1, own, sib):
    return grid_call(
        qkv_grad_body,
        "qkv_weight_grad",
        (2,),
        [
            rows_of((1024, ROWS)),
            whole((512, HALF)),
            whole((512, HALF)),
            whole((2 * HEAD, ROWS)),
            whole((2 * HEAD, ROWS)),
        ],
        [rows_of((1024, 640)), whole((2 * HEAD, ROWS))],
        [sds((D, 640), bf16), sds((2 * HEAD, ROWS), bf16)],
        [pltpu.VMEM((640, ROWS), bf16)],
        (where, n1t, dq0, dq1, own, sib),
        scalars=1,
    )


def widen_body(grads, gq, gkt, gvt):
    gq[...] = grads[:, :512].astype(f32)
    both = grads[:, 512:].astype(f32).T
    gkt[...] = both[:64]
    gvt[...] = both[64:]


def widen(grads):
    return grid_call(
        widen_body,
        "widen_grads",
        (4,),
        [rows_of((512, 640))],
        [rows_of((512, 512)), cols_of((64, 512)), cols_of((64, 512))],
        [sds((D, 512), f32), sds((64, D), f32), sds((64, D), f32)],
        [],
        (grads,),
    )


def add_body(a, b, c, d, *outs):
    for i, out in enumerate(outs):
        out[...] = (
            (a[i].astype(f32) + b[i].astype(f32)) + (c[i].astype(f32) + d[i].astype(f32))
        ).astype(bf16)


def add_parts(parts):
    shape = parts[0].shape[1:]
    return call(add_body, "add_parts", [sds(shape, bf16)] * 4, [], tuple(parts))


def normed_grad_body(wa, wb, wkv, dq0, dqr, tot, n0, n1, n2, n3, b0, b1, b2, b3, gg1, grads):
    @pl.when(pl.program_id(0) == 0)
    def _():
        flip(dq0, grads, 0, 0)
        flip(dqr, grads, 0, 512)
        flip(tot, grads, 0, 1024)

    total = (
        dot(grads[:, :512], wa[...])
        + dot(grads[:, 512:1024], wb[...])
        + dot(grads[:, 1024:], wkv[...])
    )
    gain = jnp.zeros((1, 512), f32)
    for dy, (out, rows) in enumerate(((b0, n0), (b1, n1), (b2, n2), (b3, n3))):
        part = total[dy * T : (dy + 1) * T, :]
        out[...] = part.astype(bf16)
        gain = gain + jnp.sum(part * rows[...].astype(f32), axis=0, keepdims=True)
    gg1[...] = jnp.broadcast_to(gain, (8, 512))


def normed_grad(wa, wb, wkv, dq0, dqr, tot, n1):
    return grid_call(
        normed_grad_body,
        "normed_grad",
        (4,),
        [
            cols_of((512, 512)),
            cols_of((512, 512)),
            cols_of((256, 512)),
            whole((512, HALF)),
            whole((512, HALF)),
            whole((2 * HEAD, HALF)),
        ]
        + [cols_of((T, 512))] * 4,
        [cols_of((T, 512))] * 4 + [cols_of((8, 512))],
        [sds((T, D), bf16)] * 4 + [sds((8, D), f32)],
        [pltpu.VMEM((HALF, 1280), bf16)],
        (wa, wb, wkv, dq0, dqr, tot, *n1),
    )


def add_last_body(a, b, c, d, small, out):
    out[:512, :] = (
        (a[...].astype(f32) + b[...].astype(f32)) + (c[...].astype(f32) + d[...].astype(f32))
    ).astype(bf16)

    def add(i, total):
        return total + small[i].astype(f32)

    total = lax.fori_loop(0, E, add, jnp.zeros((24, 128), f32))
    numbers = total[SEG : SEG + 1] + total[SEG + 1 : SEG + 2]
    first = numbers.astype(bf16).astype(f32)
    out[512:, :] = jnp.concatenate(
        [total[:SEG], first, numbers - first, jnp.zeros((14, 128), f32)], axis=0
    ).astype(bf16)


def add_last(parts, small):
    args = (*parts, small)
    return call(add_last_body, "add_last", [sds((544, 128), bf16)], [], args)[0]


def stack_body(a, b, c, d, out):
    for i, part in enumerate((a, b, c, d)):
        out[i] = part[...]


def stack(parts):
    shape = (4, *parts[0].shape)
    return call(stack_body, "stack_parts", [sds(shape, bf16)], [], tuple(parts))[0]


def place_out_body(where, c0, c1, c2, c3, out):
    for dx, chunks in enumerate((c0, c1, c2, c3)):
        for dz in range(4):
            chunk = lax.rem(where[1] + dx, 4) * 4 + lax.rem(where[0] + dz, 4)
            cols = pl.ds(pl.multiple_of(chunk * 128, 128), 128)
            out[:, cols] = chunks[dz, :512, :].astype(f32)


def place_out(where, chunks):
    return call(
        place_out_body,
        "place_output_grads",
        [sds((512, D), f32)],
        [],
        (where, *chunks),
        smem=(0,),
    )[0]


def final_body(b0, b1, b2, b3, x0, ghid, g1, out):
    c = (b0[...].astype(f32) + b1[...].astype(f32)) + (b2[...].astype(f32) + b3[...].astype(f32))
    v = x0[...].astype(f32)
    r = lax.rsqrt(jnp.mean(v * v, axis=-1, keepdims=True) + EPS)
    u = c * g1[...]
    m = jnp.mean(u * v, axis=-1, keepdims=True)
    out[...] = ghid[...] + r * u - v * (r * r * r * m)


def final(b, x0, ghid, g1):
    return call(final_body, "input_grad", [sds((T, D), f32)], [], (*b, x0, ghid, g1))[0]


def gather_small_body(c0, c1, c2, c3, out):
    for dx, chunks in enumerate((c0, c1, c2, c3)):
        for dz in range(4):
            out[dx * 4 + dz] = chunks[dz, 512:, :]


def gather_small(chunks):
    return call(
        gather_small_body, "gather_small", [sds((16, 32, 128), bf16)], [], tuple(chunks)
    )[0]


def place_small_body(where, a0, a1, a2, a3, b, router, numbers):
    for dy, own in enumerate((a0, a1, a2, a3)):
        for dc in range(2):
            shard = lax.rem(where[3] + dy, 4) * 2 + lax.rem(where[2] + dc, 2)
            for dx in range(4):
                for dz in range(4):
                    expert = lax.rem(where[0] + dz, 4) * 4 + lax.rem(where[1] + dx, 4)
                    index = expert * 8 + shard
                    part = own[dx * 4 + dz] if dc == 0 else b[dy, dx * 4 + dz]
                    part = part.astype(f32)
                    rows = pl.ds(pl.multiple_of(index * SEG, SEG), SEG)
                    router[rows, :] = part[:SEG]
                    numbers[pl.ds(index, 1), :] = part[SEG : SEG + 1] + part[SEG + 1 : SEG + 2]


def place_small(where, own, sib):
    return call(
        place_small_body,
        "place_small",
        [sds((D, E), f32), sds((E, 128), f32)],
        [],
        (where, *own, sib),
        smem=(0,),
    )


def sibling(x):
    return lax.ppermute(x, "shard", [(i, i ^ 1) for i in range(8)])


def from_chip(x, dy):
    return lax.ppermute(x, "shard", [(i, (i - 2 * dy) % 8) for i in range(8)])


def to_chip(x, dy):
    return lax.ppermute(x, "shard", [(i, (i + 2 * dy) % 8) for i in range(8)])


def exchange(x):
    return lax.all_to_all(x, ALL, split_axis=0, concat_axis=0, tiled=True)


def spread(x):
    return [to_chip(x[d], d) for d in (1, 3, 2)]


def on_expert(x, dz, dx):
    pairs = [
        (z * 4 + c, ((z + dz) % 4) * 4 + (c + dx) % 4) for z in range(4) for c in range(4)
    ]
    return lax.ppermute(x, "expert", pairs)


def move(x, axis, distance):
    return on_expert(x, distance, 0) if axis == 0 else on_expert(x, 0, distance)


def collect(parts, axis):
    return [parts[0]] + [move(parts[d], axis, d) for d in (1, 3, 2)]


def share(x, axis):
    return [x] + [move(x, axis, (4 - d) % 4) for d in (1, 2, 3)]


def after(value, *others):
    return lax.optimization_barrier((value, *others))[0]


def on_device(
    block_input, out_grad, norm1_gain, w_query, w_key, w_value, query_gain, key_gain, w_out,
    norm2_gain, w_router, w_gate, w_up, w_down, seq_lengths, token_places, expert_routes,
):
    shard, owner = lax.axis_index("shard"), lax.axis_index("expert")
    chip, core = shard // 2, shard % 2
    where = jnp.stack([owner // 4, owner % 4, core, chip]).astype(jnp.int32)
    core_id = core.reshape(1)
    g1 = norm1_gain.astype(f32).reshape(1, D)
    g2 = norm2_gain.astype(f32).reshape(1, D)
    gq = query_gain.astype(f32).reshape(1, HEAD)
    gk = key_gain.astype(f32).reshape(1, HEAD)

    x_own = [block_input] + [from_chip(block_input, dy) for dy in (1, 2, 3)]
    x_sib = [sibling(block_input)]

    chips = (chip + jnp.arange(4)) % 4
    order = jnp.concatenate([chips * 2 + core, chips * 2 + 1 - core])
    places = token_places[0].reshape(8, T)[order].reshape(ROWS)
    lengths = seq_lengths[0]
    ends = jnp.cumsum(lengths)
    starts = jnp.sum(
        jnp.where(places[:, None] >= ends[None, :], lengths[None, :], 0), axis=1
    )
    positions = (places - starts).astype(f32)
    info = jnp.concatenate(
        [places[None].astype(f32), starts[None].astype(f32), jnp.zeros((6, ROWS), f32)], axis=0
    )
    inverse_freq = ROPE_BASE ** (-jnp.arange(0, HEAD, 2).astype(f32) / HEAD)
    angles = inverse_freq[:, None] * positions[None, :]
    cos, sin = jnp.cos(angles), jnp.sin(angles)

    ids, ids_t = route_tables(expert_routes.T)
    assign_t = ids_t[8:12]
    expert_list = ids[:, 0:4].reshape(-1)
    slot_list = ids[:, 4:8].reshape(-1)

    wk_t, wv_t = w_key.T, w_value.T
    wk_s, wv_s = sibling(wk_t), sibling(wv_t)
    wq_t = w_query.T
    wq_ts = sibling(wq_t)

    og_wire = pack(out_grad, assign_t)
    x_own, x_sib, og_wire, wq_t, cos, sin, info, wk_s, wv_s = lax.optimization_barrier(
        (x_own, x_sib, og_wire, wq_t, cos, sin, info, wk_s, wv_s)
    )
    x_sib += [sibling(x_own[dy]) for dy in (1, 2, 3)]
    blocks = [side[dy] for dy in range(4) for side in (x_own, x_sib)]
    weights = (g1, wq_t, wk_t, wk_s, wv_t, wv_s, gq, gk, cos, sin)
    *pieces, wkv = qkv((0, 1, 2, 3), core_id, blocks, *weights)
    pieces = [pieces[7 * dy : 7 * dy + 7] for dy in range(4)]
    qh, q, kh, k, v, scales, n1 = zip(*pieces)
    got_grads = exchange(og_wire)
    wo_s = sibling(after(w_out, q[0]))
    ot0, ot1, linv, qt, kt, kn, vn = attend(q, k, v, info)
    blocks = outproj(ot0, sibling(ot1), w_out, wo_s)
    blocks = [blocks[0]] + spread(blocks)
    hidden, n2, probs, gates, wire = router(blocks, block_input, g2, w_router, ids, assign_t)
    got_rows = exchange(wire)

    n1_t = transpose_rows(after(n1, wire))
    gate_list = gates[:, :4].reshape(-1)
    grad_rows, grad_act = expert_grad(after(got_grads, wire), w_down[0])
    got_rows, n1_t, grad_act, gate_list, wq_ts = lax.optimization_barrier(
        (got_rows, n1_t, grad_act, gate_list, wq_ts)
    )

    back, rows, act, scaled_act, dg, du = expert_main(got_rows, w_gate[0], w_up[0], grad_act)
    back_wire = exchange(back)

    rows, act, scaled_act, dg, du = after((rows, act, scaled_act, dg, du), back)
    out_wire = expert_out(act, w_down[0])

    def weight_grad(a, b):
        return lax.dot_general(a, b, (((0,), (0,)), ((), ())), preferred_element_type=f32)

    grad_wgate = weight_grad(rows, dg)
    grad_wup = weight_grad(rows, du)
    grad_wdown = weight_grad(scaled_act, grad_rows)
    back_wire, out_wire, grad_wgate, grad_wup, grad_wdown = lax.optimization_barrier(
        (back_wire, out_wire, grad_wgate, grad_wup, grad_wdown)
    )

    ghid, gatt, grouter, gg2 = combine(
        where, expert_list, slot_list, gate_list, back_wire, hidden, n2, probs, gates, ids,
        out_grad, g2, w_router,
    )
    g_own = [gatt] + [from_chip(gatt, dy) for dy in (1, 2, 3)]
    g_sib = [sibling(block) for block in g_own]
    returned = exchange(after(out_wire, *g_sib))
    *out_parts, dt = pre(where, g_own + g_sib, ot0, ot1, w_out)

    dq0, dq1, dkv, ggq, ggk = bwd(
        qh, kh, scales, qt, kt, kn, vn, dt, ot0, ot1, linv, info, cos, sin, gq, gk
    )
    out_parts = collect(out_parts, 1)
    dq_sib, dkv_sib = sibling(dq1), sibling(dkv)
    gw, dkv_total = qkv_grad(where, n1_t, dq0, dq1, dkv, dkv_sib)
    returned, dq0 = lax.optimization_barrier((returned, dq0))
    blocks = normed_grad(wq_t, wq_ts, wkv, dq0, dq_sib, dkv_total, n1)
    vector = jnp.concatenate([blocks[4][0] / g1[0], gg2[0], ggq[0], ggk[0]])
    per = vector.shape[0] // E
    vector = jnp.pad(vector.reshape(E, 1, per), ((0, 0), (0, 0), (0, 128 - per)))
    first = vector.astype(bf16)
    second = (vector - first.astype(f32)).astype(bf16)
    small = jnp.concatenate(
        [grouter.reshape(E, SEG, E), first, second, jnp.zeros((E, 6, 128), bf16)], axis=1
    )
    small = exchange(small)
    blocks = [blocks[0]] + spread(blocks)
    gw = lax.psum(gw, "expert")
    out_parts = collect(add_parts(out_parts), 0)
    chunks = share(add_last(out_parts, small), 0)
    chunks, blocks = lax.optimization_barrier((chunks, blocks))
    chunks = share(stack(chunks), 1)
    grad_input = final(blocks, block_input, ghid, g1)
    result = result_rows(expert_list, slot_list, gate_list, returned, hidden)
    chunks, grad_input, result = lax.optimization_barrier((chunks, grad_input, result))
    small = gather_small(chunks)
    small = [small] + [from_chip(small, dy) for dy in (1, 2, 3)]
    small, grad_wout = lax.optimization_barrier((small, place_out(where, chunks)))
    grad_router, numbers = place_small(where, small, sibling(jnp.stack(small)))
    gw, grad_wout = lax.optimization_barrier((gw, grad_wout))
    grad_wq, grad_wk, grad_wv = widen(gw)
    vector = numbers[:, :per].reshape(-1)
    return (
        result,
        grad_input,
        vector[:D],
        grad_wq,
        grad_wk.T,
        grad_wv.T,
        vector[2 * D : 2 * D + HEAD],
        vector[2 * D + HEAD :],
        grad_wout,
        vector[D : 2 * D],
        grad_router,
        grad_wgate[None],
        grad_wup[None],
        grad_wdown[None],
    )


def solution(mesh):
    rows = P(("expert", "shard"), None)
    experts = P(("expert", "shard"), None, None)
    columns = P(None, "shard")
    return jax.shard_map(
        on_device,
        mesh=mesh,
        in_specs=(
            rows, rows, P(), columns, columns, columns, P(), P(), P("shard", None), P(), P(),
            experts, experts, experts, P("expert", None), P("expert", None), rows,
        ),
        out_specs=(
            rows, rows, P(), columns, columns, columns, P(), P(), P("shard", None), P(), P(),
            experts, experts, experts,
        ),
        check_vma=False,
    )
```

```python
import functools

import jax
import jax.numpy as jnp
from jax import lax
from jax.experimental import pallas as pl
from jax.experimental.pallas import tpu as pltpu
from jax.sharding import PartitionSpec as P

EPS = 1e-06
ROPE_BASE = 1000000.0
LOG2E = 1.4426950408889634
T = 128
D = 2048
HEAD = 128
LH = 4
E = 128
CAP = 5
SLOTS = E * CAP
SEG = D // 128
WIRE = CAP * SEG + 8
ROWS = 1024
HALF = 512
F = 768
bf16 = jnp.bfloat16
f32 = jnp.float32
ALL = ("expert", "shard")
COSTS = {
    "attend": 11,
    "out_projection": 5,
    "router": 6,
    "transpose_rows": 6,
    "expert_grad_rows": 8,
    "expert_main": 18,
    "expert_out": 7,
    "combine_grads": 7,
    "widen_grads": 10,
    "place_output_grads": 10,
    "head_grad": 4,
    "out_projection_grad": 7,
}


def cost(micros):
    return pl.CostEstimate(
        flops=1, bytes_accessed=int(micros * 0.6e6) + 1, transcendentals=0
    )


def dot(a, b):
    return jnp.dot(a, b, preferred_element_type=f32)


def dot_t(a, b):
    return lax.dot_general(a, b, (((1,), (1,)), ((), ())), preferred_element_type=f32)


def call(kernel, name, outs, scratch, args, smem=()):
    in_specs = [
        pl.BlockSpec(memory_space=pltpu.SMEM if i in smem else pltpu.VMEM)
        for i in range(len(args))
    ]
    return pl.pallas_call(
        kernel,
        out_shape=outs,
        in_specs=in_specs,
        out_specs=[pl.BlockSpec(memory_space=pltpu.VMEM) for _ in outs],
        scratch_shapes=scratch,
        compiler_params=pltpu.CompilerParams(vmem_limit_bytes=63 * 1024 * 1024),
        cost_estimate=cost(COSTS.get(name, 0)),
        name=name,
    )(*args)


def grid_call(kernel, name, grid, in_specs, out_specs, outs, scratch, args, scalars=0):
    return pl.pallas_call(
        kernel,
        out_shape=outs,
        grid_spec=pltpu.PrefetchScalarGridSpec(
            num_scalar_prefetch=scalars,
            grid=grid,
            in_specs=in_specs,
            out_specs=out_specs,
            scratch_shapes=scratch,
        ),
        compiler_params=pltpu.CompilerParams(
            vmem_limit_bytes=63 * 1024 * 1024, dimension_semantics=("arbitrary",)
        ),
        cost_estimate=cost(COSTS.get(name, 0)),
        name=name,
    )(*args)


def copy_call(kernel, name, outs, scratch, copies, args, smem=()):
    return pl.pallas_call(
        kernel,
        out_shape=outs,
        in_specs=[
            pl.BlockSpec(memory_space=pltpu.SMEM if i in smem else pl.ANY)
            for i in range(len(args))
        ],
        out_specs=[pl.BlockSpec(memory_space=pl.ANY)] * len(outs),
        scratch_shapes=[*scratch, pltpu.SemaphoreType.DMA((copies,))],
        compiler_params=pltpu.CompilerParams(vmem_limit_bytes=63 * 1024 * 1024),
        cost_estimate=cost(COSTS.get(name, 0)),
        name=name,
    )(*args)


class Copies:
    def __init__(self, sems):
        self.sems, self.count, self.leaving = sems, 0, []

    def bring(self, source, dest):
        item = pltpu.make_async_copy(source, dest, self.sems.at[self.count])
        self.count += 1
        item.start()
        return item

    def take(self, source, dest):
        self.leaving.append(self.bring(source, dest))

    def finish(self):
        for item in self.leaving:
            item.wait()


def whole(shape):
    return pl.BlockSpec(shape, lambda i, *_: (0,) * len(shape))


def rows_of(shape):
    return pl.BlockSpec(shape, lambda i, *_: (i, 0))


def cols_of(shape):
    return pl.BlockSpec(shape, lambda i, *_: (0, i))


def sds(shape, dtype):
    return jax.ShapeDtypeStruct(shape, dtype)


def split_rows(wire, dest):
    for s in range(CAP):
        for h in range(2):
            rows = slice(s * E + h * 64, s * E + (h + 1) * 64)
            block = wire[h * 64 : (h + 1) * 64, s * SEG : (s + 1) * SEG, :]
            dest[rows, :] = block.reshape(64, D)


def join_rows(source, wire):
    for s in range(CAP):
        for h in range(2):
            rows = slice(s * E + h * 64, s * E + (h + 1) * 64)
            wire[h * 64 : (h + 1) * 64, s * SEG : (s + 1) * SEG, :] = source[rows, :].reshape(
                64, SEG, 128
            )


def put_numbers(columns, wire):
    lane = lax.broadcasted_iota(jnp.int32, (E, 128), 1)
    plane = jnp.zeros((E, 128), f32)
    for s in range(CAP):
        plane = jnp.where(lane == s, columns[s], plane)
    first = plane.astype(bf16)
    rest = plane - first.astype(f32)
    second = rest.astype(bf16)
    third = (rest - second.astype(f32)).astype(bf16)
    none = jnp.zeros((E, 5 * 128), bf16)
    wide = jnp.concatenate([first, second, third, none], axis=1)
    wire[:, CAP * SEG :, :] = wide.reshape(E, 8, 128)


def get_numbers(wire):
    wide = wire[:, CAP * SEG :, :].reshape(E, 8 * 128)
    return (
        wide[:, :128].astype(f32) + wide[:, 128:256].astype(f32) + wide[:, 256:384].astype(f32)
    )


def pack_rows(x_ref, at_ref, wire, rows):
    slot = lax.broadcasted_iota(jnp.int32, (SLOTS, T), 0)
    hit = slot == at_ref[0:1, :]
    for k in range(1, 4):
        hit = hit | (slot == at_ref[k : k + 1, :])
    pick = jnp.where(hit, 1.0, 0.0).astype(bf16)
    for j in range(8):
        cols = slice(j * 256, (j + 1) * 256)
        rows[:, cols] = dot(pick, x_ref[:, cols]).astype(bf16)
    join_rows(rows, wire)


def pack_body(x_ref, at_ref, wire, rows):
    pack_rows(x_ref, at_ref, wire, rows)
    wire[:, CAP * SEG :, :] = jnp.zeros((E, 8, 128), bf16)


def pack(x, assign_t):
    return call(
        pack_body,
        "pack_rows",
        [sds((E, WIRE, 128), bf16)],
        [pltpu.VMEM((SLOTS, D), bf16)],
        (x, assign_t),
    )[0]


def sum_rows(wire, experts, slots, gates, out):
    def body(i, carry):
        for u in range(8):
            t = i * 8 + u
            total = None
            for k in range(4):
                p = t * 4 + k
                rows = pl.ds(pl.multiple_of(slots[p] * SEG, SEG), SEG)
                part = wire[experts[p], rows, :].astype(f32) * gates[p]
                total = part if total is None else total + part
            out[pl.ds(pl.multiple_of(t * SEG, SEG), SEG), :] = total
        return carry

    lax.fori_loop(0, T // 8, body, 0)


def column(row):
    return jnp.broadcast_to(row, (128, 128)).T[:, 0:1]


def qkv_body(pieces, *refs):
    count = len(pieces)
    core, blocks = refs[0], refs[1 : 1 + 2 * count]
    g1, wqt, wk, wks, wv, wvs, gq, gk, cos, sin = refs[1 + 2 * count : 11 + 2 * count]
    outs = refs[11 + 2 * count :]
    wkv = outs[-1]
    lower = core[0] == 0
    wkv[0:64, :] = jnp.where(lower, wk[...], wks[...])
    wkv[64:128, :] = jnp.where(lower, wks[...], wk[...])
    wkv[128:192, :] = jnp.where(lower, wv[...], wvs[...])
    wkv[192:256, :] = jnp.where(lower, wvs[...], wv[...])
    gain_q, gain_k = column(gq[...]), column(gk[...])
    for number, piece in enumerate(pieces):
        qn, qt, kn, kt, vt, scale, n1 = outs[7 * number : 7 * number + 7]
        for half in range(2):
            x = blocks[2 * number + half][...].astype(f32)
            r = lax.rsqrt(jnp.mean(x * x, axis=-1, keepdims=True) + EPS)
            n1[half * T : (half + 1) * T, :] = (x * r * g1[...]).astype(bf16)
        raw = dot_t(wqt[...], n1[...])
        raw_kv = dot_t(wkv[...], n1[...])
        first, second = piece * T, HALF + piece * T
        c = jnp.concatenate([cos[:, first : first + T], cos[:, second : second + T]], axis=1)
        s = jnp.concatenate([sin[:, first : first + T], sin[:, second : second + T]], axis=1)

        def path(v, gain, factor, keep, index):
            r = lax.rsqrt(jnp.mean(v * v, axis=0, keepdims=True) + EPS)
            scale[index : index + 1, :] = r
            v = v * r
            keep[...] = v.astype(bf16)
            v = v * gain
            low, high = v[:64], v[64:]
            return (
                ((low * c - high * s) * factor).astype(bf16),
                ((high * c + low * s) * factor).astype(bf16),
            )

        scale[...] = jnp.zeros_like(scale)
        for h in range(LH):
            heads = slice(h * HEAD, (h + 1) * HEAD)
            low, high = path(raw[heads], gain_q, HEAD ** (-0.5), qn.at[heads, :], h)
            qt[h * HEAD : h * HEAD + 64, :] = low
            qt[h * HEAD + 64 : (h + 1) * HEAD, :] = high
        key = raw_kv[:HEAD].astype(bf16)
        low, high = path(key.astype(f32), gain_k, 1.0, kn, LH)
        kt[:64, :] = low
        kt[64:, :] = high
        vt[...] = raw_kv[HEAD:].astype(bf16)


def qkv(pieces, core, blocks, *args):
    outs = [
        sds((LH * HEAD, 2 * T), bf16),
        sds((LH * HEAD, 2 * T), bf16),
        sds((HEAD, 2 * T), bf16),
        sds((HEAD, 2 * T), bf16),
        sds((HEAD, 2 * T), bf16),
        sds((8, 2 * T), f32),
        sds((2 * T, D), bf16),
    ] * len(pieces)
    keep = 0 in pieces
    return call(
        functools.partial(qkv_body, pieces),
        "qkv" + "".join(str(p) for p in pieces),
        outs + ([sds((2 * HEAD, D), bf16)] if keep else []),
        [] if keep else [pltpu.VMEM((2 * HEAD, D), bf16)],
        (core, *blocks, *args),
        smem=(0,),
    )


def build_mask(info, mask):
    for b in range(8):
        keys = jnp.broadcast_to(info[0:1, b * T : (b + 1) * T], (T, T)).T
        for j in range(8):
            cols = slice(j * T, (j + 1) * T)
            inside = (keys >= info[1:2, cols]) & (keys <= info[0:1, cols])
            mask[b * T : (b + 1) * T, cols] = jnp.where(inside, 1.0, 0.0)


def attend_body(*refs):
    q, k, v = refs[0:4], refs[4:8], refs[8:12]
    info, ot0, ot1, linv, qt, kt, kn, vn, mask, vt = refs[12:]
    for dy in range(4):
        for dc in range(2):
            to = slice(dc * HALF + dy * T, dc * HALF + (dy + 1) * T)
            src = slice(dc * T, (dc + 1) * T)
            qt[:, to] = q[dy][:, src]
            kt[:, to] = k[dy][:, src]
            vt[:, to] = v[dy][:, src]
    for b in range(8):
        rows = slice(b * T, (b + 1) * T)
        kn[rows, :] = kt[:, rows].astype(f32).T.astype(bf16)
        vn[rows, :] = vt[:, rows].astype(f32).T.astype(bf16)
    build_mask(info, mask)
    for half, out in ((1, ot1), (0, ot0)):
        cols = slice(half * HALF, (half + 1) * HALF)
        for h in range(LH):
            heads = slice(h * HEAD, (h + 1) * HEAD)
            scores = dot(kn[...], qt[heads, cols])
            weights = jnp.exp2(scores * LOG2E) * mask[:, cols]
            inverse = 1.0 / jnp.sum(weights, axis=0, keepdims=True)
            out[heads, :] = (dot(vt[...], weights.astype(bf16)) * inverse).astype(bf16)
            linv[h : h + 1, cols] = inverse


def attend(q, k, v, info):
    return call(
        attend_body,
        "attend",
        [
            sds((LH * HEAD, HALF), bf16),
            sds((LH * HEAD, HALF), bf16),
            sds((8, ROWS), f32),
            sds((LH * HEAD, ROWS), bf16),
            sds((HEAD, ROWS), bf16),
            sds((ROWS, HEAD), bf16),
            sds((ROWS, HEAD), bf16),
        ],
        [pltpu.VMEM((ROWS, ROWS), f32), pltpu.VMEM((HEAD, ROWS), bf16)],
        (*q, *k, *v, info),
    )


def flip(source, dest, row, col):
    height, width = source.shape
    for a in range(height // 128):
        for b in range(width // 128):
            block = source[a * 128 : (a + 1) * 128, b * 128 : (b + 1) * 128]
            rows = slice(row + b * 128, row + (b + 1) * 128)
            dest[rows, col + a * 128 : col + (a + 1) * 128] = block.astype(f32).T.astype(bf16)


def outproj_body(ot0, otr, wa, wb, b0, b1, b2, b3, heads):
    @pl.when(pl.program_id(0) == 0)
    def _():
        flip(ot0, heads, 0, 0)
        flip(otr, heads, 0, 512)

    total = dot(heads[:, :512], wa[...]) + dot(heads[:, 512:], wb[...])
    for dy, out in enumerate((b0, b1, b2, b3)):
        out[...] = total[dy * T : (dy + 1) * T, :].astype(bf16)


def outproj(ot0, otr, wa, wb):
    return grid_call(
        outproj_body,
        "out_projection",
        (2,),
        [whole((512, HALF)), whole((512, HALF)), cols_of((512, 1024)), cols_of((512, 1024))],
        [cols_of((T, 1024))] * 4,
        [sds((T, D), bf16)] * 4,
        [pltpu.VMEM((HALF, 1024), bf16)],
        (ot0, otr, wa, wb),
    )


def transpose_body(n0, n1, n2, n3, out):
    for dy, piece in enumerate((n0, n1, n2, n3)):
        for dc in range(2):
            flip(piece.at[dc * T : (dc + 1) * T, :], out, 0, dc * HALF + dy * T)


def transpose_rows(pieces):
    return call(transpose_body, "transpose_rows", [sds((D, ROWS), bf16)], [], tuple(pieces))[0]


def route_body(rt, ids, ids_t):
    lane = lax.broadcasted_iota(jnp.int32, (T, E), 1)
    row = lax.broadcasted_iota(jnp.int32, (T, E), 0)
    wide = jnp.concatenate([rt[...].astype(f32), jnp.zeros((124, T), f32)], axis=0).T
    hot = [jnp.where(lane.astype(f32) == wide[:, k : k + 1], 1.0, 0.0) for k in range(4)]
    earlier = jnp.where(lane < row, 1.0, 0.0).astype(bf16)
    before = dot(earlier, (hot[0] + hot[1] + hot[2] + hot[3]).astype(bf16))
    table = wide
    for k in range(4):
        slot = jnp.sum(before * hot[k], axis=1, keepdims=True)
        table = jnp.where(lane == 4 + k, slot, table)
        table = jnp.where(lane == 8 + k, slot * E + wide[:, k : k + 1], table)
    ids[...] = table.astype(jnp.int32)
    ids_t[...] = table.T[0:16, :].astype(jnp.int32)


def route_tables(routes_t):
    return call(
        route_body,
        "route_tables",
        [sds((T, 128), jnp.int32), sds((16, T), jnp.int32)],
        [],
        (routes_t,),
    )


def router_body(b0, b1, b2, b3, x0, g2, wr, ids, at, hidden, n2, probs, gates, wire, rows):
    v = x0[...].astype(f32) + (
        (b0[...].astype(f32) + b1[...].astype(f32))
        + (b2[...].astype(f32) + b3[...].astype(f32))
    )
    hidden[...] = v
    r = lax.rsqrt(jnp.mean(v * v, axis=-1, keepdims=True) + EPS)
    n2[...] = (v * r * g2[...]).astype(bf16)
    logits = dot(n2[...], wr[...])
    pack_rows(n2, at, wire, rows)
    expo = jnp.exp(logits - jnp.max(logits, axis=-1, keepdims=True))
    p = expo / jnp.sum(expo, axis=-1, keepdims=True)
    probs[...] = p
    lane = lax.broadcasted_iota(jnp.int32, (T, E), 1)
    chosen = [
        jnp.sum(jnp.where(lane == ids[:, k : k + 1], p, 0.0), axis=-1, keepdims=True)
        for k in range(4)
    ]
    total = chosen[0] + chosen[1] + chosen[2] + chosen[3]
    packed = jnp.where(lane == 4, total, 0.0)
    for k in range(4):
        packed = jnp.where(lane == k, chosen[k] / total, packed)
    gates[...] = packed
    across = packed.T
    expert = lax.broadcasted_iota(jnp.int32, (E, T), 0)
    columns = []
    for s in range(CAP):
        mine = jnp.zeros((E, T), f32)
        for k in range(4):
            mine = jnp.where(expert + s * E == at[k : k + 1, :], across[k : k + 1, :], mine)
        columns.append(jnp.sum(mine, axis=1, keepdims=True))
    put_numbers(columns, wire)


def router(b, x0, g2, wr, ids, assign_t):
    return call(
        router_body,
        "router",
        [
            sds((T, D), f32),
            sds((T, D), bf16),
            sds((T, E), f32),
            sds((T, E), f32),
            sds((E, WIRE, 128), bf16),
        ],
        [pltpu.VMEM((SLOTS, D), bf16)],
        (*b, x0, g2, wr, ids, assign_t),
    )


def expert_grad_body(wire, wd, gr, ga):
    split_rows(wire, gr)

    def body(i, carry):
        cols = pl.ds(pl.multiple_of(i * 256, 256), 256)
        ga[:, cols] = dot_t(gr[...], wd[cols, :])
        return carry

    lax.fori_loop(0, F // 256, body, 0)


def expert_grad(wire, wd):
    return call(
        expert_grad_body,
        "expert_grad_rows",
        [sds((SLOTS, D), bf16), sds((SLOTS, F), f32)],
        [],
        (wire, wd),
    )


def expert_main_body(
    wire, wg, wu, ga, back, xs, act, acts, dg, du,
    wire_v, w_v, ga_v, xr, xs_v, act_v, acts_v, d_v, sc, sems,
):
    half = F // 2

    def copy(source, dest, number):
        return pltpu.make_async_copy(source, dest, sems.at[number])

    first = copy(wire, wire_v, 0)
    first.start()
    arrivals = []
    for c in range(2):
        cols = slice(c * half, (c + 1) * half)
        up_cols = slice(F + c * half, F + (c + 1) * half)
        group = [
            copy(wg.at[:, cols], w_v.at[:, cols], 1 + 3 * c),
            copy(wu.at[:, cols], w_v.at[:, up_cols], 2 + 3 * c),
            copy(ga.at[:, cols], ga_v.at[:, cols], 3 + 3 * c),
        ]
        for item in group:
            item.start()
        arrivals.append(group)
    first.wait()
    split_rows(wire_v, xr)
    gates = get_numbers(wire_v)
    sc[...] = jnp.zeros_like(sc)
    for c in range(2):
        for item in arrivals[c]:
            item.wait()
        cols = slice(c * half, (c + 1) * half)
        up_cols = slice(F + c * half, F + (c + 1) * half)
        gate = dot(xr[...], w_v[:, cols])
        up = dot(xr[...], w_v[:, up_cols])
        grad = ga_v[:, cols]
        s = 1.0 / (1.0 + jnp.exp(-gate))
        silu = gate * s
        a = silu * up
        act_v[:, cols] = a.astype(bf16)
        d_v[:, cols] = (grad * up * s * (1.0 + gate * (1.0 - s))).astype(bf16)
        d_v[:, up_cols] = (grad * silu).astype(bf16)
        sc[...] += jnp.sum(a * grad, axis=1, keepdims=True)
    departures = [copy(act_v, act, 7), copy(d_v.at[:, :F], dg, 8), copy(d_v.at[:, F:], du, 9)]
    for item in departures:
        item.start()
    for s in range(CAP):
        part = slice(s * E, (s + 1) * E)
        gate = gates[:, s : s + 1]
        xs_v[part, :] = (xr[part, :].astype(f32) * gate).astype(bf16)
        acts_v[part, :] = (act_v[part, :].astype(f32) * gate).astype(bf16)
    more = [copy(xs_v, xs, 10), copy(acts_v, acts, 11)]
    for item in more:
        item.start()
    for j in range(4):
        part = slice(j * 512, (j + 1) * 512)
        xr[:, part] = dot_t(d_v[...], w_v[part, :]).astype(bf16)
    join_rows(xr, wire_v)
    put_numbers([sc[s * E : (s + 1) * E, :] for s in range(CAP)], wire_v)
    last = copy(wire_v, back, 12)
    last.start()
    for item in departures + more + [last]:
        item.wait()


def expert_main(wire, wg, wu, ga):
    args = (wire, wg, wu, ga)
    outs = [
        sds((E, WIRE, 128), bf16),
        sds((SLOTS, D), bf16),
        sds((SLOTS, F), bf16),
        sds((SLOTS, F), bf16),
        sds((SLOTS, F), bf16),
        sds((SLOTS, F), bf16),
    ]
    return pl.pallas_call(
        expert_main_body,
        out_shape=outs,
        in_specs=[pl.BlockSpec(memory_space=pl.ANY)] * 4,
        out_specs=[pl.BlockSpec(memory_space=pl.ANY)] * 6,
        scratch_shapes=[
            pltpu.VMEM((E, WIRE, 128), bf16),
            pltpu.VMEM((D, 2 * F), bf16),
            pltpu.VMEM((SLOTS, F), f32),
            pltpu.VMEM((SLOTS, D), bf16),
            pltpu.VMEM((SLOTS, D), bf16),
            pltpu.VMEM((SLOTS, F), bf16),
            pltpu.VMEM((SLOTS, F), bf16),
            pltpu.VMEM((SLOTS, 2 * F), bf16),
            pltpu.VMEM((SLOTS, 1), f32),
            pltpu.SemaphoreType.DMA((13,)),
        ],
        compiler_params=pltpu.CompilerParams(vmem_limit_bytes=63 * 1024 * 1024),
        cost_estimate=cost(COSTS["expert_main"]),
        name="expert_main",
    )(*args)


def expert_out_body(act, wd, wire, rows):
    for j in range(8):
        cols = slice(j * 256, (j + 1) * 256)
        rows[:, cols] = dot(act[...], wd[:, cols]).astype(bf16)
    join_rows(rows, wire)


def expert_out(act, wd):
    return call(
        expert_out_body,
        "expert_out",
        [sds((E, CAP * SEG, 128), bf16)],
        [pltpu.VMEM((SLOTS, D), bf16)],
        (act, wd),
    )[0]


def combine_body(
    where, experts, slots, gate_list, wire, hidden, n2, probs, gates, ids, og, g2, wr,
    ghid, gatt, grouter, gg2, sums, gn2,
):
    sum_rows(wire, experts, slots, gate_list, sums)
    scores = get_numbers(wire)
    lane = lax.broadcasted_iota(jnp.int32, (T, E), 1)
    grads = []
    for k in range(4):
        hot = jnp.where(lane == ids[:, k : k + 1], 1.0, 0.0)
        rows = lax.dot_general(
            hot, scores, (((1,), (0,)), ((), ())),
            precision=lax.Precision.HIGHEST, preferred_element_type=f32,
        )
        picked = jnp.where(lane == ids[:, 4 + k : 5 + k], rows, 0.0)
        grads.append(jnp.sum(picked, axis=-1, keepdims=True))
    inner = sum(grads[k] * gates[:, k : k + 1] for k in range(4))
    inverse = 1.0 / gates[:, 4:5]
    grad_probs = jnp.zeros((T, E), f32)
    for k in range(4):
        grad_probs = jnp.where(
            lane == ids[:, k : k + 1], (grads[k] - inner) * inverse, grad_probs
        )
    p = probs[...]
    gl = (p * (grad_probs - jnp.sum(p * grad_probs, axis=-1, keepdims=True))).astype(bf16)
    for h in range(2):
        tokens = slice(h * 64, (h + 1) * 64)
        gn2[tokens, :] = sums[h * 1024 : (h + 1) * 1024, :].reshape(64, D)
    gn2[...] += dot_t(gl, wr[...])
    c = gn2[...]
    v = hidden[...]
    r = lax.rsqrt(jnp.mean(v * v, axis=-1, keepdims=True) + EPS)
    u = c * g2[...]
    m = jnp.mean(u * v, axis=-1, keepdims=True)
    total = og[...].astype(f32) + r * u - v * (r * r * r * m)
    ghid[...] = total
    gatt[...] = total.astype(bf16)
    gg2[...] = jnp.sum(c * (v * r), axis=0, keepdims=True)
    for j in range(SEG):
        cols = slice(j * 128, (j + 1) * 128)
        grouter[cols, :] = dot(n2[:, cols].astype(f32).T.astype(bf16), gl).astype(bf16)


def combine(*args):
    return call(
        combine_body,
        "combine_grads",
        [sds((T, D), f32), sds((T, D), bf16), sds((D, E), bf16), sds((1, D), f32)],
        [pltpu.VMEM((T * SEG, 128), f32), pltpu.VMEM((T, D), f32)],
        args,
        smem=(0, 1, 2, 3),
    )


def result_body(experts, slots, gate_list, wire, hidden, out, sums):
    sum_rows(wire, experts, slots, gate_list, sums)
    for h in range(2):
        tokens = slice(h * 64, (h + 1) * 64)
        mixture = sums[h * 1024 : (h + 1) * 1024, :].reshape(64, D)
        out[tokens, :] = (hidden[tokens, :] + mixture).astype(bf16)


def result_rows(*args):
    return call(
        result_body,
        "result",
        [sds((T, D), bf16)],
        [pltpu.VMEM((T * SEG, 128), f32)],
        args,
        smem=(0, 1, 2),
    )[0]


def pre_body(where, *refs):
    blocks, (ot0, ot1, wo, *outs) = refs[:8], refs[8:16]
    dt, (heads, rows_all, wo_v, grads, dt_v, sems) = refs[15], refs[16:]
    copies = Copies(sems)
    arrivals = [copies.bring(ot0, heads.at[:, :HALF]), copies.bring(ot1, heads.at[:, HALF:])]
    columns = []
    waits = []
    for step in range(4):
        start = lax.rem(where[1] + step, 4) * 512
        columns.append(pl.ds(pl.multiple_of(start, 512), 512))
        waits.append(
            [
                copies.bring(
                    blocks[b].at[:, columns[step]],
                    rows_all.at[b * T : (b + 1) * T, columns[step]],
                )
                for b in range(8)
            ]
        )
    last = copies.bring(wo, wo_v)
    for item in arrivals:
        item.wait()
    for step in range(4):
        for item in waits[step]:
            item.wait()
        grad = dot(heads[...], rows_all[:, columns[step]]).astype(bf16)
        for col in range(4):
            grads[step, lax.rem(col + 4 - where[0], 4)] = grad[:, col * 128 : (col + 1) * 128]
        copies.take(grads.at[step], outs[step])
    last.wait()
    dt_v[...] = dot_t(wo_v[...], rows_all[...]).astype(bf16)
    copies.take(dt_v, dt)
    copies.finish()


def pre(where, blocks, ot0, ot1, wo):
    return copy_call(
        pre_body,
        "out_projection_grad",
        [sds((4, 512, 128), bf16)] * 4 + [sds((LH * HEAD, ROWS), bf16)],
        [
            pltpu.VMEM((512, ROWS), bf16),
            pltpu.VMEM((ROWS, D), bf16),
            pltpu.VMEM((512, D), bf16),
            pltpu.VMEM((4, 4, 512, 128), bf16),
            pltpu.VMEM((512, ROWS), bf16),
        ],
        2 + 32 + 1 + 5,
        (where, *blocks, ot0, ot1, wo),
        smem=(0,),
    )


def bwd_body(*refs):
    qh, kh, scales = refs[0:4], refs[4:8], refs[8:12]
    (qt, kt, kn, vn, dt, ot0, ot1, linv, info, cos, sin, gq, gk) = refs[12:25]
    dq0, dq1, dkv, ggq, ggk, mask, wb, sb, dqt, dk, dv, raw, scale = refs[25:]
    for dc in range(2):
        for dy in range(4):
            to = slice(dc * HALF + dy * T, dc * HALF + (dy + 1) * T)
            scale[:, to] = scales[dy][:, dc * T : (dc + 1) * T]
    build_mask(info, mask)
    dk[...] = jnp.zeros_like(dk)
    dv[...] = jnp.zeros_like(dv)
    for half, out in ((0, ot0), (1, ot1)):
        cols = slice(half * HALF, (half + 1) * HALF)
        for h in range(LH):
            heads = slice(h * HEAD, (h + 1) * HEAD)
            part = slice(h * HALF, (h + 1) * HALF)
            scores = dot(kn[...], qt[heads, cols])
            weights = jnp.exp2(scores * LOG2E) * (mask[:, cols] * linv[h : h + 1, cols])
            grad = dt[heads, cols]
            delta = jnp.sum(
                grad.astype(f32) * out[heads, :].astype(f32), axis=0, keepdims=True
            )
            wb[:, part] = weights.astype(bf16)
            sb[:, part] = (weights * (dot(vn[...], grad) - delta)).astype(bf16)
            dqt[heads, cols] = dot(kt[...], sb[:, part])
        grads = jnp.concatenate([dt[h * HEAD : (h + 1) * HEAD, cols] for h in range(LH)], axis=1)
        queries = jnp.concatenate([qt[h * HEAD : (h + 1) * HEAD, cols] for h in range(LH)], axis=1)
        dv[...] += dot_t(wb[...], grads)
        dk[...] += dot_t(sb[...], queries)

    def unrope(v):
        low, high = v[:64], v[64:]
        c, s = cos[...], sin[...]
        return jnp.concatenate([low * c + high * s, high * c - low * s], axis=0)

    def norm_back(n, r, grad, gain):
        gain_grad = jnp.sum(grad * n, axis=1, keepdims=True)
        u = grad * gain
        return r * (u - n * jnp.mean(u * n, axis=0, keepdims=True)), gain_grad

    gain_q, gain_k = column(gq[...]), column(gk[...])
    total = jnp.zeros((HEAD, 1), f32)
    for h in range(LH):
        heads = slice(h * HEAD, (h + 1) * HEAD)
        for dy in range(4):
            for dc in range(2):
                to = slice(dc * HALF + dy * T, dc * HALF + (dy + 1) * T)
                raw[:, to] = qh[dy][heads, dc * T : (dc + 1) * T].astype(f32)
        grad, part = norm_back(raw[...], scale[h : h + 1, :], unrope(dqt[heads, :] * (HEAD ** (-0.5))), gain_q)
        total = total + part
        dq0[heads, :] = grad[:, :HALF].astype(bf16)
        dq1[heads, :] = grad[:, HALF:].astype(bf16)
    ggq[...] = jnp.broadcast_to(total, (HEAD, 128)).T[0:8, :]
    for dy in range(4):
        for dc in range(2):
            to = slice(dc * HALF + dy * T, dc * HALF + (dy + 1) * T)
            raw[:, to] = kh[dy][:, dc * T : (dc + 1) * T].astype(f32)
    grad, part = norm_back(raw[...], scale[LH : LH + 1, :], unrope(dk[...].T), gain_k)
    ggk[...] = jnp.broadcast_to(part, (HEAD, 128)).T[0:8, :]
    dkv[:HEAD, :] = grad.astype(bf16)
    dkv[HEAD:, :] = dv[...].T.astype(bf16)


def bwd(qh, kh, scales, *rest):
    return call(
        bwd_body,
        "attend_grad",
        [
            sds((LH * HEAD, HALF), bf16),
            sds((LH * HEAD, HALF), bf16),
            sds((2 * HEAD, ROWS), bf16),
            sds((8, HEAD), f32),
            sds((8, HEAD), f32),
        ],
        [
            pltpu.VMEM((ROWS, ROWS), f32),
            pltpu.VMEM((ROWS, LH * HALF), bf16),
            pltpu.VMEM((ROWS, LH * HALF), bf16),
            pltpu.VMEM((LH * HEAD, ROWS), f32),
            pltpu.VMEM((ROWS, HEAD), f32),
            pltpu.VMEM((ROWS, HEAD), f32),
            pltpu.VMEM((HEAD, ROWS), f32),
            pltpu.VMEM((8, ROWS), f32),
        ],
        (*qh, *kh, *scales, *rest),
    )


def qkv_grad_body(where, n1t, dq0, dq1, own, sib, out, tot, dt):
    @pl.when(pl.program_id(0) == 0)
    def _():
        tot[:, :HALF] = (own[:, :HALF].astype(f32) + sib[:, HALF:].astype(f32)).astype(bf16)
        tot[:, HALF:] = (own[:, HALF:].astype(f32) + sib[:, :HALF].astype(f32)).astype(bf16)
        dt[:512, :HALF] = dq0[...]
        dt[:512, HALF:] = dq1[...]
        upper = where[2] == 1
        dt[512:576, :] = jnp.where(upper, tot[64:128, :], tot[:64, :])
        dt[576:, :] = jnp.where(upper, tot[192:, :], tot[128:192, :])

    out[...] = dot_t(n1t[...], dt[...]).astype(bf16)


def qkv_grad(where, n1t, dq0, dq1, own, sib):
    return grid_call(
        qkv_grad_body,
        "qkv_weight_grad",
        (2,),
        [
            rows_of((1024, ROWS)),
            whole((512, HALF)),
            whole((512, HALF)),
            whole((2 * HEAD, ROWS)),
            whole((2 * HEAD, ROWS)),
        ],
        [rows_of((1024, 640)), whole((2 * HEAD, ROWS))],
        [sds((D, 640), bf16), sds((2 * HEAD, ROWS), bf16)],
        [pltpu.VMEM((640, ROWS), bf16)],
        (where, n1t, dq0, dq1, own, sib),
        scalars=1,
    )


def widen_body(grads, gq, gkt, gvt):
    gq[...] = grads[:, :512].astype(f32)
    both = grads[:, 512:].astype(f32).T
    gkt[...] = both[:64]
    gvt[...] = both[64:]


def widen(grads):
    return grid_call(
        widen_body,
        "widen_grads",
        (4,),
        [rows_of((512, 640))],
        [rows_of((512, 512)), cols_of((64, 512)), cols_of((64, 512))],
        [sds((D, 512), f32), sds((64, D), f32), sds((64, D), f32)],
        [],
        (grads,),
    )


def add_body(a, b, c, d, *outs):
    for i, out in enumerate(outs):
        out[...] = (
            (a[i].astype(f32) + b[i].astype(f32)) + (c[i].astype(f32) + d[i].astype(f32))
        ).astype(bf16)


def add_parts(parts):
    shape = parts[0].shape[1:]
    return call(add_body, "add_parts", [sds(shape, bf16)] * 4, [], tuple(parts))


def normed_grad_body(wa, wb, wkv, dq0, dqr, tot, n0, n1, n2, n3, b0, b1, b2, b3, gg1, grads):
    @pl.when(pl.program_id(0) == 0)
    def _():
        flip(dq0, grads, 0, 0)
        flip(dqr, grads, 0, 512)
        flip(tot, grads, 0, 1024)

    total = (
        dot(grads[:, :512], wa[...])
        + dot(grads[:, 512:1024], wb[...])
        + dot(grads[:, 1024:], wkv[...])
    )
    gain = jnp.zeros((1, 512), f32)
    for dy, (out, rows) in enumerate(((b0, n0), (b1, n1), (b2, n2), (b3, n3))):
        part = total[dy * T : (dy + 1) * T, :]
        out[...] = part.astype(bf16)
        gain = gain + jnp.sum(part * rows[...].astype(f32), axis=0, keepdims=True)
    gg1[...] = jnp.broadcast_to(gain, (8, 512))


def normed_grad(wa, wb, wkv, dq0, dqr, tot, n1):
    return grid_call(
        normed_grad_body,
        "normed_grad",
        (4,),
        [
            cols_of((512, 512)),
            cols_of((512, 512)),
            cols_of((256, 512)),
            whole((512, HALF)),
            whole((512, HALF)),
            whole((2 * HEAD, HALF)),
        ]
        + [cols_of((T, 512))] * 4,
        [cols_of((T, 512))] * 4 + [cols_of((8, 512))],
        [sds((T, D), bf16)] * 4 + [sds((8, D), f32)],
        [pltpu.VMEM((HALF, 1280), bf16)],
        (wa, wb, wkv, dq0, dqr, tot, *n1),
    )


def add_last_body(a, b, c, d, small, out):
    out[:512, :] = (
        (a[...].astype(f32) + b[...].astype(f32)) + (c[...].astype(f32) + d[...].astype(f32))
    ).astype(bf16)

    def add(i, total):
        return total + small[i].astype(f32)

    total = lax.fori_loop(0, E, add, jnp.zeros((24, 128), f32))
    numbers = total[SEG : SEG + 1] + total[SEG + 1 : SEG + 2]
    first = numbers.astype(bf16).astype(f32)
    out[512:, :] = jnp.concatenate(
        [total[:SEG], first, numbers - first, jnp.zeros((14, 128), f32)], axis=0
    ).astype(bf16)


def add_last(parts, small):
    args = (*parts, small)
    return call(add_last_body, "add_last", [sds((544, 128), bf16)], [], args)[0]


def stack_body(a, b, c, d, out):
    for i, part in enumerate((a, b, c, d)):
        out[i] = part[...]


def stack(parts):
    shape = (4, *parts[0].shape)
    return call(stack_body, "stack_parts", [sds(shape, bf16)], [], tuple(parts))[0]


def place_out_body(where, c0, c1, c2, c3, out):
    for dx, chunks in enumerate((c0, c1, c2, c3)):
        for dz in range(4):
            chunk = lax.rem(where[1] + dx, 4) * 4 + lax.rem(where[0] + dz, 4)
            cols = pl.ds(pl.multiple_of(chunk * 128, 128), 128)
            out[:, cols] = chunks[dz, :512, :].astype(f32)


def place_out(where, chunks):
    return call(
        place_out_body,
        "place_output_grads",
        [sds((512, D), f32)],
        [],
        (where, *chunks),
        smem=(0,),
    )[0]


def final_body(b0, b1, b2, b3, x0, ghid, g1, out):
    c = (b0[...].astype(f32) + b1[...].astype(f32)) + (b2[...].astype(f32) + b3[...].astype(f32))
    v = x0[...].astype(f32)
    r = lax.rsqrt(jnp.mean(v * v, axis=-1, keepdims=True) + EPS)
    u = c * g1[...]
    m = jnp.mean(u * v, axis=-1, keepdims=True)
    out[...] = ghid[...] + r * u - v * (r * r * r * m)


def final(b, x0, ghid, g1):
    return call(final_body, "input_grad", [sds((T, D), f32)], [], (*b, x0, ghid, g1))[0]


def gather_small_body(c0, c1, c2, c3, out):
    for dx, chunks in enumerate((c0, c1, c2, c3)):
        for dz in range(4):
            out[dx * 4 + dz] = chunks[dz, 512:, :]


def gather_small(chunks):
    return call(
        gather_small_body, "gather_small", [sds((16, 32, 128), bf16)], [], tuple(chunks)
    )[0]


def place_small_body(where, a0, a1, a2, a3, b, router, numbers):
    for dy, own in enumerate((a0, a1, a2, a3)):
        for dc in range(2):
            shard = lax.rem(where[3] + dy, 4) * 2 + lax.rem(where[2] + dc, 2)
            for dx in range(4):
                for dz in range(4):
                    expert = lax.rem(where[0] + dz, 4) * 4 + lax.rem(where[1] + dx, 4)
                    index = expert * 8 + shard
                    part = own[dx * 4 + dz] if dc == 0 else b[dy, dx * 4 + dz]
                    part = part.astype(f32)
                    rows = pl.ds(pl.multiple_of(index * SEG, SEG), SEG)
                    router[rows, :] = part[:SEG]
                    numbers[pl.ds(index, 1), :] = part[SEG : SEG + 1] + part[SEG + 1 : SEG + 2]


def place_small(where, own, sib):
    return call(
        place_small_body,
        "place_small",
        [sds((D, E), f32), sds((E, 128), f32)],
        [],
        (where, *own, sib),
        smem=(0,),
    )


def sibling(x):
    return lax.ppermute(x, "shard", [(i, i ^ 1) for i in range(8)])


def from_chip(x, dy):
    return lax.ppermute(x, "shard", [(i, (i - 2 * dy) % 8) for i in range(8)])


def to_chip(x, dy):
    return lax.ppermute(x, "shard", [(i, (i + 2 * dy) % 8) for i in range(8)])


def exchange(x):
    return lax.all_to_all(x, ALL, split_axis=0, concat_axis=0, tiled=True)


def spread(x):
    return [to_chip(x[d], d) for d in (1, 3, 2)]


def on_expert(x, dz, dx):
    pairs = [
        (z * 4 + c, ((z + dz) % 4) * 4 + (c + dx) % 4) for z in range(4) for c in range(4)
    ]
    return lax.ppermute(x, "expert", pairs)


def move(x, axis, distance):
    return on_expert(x, distance, 0) if axis == 0 else on_expert(x, 0, distance)


def collect(parts, axis):
    return [parts[0]] + [move(parts[d], axis, d) for d in (1, 3, 2)]


def share(x, axis):
    return [x] + [move(x, axis, (4 - d) % 4) for d in (1, 2, 3)]


def after(value, *others):
    return lax.optimization_barrier((value, *others))[0]


def on_device(
    block_input, out_grad, norm1_gain, w_query, w_key, w_value, query_gain, key_gain, w_out,
    norm2_gain, w_router, w_gate, w_up, w_down, seq_lengths, token_places, expert_routes,
):
    shard, owner = lax.axis_index("shard"), lax.axis_index("expert")
    chip, core = shard // 2, shard % 2
    where = jnp.stack([owner // 4, owner % 4, core, chip]).astype(jnp.int32)
    core_id = core.reshape(1)
    g1 = norm1_gain.astype(f32).reshape(1, D)
    g2 = norm2_gain.astype(f32).reshape(1, D)
    gq = query_gain.astype(f32).reshape(1, HEAD)
    gk = key_gain.astype(f32).reshape(1, HEAD)

    x_own = [block_input] + [from_chip(block_input, dy) for dy in (1, 2, 3)]
    x_sib = [sibling(block_input)]

    chips = (chip + jnp.arange(4)) % 4
    order = jnp.concatenate([chips * 2 + core, chips * 2 + 1 - core])
    places = token_places[0].reshape(8, T)[order].reshape(ROWS)
    lengths = seq_lengths[0]
    ends = jnp.cumsum(lengths)
    starts = jnp.sum(
        jnp.where(places[:, None] >= ends[None, :], lengths[None, :], 0), axis=1
    )
    positions = (places - starts).astype(f32)
    info = jnp.concatenate(
        [places[None].astype(f32), starts[None].astype(f32), jnp.zeros((6, ROWS), f32)], axis=0
    )
    inverse_freq = ROPE_BASE ** (-jnp.arange(0, HEAD, 2).astype(f32) / HEAD)
    angles = inverse_freq[:, None] * positions[None, :]
    cos, sin = jnp.cos(angles), jnp.sin(angles)

    ids, ids_t = route_tables(expert_routes.T)
    assign_t = ids_t[8:12]
    expert_list = ids[:, 0:4].reshape(-1)
    slot_list = ids[:, 4:8].reshape(-1)

    wk_t, wv_t = w_key.T, w_value.T
    wk_s, wv_s = sibling(wk_t), sibling(wv_t)
    wq_t = w_query.T
    wq_ts = sibling(wq_t)

    og_wire = pack(out_grad, assign_t)
    x_own, x_sib, og_wire, wq_t, cos, sin, info, wk_s, wv_s = lax.optimization_barrier(
        (x_own, x_sib, og_wire, wq_t, cos, sin, info, wk_s, wv_s)
    )
    x_sib += [sibling(x_own[dy]) for dy in (1, 2, 3)]
    blocks = [side[dy] for dy in range(4) for side in (x_own, x_sib)]
    weights = (g1, wq_t, wk_t, wk_s, wv_t, wv_s, gq, gk, cos, sin)
    *pieces, wkv = qkv((0, 1, 2, 3), core_id, blocks, *weights)
    pieces = [pieces[7 * dy : 7 * dy + 7] for dy in range(4)]
    qh, q, kh, k, v, scales, n1 = zip(*pieces)
    got_grads = exchange(og_wire)
    wo_s = sibling(after(w_out, q[0]))
    ot0, ot1, linv, qt, kt, kn, vn = attend(q, k, v, info)
    blocks = outproj(ot0, sibling(ot1), w_out, wo_s)
    blocks = [blocks[0]] + spread(blocks)
    hidden, n2, probs, gates, wire = router(blocks, block_input, g2, w_router, ids, assign_t)
    got_rows = exchange(wire)

    n1_t = transpose_rows(after(n1, wire))
    gate_list = gates[:, :4].reshape(-1)
    grad_rows, grad_act = expert_grad(after(got_grads, wire), w_down[0])
    got_rows, n1_t, grad_act, gate_list, wq_ts = lax.optimization_barrier(
        (got_rows, n1_t, grad_act, gate_list, wq_ts)
    )

    back, rows, act, scaled_act, dg, du = expert_main(got_rows, w_gate[0], w_up[0], grad_act)
    back_wire = exchange(back)

    rows, act, scaled_act, dg, du = after((rows, act, scaled_act, dg, du), back)
    out_wire = expert_out(act, w_down[0])

    def weight_grad(a, b):
        return lax.dot_general(a, b, (((0,), (0,)), ((), ())), preferred_element_type=f32)

    grad_wgate = weight_grad(rows, dg)
    grad_wup = weight_grad(rows, du)
    grad_wdown = weight_grad(scaled_act, grad_rows)
    back_wire, out_wire, grad_wgate, grad_wup, grad_wdown = lax.optimization_barrier(
        (back_wire, out_wire, grad_wgate, grad_wup, grad_wdown)
    )

    ghid, gatt, grouter, gg2 = combine(
        where, expert_list, slot_list, gate_list, back_wire, hidden, n2, probs, gates, ids,
        out_grad, g2, w_router,
    )
    g_own = [gatt] + [from_chip(gatt, dy) for dy in (1, 2, 3)]
    g_sib = [sibling(block) for block in g_own]
    returned = exchange(after(out_wire, *g_sib))
    *out_parts, dt = pre(where, g_own + g_sib, ot0, ot1, w_out)

    dq0, dq1, dkv, ggq, ggk = bwd(
        qh, kh, scales, qt, kt, kn, vn, dt, ot0, ot1, linv, info, cos, sin, gq, gk
    )
    out_parts = collect(out_parts, 1)
    dq_sib, dkv_sib = sibling(dq1), sibling(dkv)
    gw, dkv_total = qkv_grad(where, n1_t, dq0, dq1, dkv, dkv_sib)
    returned, dq0 = lax.optimization_barrier((returned, dq0))
    blocks = normed_grad(wq_t, wq_ts, wkv, dq0, dq_sib, dkv_total, n1)
    vector = jnp.concatenate([blocks[4][0] / g1[0], gg2[0], ggq[0], ggk[0]])
    per = vector.shape[0] // E
    vector = jnp.pad(vector.reshape(E, 1, per), ((0, 0), (0, 0), (0, 128 - per)))
    first = vector.astype(bf16)
    second = (vector - first.astype(f32)).astype(bf16)
    small = jnp.concatenate(
        [grouter.reshape(E, SEG, E), first, second, jnp.zeros((E, 6, 128), bf16)], axis=1
    )
    small = exchange(small)
    blocks = [blocks[0]] + spread(blocks)
    gw = lax.psum(gw, "expert")
    out_parts = collect(add_parts(out_parts), 0)
    chunks = share(add_last(out_parts, small), 0)
    chunks, blocks = lax.optimization_barrier((chunks, blocks))
    chunks = share(stack(chunks), 1)
    grad_input = final(blocks, block_input, ghid, g1)
    result = result_rows(expert_list, slot_list, gate_list, returned, hidden)
    chunks, grad_input, result = lax.optimization_barrier((chunks, grad_input, result))
    small = gather_small(chunks)
    small = [small] + [from_chip(small, dy) for dy in (1, 2, 3)]
    small, grad_wout = lax.optimization_barrier((small, place_out(where, chunks)))
    grad_router, numbers = place_small(where, small, sibling(jnp.stack(small)))
    vector = numbers[:, :per].reshape(-1)
    gw, grad_wout, grad_router, vector = lax.optimization_barrier(
        (gw, grad_wout, grad_router, vector)
    )
    grad_wq, grad_wk, grad_wv = widen(gw)
    return (
        result,
        grad_input,
        vector[:D],
        grad_wq,
        grad_wk.T,
        grad_wv.T,
        vector[2 * D : 2 * D + HEAD],
        vector[2 * D + HEAD :],
        grad_wout,
        vector[D : 2 * D],
        grad_router,
        grad_wgate[None],
        grad_wup[None],
        grad_wdown[None],
    )


def solution(mesh):
    rows = P(("expert", "shard"), None)
    experts = P(("expert", "shard"), None, None)
    columns = P(None, "shard")
    return jax.shard_map(
        on_device,
        mesh=mesh,
        in_specs=(
            rows, rows, P(), columns, columns, columns, P(), P(), P("shard", None), P(), P(),
            experts, experts, experts, P("expert", None), P("expert", None), rows,
        ),
        out_specs=(
            rows, rows, P(), columns, columns, columns, P(), P(), P("shard", None), P(), P(),
            experts, experts, experts,
        ),
        check_vma=False,
    )
```
